32 devices in a mesh: dp: 2 (over x), fsdp: 16 (over z, y, core).
Axes of the slice: x: 2, y: 2, z: 4, core: 2. Of those that a mesh axis runs over, the one named last changes fastest.
Arguments:
- token_ids: int32 [8192], P(('dp', 'fsdp')), may hold values from 0 to 31999
- seq_lengths: int32 [32, 8], P(('dp', 'fsdp')), may hold values from 0 to 256, as said below
- noise: bfloat16 [8192, 256], P(('dp', 'fsdp')), may hold values from -6 to 6
- noise_level: float32 [8192], P(('dp', 'fsdp')), may hold values from 0.2 to 2
- table: bfloat16 [32000, 256], P('fsdp'), may hold values from -6 to 6
- w_in: bfloat16 [256, 1024], P('fsdp'), may hold values from -0.375 to 0.375
- b_in: bfloat16 [1024], P('fsdp'), may hold values from -3 to 3
- gain_first: bfloat16 [1024], P('fsdp'), may hold values from 0.25 to 1.75
- shift_first: bfloat16 [1024], P('fsdp'), may hold values from -3 to 3
- w_qkv: bfloat16 [1024, 3072], P('fsdp'), may hold values from -0.1875 to 0.1875
- w_out: bfloat16 [1024, 1024], P('fsdp'), may hold values from -0.75 to 0.75
- b_out: bfloat16 [1024], P('fsdp'), may hold values from -3 to 3
- gain_second: bfloat16 [1024], P('fsdp'), may hold values from 0.25 to 1.75
- shift_second: bfloat16 [1024], P('fsdp'), may hold values from -3 to 3
- w_up: bfloat16 [1024, 4096], P('fsdp'), may hold values from -0.1875 to 0.1875
- b_up: bfloat16 [4096], P('fsdp'), may hold values from -3 to 3
- w_down: bfloat16 [4096, 1024], P('fsdp'), may hold values from -0.09375 to 0.09375
- b_down: bfloat16 [1024], P('fsdp'), may hold values from -3 to 3
- cotangent: bfloat16 [8192, 1024], P(('dp', 'fsdp')), may hold values from -6 to 6
Outputs:
- activations: bfloat16 [8192, 1024], P(('dp', 'fsdp'))
- noise_grad: float32 [8192, 256], P(('dp', 'fsdp'))
- table_grad: float32 [32000, 256], P('fsdp')
- w_in_grad: float32 [256, 1024], P('fsdp')
- b_in_grad: float32 [1024], P('fsdp')
- gain_first_grad: float32 [1024], P('fsdp')
- shift_first_grad: float32 [1024], P('fsdp')
- w_qkv_grad: float32 [1024, 3072], P('fsdp')
- w_out_grad: float32 [1024, 1024], P('fsdp')
- b_out_grad: float32 [1024], P('fsdp')
- gain_second_grad: float32 [1024], P('fsdp')
- shift_second_grad: float32 [1024], P('fsdp')
- w_up_grad: float32 [1024, 4096], P('fsdp')
- b_up_grad: float32 [4096], P('fsdp')
- w_down_grad: float32 [4096, 1024], P('fsdp')
- b_down_grad: float32 [1024], P('fsdp')
The draws below stay inside these ranges and needn't reach their ends.
Inputs may be any that keep to these rules, and one draw needn't show every extreme that they name: `seq_lengths`: each length is a multiple of 8, a row's lengths sum to 64 or more and to 256 at most; in every draw some row holds one sequence of exactly 256 tokens; slots may be empty.
All inputs are finite; a program needn't handle non-finite values.
Results may differ from the reference program's by a relative error of at most 0.014.
Values may be sent and summed in bfloat16 or wider, within the bound.
A program may use at most 192 MiB of HBM per device.

```python
import math
import jax
import jax.numpy as jnp
import numpy as np
from jax import lax

D = 1024
HEADS = 16
HEAD_DIM = 64
FF = 4096
EMB = 256
VOCAB = 32000
TOK_DEV = 256
SLOTS = 8
GROUPS = 32
TOKENS = 8192


def draw_seq_lengths(key, part):
    key = jax.random.fold_in(key, 11)
    unit = TOK_DEV // 32
    key_live, key_cuts, key_full = jax.random.split(key, 3)
    live_count = TOK_DEV - unit * jax.random.randint(key_live, (GROUPS,), 0, 25)
    cut_points = jax.random.randint(key_cuts, (GROUPS, SLOTS - 1), 0, 33) * unit
    cut_points = jnp.sort(jnp.minimum(cut_points, live_count[:, None]), axis=1)
    edges = jnp.concatenate([jnp.zeros((GROUPS, 1), jnp.int32), cut_points.astype(jnp.int32), live_count[:, None].astype(jnp.int32)], axis=1)
    lengths = edges[:, 1:] - edges[:, :-1]
    full_row = jax.random.randint(key_full, (), 0, GROUPS)
    single = jnp.zeros((SLOTS,), jnp.int32).at[0].set(TOK_DEV)
    row_index = jnp.arange(GROUPS)
    return jnp.where((row_index == full_row)[:, None], single[None, :], lengths).astype(jnp.int32)


def place_ends(entries, own_key, low, top_value):
    extent = entries.shape
    spot = [jax.random.randint(jax.random.fold_in(own_key, axis), (), 0, extent[axis]) for axis in range(len(extent))]
    entries = entries.at[tuple(spot)].set(low)
    longest = extent.index(max(extent))
    spot[longest] = (spot[longest] + 1) % extent[longest]
    return entries.at[tuple(spot)].set(top_value)


def levels(key, dims, pieces, low, largest):
    def one(dim, shards_of):
        draws = jax.random.uniform(jax.random.fold_in(jax.random.fold_in(key, 6), dim), (shards_of,), jnp.float32, low / len(pieces), largest / len(pieces))
        return jnp.repeat(jnp.exp(draws), dims[dim] // shards_of).reshape((-1,) + (1,) * (len(dims) - dim - 1))

    loudness = one(*pieces[0])
    for cut in pieces[1:]:
        loudness = loudness * one(*cut)
    return loudness


def cumulative_ranks(number_of, slope):
    weights = [(1 << 20) // math.isqrt(standing ** slope) + 1 for standing in range(1, number_of + 1)]
    scale = 1 + sum(weights) // (1 << 30)
    return np.cumsum(np.array([max(1, weight // scale) for weight in weights]))


def ranked(own_key, shape, number_of, skew):
    listing = cumulative_ranks(number_of, skew)
    pick = jax.random.randint(jax.random.fold_in(own_key, 1), shape, 0, int(listing[number_of - 1]))
    standing = jnp.searchsorted(jnp.asarray(listing, jnp.int32), pick, side="right")
    return jax.random.permutation(jax.random.fold_in(own_key, 2), number_of)[standing].astype(jnp.int32)


def bell_draw(key, shape, scale, most, shards=(), held_as=jnp.bfloat16):
    level = levels(key, shape, shards, -0.22, 0.18) if shards else 1.0
    values = jax.random.normal(key, shape, jnp.float32) * scale * level
    return jnp.minimum(jnp.maximum(values, -most), most).astype(held_as)


def setup_inputs(seed: int = 0) -> dict:
    streams_of = jax.random.split(jax.random.key(seed), 20)
    token_ids = place_ends(ranked(streams_of[0], (TOKENS,), VOCAB, 2), jax.random.fold_in(streams_of[0], 3), 0, VOCAB - 1).astype(jnp.int32)
    seq_lengths = draw_seq_lengths(jax.random.fold_in(streams_of[19], 71), 0)
    noise = bell_draw(streams_of[2], (TOKENS, EMB), 1.0, 6.0, ((0, 32),))
    noise_level = jnp.clip(jnp.exp(math.log(2.0) - 2.3025851 * jax.random.uniform(streams_of[3], (TOKENS,), jnp.float32) ** levels(streams_of[3], (TOKENS,), ((0, 32),), -0.2, 0.2)), 0.2, 2.0)
    table = bell_draw(streams_of[4], (VOCAB, EMB), 1.0, 6.0, ((0, 16),))
    w_in = bell_draw(streams_of[5], (EMB, D), EMB ** -0.5, 0.375, ((0, 16),))
    b_in = bell_draw(streams_of[6], (D,), 0.3, 3.0, ((0, 16),))
    gain_first = jnp.clip(1.0 + 0.15 * jax.random.normal(streams_of[7], (D,), jnp.float32), 0.25, 1.75).astype(jnp.bfloat16)
    shift_first = bell_draw(streams_of[8], (D,), 0.3, 3.0, ((0, 16),))
    w_qkv = bell_draw(streams_of[9], (D, 3 * D), D ** -0.5, 0.1875, ((0, 16),))
    w_out = bell_draw(streams_of[10], (D, D), (D // 16) ** -0.5, 0.75, ((0, 16),))
    b_out = bell_draw(streams_of[11], (D,), 0.3, 3.0, ((0, 16),))
    gain_second = jnp.clip(1.0 + 0.15 * jax.random.normal(streams_of[12], (D,), jnp.float32), 0.25, 1.75).astype(jnp.bfloat16)
    shift_second = bell_draw(streams_of[13], (D,), 0.3, 3.0, ((0, 16),))
    w_up = bell_draw(streams_of[14], (D, FF), D ** -0.5, 0.1875, ((0, 16),))
    b_up = bell_draw(streams_of[15], (FF,), 0.3, 3.0, ((0, 16),))
    w_down = bell_draw(streams_of[16], (FF, D), FF ** -0.5, 0.09375, ((0, 16),))
    b_down = bell_draw(streams_of[17], (D,), 0.3, 3.0, ((0, 16),))
    cotangent = bell_draw(streams_of[18], (TOKENS, D), 1.0, 6.0, ((0, 32),))
    return {"token_ids": token_ids, "seq_lengths": seq_lengths, "noise": noise, "noise_level": noise_level, "table": table, "w_in": w_in, "b_in": b_in, "gain_first": gain_first, "shift_first": shift_first, "w_qkv": w_qkv, "w_out": w_out, "b_out": b_out, "gain_second": gain_second, "shift_second": shift_second, "w_up": w_up, "b_up": b_up, "w_down": w_down, "b_down": b_down, "cotangent": cotangent}


@jax.custom_vjp
def low(v):
    return lax.optimization_barrier(v.astype(jnp.bfloat16)).astype(jnp.float32)

@jax.custom_vjp
def low_back(v):
    return v

def low_keep(v):
    return (low(v), None)

def low_pass(kept, grad):
    return (grad,)

def back_keep(v):
    return (v, None)

def back_low(kept, grad):
    return (low(grad),)
low.defvjp(low_keep, low_pass)
low_back.defvjp(back_keep, back_low)
norm_eps = 1e-05

def matmul_hi(left, right):
    return jnp.dot(left, right, precision=lax.Precision.HIGHEST, preferred_element_type=jnp.float32)

def layer_norm(resid, gain, shift):
    centred = resid - lax.optimization_barrier(jnp.mean(resid, axis=-1, keepdims=True))
    spread = lax.optimization_barrier(jnp.mean(centred * centred, axis=-1, keepdims=True))
    return centred * lax.rsqrt(spread + norm_eps) * gain + shift

def segment_ids(length_row):
    seq_ends = jnp.cumsum(length_row, dtype=jnp.int32)
    positions = jnp.arange(TOK_DEV, dtype=jnp.int32)
    return lax.optimization_barrier(jnp.sum((positions[:, None] >= seq_ends[None, :]).astype(jnp.int32), axis=1))

def attend_group(group_pair):
    projected, segment = group_pair
    query_heads = projected[:, :D].reshape(TOK_DEV, HEADS, HEAD_DIM)
    key_heads = projected[:, D:2 * D].reshape(TOK_DEV, HEADS, HEAD_DIM)
    value_heads = projected[:, 2 * D:].reshape(TOK_DEV, HEADS, HEAD_DIM)
    raw_scores = jnp.einsum('qhd,khd->hqk', query_heads, key_heads, precision=lax.Precision.HIGHEST)
    scores = low_back(raw_scores) * 0.125
    same_seq = segment[:, None] == segment[None, :]
    scores = jnp.where(same_seq[None, :, :], scores, -1000000000.0)
    row_max = lax.optimization_barrier(jnp.max(scores, axis=-1, keepdims=True))
    exp_scores = jnp.exp(scores - row_max)
    soft_probs = exp_scores / lax.optimization_barrier(jnp.sum(exp_scores, axis=-1, keepdims=True))
    attended = jnp.einsum('hqk,khd->qhd', low(soft_probs), value_heads, precision=lax.Precision.HIGHEST)
    return attended.reshape(TOK_DEV, D)

def forward(params, noise_in, token_ids, noise_level, segments, live_rows):
    table, w_in, b_in, gain_first, shift_first, w_qkv, w_out, b_out, gain_second, shift_second, w_up, b_up, w_down, b_down = params
    normed_table = table * lax.rsqrt(lax.optimization_barrier(jnp.mean(table * table, axis=1, keepdims=True)) + norm_eps)
    embedded = jnp.take(normed_table, token_ids, axis=0)
    scale_in = lax.rsqrt(1.0 + noise_level * noise_level)[:, None]
    scaled = low((embedded + noise_level[:, None] * noise_in) * scale_in)
    resid_in = low_back(matmul_hi(scaled, w_in) + b_in)
    normed_a = low(layer_norm(resid_in, gain_first, shift_first))
    projected = low(low_back(matmul_hi(normed_a, w_qkv)))
    attended = lax.map(jax.checkpoint(attend_group), (projected.reshape(GROUPS, TOK_DEV, 3 * D), segments))
    attended = low(low_back(attended.reshape(TOKENS, D)))
    resid_mid = resid_in + low_back(matmul_hi(attended, w_out) + b_out)
    normed_b = low(layer_norm(resid_mid, gain_second, shift_second))
    pre_act = low_back(matmul_hi(normed_b, w_up) + b_up)
    hidden = low(jax.nn.gelu(pre_act, approximate=False))
    resid_out = resid_mid + low_back(matmul_hi(hidden, w_down) + b_down)
    return resid_out * live_rows[:, None]

def reference(token_ids, seq_lengths, noise, noise_level, table, w_in, b_in, gain_first, shift_first, w_qkv, w_out, b_out, gain_second, shift_second, w_up, b_up, w_down, b_down, cotangent):
    params = tuple((item.astype(jnp.float32) for item in (table, w_in, b_in, gain_first, shift_first, w_qkv, w_out, b_out, gain_second, shift_second, w_up, b_up, w_down, b_down)))
    segments = jax.vmap(segment_ids)(seq_lengths)
    live_rows = (segments < SLOTS).astype(jnp.float32).reshape(TOKENS)

    def run(param_set, noise_in):
        return forward(param_set, noise_in, token_ids, noise_level, segments, live_rows)
    result, pull = jax.vjp(run, params, noise.astype(jnp.float32))
    grads, noise_grad = pull(cotangent.astype(jnp.float32))
    return (result.astype(jnp.bfloat16), noise_grad, grads[0], grads[1], grads[2], grads[3], grads[4], grads[5], grads[6], grads[7], grads[8], grads[9], grads[10], grads[11], grads[12], grads[13])
```

```python
import jax
import jax.numpy as jnp
from jax import lax
from jax.sharding import PartitionSpec as P

HEADS = 16
VOCAB = 32000


norm_eps = 1e-05


def standardize(resid):
    centred = resid - jnp.mean(resid, axis=-1, keepdims=True)
    spread = jnp.mean(centred * centred, axis=-1, keepdims=True)
    return centred * lax.rsqrt(spread + norm_eps)


def row_normalize(tok_rows):
    return tok_rows * lax.rsqrt(jnp.mean(tok_rows * tok_rows, axis=1, keepdims=True) + norm_eps)


def exact_gelu(pre_act):
    return jax.nn.gelu(pre_act, approximate=False)


def split_heads(projected):
    tok_count = projected.shape[0]
    width = projected.shape[1] // 3
    head_size = width // HEADS
    key_heads = projected[:, width : 2 * width].reshape(tok_count, HEADS, head_size)
    value_heads = projected[:, 2 * width :].reshape(tok_count, HEADS, head_size)
    row_block = min(512, tok_count)
    query_blocks = projected[:, :width].reshape(tok_count // row_block, row_block, HEADS, head_size)
    return (query_blocks, key_heads, value_heads, row_block)


def block_scores(query_block, key_heads, seg_block, segment):
    raw_scores = (
        jnp.einsum("qhd,khd->hqk", query_block, key_heads, preferred_element_type=jnp.float32)
        * 0.125
    )
    same_seq = seg_block[:, None] == segment[None, :]
    return jnp.where(same_seq[None, :, :], raw_scores, -1000000000.0)


def attention_forward(projected, segment):
    query_blocks, key_heads, value_heads, row_block = split_heads(projected)
    seg_blocks = segment.reshape(-1, row_block)

    def block_step(items_in):
        query_block, seg_block = items_in
        scores = block_scores(query_block, key_heads, seg_block, segment)
        row_max = jnp.max(scores, axis=-1, keepdims=True)
        exp_scores = jnp.exp(scores - row_max)
        row_total = jnp.sum(exp_scores, axis=-1, keepdims=True)
        soft_probs = (exp_scores / row_total).astype(jnp.bfloat16)
        attended = jnp.einsum(
            "hqk,khd->qhd", soft_probs, value_heads, preferred_element_type=jnp.float32
        )
        return (attended, (row_max + jnp.log(row_total))[:, :, 0])

    attended, log_total = lax.map(block_step, (query_blocks, seg_blocks))
    return (attended.reshape(projected.shape[0], -1), log_total)


def attention_backward(projected, segment, log_total, grad_attended):
    query_blocks, key_heads, value_heads, row_block = split_heads(projected)
    seg_blocks = segment.reshape(-1, row_block)
    grad_blocks = grad_attended.reshape(query_blocks.shape)

    def block_step(totals, items_in):
        grad_keys, grad_values = totals
        query_block, seg_block, log_block, grad_block = items_in
        scores = block_scores(query_block, key_heads, seg_block, segment)
        soft_probs = jnp.exp(scores - log_block[:, :, None])
        grad_values = grad_values + jnp.einsum(
            "hqk,qhd->khd",
            soft_probs.astype(jnp.bfloat16),
            grad_block,
            preferred_element_type=jnp.float32,
        )
        grad_probs = jnp.einsum(
            "qhd,khd->hqk", grad_block, value_heads, preferred_element_type=jnp.float32
        )
        grad_scores = soft_probs * (
            grad_probs - jnp.sum(grad_probs * soft_probs, axis=-1, keepdims=True)
        )
        scaled_grad = (grad_scores * 0.125).astype(jnp.bfloat16)
        grad_query = jnp.einsum(
            "hqk,khd->qhd", scaled_grad, key_heads, preferred_element_type=jnp.float32
        )
        grad_keys = grad_keys + jnp.einsum(
            "hqk,qhd->khd", scaled_grad, query_block, preferred_element_type=jnp.float32
        )
        return ((grad_keys, grad_values), grad_query.astype(jnp.bfloat16))

    zero_heads = jnp.zeros(key_heads.shape, jnp.float32)
    (grad_keys, grad_values), grad_queries = lax.scan(
        block_step, (zero_heads, zero_heads), (query_blocks, seg_blocks, log_total, grad_blocks)
    )
    tok_count = projected.shape[0]
    return jnp.concatenate(
        [
            grad_queries.reshape(tok_count, -1),
            grad_keys.astype(jnp.bfloat16).reshape(tok_count, -1),
            grad_values.astype(jnp.bfloat16).reshape(tok_count, -1),
        ],
        axis=1,
    )


def shards(
    token_ids,
    seq_lengths,
    noise,
    noise_level,
    table,
    w_in,
    b_in,
    gain_first,
    shift_first,
    w_qkv,
    w_out,
    b_out,
    gain_second,
    shift_second,
    w_up,
    b_up,
    w_down,
    b_down,
    cotangent,
):
    tok_count = token_ids.shape[0]
    row_count = table.shape[0]
    group_ids = lax.all_gather(token_ids, "fsdp", axis=0, tiled=True)
    first_row = lax.axis_index("fsdp") * row_count
    owned = (group_ids[:, None] == first_row + jnp.arange(row_count)[None, :]).astype(jnp.bfloat16)
    owned_rows = jnp.dot(owned, table, preferred_element_type=jnp.float32).astype(jnp.bfloat16)
    tok_rows = lax.psum_scatter(owned_rows, "fsdp", scatter_dimension=0, tiled=True)
    tok_rows = tok_rows.astype(jnp.float32)
    vectors = (b_in, gain_first, shift_first, b_out, gain_second, shift_second, b_up, b_down)
    vec_all = lax.all_gather(jnp.concatenate(vectors), "fsdp", axis=0, tiled=False)
    vec_at = [0]
    for vector in vectors:
        vec_at.append(vec_at[-1] + vector.shape[0])
    (
        b_in_all,
        gain_first_all,
        shift_first_all,
        b_out_all,
        gain_second_all,
        shift_second_all,
        b_up_all,
        b_down_all,
    ) = [vec_all[:, lo:hi].reshape(-1) for lo, hi in zip(vec_at[:-1], vec_at[1:])]
    w_in_all = lax.all_gather(w_in, "fsdp", axis=0, tiled=True)
    w_qkv_all = lax.all_gather(w_qkv, "fsdp", axis=0, tiled=True)
    w_out_all = lax.all_gather(w_out, "fsdp", axis=0, tiled=True)
    w_up_all = lax.all_gather(w_up, "fsdp", axis=0, tiled=True)
    w_down_all = lax.all_gather(w_down, "fsdp", axis=0, tiled=True)
    seq_ends = jnp.cumsum(seq_lengths[0], dtype=jnp.int32)
    positions = jnp.arange(tok_count, dtype=jnp.int32)
    segment = jnp.sum((positions[:, None] >= seq_ends[None, :]).astype(jnp.int32), axis=1)
    live_rows = (segment < seq_lengths.shape[1]).astype(jnp.float32)[:, None]
    embedded = row_normalize(tok_rows)
    scale_in = lax.rsqrt(1.0 + noise_level * noise_level)[:, None]
    scaled = ((embedded + noise_level[:, None] * noise.astype(jnp.float32)) * scale_in).astype(
        jnp.bfloat16
    )
    resid_in = jnp.dot(scaled, w_in_all, preferred_element_type=jnp.float32) + b_in_all.astype(
        jnp.float32
    )
    std_first, first_pull = jax.vjp(standardize, resid_in)
    normed_a = (
        std_first * gain_first_all.astype(jnp.float32) + shift_first_all.astype(jnp.float32)
    ).astype(jnp.bfloat16)
    projected = jnp.dot(normed_a, w_qkv_all, preferred_element_type=jnp.float32).astype(
        jnp.bfloat16
    )
    attended, log_total = attention_forward(projected, segment)
    attended = attended.astype(jnp.bfloat16)
    resid_mid = (
        resid_in
        + jnp.dot(attended, w_out_all, preferred_element_type=jnp.float32)
        + b_out_all.astype(jnp.float32)
    )
    std_second, second_pull = jax.vjp(standardize, resid_mid)
    normed_b = (
        std_second * gain_second_all.astype(jnp.float32) + shift_second_all.astype(jnp.float32)
    ).astype(jnp.bfloat16)
    pre_act = jnp.dot(normed_b, w_up_all, preferred_element_type=jnp.float32) + b_up_all.astype(
        jnp.float32
    )
    activated, gelu_pull = jax.vjp(exact_gelu, pre_act)
    hidden = activated.astype(jnp.bfloat16)
    resid_out = (
        resid_mid
        + jnp.dot(hidden, w_down_all, preferred_element_type=jnp.float32)
        + b_down_all.astype(jnp.float32)
    )
    activations = (resid_out * live_rows).astype(jnp.bfloat16)
    grad_out = cotangent.astype(jnp.float32) * live_rows
    grad_down = grad_out.astype(jnp.bfloat16)
    b_down_term = jnp.sum(grad_down.astype(jnp.float32), axis=0)
    w_down_term = jnp.einsum("tf,td->fd", hidden, grad_down, preferred_element_type=jnp.float32)
    grad_hidden = jnp.einsum("td,fd->tf", grad_down, w_down_all, preferred_element_type=jnp.float32)
    grad_act = gelu_pull(grad_hidden)[0].astype(jnp.bfloat16)
    b_up_term = jnp.sum(grad_act.astype(jnp.float32), axis=0)
    w_up_term = jnp.einsum("td,tf->df", normed_b, grad_act, preferred_element_type=jnp.float32)
    grad_nb = jnp.einsum("tf,df->td", grad_act, w_up_all, preferred_element_type=jnp.float32)
    gain_second_term = jnp.sum(grad_nb * std_second, axis=0)
    shift_second_term = jnp.sum(grad_nb, axis=0)
    grad_mid = grad_out + second_pull(grad_nb * gain_second_all.astype(jnp.float32))[0]
    grad_att = grad_mid.astype(jnp.bfloat16)
    b_out_term = jnp.sum(grad_att.astype(jnp.float32), axis=0)
    w_out_term = jnp.einsum("tc,td->cd", attended, grad_att, preferred_element_type=jnp.float32)
    grad_attended = jnp.einsum(
        "td,cd->tc", grad_att, w_out_all, preferred_element_type=jnp.float32
    ).astype(jnp.bfloat16)
    grad_proj = attention_backward(projected, segment, log_total, grad_attended)
    w_qkv_term = jnp.einsum("td,te->de", normed_a, grad_proj, preferred_element_type=jnp.float32)
    grad_na = jnp.einsum("te,de->td", grad_proj, w_qkv_all, preferred_element_type=jnp.float32)
    gain_first_term = jnp.sum(grad_na * std_first, axis=0)
    shift_first_term = jnp.sum(grad_na, axis=0)
    grad_in = grad_mid + first_pull(grad_na * gain_first_all.astype(jnp.float32))[0]
    grad_pin = grad_in.astype(jnp.bfloat16)
    b_in_term = jnp.sum(grad_pin.astype(jnp.float32), axis=0)
    w_in_term = jnp.einsum("te,td->ed", scaled, grad_pin, preferred_element_type=jnp.float32)
    grad_scaled = jnp.einsum("td,ed->te", grad_pin, w_in_all, preferred_element_type=jnp.float32)
    noise_grad = grad_scaled * noise_level[:, None] * scale_in
    grad_embedded = grad_scaled * scale_in
    all_ids = lax.all_gather(token_ids, ("dp", "fsdp"), axis=0, tiled=True)
    all_grads = lax.all_gather(
        grad_embedded.astype(jnp.bfloat16), ("dp", "fsdp"), axis=0, tiled=True
    )
    owners = (first_row + jnp.arange(row_count)[:, None] == all_ids[None, :]).astype(jnp.bfloat16)
    row_grad = jnp.dot(owners, all_grads, preferred_element_type=jnp.float32)
    own_table = table.astype(jnp.float32)
    unused_rows, table_pull = jax.vjp(row_normalize, own_table)
    table_part = table_pull(row_grad)[0]

    def reduce_matrix(term):
        part = lax.psum_scatter(
            term.astype(jnp.bfloat16), "fsdp", scatter_dimension=0, tiled=True
        )
        return lax.psum(part, "dp").astype(jnp.float32)

    vec_terms = (
        b_in_term,
        gain_first_term,
        shift_first_term,
        b_out_term,
        gain_second_term,
        shift_second_term,
        b_up_term,
        b_down_term,
    )
    shard_count = lax.axis_size("fsdp")
    vec_term = jnp.concatenate([v.reshape(shard_count, -1) for v in vec_terms], axis=1)
    vec_part = lax.psum(vec_term, ("dp", "fsdp"))
    own_vec = lax.dynamic_index_in_dim(vec_part, lax.axis_index("fsdp"), 0, keepdims=False)
    vec_grads = [own_vec[lo:hi] for lo, hi in zip(vec_at[:-1], vec_at[1:])]
    return (
        activations,
        noise_grad,
        table_part,
        reduce_matrix(w_in_term),
        vec_grads[0],
        vec_grads[1],
        vec_grads[2],
        reduce_matrix(w_qkv_term),
        reduce_matrix(w_out_term),
        vec_grads[3],
        vec_grads[4],
        vec_grads[5],
        reduce_matrix(w_up_term),
        vec_grads[6],
        reduce_matrix(w_down_term),
        vec_grads[7],
    )


def solution(mesh):
    in_specs = (
        P(("dp", "fsdp")),
        P(("dp", "fsdp"), None),
        P(("dp", "fsdp"), None),
        P(("dp", "fsdp")),
        P("fsdp", None),
        P("fsdp", None),
        P("fsdp"),
        P("fsdp"),
        P("fsdp"),
        P("fsdp", None),
        P("fsdp", None),
        P("fsdp"),
        P("fsdp"),
        P("fsdp"),
        P("fsdp", None),
        P("fsdp"),
        P("fsdp", None),
        P("fsdp"),
        P(("dp", "fsdp"), None),
    )
    out_specs = (
        P(("dp", "fsdp"), None),
        P(("dp", "fsdp"), None),
        P("fsdp", None),
        P("fsdp", None),
        P("fsdp"),
        P("fsdp"),
        P("fsdp"),
        P("fsdp", None),
        P("fsdp", None),
        P("fsdp"),
        P("fsdp"),
        P("fsdp"),
        P("fsdp", None),
        P("fsdp"),
        P("fsdp", None),
        P("fsdp"),
    )
    return jax.shard_map(shards, mesh=mesh, in_specs=in_specs, out_specs=out_specs, check_vma=False)
```

```python
import jax
import jax.numpy as jnp
from jax import lax
from jax.experimental import pallas as pl
from jax.experimental.pallas import tpu as pltpu
from jax.sharding import PartitionSpec as P

HEADS = 16
VOCAB = 32000


norm_eps = 1e-05


def standardize(resid):
    centred = resid - jnp.mean(resid, axis=-1, keepdims=True)
    spread = jnp.mean(centred * centred, axis=-1, keepdims=True)
    return centred * lax.rsqrt(spread + norm_eps)


def row_normalize(tok_rows):
    return tok_rows * lax.rsqrt(jnp.mean(tok_rows * tok_rows, axis=1, keepdims=True) + norm_eps)


def exact_gelu(pre_act):
    return jax.nn.gelu(pre_act, approximate=False)


def split_heads(projected):
    tok_count = projected.shape[0]
    width = projected.shape[1] // 3
    head_size = width // HEADS
    key_heads = projected[:, width : 2 * width].reshape(tok_count, HEADS, head_size)
    value_heads = projected[:, 2 * width :].reshape(tok_count, HEADS, head_size)
    row_block = min(512, tok_count)
    query_blocks = projected[:, :width].reshape(tok_count // row_block, row_block, HEADS, head_size)
    return (query_blocks, key_heads, value_heads, row_block)


def block_scores(query_block, key_heads, seg_block, segment):
    raw_scores = (
        jnp.einsum("qhd,khd->hqk", query_block, key_heads, preferred_element_type=jnp.float32)
        * 0.125
    )
    same_seq = seg_block[:, None] == segment[None, :]
    return jnp.where(same_seq[None, :, :], raw_scores, -1000000000.0)


def attention_forward(projected, segment):
    query_blocks, key_heads, value_heads, row_block = split_heads(projected)
    seg_blocks = segment.reshape(-1, row_block)

    def block_step(items_in):
        query_block, seg_block = items_in
        scores = block_scores(query_block, key_heads, seg_block, segment)
        row_max = jnp.max(scores, axis=-1, keepdims=True)
        exp_scores = jnp.exp(scores - row_max)
        row_total = jnp.sum(exp_scores, axis=-1, keepdims=True)
        soft_probs = (exp_scores / row_total).astype(jnp.bfloat16)
        attended = jnp.einsum(
            "hqk,khd->qhd", soft_probs, value_heads, preferred_element_type=jnp.float32
        )
        return (attended, (row_max + jnp.log(row_total))[:, :, 0])

    attended, log_total = lax.map(block_step, (query_blocks, seg_blocks))
    return (attended.reshape(projected.shape[0], -1), log_total)


def attention_backward(projected, segment, log_total, grad_attended):
    query_blocks, key_heads, value_heads, row_block = split_heads(projected)
    seg_blocks = segment.reshape(-1, row_block)
    grad_blocks = grad_attended.reshape(query_blocks.shape)

    def block_step(totals, items_in):
        grad_keys, grad_values = totals
        query_block, seg_block, log_block, grad_block = items_in
        scores = block_scores(query_block, key_heads, seg_block, segment)
        soft_probs = jnp.exp(scores - log_block[:, :, None])
        grad_values = grad_values + jnp.einsum(
            "hqk,qhd->khd",
            soft_probs.astype(jnp.bfloat16),
            grad_block,
            preferred_element_type=jnp.float32,
        )
        grad_probs = jnp.einsum(
            "qhd,khd->hqk", grad_block, value_heads, preferred_element_type=jnp.float32
        )
        grad_scores = soft_probs * (
            grad_probs - jnp.sum(grad_probs * soft_probs, axis=-1, keepdims=True)
        )
        scaled_grad = (grad_scores * 0.125).astype(jnp.bfloat16)
        grad_query = jnp.einsum(
            "hqk,khd->qhd", scaled_grad, key_heads, preferred_element_type=jnp.float32
        )
        grad_keys = grad_keys + jnp.einsum(
            "hqk,qhd->khd", scaled_grad, query_block, preferred_element_type=jnp.float32
        )
        return ((grad_keys, grad_values), grad_query.astype(jnp.bfloat16))

    zero_heads = jnp.zeros(key_heads.shape, jnp.float32)
    (grad_keys, grad_values), grad_queries = lax.scan(
        block_step, (zero_heads, zero_heads), (query_blocks, seg_blocks, log_total, grad_blocks)
    )
    tok_count = projected.shape[0]
    return jnp.concatenate(
        [
            grad_queries.reshape(tok_count, -1),
            grad_keys.astype(jnp.bfloat16).reshape(tok_count, -1),
            grad_values.astype(jnp.bfloat16).reshape(tok_count, -1),
        ],
        axis=1,
    )


def shards(
    token_ids,
    seq_lengths,
    noise,
    noise_level,
    table,
    w_in,
    b_in,
    gain_first,
    shift_first,
    w_qkv,
    w_out,
    b_out,
    gain_second,
    shift_second,
    w_up,
    b_up,
    w_down,
    b_down,
    cotangent,
):
    tok_count = token_ids.shape[0]
    row_count = table.shape[0]
    group_ids = lax.all_gather(token_ids, "fsdp", axis=0, tiled=True)
    first_row = lax.axis_index("fsdp") * row_count
    owned = (group_ids[:, None] == first_row + jnp.arange(row_count)[None, :]).astype(jnp.bfloat16)
    owned_rows = jnp.dot(owned, table, preferred_element_type=jnp.float32).astype(jnp.bfloat16)
    tok_rows = lax.psum_scatter(owned_rows, "fsdp", scatter_dimension=0, tiled=True)
    tok_rows = tok_rows.astype(jnp.float32)
    vectors = (b_in, gain_first, shift_first, b_out, gain_second, shift_second, b_up, b_down)
    vec_all = lax.all_gather(jnp.concatenate(vectors), "fsdp", axis=0, tiled=False)
    vec_at = [0]
    for vector in vectors:
        vec_at.append(vec_at[-1] + vector.shape[0])
    (
        b_in_all,
        gain_first_all,
        shift_first_all,
        b_out_all,
        gain_second_all,
        shift_second_all,
        b_up_all,
        b_down_all,
    ) = [vec_all[:, lo:hi].reshape(-1) for lo, hi in zip(vec_at[:-1], vec_at[1:])]
    w_in_all = lax.all_gather(w_in, "fsdp", axis=0, tiled=True)
    w_qkv_all = lax.all_gather(w_qkv, "fsdp", axis=0, tiled=True)
    w_out_all = lax.all_gather(w_out, "fsdp", axis=0, tiled=True)
    w_up_all = lax.all_gather(w_up, "fsdp", axis=0, tiled=True)
    w_down_all = lax.all_gather(w_down, "fsdp", axis=0, tiled=True)
    seq_ends = jnp.cumsum(seq_lengths[0], dtype=jnp.int32)
    positions = jnp.arange(tok_count, dtype=jnp.int32)
    segment = jnp.sum((positions[:, None] >= seq_ends[None, :]).astype(jnp.int32), axis=1)
    live_rows = (segment < seq_lengths.shape[1]).astype(jnp.float32)[:, None]
    embedded = row_normalize(tok_rows)
    scale_in = lax.rsqrt(1.0 + noise_level * noise_level)[:, None]
    scaled = ((embedded + noise_level[:, None] * noise.astype(jnp.float32)) * scale_in).astype(
        jnp.bfloat16
    )
    resid_in = jnp.dot(scaled, w_in_all, preferred_element_type=jnp.float32) + b_in_all.astype(
        jnp.float32
    )
    std_first, first_pull = jax.vjp(standardize, resid_in)
    normed_a = (
        std_first * gain_first_all.astype(jnp.float32) + shift_first_all.astype(jnp.float32)
    ).astype(jnp.bfloat16)
    projected = jnp.dot(normed_a, w_qkv_all, preferred_element_type=jnp.float32).astype(
        jnp.bfloat16
    )
    attended, log_total = attention_forward(projected, segment)
    attended = attended.astype(jnp.bfloat16)
    resid_mid = (
        resid_in
        + jnp.dot(attended, w_out_all, preferred_element_type=jnp.float32)
        + b_out_all.astype(jnp.float32)
    )
    std_second, second_pull = jax.vjp(standardize, resid_mid)
    normed_b = (
        std_second * gain_second_all.astype(jnp.float32) + shift_second_all.astype(jnp.float32)
    ).astype(jnp.bfloat16)
    pre_act = jnp.dot(normed_b, w_up_all, preferred_element_type=jnp.float32) + b_up_all.astype(
        jnp.float32
    )
    activated, gelu_pull = jax.vjp(exact_gelu, pre_act)
    hidden = activated.astype(jnp.bfloat16)
    resid_out = (
        resid_mid
        + jnp.dot(hidden, w_down_all, preferred_element_type=jnp.float32)
        + b_down_all.astype(jnp.float32)
    )
    activations = (resid_out * live_rows).astype(jnp.bfloat16)
    grad_out = cotangent.astype(jnp.float32) * live_rows
    grad_down = grad_out.astype(jnp.bfloat16)
    b_down_term = jnp.sum(grad_down.astype(jnp.float32), axis=0)
    w_down_term = jnp.einsum("tf,td->fd", hidden, grad_down, preferred_element_type=jnp.float32)
    grad_hidden = jnp.einsum("td,fd->tf", grad_down, w_down_all, preferred_element_type=jnp.float32)
    grad_act = gelu_pull(grad_hidden)[0].astype(jnp.bfloat16)
    b_up_term = jnp.sum(grad_act.astype(jnp.float32), axis=0)
    w_up_term = jnp.einsum("td,tf->df", normed_b, grad_act, preferred_element_type=jnp.float32)
    grad_nb = jnp.einsum("tf,df->td", grad_act, w_up_all, preferred_element_type=jnp.float32)
    gain_second_term = jnp.sum(grad_nb * std_second, axis=0)
    shift_second_term = jnp.sum(grad_nb, axis=0)
    grad_mid = grad_out + second_pull(grad_nb * gain_second_all.astype(jnp.float32))[0]
    grad_att = grad_mid.astype(jnp.bfloat16)
    b_out_term = jnp.sum(grad_att.astype(jnp.float32), axis=0)
    w_out_term = jnp.einsum("tc,td->cd", attended, grad_att, preferred_element_type=jnp.float32)
    grad_attended = jnp.einsum(
        "td,cd->tc", grad_att, w_out_all, preferred_element_type=jnp.float32
    ).astype(jnp.bfloat16)
    grad_proj = attention_backward(projected, segment, log_total, grad_attended)
    w_qkv_term = jnp.einsum("td,te->de", normed_a, grad_proj, preferred_element_type=jnp.float32)
    grad_na = jnp.einsum("te,de->td", grad_proj, w_qkv_all, preferred_element_type=jnp.float32)
    gain_first_term = jnp.sum(grad_na * std_first, axis=0)
    shift_first_term = jnp.sum(grad_na, axis=0)
    grad_in = grad_mid + first_pull(grad_na * gain_first_all.astype(jnp.float32))[0]
    grad_pin = grad_in.astype(jnp.bfloat16)
    b_in_term = jnp.sum(grad_pin.astype(jnp.float32), axis=0)
    w_in_term = jnp.einsum("te,td->ed", scaled, grad_pin, preferred_element_type=jnp.float32)
    grad_scaled = jnp.einsum("td,ed->te", grad_pin, w_in_all, preferred_element_type=jnp.float32)
    noise_grad = grad_scaled * noise_level[:, None] * scale_in
    grad_embedded = grad_scaled * scale_in
    all_ids = lax.all_gather(token_ids, ("dp", "fsdp"), axis=0, tiled=True)
    all_grads = lax.all_gather(
        grad_embedded.astype(jnp.bfloat16), ("dp", "fsdp"), axis=0, tiled=True
    )
    owners = (first_row + jnp.arange(row_count)[:, None] == all_ids[None, :]).astype(jnp.bfloat16)
    row_grad = jnp.dot(owners, all_grads, preferred_element_type=jnp.float32)
    own_table = table.astype(jnp.float32)
    unused_rows, table_pull = jax.vjp(row_normalize, own_table)
    table_part = table_pull(row_grad)[0]

    def reduce_matrix(term):
        part = lax.psum_scatter(
            term.astype(jnp.bfloat16), "fsdp", scatter_dimension=0, tiled=True
        )
        return lax.psum(part, "dp").astype(jnp.float32)

    vec_terms = (
        b_in_term,
        gain_first_term,
        shift_first_term,
        b_out_term,
        gain_second_term,
        shift_second_term,
        b_up_term,
        b_down_term,
    )
    shard_count = lax.axis_size("fsdp")
    vec_term = jnp.concatenate([v.reshape(shard_count, -1) for v in vec_terms], axis=1)
    vec_part = lax.psum(vec_term, ("dp", "fsdp"))
    own_vec = lax.dynamic_index_in_dim(vec_part, lax.axis_index("fsdp"), 0, keepdims=False)
    vec_grads = [own_vec[lo:hi] for lo, hi in zip(vec_at[:-1], vec_at[1:])]
    return (
        activations,
        noise_grad,
        table_part,
        reduce_matrix(w_in_term),
        vec_grads[0],
        vec_grads[1],
        vec_grads[2],
        reduce_matrix(w_qkv_term),
        reduce_matrix(w_out_term),
        vec_grads[3],
        vec_grads[4],
        vec_grads[5],
        reduce_matrix(w_up_term),
        vec_grads[6],
        reduce_matrix(w_down_term),
        vec_grads[7],
    )


BF = jnp.bfloat16
F32 = jnp.float32
MESH_ID = pl.DeviceIdType.MESH
SEM_COUNT = 400
VMEM_LIMIT = 63 * 2**20
NT = (((1,), (1,)), ((), ()))
TN = (((0,), (0,)), ((), ()))
DIAG, ACROSS, TWIN = 0, 1, 2
FLIPS = ((1, 1), (1, 0), (0, 1))


def mm(a, b):
    return jnp.dot(a, b, preferred_element_type=F32)


def mm_nt(a, b):
    return lax.dot_general(a, b, NT, preferred_element_type=F32)


def mm_tn(a, b):
    return lax.dot_general(a, b, TN, preferred_element_type=F32)


def part(start, size):
    return pl.ds(pl.multiple_of(start, size), size)


def as_row(pair):
    return jnp.concatenate([pair[0:1, :], pair[1:2, :]], axis=1)


def as_col(pair):
    eye = lax.broadcasted_iota(jnp.int32, (128, 128), 0) == lax.broadcasted_iota(
        jnp.int32, (128, 128), 1
    )
    cols = [
        jnp.sum(jnp.where(eye, pair[k : k + 1, :], 0.0), axis=1, keepdims=True) for k in (0, 1)
    ]
    return jnp.concatenate(cols, axis=0)


def norm_parts(v):
    centred = v - jnp.mean(v, axis=-1, keepdims=True)
    rstd = lax.rsqrt(jnp.mean(centred * centred, axis=-1, keepdims=True) + norm_eps)
    return centred * rstd, rstd


def norm_back(u, n, rstd):
    return rstd * (
        u - jnp.mean(u, axis=-1, keepdims=True) - n * jnp.mean(u * n, axis=-1, keepdims=True)
    )


def layer_kernel(
    small, noise, table, w_in, w_qkv, w_out, w_up, w_down, cot,
    act, ngrad, tgrad, vout, f_in, f_qkv, f_out, f_up, f_dn,
    sm, smx, gsm, vec, vg, vq, vgy, vgz, vgf, bup, lives, idr,
    tp, tok, sc, win, wqkv, wout, wup, wdn, s_in, s_qkv, s_out, s_up,
    rin, rmid, gmid, t1, t2, t3, t4, na, proj, pr, att, asend, nb, gd, hid, ga,
    xs, xr, gatt, gos, go, g_in, g_qkv, g_out, g_dn,
    y_in, y_qkv, y_out, y_up, y_dn, z_in, z_qkv, z_out, z_up, z_dn, wis, wir,
    ss, rr, ls, credit,
):
    x = lax.axis_index("dp")
    f = lax.axis_index("fsdp")
    z, y, c = f // 4, lax.rem(f // 2, 2), lax.rem(f, 2)
    q = 2 * z + y
    g = 2 * x + c
    rows_here = table.shape[0]

    def dev(dx, dz, dy, dc):
        xx = lax.rem(x + dx, 2)
        zz = lax.rem(z + dz, 4)
        yy = lax.rem(y + dy, 2)
        cc = lax.rem(c + dc, 2)
        return (xx, zz * 4 + yy * 2 + cc)

    twin = dev(0, 0, 0, 1)
    across = dev(1, 0, 0, 0)
    pair_y = dev(0, 0, 1, 0)
    rel_dev = [dev(dx, 0, 0, dc) for dx, dc in FLIPS]
    rel_g = [2 * lax.rem(x + dx, 2) + lax.rem(c + dc, 2) for dx, dc in FLIPS]
    other_c = 1 - c

    def far(d):
        return lax.rem(z + 4 - d, 4)

    def to(d):
        return lax.rem(z + d, 4)

    sems = [0]
    pending = []

    class Link:
        def __init__(self):
            self.at = sems[0]
            sems[0] += 1
            assert sems[0] <= SEM_COUNT

        def send(self, src, dst, device):
            self.copy = pltpu.make_async_remote_copy(
                src_ref=src, dst_ref=dst, send_sem=ss.at[self.at], recv_sem=rr.at[self.at],
                device_id=device, device_id_type=MESH_ID,
            )
            self.copy.start()
            pending.append(self)
            return self

        def sent(self):
            pending.remove(self)
            self.copy.wait_send()

        def got(self, ref):
            pltpu.make_async_remote_copy(
                src_ref=ref, dst_ref=ref, send_sem=ss.at[self.at], recv_sem=rr.at[self.at],
                device_id=twin, device_id_type=MESH_ID,
            ).wait_recv()

    def each_rows(count, size, body):
        def step(i, carry):
            body(part(i * size, size))
            return carry

        lax.fori_loop(0, count // size, step, 0)

    def each(count, body):
        def step(i, carry):
            body(i)
            return carry

        lax.fori_loop(0, count, step, 0)

    barrier = pltpu.get_barrier_semaphore()
    peers = [dev(0, d, 0, dc) for d in (1, 2, 3) for dc in (0, 1)] + rel_dev + [pair_y]
    for peer in peers:
        pl.semaphore_signal(barrier, inc=1, device_id=peer, device_id_type=MESH_ID)
    pl.semaphore_wait(barrier, len(peers))

    class Gather:
        def __init__(self, whole, mine, theirs, height, twins=None):
            self.whole, self.height = whole, height
            places = (self.sub(q, c), self.sub(q, c, twins))
            self.z_links = {}
            for d in (0, 1, 2, 3):
                for dc in (0, 1):
                    if (d, dc) == (0, 0):
                        continue
                    link = Link()
                    link.send(theirs if dc else mine, places[dc], dev(0, d, 0, dc))
                    self.z_links[d, dc] = link

        def sub(self, block, core, whole=None):
            whole = self.whole if whole is None else whole
            if self.height is None:
                return whole.at[block, core]
            return whole.at[block, part(core * self.height, self.height)]

        def forward(self):
            self.y_links = []
            for d in (0, 1, 2, 3):
                block = 2 * far(d) + y
                for dc in (0, 1):
                    if (d, dc) != (0, 0):
                        self.z_links[d, dc].got(self.sub(block, other_c if dc else c))
                self.y_links.append(
                    Link().send(self.whole.at[block], self.whole.at[block], pair_y)
                )

        def finish(self):
            for d in (0, 1, 2, 3):
                self.y_links[d].got(self.whole.at[2 * far(d) + 1 - y])

    sm[q, c] = small[...]
    small_links = [Link().send(small, gsm.at[rel], rel_dev[rel]) for rel in (DIAG, ACROSS)]
    gather_small = Gather(sm, small, small, None)

    own_rows = tp.at[c, pl.ds(0, rows_here)]
    own_table = pltpu.make_async_copy(table, own_rows, ls.at[0])
    own_table.start()
    table_link = Link().send(table, own_rows, twin)
    spare = tp.shape[1] - rows_here
    if spare:
        for core in (0, 1):
            tp[core, pl.ds(rows_here, spare), :] = jnp.zeros((spare, tp.shape[2]), BF)

    def pack(whole, spare_buf, height, pick):
        mine, theirs = pick(g), pick(2 * x + other_c)
        whole[q, part(c * height, height), :] = mine
        spare_buf[...] = theirs

    h = w_qkv.shape[0]
    hin = w_in.shape[0]

    def cols(ref, start, size=256):
        return ref[:, part(start, size)]

    win_at, wout_at = win.at[g], wout.at[g]
    win_at[q, c] = cols(w_in, 256 * g)
    s_in[0] = cols(w_in, 256 * (2 * x + other_c))
    gather_in = Gather(win_at, win_at.at[q, c], s_in.at[0], None, win.at[2 * x + other_c])
    pack(
        wqkv, s_qkv, h,
        lambda k: jnp.concatenate([cols(w_qkv, 1024 * n + 256 * k) for n in (0, 1, 2)], axis=1),
    )
    gather_qkv = Gather(wqkv, wqkv.at[q, part(c * h, h)], s_qkv, h)


    lives[:, 0:1] = jnp.where(as_col(small[18:20, :]) < 7.5, 1.0, 0.0)
    vg[...] = jnp.zeros_like(vg)

    def grad_down_rows(at):
        masked = cot[at, :].astype(F32) * lives[at, 0:1]
        gd[g, at, :] = masked.astype(BF)
        vg[6:7, :] += jnp.sum(masked, axis=0, keepdims=True)

    each_rows(256, 32, grad_down_rows)
    gd_links = [Link().send(gd.at[g], gd.at[g], rel_dev[rel]) for rel in range(3)]

    gather_small.forward()
    pack(wout_at, s_out, h, lambda k: cols(w_out, 256 * k))
    gather_out = Gather(
        wout_at, wout_at.at[q, part(c * h, h)], s_out, h, wout.at[2 * x + other_c]
    )

    gather_small.finish()
    smx_link = Link().send(sm, smx, across)
    own_table.wait()
    table_link.got(tp.at[other_c, pl.ds(0, rows_here)])
    lane = lax.broadcasted_iota(jnp.int32, (256, tp.shape[1]), 1)

    def look_up(block):
        ids = as_col(sm[block, c, 16:18, :]).astype(jnp.int32)
        total = jnp.zeros((256, 256), F32)
        for core in (0, 1):
            first = (4 * z + 2 * y + core) * rows_here
            hit = jnp.where(lane == ids - first, 1.0, 0.0).astype(BF)
            total += mm(hit, tp[core])
        return total.astype(BF)

    emb_y = [Link() for _ in range(4)]
    for d in range(4):
        tok[d] = look_up(2 * to(d) + 1 - y)
        emb_y[d].send(tok.at[d], tok.at[8 + d], pair_y)

    def own_blocks(d):
        tok[4 + d] = look_up(2 * lax.rem(z + d, 4) + y)

    each(4, own_blocks)
    emb_z = [None]
    for d in (1, 2, 3):
        emb_y[d].got(tok.at[8 + d])
        tok[4 + d] = tok[4 + d] + tok[8 + d]
        emb_z.append(Link().send(tok.at[4 + d], tok.at[11 + d], dev(0, d, 0, 0)))
    emb_y[0].got(tok.at[8])
    gather_in.forward()
    gather_qkv.forward()

    ct = lax.broadcasted_iota(jnp.int32, (h, 128), 1) < 64
    for j in range(8):
        first = w_up[:, part(128 * (4 * j + x), 128)].astype(F32)
        second = w_up[:, part(128 * (4 * j + 2 + x), 128)].astype(F32)
        low = jnp.where(ct, first, pltpu.roll(second, 64, 1)).astype(BF)
        high = jnp.where(ct, pltpu.roll(first, 64, 1), second).astype(BF)
        wup[q, part(c * h, h), 128 * j : 128 * j + 128] = jnp.where(c == 0, low, high)
        s_up[:, 128 * j : 128 * j + 128] = jnp.where(c == 0, high, low)
    gather_up = Gather(wup, wup.at[q, part(c * h, h)], s_up, h)
    wdn[q, part(c * h, h), :] = w_down[part(g * h, h), :]
    gather_dn = Gather(
        wdn, w_down.at[part(g * h, h)], w_down.at[part((2 * x + other_c) * h, h)], h
    )

    for j in range(8):
        vec[:, 128 * j : 128 * j + 128] = sm[j, 0, 0:16, :] + sm[j, 1, 0:16, :]

    rows_sum = tok[4].astype(F32) + tok[8].astype(F32)
    for d in (1, 2, 3):
        emb_z[d].got(tok.at[11 + d])
        rows_sum += tok[11 + d].astype(F32)
    for d in range(4):
        emb_y[d].sent()
    for d in (1, 2, 3):
        emb_z[d].sent()
    level = as_col(small[20:22, :])
    scale_in = lax.rsqrt(1.0 + level * level)
    embedded = rows_sum * lax.rsqrt(jnp.mean(rows_sum * rows_sum, axis=1, keepdims=True) + norm_eps)
    sc[g] = ((embedded + level * noise[...].astype(F32)) * scale_in).astype(BF)
    sc_links = [Link().send(sc.at[g], sc.at[g], rel_dev[rel]) for rel in range(3)]

    gather_in.finish()
    in_links = [Link().send(win_at, win_at, rel_dev[rel]) for rel in range(3)]
    gather_out.forward()
    for rel in (TWIN, ACROSS, DIAG):
        in_links[rel].got(win.at[rel_g[rel]])

    def win_mat(k):
        return win[k].reshape(256, 256)

    def first_norm(row, keep):
        for k in range(4):
            keep[:, 256 * k : 256 * k + 256] = (
                mm(sc[row], win_mat(k)) + vec[0:1, 256 * k : 256 * k + 256]
            )

        def chunk(at):
            n, _ = norm_parts(keep[at, :])
            na[row, at, :] = (n * vec[1:2, :] + vec[2:3, :]).astype(BF)

        each_rows(256, 32, chunk)

    def project(row):
        def block(k):
            at = part(k * 256, 256)
            proj[row, :, at] = mm(na[row], wqkv[:, :, at].reshape(1024, 256)).astype(BF)

        each(3, block)

    first_norm(g, rin)
    gather_qkv.finish()
    project(g)
    for rel in (TWIN, ACROSS, DIAG):
        sc_links[rel].got(sc.at[rel_g[rel]])
        first_norm(rel_g[rel], t1)
        project(rel_g[rel])

    gather_out.finish()
    out_links = [Link().send(wout_at, wout_at, rel_dev[rel]) for rel in range(3)]

    head_of = lax.broadcasted_iota(jnp.int32, (1, 256), 1) // 64
    small_links[DIAG].got(gsm.at[DIAG])
    small_links[ACROSS].got(gsm.at[ACROSS])

    def attend(row, pair):
        same = as_col(pair) == as_row(pair)
        keys = proj[row, :, 256:512]
        values = proj[row, :, 512:768]
        queries = proj[row, :, 0:256]
        t2[...] = jnp.zeros_like(t2)

        def head(k):
            mine = head_of == k
            q_head = jnp.where(mine, queries, jnp.zeros_like(queries))
            scores = jnp.where(same, mm_nt(q_head, keys) * 0.125, -1e9)
            weights = jnp.exp(scores - jnp.max(scores, axis=-1, keepdims=True))
            low_probs = (weights / jnp.sum(weights, axis=-1, keepdims=True)).astype(BF)
            pr[row * 4 + k] = low_probs
            t2[...] += mm(low_probs, jnp.where(mine, values, jnp.zeros_like(values)))

        each(4, head)
        return t2[...].astype(BF)

    att_links = []
    my_cols = part(256 * g, 256)
    for rel in range(3):
        pair = sm[q, other_c, 18:20, :] if rel == TWIN else gsm[rel, 18:20, :]
        asend[rel] = attend(rel_g[rel], pair)
        att_links.append(Link().send(asend.at[rel], att.at[:, my_cols], rel_dev[rel]))
    att[:, my_cols] = attend(g, small[18:20, :])
    gather_up.forward()

    for rel in (TWIN, ACROSS, DIAG):
        out_links[rel].got(wout.at[rel_g[rel]])
    for rel in (TWIN, ACROSS, DIAG):
        att_links[rel].got(att.at[:, part(256 * rel_g[rel], 256)])

    def out_block(k):
        at = part(k * 256, 256)
        rmid[:, at] = rin[:, at] + mm(att[...], wout[k].reshape(1024, 256)) + vec[3:4, at]

    each(4, out_block)

    def second_norm(at):
        n, _ = norm_parts(rmid[at, :])
        nb[g, at, :] = (n * vec[4:5, :] + vec[5:6, :]).astype(BF)

    each_rows(256, 32, second_norm)
    nb_across = Link().send(nb.at[g], nb.at[g], across)
    nb_twin = Link().send(nb.at[g], nb.at[g], twin)
    nb_pass = Link()
    gather_dn.forward()
    for rel in range(3):
        gd_links[rel].got(gd.at[rel_g[rel]])

    bup[...] = jnp.zeros_like(bup)
    for k in range(4):
        bup[0:1, :] += jnp.where(g == k, vec[7 + k : 8 + k, :], 0.0)

    def ff_row(row):
        def block(k):
            at = part(k * 256, 256)
            t2[...] = mm(nb[row], wup[:, :, at].reshape(1024, 256)) + bup[0:1, at]
            t3[...] = mm_nt(gd[row], wdn[pl.ds(2 * k, 2)].reshape(256, 1024))

            def chunk(rows_at):
                pre = t2[rows_at, :]
                cdf = 0.5 + 0.5 * lax.erf(pre * 0.7071067811865476)
                pdf = jnp.exp(-0.5 * pre * pre) * 0.3989422804014327
                t2[rows_at, :] = pre * cdf
                ga_low = (t3[rows_at, :] * (cdf + pre * pdf)).astype(BF)
                ga[row, rows_at, at] = ga_low
                bup[1:2, at] += jnp.sum(ga_low.astype(F32), axis=0, keepdims=True)

            each_rows(256, 32, chunk)
            hid[pl.ds(2 * row, 2), :, at] = t2[...].astype(BF).reshape(2, 128, 256)

        each(4, block)

    gather_up.finish()
    gather_dn.finish()
    ff_row(g)
    nb_twin.got(nb.at[rel_g[TWIN]])
    ff_row(rel_g[TWIN])
    nb_across.got(nb.at[rel_g[ACROSS]])
    nb_pass.send(nb.at[rel_g[ACROSS]], nb.at[rel_g[ACROSS]], twin)
    ff_row(rel_g[ACROSS])
    nb_pass.got(nb.at[rel_g[DIAG]])
    ff_row(rel_g[DIAG])

    class GroupSum:
        def __init__(self, slot, partial):
            self.slot, self.partial = slot, partial

        def first(self):
            self.partial(rel_g[DIAG], xs.at[self.slot, 0])
            self.a = Link().send(xs.at[self.slot, 0], xr.at[self.slot, 0], twin)

        def second(self):
            self.partial(rel_g[ACROSS], t1)
            self.a.got(xr.at[self.slot, 0])

            def chunk(at):
                xs[self.slot, 1, at, :] = (t1[at, :] + xr[self.slot, 0, at, :].astype(F32)).astype(BF)

            each_rows(256, 32, chunk)
            self.b = Link().send(xs.at[self.slot, 1], xr.at[self.slot, 1], across)

        def third(self):
            self.partial(rel_g[TWIN], xs.at[self.slot, 2])
            self.c = Link().send(xs.at[self.slot, 2], xr.at[self.slot, 2], twin)

        def own(self, into):
            self.partial(g, into)
            self.into = into

        def total(self):
            self.c.got(xr.at[self.slot, 2])
            self.b.got(xr.at[self.slot, 1])

        def rows(self, at):
            return (
                self.into[at, :].astype(F32)
                + xr[self.slot, 1, at, :].astype(F32)
                + xr[self.slot, 2, at, :].astype(F32)
            )

        def release(self):
            for link in (self.a, self.b, self.c):
                link.sent()

    def nb_partial(row, into):
        def block(k):
            into[:, part(k * 256, 256)] = mm_nt(
                ga[row], wup[pl.ds(2 * k, 2)].reshape(256, 1024)
            ).astype(into.dtype)

        each(4, block)

    def out_partial(row, into):
        def block(k):
            at = part(k * 256, 256)
            into[:, at] = mm(
                hid[pl.ds(2 * row, 2)].reshape(256, 1024), wdn[:, :, at].reshape(1024, 256)
            ).astype(into.dtype)

        each(4, block)

    class Scatter:
        def __init__(self, grad, y_buf, z_buf, final, height):
            self.grad, self.y_buf, self.z_buf, self.final, self.height = (
                grad, y_buf, z_buf, final, height,
            )

        def chunks(self, body):
            if self.height is None:
                each(2, body)
            else:
                each_rows(2 * self.height, 32, body)

        def half(self, core):
            if self.height is None:
                return self.grad.at[q, core]
            return self.grad.at[q, part(core * self.height, self.height)]

        def start(self):
            self.y_links = [
                Link().send(self.grad.at[2 * to(d) + 1 - y], self.y_buf.at[d], pair_y)
                for d in range(4)
            ]

        def middle(self):
            self.z_links = [None]
            for d in (1, 2, 3, 0):
                block = 2 * to(d) + y
                self.y_links[d].got(self.y_buf.at[d])

                def chunk(at):
                    self.grad[block, at] = (
                        self.grad[block, at].astype(F32) + self.y_buf[d, at].astype(F32)
                    ).astype(BF)

                self.chunks(chunk)
                if d:
                    self.z_links.append(
                        Link().send(self.grad.at[block], self.z_buf.at[d - 1], dev(0, d, 0, 0))
                    )

        def last(self):
            for d in (1, 2, 3):
                self.z_links[d].got(self.z_buf.at[d - 1])

            def chunk(at):
                total = self.grad[q, at].astype(F32)
                for d in (0, 1, 2):
                    total += self.z_buf[d, at].astype(F32)
                self.grad[q, at] = total.astype(BF)

            self.chunks(chunk)
            self.f_links = []
            for rel in range(3):
                core = lax.rem(c + FLIPS[rel][1], 2)
                self.f_links.append(
                    Link().send(
                        self.half(core),
                        self.final.at[g],
                        rel_dev[rel],
                    )
                )
            self.final[g] = self.half(c)[...]

        def finish(self):
            for rel in range(3):
                self.f_links[rel].got(self.final.at[rel_g[rel]])

    sum_nb = GroupSum(0, nb_partial)
    sum_nb.first()
    sum_nb.second()
    sum_nb.third()

    scatter_dn = Scatter(g_dn, y_dn, z_dn, f_dn, h)
    scatter_up = Scatter(hid, y_up, z_up, f_up, h)
    sum_out = GroupSum(1, out_partial)

    def dn_block(k):
        at = part(k * 256, 256)
        lhs = hid[:, :, at].reshape(1024, 256)
        g_dn[pl.ds(2 * k, 2)] = mm_tn(lhs, gd[...].reshape(1024, 1024)).astype(BF).reshape(
            2, 128, 1024
        )

    each(4, dn_block)
    scatter_dn.start()
    sum_out.first()
    sum_out.second()
    sum_out.third()

    sum_out.own(act)

    def up_block(k):
        at = part(k * 256, 256)
        lhs = nb[:, :, at].reshape(1024, 256)
        hid[pl.ds(2 * k, 2)] = mm_tn(lhs, ga[...].reshape(1024, 1024)).astype(BF).reshape(
            2, 128, 1024
        )

    each(4, up_block)
    scatter_up.start()

    sum_nb.own(t1)
    sum_nb.total()

    def second_back(at):
        grad_nb = sum_nb.rows(at)
        n, rstd = norm_parts(rmid[at, :])
        vg[4:5, :] += jnp.sum(grad_nb * n, axis=0, keepdims=True)
        vg[5:6, :] += jnp.sum(grad_nb, axis=0, keepdims=True)
        mid = gd[g, at, :].astype(F32) + norm_back(grad_nb * vec[4:5, :], n, rstd)
        gmid[at, :] = mid
        low_mid = mid.astype(BF)
        gatt[at, :] = low_mid
        vg[3:4, :] += jnp.sum(low_mid.astype(F32), axis=0, keepdims=True)

    each_rows(256, 32, second_back)

    def grad_o_part(to_g):
        total = jnp.zeros((256, 256), F32)
        for k in range(4):
            total += mm_nt(
                gatt[:, 256 * k : 256 * k + 256], wout[k, pl.ds(2 * to_g, 2)].reshape(256, 256)
            )
        return total.astype(BF)

    go_links = []
    for rel in range(3):
        gos[rel] = grad_o_part(rel_g[rel])
        go_links.append(Link().send(gos.at[rel], go.at[g], rel_dev[rel]))
    go[g] = grad_o_part(g)

    sum_out.total()

    def out_rows(at):
        whole = rmid[at, :] + sum_out.rows(at) + vec[6:7, :]
        act[at, :] = (whole * lives[at, 0:1]).astype(BF)

    each_rows(256, 32, out_rows)
    sum_out.release()
    sum_nb.release()
    for rel in range(3):
        pl.semaphore_signal(credit, inc=1, device_id=rel_dev[rel], device_id_type=MESH_ID)

    def wog(rel_slot, k):
        for j in range(4):
            block = mm_tn(att[:, 256 * j : 256 * j + 256], gatt[:, part(256 * k, 256)]).astype(BF)
            if rel_slot is None:
                g_out[2 * j : 2 * j + 2] = block.reshape(2, 128, 256)
            else:
                xs[1, rel_slot, :, 256 * j : 256 * j + 256] = block

    for rel in range(3):
        wog(rel, rel_g[rel])
    wog(None, g)
    for rel in (TWIN, ACROSS, DIAG):
        go_links[rel].got(go.at[rel_g[rel]])
    pl.semaphore_wait(credit, 3)
    wog_links = [Link().send(xs.at[1, rel], xr.at[1, rel], rel_dev[rel]) for rel in range(3)]

    def attend_back(row):
        keys = proj[row, :, 256:512]
        values = proj[row, :, 512:768]
        queries = proj[row, :, 0:256]
        grad_rows = go[row]
        zero = jnp.zeros_like(keys)
        for buf in (t2, t3, t4):
            buf[...] = jnp.zeros_like(buf)

        def head(k):
            mine = head_of == k
            probs = pr[row * 4 + k]
            g_head = jnp.where(mine, grad_rows, zero)
            t4[...] += mm_tn(probs, g_head)
            grad_p = mm_nt(g_head, values)
            wide = probs.astype(F32)
            grad_s = wide * (grad_p - jnp.sum(grad_p * wide, axis=-1, keepdims=True))
            low_s = (grad_s * 0.125).astype(BF)
            t2[...] += mm(low_s, jnp.where(mine, keys, zero))
            t3[...] += mm_tn(low_s, jnp.where(mine, queries, zero))

        each(4, head)
        proj[row, :, 0:256] = t2[...].astype(BF)
        proj[row, :, 256:512] = t3[...].astype(BF)
        proj[row, :, 512:768] = t4[...].astype(BF)

    def na_partial(row, into):
        def block(k):
            into[:, part(k * 256, 256)] = mm_nt(
                proj[row], wqkv[pl.ds(2 * k, 2)].reshape(256, 768)
            ).astype(into.dtype)

        each(4, block)

    sum_na = GroupSum(0, na_partial)
    attend_back(rel_g[DIAG])
    sum_na.first()
    attend_back(rel_g[ACROSS])
    sum_na.second()
    scatter_dn.middle()
    attend_back(rel_g[TWIN])
    sum_na.third()
    attend_back(g)
    sum_na.own(t1)

    scatter_qkv = Scatter(g_qkv, y_qkv, z_qkv, f_qkv, h)
    scatter_out = Scatter(g_out, y_out, z_out, f_out, h)
    scatter_in = Scatter(g_in, y_in, z_in, f_in, None)

    def qkv_block(k):
        at = part(k * 256, 256)
        lhs = na[:, :, at].reshape(1024, 256)
        g_qkv[pl.ds(2 * k, 2)] = mm_tn(lhs, proj[...].reshape(1024, 768)).astype(BF).reshape(
            2, 128, 768
        )

    each(4, qkv_block)
    scatter_qkv.start()

    for rel in range(3):
        wog_links[rel].got(xr.at[1, rel])
    for j in range(4):
        block = g_out[2 * j : 2 * j + 2].reshape(256, 256).astype(F32)
        for rel in range(3):
            block += xr[1, rel, :, 256 * j : 256 * j + 256].astype(F32)
        g_out[2 * j : 2 * j + 2] = block.astype(BF).reshape(2, 128, 256)
    scatter_out.start()
    scatter_up.middle()

    sum_na.total()

    def first_back(at):
        grad_na = sum_na.rows(at)
        n, rstd = norm_parts(rin[at, :])
        vg[1:2, :] += jnp.sum(grad_na * n, axis=0, keepdims=True)
        vg[2:3, :] += jnp.sum(grad_na, axis=0, keepdims=True)
        low_in = (gmid[at, :] + norm_back(grad_na * vec[1:2, :], n, rstd)).astype(BF)
        gatt[at, :] = low_in
        vg[0:1, :] += jnp.sum(low_in.astype(F32), axis=0, keepdims=True)

    each_rows(256, 32, first_back)
    for k in range(4):
        vg[7 + k : 8 + k, :] = jnp.where(g == k, bup[1:2, :], 0.0)
    for j in range(8):
        vq[j % 2, j // 2] = vg[:, 128 * j : 128 * j + 128]
    vy_link = Link().send(vq.at[1 - y], vgy, pair_y)

    grad_scaled = jnp.zeros((256, 256), F32)
    for k in range(4):
        grad_scaled += mm_nt(gatt[:, 256 * k : 256 * k + 256], win_mat(k))
    level = as_col(small[20:22, :])
    scale_in = lax.rsqrt(1.0 + level * level)
    ngrad[...] = grad_scaled * (level * scale_in)

    def set_at(other_x, other_y, other_core):
        return ((lax.rem(x + other_x, 2) * 2 + lax.rem(y + other_y, 2)) * 2 + lax.rem(c + other_core, 2)) * 4

    scatter_dn.last()
    home = tok.at[set_at(0, 0, 0) + z]
    tok[set_at(0, 0, 0) + z] = (grad_scaled * scale_in).astype(BF)
    tok_z = [None] + [Link().send(home, home, dev(0, d, 0, 0)) for d in (1, 2, 3)]
    tok_x = {}
    tok_y = {}
    tok_t = {}

    def spread(spot, key, across_too):
        ref = tok.at[spot]
        if across_too:
            tok_x[key] = Link().send(ref, ref, across)
        tok_t[across_too, key] = Link().send(ref, ref, twin)

    tok_y[0] = Link().send(home, home, pair_y)
    spread(set_at(0, 0, 0) + z, (0, 0), True)

    wi_links = []
    for rel in range(3):
        wis[rel] = mm_tn(sc[g], gatt[:, part(256 * rel_g[rel], 256)]).astype(BF)
        wi_links.append(Link().send(wis.at[rel], wir.at[rel], rel_dev[rel]))
    wi_own = mm_tn(sc[g], gatt[:, part(256 * g, 256)])

    for d in (1, 2, 3):
        spot = set_at(0, 0, 0) + far(d)
        tok_z[d].got(tok.at[spot])
        tok_y[d] = Link().send(tok.at[spot], tok.at[spot], pair_y)
        spread(spot, (0, d), True)

    for rel in range(3):
        wi_links[rel].got(wir.at[rel])
        wi_own += wir[rel].astype(F32)
    g_in[...] = wi_own.astype(BF).reshape(8, 2, 16, 256)
    scatter_in.start()

    vy_link.got(vgy)
    vq[y] = vq[y] + vgy[...]
    vz_links = [
        Link().send(vq.at[y, to(d)], vgz.at[d - 1], dev(0, d, 0, 0)) for d in (1, 2, 3)
    ]

    for d in range(4):
        spot = set_at(0, 1, 0) + far(d)
        tok_y[d].got(tok.at[spot])
        spread(spot, (1, d), True)

    scatter_qkv.middle()
    scatter_out.middle()

    for d in (1, 2, 3):
        vz_links[d - 1].got(vgz.at[d - 1])
    vtot = vq[y, z] + vgz[0] + vgz[1] + vgz[2]
    vgf[3] = vtot
    vf_links = [Link().send(vgf.at[3], vgf.at[rel], rel_dev[rel]) for rel in range(3)]

    smx_link.got(smx)
    for other_x in (0, 1):
        for yy in (0, 1):
            for core in (0, 1):
                source = sm if other_x == 0 else smx
                for zz in range(4):
                    idr[(other_x * 2 + yy) * 2 + core : (other_x * 2 + yy) * 2 + core + 1, 256 * zz : 256 * zz + 256] = (
                        as_row(source[2 * zz + yy, core, 16:18, :])
                    )

    tile = 400
    base = (f * rows_here).astype(F32)
    tile_row = lax.broadcasted_iota(jnp.int32, (tile, 1024), 0).astype(F32)

    def table_add(other_x, other_y, other_core, begin):
        spot = set_at(other_x, other_y, other_core)
        row = (other_x * 2 + lax.rem(y + other_y, 2)) * 2 + lax.rem(c + other_core, 2)
        ids = idr[pl.ds(row, 1), :] - base

        def block(k):
            at = part(k * tile, tile)
            hit = jnp.where(tile_row == ids - (k * tile).astype(F32), 1.0, 0.0).astype(BF)
            add = mm(hit, tok[pl.ds(spot, 4)].reshape(1024, 256))
            if begin:
                tgrad[at, :] = add
            else:
                tgrad[at, :] += add

        each(rows_here // tile, block)

    def twin_set(from_x, other_y):
        for d in range(4):
            tok_t[from_x == 0, (other_y, d)].got(tok.at[set_at(from_x, other_y, 1) + far(d)])

    table_add(0, 0, 0, True)
    twin_set(0, 0)
    table_add(0, 0, 1, False)
    scatter_up.last()
    table_add(0, 1, 0, False)
    twin_set(0, 1)
    table_add(0, 1, 1, False)
    scatter_in.middle()
    for other_y in (0, 1):
        for d in range(4):
            spot = set_at(1, other_y, 0) + far(d)
            tok_x[other_y, d].got(tok.at[spot])
            spread(spot, (other_y, d), False)
        table_add(1, other_y, 0, False)
    scatter_qkv.last()
    scatter_out.last()
    scatter_in.last()
    for other_y in (0, 1):
        twin_set(1, other_y)
        table_add(1, other_y, 1, False)

    def table_rows(at):
        values = tp[c, at, :].astype(F32)
        r = lax.rsqrt(jnp.mean(values * values, axis=1, keepdims=True) + norm_eps)
        row_grad = tgrad[at, :]
        slope = jnp.mean(row_grad * values, axis=1, keepdims=True)
        tgrad[at, :] = r * row_grad - values * (r * r * r * slope)

    each_rows(rows_here, 80, table_rows)

    for rel in range(3):
        vf_links[rel].got(vgf.at[rel])
    vout[...] = vgf[0] + vgf[1] + vgf[2] + vgf[3]
    for scatter in (scatter_dn, scatter_up, scatter_qkv, scatter_out, scatter_in):
        scatter.finish()
    for link in list(pending):
        link.sent()


def finish_kernel(
    act_in, ngrad_in, tgrad_in, vout, f_in, f_qkv, f_out, f_up, f_dn,
    act, ngrad, tgrad, w_in, b_in, gain_a, shift_a, w_qkv, w_out, b_out, gain_b, shift_b,
    w_up, b_up, w_dn, b_dn,
):
    c = lax.rem(lax.axis_index("fsdp"), 2)
    act[...] = act_in[...]
    ngrad[...] = ngrad_in[...]
    tgrad[...] = tgrad_in[...]
    rows = jnp.where(c == 0, vout[...], pltpu.roll(vout[...], 64, 1))
    for k, ref in enumerate((b_in, gain_a, shift_a, b_out, gain_b, shift_b, b_dn)):
        ref[...] = rows[k, 0:64]
    for k in range(4):
        b_up[64 * k : 64 * k + 64] = rows[7 + k, 0:64]
    h = w_out.shape[0]
    low_half = lax.broadcasted_iota(jnp.int32, (h, 128), 1) < 64
    for g in range(4):
        at = slice(256 * g, 256 * g + 256)
        w_in[:, at] = f_in[g].astype(F32)
        w_out[:, at] = f_out[g].astype(F32)
        for n in range(3):
            w_qkv[:, 1024 * n + 256 * g : 1024 * n + 256 * g + 256] = f_qkv[
                g, :, 256 * n : 256 * n + 256
            ].astype(F32)
        w_dn[h * g : h * g + h, :] = f_dn[g].astype(F32)
    for shard in range(16):
        at = slice(128 * (shard // 2), 128 * (shard // 2) + 128)
        for half in (0, 1):
            first, second = f_up[2 * half, :, at].astype(F32), f_up[2 * half + 1, :, at].astype(F32)
            if shard % 2 == 0:
                both = jnp.where(low_half, first, pltpu.roll(second, 64, 1))
            else:
                both = jnp.where(low_half, pltpu.roll(first, 64, 1), second)
            w_up[:, 256 * shard + 128 * half : 256 * shard + 128 * half + 128] = both


def small_pack(seq_lengths, token_ids, noise_level, vectors, b_up):
    tok_count = token_ids.shape[0]
    seq_ends = jnp.cumsum(seq_lengths[0], dtype=jnp.int32)
    positions = jnp.arange(tok_count, dtype=jnp.int32)
    segment = jnp.sum((positions[:, None] >= seq_ends[None, :]).astype(jnp.int32), axis=1)
    vecs = jnp.concatenate([v.reshape(1, -1) for v in vectors] + [b_up.reshape(4, -1)], axis=0)
    vecs = vecs.astype(F32)
    half = (jnp.arange(128) // 64) == lax.axis_index("fsdp") % 2
    vecs = jnp.where(half[None, :], jnp.concatenate([vecs, vecs], axis=1), 0.0)
    blank = jnp.zeros((16 - vecs.shape[0], 128), F32)
    tail = jnp.zeros((2, 128), F32)
    return jnp.concatenate(
        [
            vecs,
            blank,
            token_ids.astype(F32).reshape(2, 128),
            segment.astype(F32).reshape(2, 128),
            noise_level.reshape(2, 128),
            tail,
        ],
        axis=0,
    )


def fused_shards(
    token_ids, seq_lengths, noise, noise_level, table, w_in, b_in, gain_first, shift_first, w_qkv,
    w_out, b_out, gain_second, shift_second, w_up, b_up, w_down, b_down, cotangent,
):
    small = small_pack(
        seq_lengths, token_ids, noise_level,
        (b_in, gain_first, shift_first, b_out, gain_second, shift_second, b_down), b_up,
    )
    vmem = pl.BlockSpec(memory_space=pltpu.VMEM)
    hbm = pl.BlockSpec(memory_space=pl.ANY)

    def shape(*dims, dtype=BF):
        return jax.ShapeDtypeStruct(dims, dtype)

    rows_here = table.shape[0]
    padded = -(-rows_here // 256) * 256
    outs = [
        shape(256, 1024), shape(256, 256, dtype=F32), shape(rows_here, 256, dtype=F32),
        shape(16, 128, dtype=F32), shape(4, 16, 256), shape(4, 64, 768), shape(4, 64, 256),
        shape(4, 64, 1024), shape(4, 64, 1024),
    ]

    def bf(*dims):
        return pltpu.VMEM(dims, BF)

    def fl(*dims):
        return pltpu.VMEM(dims, F32)

    scratch = [
        fl(8, 2, 24, 128), fl(8, 2, 24, 128), fl(2, 24, 128),
        fl(16, 1024), fl(16, 1024), fl(2, 4, 16, 128), fl(4, 16, 128), fl(3, 16, 128),
        fl(4, 16, 128), fl(8, 1024), fl(256, 128), fl(8, 1024),
        bf(2, padded, 256), bf(32, 256, 256), bf(4, 256, 256), bf(4, 8, 2, 16, 256),
        bf(8, 128, 768), bf(4, 8, 128, 256), bf(8, 128, 1024), bf(8, 128, 1024),
        bf(2, 16, 256), bf(64, 768), bf(64, 256), bf(64, 1024),
        fl(256, 1024), fl(256, 1024), fl(256, 1024), fl(256, 1024),
        fl(256, 256), fl(256, 256), fl(256, 256),
        bf(4, 256, 1024), bf(4, 256, 768), bf(16, 256, 256), bf(256, 1024), bf(3, 256, 256),
        bf(4, 256, 1024), bf(4, 256, 1024), bf(8, 128, 1024), bf(4, 256, 1024),
        bf(2, 3, 256, 1024), bf(2, 3, 256, 1024), bf(256, 1024), bf(3, 256, 256), bf(4, 256, 256),
        bf(8, 2, 16, 256), bf(8, 128, 768), bf(8, 128, 256), bf(8, 128, 1024),
        bf(4, 2, 16, 256), bf(4, 128, 768), bf(4, 128, 256), bf(4, 128, 1024), bf(4, 128, 1024),
        bf(3, 2, 16, 256), bf(3, 128, 768), bf(3, 128, 256), bf(3, 128, 1024), bf(3, 128, 1024),
        bf(3, 256, 256), bf(3, 256, 256),
        pltpu.SemaphoreType.DMA((SEM_COUNT,)), pltpu.SemaphoreType.DMA((SEM_COUNT,)),
        pltpu.SemaphoreType.DMA((1,)), pltpu.SemaphoreType.REGULAR,
    ]
    parts = pl.pallas_call(
        layer_kernel,
        out_shape=outs,
        in_specs=[vmem, vmem, hbm] + [vmem] * 6,
        out_specs=[vmem] * len(outs),
        scratch_shapes=scratch,
        compiler_params=pltpu.CompilerParams(
            collective_id=0, has_side_effects=True, vmem_limit_bytes=VMEM_LIMIT
        ),
        cost_estimate=pl.CostEstimate(flops=40 * 10**9, bytes_accessed=30 * 10**6, transcendentals=0),
    )(small, noise, table, w_in, w_qkv, w_out, w_up, w_down, cotangent)
    f32 = lambda a: jax.ShapeDtypeStruct(a.shape, F32)
    finals = [
        outs[0], outs[1], outs[2], f32(w_in), f32(b_in), f32(gain_first), f32(shift_first),
        f32(w_qkv), f32(w_out), f32(b_out), f32(gain_second), f32(shift_second), f32(w_up),
        f32(b_up), f32(w_down), f32(b_down),
    ]
    return tuple(
        pl.pallas_call(
            finish_kernel,
            out_shape=finals,
            in_specs=[vmem] * len(outs),
            out_specs=[vmem] * len(finals),
            compiler_params=pltpu.CompilerParams(vmem_limit_bytes=40 * 2**20),
        )(*parts)
    )


def solution(mesh):
    in_specs = (
        P(("dp", "fsdp")),
        P(("dp", "fsdp"), None),
        P(("dp", "fsdp"), None),
        P(("dp", "fsdp")),
        P("fsdp", None),
        P("fsdp", None),
        P("fsdp"),
        P("fsdp"),
        P("fsdp"),
        P("fsdp", None),
        P("fsdp", None),
        P("fsdp"),
        P("fsdp"),
        P("fsdp"),
        P("fsdp", None),
        P("fsdp"),
        P("fsdp", None),
        P("fsdp"),
        P(("dp", "fsdp"), None),
    )
    out_specs = (
        P(("dp", "fsdp"), None),
        P(("dp", "fsdp"), None),
        P("fsdp", None),
        P("fsdp", None),
        P("fsdp"),
        P("fsdp"),
        P("fsdp"),
        P("fsdp", None),
        P("fsdp", None),
        P("fsdp"),
        P("fsdp"),
        P("fsdp"),
        P("fsdp", None),
        P("fsdp"),
        P("fsdp", None),
        P("fsdp"),
    )
    fused = mesh.shape["dp"] == 2 and mesh.shape["fsdp"] == 16
    body = fused_shards if fused else shards
    return jax.shard_map(body, mesh=mesh, in_specs=in_specs, out_specs=out_specs, check_vma=False)
```

```python
import jax
import jax.numpy as jnp
from jax import lax
from jax.experimental import pallas as pl
from jax.experimental.pallas import tpu as pltpu
from jax.sharding import PartitionSpec as P

HEADS = 16
VOCAB = 32000


norm_eps = 1e-05


def standardize(resid):
    centred = resid - jnp.mean(resid, axis=-1, keepdims=True)
    spread = jnp.mean(centred * centred, axis=-1, keepdims=True)
    return centred * lax.rsqrt(spread + norm_eps)


def row_normalize(tok_rows):
    return tok_rows * lax.rsqrt(jnp.mean(tok_rows * tok_rows, axis=1, keepdims=True) + norm_eps)


def exact_gelu(pre_act):
    return jax.nn.gelu(pre_act, approximate=False)


def split_heads(projected):
    tok_count = projected.shape[0]
    width = projected.shape[1] // 3
    head_size = width // HEADS
    key_heads = projected[:, width : 2 * width].reshape(tok_count, HEADS, head_size)
    value_heads = projected[:, 2 * width :].reshape(tok_count, HEADS, head_size)
    row_block = min(512, tok_count)
    query_blocks = projected[:, :width].reshape(tok_count // row_block, row_block, HEADS, head_size)
    return (query_blocks, key_heads, value_heads, row_block)


def block_scores(query_block, key_heads, seg_block, segment):
    raw_scores = (
        jnp.einsum("qhd,khd->hqk", query_block, key_heads, preferred_element_type=jnp.float32)
        * 0.125
    )
    same_seq = seg_block[:, None] == segment[None, :]
    return jnp.where(same_seq[None, :, :], raw_scores, -1000000000.0)


def attention_forward(projected, segment):
    query_blocks, key_heads, value_heads, row_block = split_heads(projected)
    seg_blocks = segment.reshape(-1, row_block)

    def block_step(items_in):
        query_block, seg_block = items_in
        scores = block_scores(query_block, key_heads, seg_block, segment)
        row_max = jnp.max(scores, axis=-1, keepdims=True)
        exp_scores = jnp.exp(scores - row_max)
        row_total = jnp.sum(exp_scores, axis=-1, keepdims=True)
        soft_probs = (exp_scores / row_total).astype(jnp.bfloat16)
        attended = jnp.einsum(
            "hqk,khd->qhd", soft_probs, value_heads, preferred_element_type=jnp.float32
        )
        return (attended, (row_max + jnp.log(row_total))[:, :, 0])

    attended, log_total = lax.map(block_step, (query_blocks, seg_blocks))
    return (attended.reshape(projected.shape[0], -1), log_total)


def attention_backward(projected, segment, log_total, grad_attended):
    query_blocks, key_heads, value_heads, row_block = split_heads(projected)
    seg_blocks = segment.reshape(-1, row_block)
    grad_blocks = grad_attended.reshape(query_blocks.shape)

    def block_step(totals, items_in):
        grad_keys, grad_values = totals
        query_block, seg_block, log_block, grad_block = items_in
        scores = block_scores(query_block, key_heads, seg_block, segment)
        soft_probs = jnp.exp(scores - log_block[:, :, None])
        grad_values = grad_values + jnp.einsum(
            "hqk,qhd->khd",
            soft_probs.astype(jnp.bfloat16),
            grad_block,
            preferred_element_type=jnp.float32,
        )
        grad_probs = jnp.einsum(
            "qhd,khd->hqk", grad_block, value_heads, preferred_element_type=jnp.float32
        )
        grad_scores = soft_probs * (
            grad_probs - jnp.sum(grad_probs * soft_probs, axis=-1, keepdims=True)
        )
        scaled_grad = (grad_scores * 0.125).astype(jnp.bfloat16)
        grad_query = jnp.einsum(
            "hqk,khd->qhd", scaled_grad, key_heads, preferred_element_type=jnp.float32
        )
        grad_keys = grad_keys + jnp.einsum(
            "hqk,qhd->khd", scaled_grad, query_block, preferred_element_type=jnp.float32
        )
        return ((grad_keys, grad_values), grad_query.astype(jnp.bfloat16))

    zero_heads = jnp.zeros(key_heads.shape, jnp.float32)
    (grad_keys, grad_values), grad_queries = lax.scan(
        block_step, (zero_heads, zero_heads), (query_blocks, seg_blocks, log_total, grad_blocks)
    )
    tok_count = projected.shape[0]
    return jnp.concatenate(
        [
            grad_queries.reshape(tok_count, -1),
            grad_keys.astype(jnp.bfloat16).reshape(tok_count, -1),
            grad_values.astype(jnp.bfloat16).reshape(tok_count, -1),
        ],
        axis=1,
    )


def shards(
    token_ids,
    seq_lengths,
    noise,
    noise_level,
    table,
    w_in,
    b_in,
    gain_first,
    shift_first,
    w_qkv,
    w_out,
    b_out,
    gain_second,
    shift_second,
    w_up,
    b_up,
    w_down,
    b_down,
    cotangent,
):
    tok_count = token_ids.shape[0]
    row_count = table.shape[0]
    group_ids = lax.all_gather(token_ids, "fsdp", axis=0, tiled=True)
    first_row = lax.axis_index("fsdp") * row_count
    owned = (group_ids[:, None] == first_row + jnp.arange(row_count)[None, :]).astype(jnp.bfloat16)
    owned_rows = jnp.dot(owned, table, preferred_element_type=jnp.float32).astype(jnp.bfloat16)
    tok_rows = lax.psum_scatter(owned_rows, "fsdp", scatter_dimension=0, tiled=True)
    tok_rows = tok_rows.astype(jnp.float32)
    vectors = (b_in, gain_first, shift_first, b_out, gain_second, shift_second, b_up, b_down)
    vec_all = lax.all_gather(jnp.concatenate(vectors), "fsdp", axis=0, tiled=False)
    vec_at = [0]
    for vector in vectors:
        vec_at.append(vec_at[-1] + vector.shape[0])
    (
        b_in_all,
        gain_first_all,
        shift_first_all,
        b_out_all,
        gain_second_all,
        shift_second_all,
        b_up_all,
        b_down_all,
    ) = [vec_all[:, lo:hi].reshape(-1) for lo, hi in zip(vec_at[:-1], vec_at[1:])]
    w_in_all = lax.all_gather(w_in, "fsdp", axis=0, tiled=True)
    w_qkv_all = lax.all_gather(w_qkv, "fsdp", axis=0, tiled=True)
    w_out_all = lax.all_gather(w_out, "fsdp", axis=0, tiled=True)
    w_up_all = lax.all_gather(w_up, "fsdp", axis=0, tiled=True)
    w_down_all = lax.all_gather(w_down, "fsdp", axis=0, tiled=True)
    seq_ends = jnp.cumsum(seq_lengths[0], dtype=jnp.int32)
    positions = jnp.arange(tok_count, dtype=jnp.int32)
    segment = jnp.sum((positions[:, None] >= seq_ends[None, :]).astype(jnp.int32), axis=1)
    live_rows = (segment < seq_lengths.shape[1]).astype(jnp.float32)[:, None]
    embedded = row_normalize(tok_rows)
    scale_in = lax.rsqrt(1.0 + noise_level * noise_level)[:, None]
    scaled = ((embedded + noise_level[:, None] * noise.astype(jnp.float32)) * scale_in).astype(
        jnp.bfloat16
    )
    resid_in = jnp.dot(scaled, w_in_all, preferred_element_type=jnp.float32) + b_in_all.astype(
        jnp.float32
    )
    std_first, first_pull = jax.vjp(standardize, resid_in)
    normed_a = (
        std_first * gain_first_all.astype(jnp.float32) + shift_first_all.astype(jnp.float32)
    ).astype(jnp.bfloat16)
    projected = jnp.dot(normed_a, w_qkv_all, preferred_element_type=jnp.float32).astype(
        jnp.bfloat16
    )
    attended, log_total = attention_forward(projected, segment)
    attended = attended.astype(jnp.bfloat16)
    resid_mid = (
        resid_in
        + jnp.dot(attended, w_out_all, preferred_element_type=jnp.float32)
        + b_out_all.astype(jnp.float32)
    )
    std_second, second_pull = jax.vjp(standardize, resid_mid)
    normed_b = (
        std_second * gain_second_all.astype(jnp.float32) + shift_second_all.astype(jnp.float32)
    ).astype(jnp.bfloat16)
    pre_act = jnp.dot(normed_b, w_up_all, preferred_element_type=jnp.float32) + b_up_all.astype(
        jnp.float32
    )
    activated, gelu_pull = jax.vjp(exact_gelu, pre_act)
    hidden = activated.astype(jnp.bfloat16)
    resid_out = (
        resid_mid
        + jnp.dot(hidden, w_down_all, preferred_element_type=jnp.float32)
        + b_down_all.astype(jnp.float32)
    )
    activations = (resid_out * live_rows).astype(jnp.bfloat16)
    grad_out = cotangent.astype(jnp.float32) * live_rows
    grad_down = grad_out.astype(jnp.bfloat16)
    b_down_term = jnp.sum(grad_down.astype(jnp.float32), axis=0)
    w_down_term = jnp.einsum("tf,td->fd", hidden, grad_down, preferred_element_type=jnp.float32)
    grad_hidden = jnp.einsum("td,fd->tf", grad_down, w_down_all, preferred_element_type=jnp.float32)
    grad_act = gelu_pull(grad_hidden)[0].astype(jnp.bfloat16)
    b_up_term = jnp.sum(grad_act.astype(jnp.float32), axis=0)
    w_up_term = jnp.einsum("td,tf->df", normed_b, grad_act, preferred_element_type=jnp.float32)
    grad_nb = jnp.einsum("tf,df->td", grad_act, w_up_all, preferred_element_type=jnp.float32)
    gain_second_term = jnp.sum(grad_nb * std_second, axis=0)
    shift_second_term = jnp.sum(grad_nb, axis=0)
    grad_mid = grad_out + second_pull(grad_nb * gain_second_all.astype(jnp.float32))[0]
    grad_att = grad_mid.astype(jnp.bfloat16)
    b_out_term = jnp.sum(grad_att.astype(jnp.float32), axis=0)
    w_out_term = jnp.einsum("tc,td->cd", attended, grad_att, preferred_element_type=jnp.float32)
    grad_attended = jnp.einsum(
        "td,cd->tc", grad_att, w_out_all, preferred_element_type=jnp.float32
    ).astype(jnp.bfloat16)
    grad_proj = attention_backward(projected, segment, log_total, grad_attended)
    w_qkv_term = jnp.einsum("td,te->de", normed_a, grad_proj, preferred_element_type=jnp.float32)
    grad_na = jnp.einsum("te,de->td", grad_proj, w_qkv_all, preferred_element_type=jnp.float32)
    gain_first_term = jnp.sum(grad_na * std_first, axis=0)
    shift_first_term = jnp.sum(grad_na, axis=0)
    grad_in = grad_mid + first_pull(grad_na * gain_first_all.astype(jnp.float32))[0]
    grad_pin = grad_in.astype(jnp.bfloat16)
    b_in_term = jnp.sum(grad_pin.astype(jnp.float32), axis=0)
    w_in_term = jnp.einsum("te,td->ed", scaled, grad_pin, preferred_element_type=jnp.float32)
    grad_scaled = jnp.einsum("td,ed->te", grad_pin, w_in_all, preferred_element_type=jnp.float32)
    noise_grad = grad_scaled * noise_level[:, None] * scale_in
    grad_embedded = grad_scaled * scale_in
    all_ids = lax.all_gather(token_ids, ("dp", "fsdp"), axis=0, tiled=True)
    all_grads = lax.all_gather(
        grad_embedded.astype(jnp.bfloat16), ("dp", "fsdp"), axis=0, tiled=True
    )
    owners = (first_row + jnp.arange(row_count)[:, None] == all_ids[None, :]).astype(jnp.bfloat16)
    row_grad = jnp.dot(owners, all_grads, preferred_element_type=jnp.float32)
    own_table = table.astype(jnp.float32)
    unused_rows, table_pull = jax.vjp(row_normalize, own_table)
    table_part = table_pull(row_grad)[0]

    def reduce_matrix(term):
        part = lax.psum_scatter(
            term.astype(jnp.bfloat16), "fsdp", scatter_dimension=0, tiled=True
        )
        return lax.psum(part, "dp").astype(jnp.float32)

    vec_terms = (
        b_in_term,
        gain_first_term,
        shift_first_term,
        b_out_term,
        gain_second_term,
        shift_second_term,
        b_up_term,
        b_down_term,
    )
    shard_count = lax.axis_size("fsdp")
    vec_term = jnp.concatenate([v.reshape(shard_count, -1) for v in vec_terms], axis=1)
    vec_part = lax.psum(vec_term, ("dp", "fsdp"))
    own_vec = lax.dynamic_index_in_dim(vec_part, lax.axis_index("fsdp"), 0, keepdims=False)
    vec_grads = [own_vec[lo:hi] for lo, hi in zip(vec_at[:-1], vec_at[1:])]
    return (
        activations,
        noise_grad,
        table_part,
        reduce_matrix(w_in_term),
        vec_grads[0],
        vec_grads[1],
        vec_grads[2],
        reduce_matrix(w_qkv_term),
        reduce_matrix(w_out_term),
        vec_grads[3],
        vec_grads[4],
        vec_grads[5],
        reduce_matrix(w_up_term),
        vec_grads[6],
        reduce_matrix(w_down_term),
        vec_grads[7],
    )


BF = jnp.bfloat16
F32 = jnp.float32
MESH_ID = pl.DeviceIdType.MESH
SEM_COUNT = 400
VMEM_LIMIT = 63 * 2**20
NT = (((1,), (1,)), ((), ()))
TN = (((0,), (0,)), ((), ()))
DIAG, ACROSS, TWIN = 0, 1, 2
FLIPS = ((1, 1), (1, 0), (0, 1))


def mm(a, b):
    return jnp.dot(a, b, preferred_element_type=F32)


def mm_nt(a, b):
    return lax.dot_general(a, b, NT, preferred_element_type=F32)


def mm_tn(a, b):
    return lax.dot_general(a, b, TN, preferred_element_type=F32)


def part(start, size):
    return pl.ds(pl.multiple_of(start, size), size)


def as_row(pair):
    return jnp.concatenate([pair[0:1, :], pair[1:2, :]], axis=1)


def as_col(pair):
    eye = lax.broadcasted_iota(jnp.int32, (128, 128), 0) == lax.broadcasted_iota(
        jnp.int32, (128, 128), 1
    )
    cols = [
        jnp.sum(jnp.where(eye, pair[k : k + 1, :], 0.0), axis=1, keepdims=True) for k in (0, 1)
    ]
    return jnp.concatenate(cols, axis=0)


def norm_parts(v):
    centred = v - jnp.mean(v, axis=-1, keepdims=True)
    rstd = lax.rsqrt(jnp.mean(centred * centred, axis=-1, keepdims=True) + norm_eps)
    return centred * rstd, rstd


def norm_back(u, n, rstd):
    return rstd * (
        u - jnp.mean(u, axis=-1, keepdims=True) - n * jnp.mean(u * n, axis=-1, keepdims=True)
    )


def layer_kernel(
    small_hbm, noise_hbm, table, w_in_hbm, w_qkv_hbm, w_out_hbm, w_up_hbm, w_down_hbm, cot_hbm,
    act_hbm, ngrad_hbm, tgrad_hbm, vout_hbm, f_in_hbm, f_qkv_hbm, f_out_hbm, f_up_hbm, f_dn_hbm,
    small, noise, w_in, w_qkv, w_out, w_up, w_down, cot,
    act, ngrad, tgrad, vout, f_in, f_qkv, f_out, f_up, f_dn,
    sm, smx, gsm, vec, vg, vq, vgy, vgz, vgf, bup, lives, idr,
    tp, tok, sc, win, wqkv, wout, wup, wdn, s_in, s_qkv, s_out, s_up,
    rin, rmid, gmid, t1, t2, t3, t4, na, proj, pr, att, asend, nb, gd, hid, ga,
    xs, xr, gatt, gos, go, g_in, g_qkv, g_out, g_dn,
    y_in, y_qkv, y_out, y_up, y_dn, z_in, z_qkv, z_out, z_up, z_dn, wis, wir,
    ss, rr, ls, credit,
):
    x = lax.axis_index("dp")
    f = lax.axis_index("fsdp")
    z, y, c = f // 4, lax.rem(f // 2, 2), lax.rem(f, 2)
    q = 2 * z + y
    g = 2 * x + c
    rows_here = table.shape[0]

    def dev(dx, dz, dy, dc):
        xx = lax.rem(x + dx, 2)
        zz = lax.rem(z + dz, 4)
        yy = lax.rem(y + dy, 2)
        cc = lax.rem(c + dc, 2)
        return (xx, zz * 4 + yy * 2 + cc)

    twin = dev(0, 0, 0, 1)
    across = dev(1, 0, 0, 0)
    pair_y = dev(0, 0, 1, 0)
    relay_to = (x, jnp.where(z == 2, 3, 0) * 4 + y * 2 + c)
    rel_dev = [dev(dx, 0, 0, dc) for dx, dc in FLIPS]
    rel_g = [2 * lax.rem(x + dx, 2) + lax.rem(c + dc, 2) for dx, dc in FLIPS]
    other_c = 1 - c

    def far(d):
        return lax.rem(z + 4 - d, 4)

    def to(d):
        return lax.rem(z + d, 4)

    sems = [0]
    pending = []
    inner = jnp.logical_or(z == 1, z == 2)
    outer = jnp.logical_not(inner)

    class Link:
        def __init__(self):
            self.at = sems[0]
            sems[0] += 1
            assert sems[0] <= SEM_COUNT

        def send(self, src, dst, device, arrives=None, only=None):
            self.only = only
            self.copy = pltpu.make_async_remote_copy(
                src_ref=src, dst_ref=dst, send_sem=ss.at[self.at],
                recv_sem=rr.at[self.at if arrives is None else arrives],
                device_id=device, device_id_type=MESH_ID,
            )
            if only is None:
                self.copy.start()
            else:
                pl.when(only)(self.copy.start)
            pending.append(self)
            return self

        def sent(self):
            pending.remove(self)
            if self.only is None:
                self.copy.wait_send()
            else:
                pl.when(self.only)(self.copy.wait_send)

        def got(self, ref):
            arrived(self.at, ref)

    def arrived(at, ref):
        pltpu.make_async_remote_copy(
            src_ref=ref, dst_ref=ref, send_sem=ss.at[0], recv_sem=rr.at[at],
            device_id=twin, device_id_type=MESH_ID,
        ).wait_recv()

    def each_rows(count, size, body):
        def step(i, carry):
            body(part(i * size, size))
            return carry

        lax.fori_loop(0, count // size, step, 0)

    def each(count, body):
        def step(i, carry):
            body(i)
            return carry

        lax.fori_loop(0, count, step, 0)

    local = [0]

    def moved(src, dst):
        copy = pltpu.make_async_copy(src, dst, ls.at[local[0]])
        local[0] += 1
        copy.start()
        return copy

    load_small = moved(small_hbm, small)
    load_in = moved(w_in_hbm, w_in)
    load_qkv = moved(w_qkv_hbm, w_qkv)
    load_cot = moved(cot_hbm, cot)
    own_table = moved(table, tp.at[c, pl.ds(0, rows_here)])
    load_noise = moved(noise_hbm, noise)
    load_out = moved(w_out_hbm, w_out)
    load_up = moved(w_up_hbm, w_up)
    load_down = moved(w_down_hbm, w_down)

    barrier = pltpu.get_barrier_semaphore()
    peers = [dev(0, d, 0, dc) for d in (1, 2, 3) for dc in (0, 1)] + rel_dev + [pair_y]
    for peer in peers:
        pl.semaphore_signal(barrier, inc=1, device_id=peer, device_id_type=MESH_ID)
    pl.semaphore_wait(barrier, len(peers))

    class GroupGather:
        def __init__(self, at):
            self.at = at
            self.across = Link().send(at(g), at(g), across)
            self.twin = Link().send(at(g), at(g), twin)

        def hop(self):
            self.across.got(self.at(rel_g[ACROSS]))
            self.second = Link().send(self.at(rel_g[ACROSS]), self.at(rel_g[ACROSS]), twin)

        def got_twin(self):
            self.twin.got(self.at(rel_g[TWIN]))

        def got_diag(self):
            self.second.got(self.at(rel_g[DIAG]))

    class Gather:
        def __init__(self, whole, mine, theirs, height, twins=None):
            self.whole, self.height = whole, height
            places = (self.sub(q, c), self.sub(q, c, twins))
            self.links = {}
            for d in (0, 2, 1, 3):
                only = {0: None, 2: None, 1: z != 3, 3: z != 0}[d]
                for dc in (1, 0):
                    if (d, dc) != (0, 0):
                        self.links[d, dc] = Link().send(
                            theirs if dc else mine, places[dc], dev(0, d, 0, dc), only=only
                        )

        def sub(self, block, core, whole=None):
            whole = self.whole if whole is None else whole
            if self.height is None:
                return whole.at[block, core]
            return whole.at[block, part(core * self.height, self.height)]

        def over_y(self, block):
            return Link().send(self.whole.at[block], self.whole.at[block], pair_y)

        def own(self):
            self.links[0, 1].got(self.sub(q, other_c))
            self.y_own = self.over_y(q)

        def second(self):
            block = 2 * far(2) + y
            for dc in (1, 0):
                ref = self.sub(block, other_c if dc else c)
                self.links[2, dc].got(ref)
                Link().send(
                    ref, ref, relay_to, only=inner,
                    arrives=jnp.where(z == 2, self.links[3, dc].at, self.links[1, dc].at),
                )
            self.y_second = self.over_y(block)

        def near(self):
            self.y_near = self.one(3, 1)

        def last(self):
            self.y_last = self.one(1, 3)

        def one(self, low, high):
            block = 2 * jnp.where(z < 2, far(low), far(high)) + y
            for dc in (1, 0):
                arrived(
                    jnp.where(z < 2, self.links[low, dc].at, self.links[high, dc].at),
                    self.sub(block, other_c if dc else c),
                )
            return self.over_y(block)

        def forward(self):
            self.second()
            self.near()
            self.last()

        def finish(self):
            self.y_own.got(self.whole.at[2 * z + 1 - y])
            self.y_second.got(self.whole.at[2 * far(2) + 1 - y])
            self.y_near.got(self.whole.at[2 * jnp.where(z < 2, far(3), far(1)) + 1 - y])
            self.y_last.got(self.whole.at[2 * jnp.where(z < 2, far(1), far(3)) + 1 - y])

    load_small.wait()
    sm[q, c] = small[...]
    small_links = [Link().send(small, gsm.at[rel], rel_dev[rel]) for rel in (DIAG, ACROSS)]
    gather_small = Gather(sm, small, small, None)

    own_rows = tp.at[c, pl.ds(0, rows_here)]
    table_link = Link().send(table, own_rows, twin)
    spare = tp.shape[1] - rows_here
    if spare:
        for core in (0, 1):
            tp[core, pl.ds(rows_here, spare), :] = jnp.zeros((spare, tp.shape[2]), BF)

    def pack(whole, spare_buf, height, pick):
        mine, theirs = pick(g), pick(2 * x + other_c)
        whole[q, part(c * height, height), :] = mine
        spare_buf[...] = theirs

    h = w_qkv.shape[0]
    hin = w_in.shape[0]

    def cols(ref, start, size=256):
        return ref[:, part(start, size)]

    win_at, wout_at = win.at[g], wout.at[g]
    load_in.wait()
    load_qkv.wait()
    win_at[q, c] = cols(w_in, 256 * g)
    s_in[0] = cols(w_in, 256 * (2 * x + other_c))
    gather_in = Gather(win_at, win_at.at[q, c], s_in.at[0], None, win.at[2 * x + other_c])
    pack(
        wqkv, s_qkv, h,
        lambda k: jnp.concatenate([cols(w_qkv, 1024 * n + 256 * k) for n in (0, 1, 2)], axis=1),
    )
    gather_qkv = Gather(wqkv, wqkv.at[q, part(c * h, h)], s_qkv, h)


    lives[:, 0:1] = jnp.where(as_col(small[18:20, :]) < 7.5, 1.0, 0.0)
    vg[...] = jnp.zeros_like(vg)

    def grad_down_rows(at):
        masked = cot[at, :].astype(F32) * lives[at, 0:1]
        gd[g, at, :] = masked.astype(BF)
        vg[6:7, :] += jnp.sum(masked, axis=0, keepdims=True)

    load_cot.wait()
    each_rows(256, 32, grad_down_rows)
    group_gd = GroupGather(lambda k: gd.at[k])

    gather_small.own()
    gather_small.forward()

    gather_small.finish()
    smx_link = Link().send(sm, smx, across)
    own_table.wait()
    table_link.got(tp.at[other_c, pl.ds(0, rows_here)])
    lane = lax.broadcasted_iota(jnp.int32, (256, tp.shape[1]), 1)

    def look_up(block):
        ids = as_col(sm[block, c, 16:18, :]).astype(jnp.int32)
        total = jnp.zeros((256, 256), F32)
        for core in (0, 1):
            first = (4 * z + 2 * y + core) * rows_here
            hit = jnp.where(lane == ids - first, 1.0, 0.0).astype(BF)
            total += mm(hit, tp[core])
        return total.astype(BF)

    emb_y = [Link() for _ in range(4)]
    for d in range(4):
        tok[d] = look_up(2 * to(d) + 1 - y)
        emb_y[d].send(tok.at[d], tok.at[8 + d], pair_y)

    def own_blocks(d):
        tok[4 + d] = look_up(2 * lax.rem(z + d, 4) + y)

    each(4, own_blocks)
    gather_in.own()
    gather_qkv.own()
    emb_z = [None]
    for d in (1, 2, 3):
        emb_y[d].got(tok.at[8 + d])
        tok[4 + d] = tok[4 + d] + tok[8 + d]
        emb_z.append(Link().send(tok.at[4 + d], tok.at[11 + d], dev(0, d, 0, 0)))
    emb_y[0].got(tok.at[8])

    for load in (load_noise, load_out, load_up, load_down):
        load.wait()
    pack(wout_at, s_out, h, lambda k: cols(w_out, 256 * k))
    ct = lax.broadcasted_iota(jnp.int32, (h, 128), 1) < 64
    for j in range(8):
        first = w_up[:, part(128 * (4 * j + x), 128)].astype(F32)
        second = w_up[:, part(128 * (4 * j + 2 + x), 128)].astype(F32)
        low = jnp.where(ct, first, pltpu.roll(second, 64, 1)).astype(BF)
        high = jnp.where(ct, pltpu.roll(first, 64, 1), second).astype(BF)
        wup[q, part(c * h, h), 128 * j : 128 * j + 128] = jnp.where(c == 0, low, high)
        s_up[:, 128 * j : 128 * j + 128] = jnp.where(c == 0, high, low)
    wdn[q, part(c * h, h), :] = w_down[part(g * h, h), :]
    gather_in.forward()
    gather_qkv.forward()
    for j in range(8):
        vec[:, 128 * j : 128 * j + 128] = sm[j, 0, 0:16, :] + sm[j, 1, 0:16, :]

    gather_in.finish()
    group_in = GroupGather(lambda k: win.at[k])
    group_gd.hop()
    rows_sum = tok[4].astype(F32) + tok[8].astype(F32)
    for d in (1, 2, 3):
        emb_z[d].got(tok.at[11 + d])
        rows_sum += tok[11 + d].astype(F32)
    gather_out = Gather(
        wout_at, wout_at.at[q, part(c * h, h)], s_out, h, wout.at[2 * x + other_c]
    )
    gather_up = Gather(wup, wup.at[q, part(c * h, h)], s_up, h)
    gather_dn = Gather(
        wdn, w_down.at[part(g * h, h)], w_down.at[part((2 * x + other_c) * h, h)], h
    )

    for d in range(4):
        emb_y[d].sent()
    for d in (1, 2, 3):
        emb_z[d].sent()
    level = as_col(small[20:22, :])
    scale_in = lax.rsqrt(1.0 + level * level)
    embedded = rows_sum * lax.rsqrt(jnp.mean(rows_sum * rows_sum, axis=1, keepdims=True) + norm_eps)
    sc[g] = ((embedded + level * noise[...].astype(F32)) * scale_in).astype(BF)
    group_sc = GroupGather(lambda k: sc.at[k])

    group_in.hop()
    group_in.got_twin()
    group_in.got_diag()

    def win_mat(k):
        return win[k].reshape(256, 256)

    def first_norm(row, keep):
        for k in range(4):
            keep[:, 256 * k : 256 * k + 256] = (
                mm(sc[row], win_mat(k)) + vec[0:1, 256 * k : 256 * k + 256]
            )

        def chunk(at):
            n, _ = norm_parts(keep[at, :])
            na[row, at, :] = (n * vec[1:2, :] + vec[2:3, :]).astype(BF)

        each_rows(256, 32, chunk)

    def project(row):
        def block(k):
            at = part(k * 256, 256)
            proj[row, :, at] = mm(na[row], wqkv[:, :, at].reshape(1024, 256)).astype(BF)

        each(3, block)

    first_norm(g, rin)
    group_sc.hop()
    gather_out.own()
    gather_out.forward()
    gather_up.own()
    gather_dn.own()
    group_sc.got_twin()
    first_norm(rel_g[TWIN], t1)
    first_norm(rel_g[ACROSS], t1)
    group_sc.got_diag()
    first_norm(rel_g[DIAG], t1)
    gather_qkv.finish()
    for rel in range(3):
        project(rel_g[rel])
    project(g)
    gather_out.finish()
    group_out = GroupGather(lambda k: wout.at[k])

    head_of = lax.broadcasted_iota(jnp.int32, (1, 256), 1) // 64
    small_links[DIAG].got(gsm.at[DIAG])
    small_links[ACROSS].got(gsm.at[ACROSS])

    def attend(row, pair):
        same = as_col(pair) == as_row(pair)
        keys = proj[row, :, 256:512]
        values = proj[row, :, 512:768]
        queries = proj[row, :, 0:256]
        t2[...] = jnp.zeros_like(t2)

        def head(k):
            mine = head_of == k
            q_head = jnp.where(mine, queries, jnp.zeros_like(queries))
            scores = jnp.where(same, mm_nt(q_head, keys) * 0.125, -1e9)
            weights = jnp.exp(scores - jnp.max(scores, axis=-1, keepdims=True))
            low_probs = (weights / jnp.sum(weights, axis=-1, keepdims=True)).astype(BF)
            pr[row * 4 + k] = low_probs
            t2[...] += mm(low_probs, jnp.where(mine, values, jnp.zeros_like(values)))

        each(4, head)
        return t2[...].astype(BF)

    att_links = []
    my_cols = part(256 * g, 256)
    for rel in range(3):
        pair = sm[q, other_c, 18:20, :] if rel == TWIN else gsm[rel, 18:20, :]
        asend[rel] = attend(rel_g[rel], pair)
        att_links.append(Link().send(asend.at[rel], att.at[:, my_cols], rel_dev[rel]))
        if rel == DIAG:
            gather_up.second()
        if rel == TWIN:
            gather_up.near()
            gather_up.last()
    att[:, my_cols] = attend(g, small[18:20, :])
    group_out.hop()
    group_out.got_twin()
    group_out.got_diag()
    for rel in (TWIN, ACROSS, DIAG):
        att_links[rel].got(att.at[:, part(256 * rel_g[rel], 256)])

    def out_block(k):
        at = part(k * 256, 256)
        rmid[:, at] = rin[:, at] + mm(att[...], wout[k].reshape(1024, 256)) + vec[3:4, at]

    each(4, out_block)

    def second_norm(at):
        n, _ = norm_parts(rmid[at, :])
        nb[g, at, :] = (n * vec[4:5, :] + vec[5:6, :]).astype(BF)

    each_rows(256, 32, second_norm)
    nb_across = Link().send(nb.at[g], nb.at[g], across)
    nb_twin = Link().send(nb.at[g], nb.at[g], twin)
    nb_pass = Link()
    gather_dn.forward()
    group_gd.got_twin()
    group_gd.got_diag()

    bup[...] = jnp.zeros_like(bup)
    for k in range(4):
        bup[0:1, :] += jnp.where(g == k, vec[7 + k : 8 + k, :], 0.0)

    def ff_row(row):
        def block(k):
            at = part(k * 256, 256)
            t2[...] = mm(nb[row], wup[:, :, at].reshape(1024, 256)) + bup[0:1, at]
            t3[...] = mm_nt(gd[row], wdn[pl.ds(2 * k, 2)].reshape(256, 1024))

            def chunk(rows_at):
                pre = t2[rows_at, :]
                cdf = 0.5 + 0.5 * lax.erf(pre * 0.7071067811865476)
                pdf = jnp.exp(-0.5 * pre * pre) * 0.3989422804014327
                t2[rows_at, :] = pre * cdf
                ga_low = (t3[rows_at, :] * (cdf + pre * pdf)).astype(BF)
                ga[row, rows_at, at] = ga_low
                bup[1:2, at] += jnp.sum(ga_low.astype(F32), axis=0, keepdims=True)

            each_rows(256, 32, chunk)
            hid[pl.ds(2 * row, 2), :, at] = t2[...].astype(BF).reshape(2, 128, 256)

        each(4, block)

    gather_up.finish()
    gather_dn.finish()
    ff_row(g)
    nb_twin.got(nb.at[rel_g[TWIN]])
    ff_row(rel_g[TWIN])
    nb_across.got(nb.at[rel_g[ACROSS]])
    nb_pass.send(nb.at[rel_g[ACROSS]], nb.at[rel_g[ACROSS]], twin)
    ff_row(rel_g[ACROSS])
    nb_pass.got(nb.at[rel_g[DIAG]])
    ff_row(rel_g[DIAG])

    class GroupSum:
        def __init__(self, slot, partial):
            self.slot, self.partial = slot, partial

        def first(self):
            self.partial(rel_g[DIAG], xs.at[self.slot, 0])
            self.a = Link().send(xs.at[self.slot, 0], xr.at[self.slot, 0], twin)

        def second(self):
            self.partial(rel_g[ACROSS], t1)
            self.a.got(xr.at[self.slot, 0])

            def chunk(at):
                xs[self.slot, 1, at, :] = (t1[at, :] + xr[self.slot, 0, at, :].astype(F32)).astype(BF)

            each_rows(256, 32, chunk)

        def second_send(self):
            self.b = Link().send(xs.at[self.slot, 1], xr.at[self.slot, 1], across)

        def third(self):
            self.partial(rel_g[TWIN], xs.at[self.slot, 2])
            self.c = Link().send(xs.at[self.slot, 2], xr.at[self.slot, 2], twin)

        def own(self, into):
            self.partial(g, into)
            self.into = into

        def total(self):
            self.c.got(xr.at[self.slot, 2])
            self.b.got(xr.at[self.slot, 1])

        def rows(self, at):
            return (
                self.into[at, :].astype(F32)
                + xr[self.slot, 1, at, :].astype(F32)
                + xr[self.slot, 2, at, :].astype(F32)
            )

        def release(self):
            for link in (self.a, self.b, self.c):
                link.sent()

    def nb_partial(row, into):
        def block(k):
            into[:, part(k * 256, 256)] = mm_nt(
                ga[row], wup[pl.ds(2 * k, 2)].reshape(256, 1024)
            ).astype(into.dtype)

        each(4, block)

    def out_partial(row, into):
        def block(k):
            at = part(k * 256, 256)
            into[:, at] = mm(
                hid[pl.ds(2 * row, 2)].reshape(256, 1024), wdn[:, :, at].reshape(1024, 256)
            ).astype(into.dtype)

        each(4, block)

    class Scatter:
        def __init__(self, grad, y_buf, z_buf, final, height):
            self.grad, self.y_buf, self.z_buf, self.final, self.height = (
                grad, y_buf, z_buf, final, height,
            )

        def chunks(self, body):
            if self.height is None:
                each(2, body)
            else:
                each_rows(2 * self.height, 32, body)

        def half(self, core):
            if self.height is None:
                return self.grad.at[q, core]
            return self.grad.at[q, part(core * self.height, self.height)]

        def start(self, count=4):
            even = lax.rem(z, 2) == 0
            self.goals = (
                jnp.where(even, 3, 0), jnp.where(even, 1, 2), lax.rem(z + 2, 4), z,
            )
            self.y_links = []
            self.z_links = [Link() for _ in range(4)]
            self.more(count)

        def more(self, count=1):
            for _ in range(count):
                e = len(self.y_links)
                self.y_links.append(
                    Link().send(self.grad.at[2 * self.goals[e] + 1 - y], self.y_buf.at[e], pair_y)
                )

        def add_y(self, e):
            self.y_links[e].got(self.y_buf.at[e])
            block = 2 * self.goals[e] + y

            def chunk(at):
                self.grad[block, at] = (
                    self.grad[block, at].astype(F32) + self.y_buf[e, at].astype(F32)
                ).astype(BF)

            self.chunks(chunk)
            return self.grad.at[block]

        def end_to_end(self):
            ref = self.add_y(0)
            self.z_links[0].send(
                ref, self.z_buf.at[0], (x, (z + 1 - 2 * lax.rem(z, 2)) * 4 + y * 2 + c)
            )

        def near(self):
            ref = self.add_y(1)
            slot = jnp.where(inner, 2, 1)
            self.z_links[1].send(
                ref, self.z_buf.at[slot], (x, self.goals[1] * 4 + y * 2 + c),
                arrives=jnp.where(inner, self.z_links[2].at, self.z_links[1].at),
            )

        def second(self):
            ref = self.add_y(2)
            block = 2 * self.goals[2] + y

            def relayed():
                self.z_links[0].got(self.z_buf.at[0])

                def chunk(at):
                    self.grad[block, at] = (
                        self.grad[block, at].astype(F32) + self.z_buf[0, at].astype(F32)
                    ).astype(BF)

                self.chunks(chunk)

            pl.when(inner)(relayed)
            self.z_links[3].send(ref, self.z_buf.at[3], dev(0, 2, 0, 0))

        def own(self):
            self.add_y(3)

        def middle(self):
            self.end_to_end()
            self.near()
            self.second()
            self.own()

        def last(self):
            def summed(slots):
                def run():
                    for slot in slots:
                        self.z_links[slot].got(self.z_buf.at[slot])

                    def chunk(at):
                        total = self.grad[q, at].astype(F32)
                        for slot in slots:
                            total += self.z_buf[slot, at].astype(F32)
                        self.grad[q, at] = total.astype(BF)

                    self.chunks(chunk)

                return run

            pl.when(inner)(summed((1, 2, 3)))
            pl.when(outer)(summed((0, 3)))
            self.f_links = []
            for rel in range(3):
                core = lax.rem(c + FLIPS[rel][1], 2)
                self.f_links.append(
                    Link().send(
                        self.half(core),
                        self.final.at[g],
                        rel_dev[rel],
                    )
                )
            self.final[g] = self.half(c)[...]

        def finish(self):
            for rel in range(3):
                self.f_links[rel].got(self.final.at[rel_g[rel]])

    sum_nb = GroupSum(0, nb_partial)
    sum_nb.first()
    sum_nb.second()
    sum_nb.second_send()
    sum_nb.third()

    scatter_dn = Scatter(g_dn, y_dn, z_dn, f_dn, h)
    scatter_up = Scatter(hid, y_up, z_up, f_up, h)
    sum_out = GroupSum(1, out_partial)

    def dn_block(k):
        at = part(k * 256, 256)
        lhs = hid[:, :, at].reshape(1024, 256)
        g_dn[pl.ds(2 * k, 2)] = mm_tn(lhs, gd[...].reshape(1024, 1024)).astype(BF).reshape(
            2, 128, 1024
        )

    each(4, dn_block)
    scatter_dn.start()
    sum_out.first()
    sum_out.second()
    sum_out.third()

    sum_out.own(act)

    def up_block(k):
        at = part(k * 256, 256)
        lhs = nb[:, :, at].reshape(1024, 256)
        hid[pl.ds(2 * k, 2)] = mm_tn(lhs, ga[...].reshape(1024, 1024)).astype(BF).reshape(
            2, 128, 1024
        )

    each(4, up_block)
    scatter_up.start()

    sum_nb.own(t1)
    scatter_dn.end_to_end()
    sum_nb.total()

    def second_back(at):
        grad_nb = sum_nb.rows(at)
        n, rstd = norm_parts(rmid[at, :])
        vg[4:5, :] += jnp.sum(grad_nb * n, axis=0, keepdims=True)
        vg[5:6, :] += jnp.sum(grad_nb, axis=0, keepdims=True)
        mid = gd[g, at, :].astype(F32) + norm_back(grad_nb * vec[4:5, :], n, rstd)
        gmid[at, :] = mid
        low_mid = mid.astype(BF)
        gatt[1, at, :] = low_mid
        vg[3:4, :] += jnp.sum(low_mid.astype(F32), axis=0, keepdims=True)

    each_rows(256, 32, second_back)

    def grad_o_part(to_g):
        total = jnp.zeros((256, 256), F32)
        for k in range(4):
            total += mm_nt(
                gatt[1, :, 256 * k : 256 * k + 256], wout[k, pl.ds(2 * to_g, 2)].reshape(256, 256)
            )
        return total.astype(BF)

    go_links = []
    for rel in range(3):
        gos[rel] = grad_o_part(rel_g[rel])
        go_links.append(Link().send(gos.at[rel], go.at[g], rel_dev[rel]))
    go[g] = grad_o_part(g)

    sum_out.second_send()
    sum_nb.release()
    scatter_dn.near()
    scatter_dn.second()
    for rel in (TWIN, ACROSS, DIAG):
        go_links[rel].got(go.at[rel_g[rel]])

    def attend_back(row):
        keys = proj[row, :, 256:512]
        values = proj[row, :, 512:768]
        queries = proj[row, :, 0:256]
        grad_rows = go[row]
        zero = jnp.zeros_like(keys)
        for buf in (t2, t3, t4):
            buf[...] = jnp.zeros_like(buf)

        def head(k):
            mine = head_of == k
            probs = pr[row * 4 + k]
            g_head = jnp.where(mine, grad_rows, zero)
            t4[...] += mm_tn(probs, g_head)
            grad_p = mm_nt(g_head, values)
            wide = probs.astype(F32)
            grad_s = wide * (grad_p - jnp.sum(grad_p * wide, axis=-1, keepdims=True))
            low_s = (grad_s * 0.125).astype(BF)
            t2[...] += mm(low_s, jnp.where(mine, keys, zero))
            t3[...] += mm_tn(low_s, jnp.where(mine, queries, zero))

        each(4, head)
        proj[row, :, 0:256] = t2[...].astype(BF)
        proj[row, :, 256:512] = t3[...].astype(BF)
        proj[row, :, 512:768] = t4[...].astype(BF)

    def na_partial(row, into):
        def block(k):
            into[:, part(k * 256, 256)] = mm_nt(
                proj[row], wqkv[pl.ds(2 * k, 2)].reshape(256, 768)
            ).astype(into.dtype)

        each(4, block)

    sum_na = GroupSum(0, na_partial)
    attend_back(rel_g[DIAG])
    sum_na.first()
    attend_back(rel_g[ACROSS])
    sum_na.second()
    sum_na.second_send()
    scatter_dn.own()
    scatter_up.end_to_end()
    attend_back(rel_g[TWIN])
    sum_na.third()
    scatter_up.near()
    attend_back(g)
    sum_na.own(t1)

    scatter_qkv = Scatter(g_qkv, y_qkv, z_qkv, f_qkv, h)
    scatter_out = Scatter(g_out, y_out, z_out, f_out, h)
    scatter_in = Scatter(g_in, y_in, z_in, f_in, None)

    def qkv_block(k):
        at = part(k * 256, 256)
        lhs = na[:, :, at].reshape(1024, 256)
        g_qkv[pl.ds(2 * k, 2)] = mm_tn(lhs, proj[...].reshape(1024, 768)).astype(BF).reshape(
            2, 128, 768
        )

    each(4, qkv_block)
    scatter_qkv.start(1)
    scatter_up.second()
    scatter_dn.last()

    sum_out.total()

    def out_rows(at):
        whole = rmid[at, :] + sum_out.rows(at) + vec[6:7, :]
        act[at, :] = (whole * lives[at, 0:1]).astype(BF)

    each_rows(256, 32, out_rows)
    stores = [moved(act, act_hbm)]
    sum_out.release()
    for rel in range(3):
        pl.semaphore_signal(credit, inc=1, device_id=rel_dev[rel], device_id_type=MESH_ID)

    sum_na.total()

    def first_back(at):
        grad_na = sum_na.rows(at)
        n, rstd = norm_parts(rin[at, :])
        vg[1:2, :] += jnp.sum(grad_na * n, axis=0, keepdims=True)
        vg[2:3, :] += jnp.sum(grad_na, axis=0, keepdims=True)
        low_in = (gmid[at, :] + norm_back(grad_na * vec[1:2, :], n, rstd)).astype(BF)
        gatt[0, at, :] = low_in
        vg[0:1, :] += jnp.sum(low_in.astype(F32), axis=0, keepdims=True)

    each_rows(256, 32, first_back)
    for k in range(4):
        vg[7 + k : 8 + k, :] = jnp.where(g == k, bup[1:2, :], 0.0)
    for j in range(8):
        vq[j % 2, j // 2] = vg[:, 128 * j : 128 * j + 128]
    vy_link = Link().send(vq.at[1 - y], vgy, pair_y)

    grad_scaled = jnp.zeros((256, 256), F32)
    for k in range(4):
        grad_scaled += mm_nt(gatt[0, :, 256 * k : 256 * k + 256], win_mat(k))
    level = as_col(small[20:22, :])
    scale_in = lax.rsqrt(1.0 + level * level)
    ngrad[...] = grad_scaled * (level * scale_in)
    stores.append(moved(ngrad, ngrad_hbm))

    def set_at(other_x, other_y, other_core):
        return ((lax.rem(x + other_x, 2) * 2 + lax.rem(y + other_y, 2)) * 2 + lax.rem(c + other_core, 2)) * 4

    home = tok.at[set_at(0, 0, 0) + z]
    tok[set_at(0, 0, 0) + z] = (grad_scaled * scale_in).astype(BF)
    tok_z = [None] + [Link().send(home, home, dev(0, d, 0, 0)) for d in (1, 2, 3)]
    tok_x = {}
    tok_y = {}
    tok_t = {}

    def spread(spot, key, across_too):
        ref = tok.at[spot]
        if across_too:
            tok_x[key] = Link().send(ref, ref, across)
        tok_t[across_too, key] = Link().send(ref, ref, twin)

    tok_y[0] = Link().send(home, home, pair_y)
    spread(set_at(0, 0, 0) + z, (0, 0), True)

    def wog_partial(k, into):
        for j in range(4):
            into[:, 256 * j : 256 * j + 256] = mm_tn(
                att[:, 256 * j : 256 * j + 256], gatt[1, :, part(256 * k, 256)]
            ).astype(into.dtype)

    pl.semaphore_wait(credit, 3)
    sum_wog = GroupSum(1, wog_partial)
    sum_wog.first()
    sum_wog.second()
    sum_wog.second_send()
    sum_wog.third()
    sum_wog.own(t1)
    wi_links = []
    for rel in range(3):
        wis[rel] = mm_tn(sc[g], gatt[0, :, part(256 * rel_g[rel], 256)]).astype(BF)
        wi_links.append(Link().send(wis.at[rel], wir.at[rel], rel_dev[rel]))
    wi_own = mm_tn(sc[g], gatt[0, :, part(256 * g, 256)])

    for d in (1, 2, 3):
        spot = set_at(0, 0, 0) + far(d)
        tok_z[d].got(tok.at[spot])
        tok_y[d] = Link().send(tok.at[spot], tok.at[spot], pair_y)
        spread(spot, (0, d), True)
        scatter_qkv.more()
        if d == 1:
            scatter_up.own()
            scatter_qkv.end_to_end()

    sum_wog.total()
    for j in range(4):
        at = slice(256 * j, 256 * j + 256)
        block = t1[:, at] + xr[1, 1, :, at].astype(F32) + xr[1, 2, :, at].astype(F32)
        g_out[2 * j : 2 * j + 2] = block.astype(BF).reshape(2, 128, 256)
    scatter_out.start()
    for rel in range(3):
        wi_links[rel].got(wir.at[rel])
        wi_own += wir[rel].astype(F32)
    g_in[...] = wi_own.astype(BF).reshape(8, 2, 16, 256)
    scatter_in.start()

    vy_link.got(vgy)
    vq[y] = vq[y] + vgy[...]
    vz_links = [
        Link().send(vq.at[y, to(d)], vgz.at[d - 1], dev(0, d, 0, 0)) for d in (1, 2, 3)
    ]

    for d in range(4):
        spot = set_at(0, 1, 0) + far(d)
        tok_y[d].got(tok.at[spot])
        spread(spot, (1, d), True)

    scatter_qkv.near()
    scatter_qkv.second()
    scatter_qkv.own()
    scatter_out.middle()

    for d in (1, 2, 3):
        vz_links[d - 1].got(vgz.at[d - 1])
    vtot = vq[y, z] + vgz[0] + vgz[1] + vgz[2]
    vgf[3] = vtot
    vf_links = [Link().send(vgf.at[3], vgf.at[rel], rel_dev[rel]) for rel in range(3)]

    smx_link.got(smx)
    for other_x in (0, 1):
        for yy in (0, 1):
            for core in (0, 1):
                source = sm if other_x == 0 else smx
                for zz in range(4):
                    idr[(other_x * 2 + yy) * 2 + core : (other_x * 2 + yy) * 2 + core + 1, 256 * zz : 256 * zz + 256] = (
                        as_row(source[2 * zz + yy, core, 16:18, :])
                    )

    tile = 400
    base = (f * rows_here).astype(F32)
    tile_row = lax.broadcasted_iota(jnp.int32, (tile, 1024), 0).astype(F32)

    def table_add(other_x, other_y, other_core, begin):
        spot = set_at(other_x, other_y, other_core)
        row = (other_x * 2 + lax.rem(y + other_y, 2)) * 2 + lax.rem(c + other_core, 2)
        ids = idr[pl.ds(row, 1), :] - base

        def block(k):
            at = part(k * tile, tile)
            hit = jnp.where(tile_row == ids - (k * tile).astype(F32), 1.0, 0.0).astype(BF)
            add = mm(hit, tok[pl.ds(spot, 4)].reshape(1024, 256))
            if begin:
                tgrad[at, :] = add
            else:
                tgrad[at, :] += add

        each(rows_here // tile, block)

    def twin_set(from_x, other_y):
        for d in range(4):
            tok_t[from_x == 0, (other_y, d)].got(tok.at[set_at(from_x, other_y, 1) + far(d)])

    table_add(0, 0, 0, True)
    twin_set(0, 0)
    table_add(0, 0, 1, False)
    scatter_up.last()
    table_add(0, 1, 0, False)
    twin_set(0, 1)
    table_add(0, 1, 1, False)
    scatter_in.middle()
    for other_y in (0, 1):
        for d in range(4):
            spot = set_at(1, other_y, 0) + far(d)
            tok_x[other_y, d].got(tok.at[spot])
            spread(spot, (other_y, d), False)
        table_add(1, other_y, 0, False)
    scatter_qkv.last()
    scatter_out.last()
    scatter_in.last()
    for other_y in (0, 1):
        twin_set(1, other_y)
        table_add(1, other_y, 1, False)

    def table_rows(at):
        values = tp[c, at, :].astype(F32)
        r = lax.rsqrt(jnp.mean(values * values, axis=1, keepdims=True) + norm_eps)
        row_grad = tgrad[at, :]
        slope = jnp.mean(row_grad * values, axis=1, keepdims=True)
        tgrad[at, :] = r * row_grad - values * (r * r * r * slope)

    each_rows(rows_here, 80, table_rows)
    stores.append(moved(tgrad, tgrad_hbm))

    for rel in range(3):
        vf_links[rel].got(vgf.at[rel])
    vout[...] = vgf[0] + vgf[1] + vgf[2] + vgf[3]
    for scatter in (scatter_dn, scatter_up, scatter_qkv, scatter_out, scatter_in):
        scatter.finish()
    for k, (src, dst) in enumerate(((f_in, f_in_hbm), (f_qkv, f_qkv_hbm), (f_out, f_out_hbm), (f_up, f_up_hbm), (f_dn, f_dn_hbm), (vout, vout_hbm))):
        stores.append(moved(src, dst))
    for link in list(pending):
        link.sent()
    for store in stores:
        store.wait()


def finish_kernel(
    act_in, ngrad_in, tgrad_in, vout, f_in, f_qkv, f_out, f_up, f_dn,
    act, ngrad, tgrad, w_in, b_in, gain_a, shift_a, w_qkv, w_out, b_out, gain_b, shift_b,
    w_up, b_up, w_dn, b_dn,
):
    c = lax.rem(lax.axis_index("fsdp"), 2)
    act[...] = act_in[...]
    ngrad[...] = ngrad_in[...]
    tgrad[...] = tgrad_in[...]
    rows = jnp.where(c == 0, vout[...], pltpu.roll(vout[...], 64, 1))
    for k, ref in enumerate((b_in, gain_a, shift_a, b_out, gain_b, shift_b, b_dn)):
        ref[...] = rows[k, 0:64]
    for k in range(4):
        b_up[64 * k : 64 * k + 64] = rows[7 + k, 0:64]
    h = w_out.shape[0]
    low_half = lax.broadcasted_iota(jnp.int32, (h, 128), 1) < 64
    for g in range(4):
        at = slice(256 * g, 256 * g + 256)
        w_in[:, at] = f_in[g].astype(F32)
        w_out[:, at] = f_out[g].astype(F32)
        for n in range(3):
            w_qkv[:, 1024 * n + 256 * g : 1024 * n + 256 * g + 256] = f_qkv[
                g, :, 256 * n : 256 * n + 256
            ].astype(F32)
        w_dn[h * g : h * g + h, :] = f_dn[g].astype(F32)
    for shard in range(16):
        at = slice(128 * (shard // 2), 128 * (shard // 2) + 128)
        for half in (0, 1):
            first, second = f_up[2 * half, :, at].astype(F32), f_up[2 * half + 1, :, at].astype(F32)
            if shard % 2 == 0:
                both = jnp.where(low_half, first, pltpu.roll(second, 64, 1))
            else:
                both = jnp.where(low_half, pltpu.roll(first, 64, 1), second)
            w_up[:, 256 * shard + 128 * half : 256 * shard + 128 * half + 128] = both


def small_pack(seq_lengths, token_ids, noise_level, vectors, b_up):
    tok_count = token_ids.shape[0]
    seq_ends = jnp.cumsum(seq_lengths[0], dtype=jnp.int32)
    positions = jnp.arange(tok_count, dtype=jnp.int32)
    segment = jnp.sum((positions[:, None] >= seq_ends[None, :]).astype(jnp.int32), axis=1)
    vecs = jnp.concatenate([v.reshape(1, -1) for v in vectors] + [b_up.reshape(4, -1)], axis=0)
    vecs = vecs.astype(F32)
    half = (jnp.arange(128) // 64) == lax.axis_index("fsdp") % 2
    vecs = jnp.where(half[None, :], jnp.concatenate([vecs, vecs], axis=1), 0.0)
    blank = jnp.zeros((16 - vecs.shape[0], 128), F32)
    tail = jnp.zeros((2, 128), F32)
    return jnp.concatenate(
        [
            vecs,
            blank,
            token_ids.astype(F32).reshape(2, 128),
            segment.astype(F32).reshape(2, 128),
            noise_level.reshape(2, 128),
            tail,
        ],
        axis=0,
    )


def fused_shards(
    token_ids, seq_lengths, noise, noise_level, table, w_in, b_in, gain_first, shift_first, w_qkv,
    w_out, b_out, gain_second, shift_second, w_up, b_up, w_down, b_down, cotangent,
):
    small = small_pack(
        seq_lengths, token_ids, noise_level,
        (b_in, gain_first, shift_first, b_out, gain_second, shift_second, b_down), b_up,
    )
    vmem = pl.BlockSpec(memory_space=pltpu.VMEM)
    hbm = pl.BlockSpec(memory_space=pl.ANY)

    def shape(*dims, dtype=BF):
        return jax.ShapeDtypeStruct(dims, dtype)

    rows_here = table.shape[0]
    padded = -(-rows_here // 256) * 256
    outs = [
        shape(256, 1024), shape(256, 256, dtype=F32), shape(rows_here, 256, dtype=F32),
        shape(16, 128, dtype=F32), shape(4, 16, 256), shape(4, 64, 768), shape(4, 64, 256),
        shape(4, 64, 1024), shape(4, 64, 1024),
    ]

    held = [pltpu.VMEM(v.shape, v.dtype) for v in (small, noise, w_in, w_qkv, w_out, w_up, w_down, cotangent)]
    held += [pltpu.VMEM(v.shape, v.dtype) for v in outs]

    def bf(*dims):
        return pltpu.VMEM(dims, BF)

    def fl(*dims):
        return pltpu.VMEM(dims, F32)

    scratch = [
        fl(8, 2, 24, 128), fl(8, 2, 24, 128), fl(2, 24, 128),
        fl(16, 1024), fl(16, 1024), fl(2, 4, 16, 128), fl(4, 16, 128), fl(3, 16, 128),
        fl(4, 16, 128), fl(8, 1024), fl(256, 128), fl(8, 1024),
        bf(2, padded, 256), bf(32, 256, 256), bf(4, 256, 256), bf(4, 8, 2, 16, 256),
        bf(8, 128, 768), bf(4, 8, 128, 256), bf(8, 128, 1024), bf(8, 128, 1024),
        bf(2, 16, 256), bf(64, 768), bf(64, 256), bf(64, 1024),
        fl(256, 1024), fl(256, 1024), fl(256, 1024), fl(256, 1024),
        fl(256, 256), fl(256, 256), fl(256, 256),
        bf(4, 256, 1024), bf(4, 256, 768), bf(16, 256, 256), bf(256, 1024), bf(3, 256, 256),
        bf(4, 256, 1024), bf(4, 256, 1024), bf(8, 128, 1024), bf(4, 256, 1024),
        bf(2, 3, 256, 1024), bf(2, 3, 256, 1024), bf(2, 256, 1024), bf(3, 256, 256), bf(4, 256, 256),
        bf(8, 2, 16, 256), bf(8, 128, 768), bf(8, 128, 256), bf(8, 128, 1024),
        bf(4, 2, 16, 256), bf(4, 128, 768), bf(4, 128, 256), bf(4, 128, 1024), bf(4, 128, 1024),
        bf(4, 2, 16, 256), bf(4, 128, 768), bf(4, 128, 256), bf(4, 128, 1024), bf(4, 128, 1024),
        bf(3, 256, 256), bf(3, 256, 256),
        pltpu.SemaphoreType.DMA((SEM_COUNT,)), pltpu.SemaphoreType.DMA((SEM_COUNT,)),
        pltpu.SemaphoreType.DMA((20,)), pltpu.SemaphoreType.REGULAR,
    ]
    parts = pl.pallas_call(
        layer_kernel,
        out_shape=outs,
        in_specs=[hbm] * 9,
        out_specs=[hbm] * len(outs),
        scratch_shapes=held + scratch,
        compiler_params=pltpu.CompilerParams(
            collective_id=0, has_side_effects=True, vmem_limit_bytes=VMEM_LIMIT
        ),
        cost_estimate=pl.CostEstimate(flops=40 * 10**9, bytes_accessed=30 * 10**6, transcendentals=0),
    )(small, noise, table, w_in, w_qkv, w_out, w_up, w_down, cotangent)
    f32 = lambda a: jax.ShapeDtypeStruct(a.shape, F32)
    finals = [
        outs[0], outs[1], outs[2], f32(w_in), f32(b_in), f32(gain_first), f32(shift_first),
        f32(w_qkv), f32(w_out), f32(b_out), f32(gain_second), f32(shift_second), f32(w_up),
        f32(b_up), f32(w_down), f32(b_down),
    ]
    return tuple(
        pl.pallas_call(
            finish_kernel,
            out_shape=finals,
            in_specs=[vmem] * len(outs),
            out_specs=[vmem] * len(finals),
            compiler_params=pltpu.CompilerParams(vmem_limit_bytes=VMEM_LIMIT),
        )(*parts)
    )


def solution(mesh):
    in_specs = (
        P(("dp", "fsdp")),
        P(("dp", "fsdp"), None),
        P(("dp", "fsdp"), None),
        P(("dp", "fsdp")),
        P("fsdp", None),
        P("fsdp", None),
        P("fsdp"),
        P("fsdp"),
        P("fsdp"),
        P("fsdp", None),
        P("fsdp", None),
        P("fsdp"),
        P("fsdp"),
        P("fsdp"),
        P("fsdp", None),
        P("fsdp"),
        P("fsdp", None),
        P("fsdp"),
        P(("dp", "fsdp"), None),
    )
    out_specs = (
        P(("dp", "fsdp"), None),
        P(("dp", "fsdp"), None),
        P("fsdp", None),
        P("fsdp", None),
        P("fsdp"),
        P("fsdp"),
        P("fsdp"),
        P("fsdp", None),
        P("fsdp", None),
        P("fsdp"),
        P("fsdp"),
        P("fsdp"),
        P("fsdp", None),
        P("fsdp"),
        P("fsdp", None),
        P("fsdp"),
    )
    fused = mesh.shape["dp"] == 2 and mesh.shape["fsdp"] == 16
    body = fused_shards if fused else shards
    return jax.shard_map(body, mesh=mesh, in_specs=in_specs, out_specs=out_specs, check_vma=False)
```

```python
import jax
import jax.numpy as jnp
from jax import lax
from jax.experimental import pallas as pl
from jax.experimental.pallas import tpu as pltpu
from jax.sharding import PartitionSpec as P

HEADS = 16
VOCAB = 32000


norm_eps = 1e-05


def standardize(resid):
    centred = resid - jnp.mean(resid, axis=-1, keepdims=True)
    spread = jnp.mean(centred * centred, axis=-1, keepdims=True)
    return centred * lax.rsqrt(spread + norm_eps)


def row_normalize(tok_rows):
    return tok_rows * lax.rsqrt(jnp.mean(tok_rows * tok_rows, axis=1, keepdims=True) + norm_eps)


def exact_gelu(pre_act):
    return jax.nn.gelu(pre_act, approximate=False)


def split_heads(projected):
    tok_count = projected.shape[0]
    width = projected.shape[1] // 3
    head_size = width // HEADS
    key_heads = projected[:, width : 2 * width].reshape(tok_count, HEADS, head_size)
    value_heads = projected[:, 2 * width :].reshape(tok_count, HEADS, head_size)
    row_block = min(512, tok_count)
    query_blocks = projected[:, :width].reshape(tok_count // row_block, row_block, HEADS, head_size)
    return (query_blocks, key_heads, value_heads, row_block)


def block_scores(query_block, key_heads, seg_block, segment):
    raw_scores = (
        jnp.einsum("qhd,khd->hqk", query_block, key_heads, preferred_element_type=jnp.float32)
        * 0.125
    )
    same_seq = seg_block[:, None] == segment[None, :]
    return jnp.where(same_seq[None, :, :], raw_scores, -1000000000.0)


def attention_forward(projected, segment):
    query_blocks, key_heads, value_heads, row_block = split_heads(projected)
    seg_blocks = segment.reshape(-1, row_block)

    def block_step(items_in):
        query_block, seg_block = items_in
        scores = block_scores(query_block, key_heads, seg_block, segment)
        row_max = jnp.max(scores, axis=-1, keepdims=True)
        exp_scores = jnp.exp(scores - row_max)
        row_total = jnp.sum(exp_scores, axis=-1, keepdims=True)
        soft_probs = (exp_scores / row_total).astype(jnp.bfloat16)
        attended = jnp.einsum(
            "hqk,khd->qhd", soft_probs, value_heads, preferred_element_type=jnp.float32
        )
        return (attended, (row_max + jnp.log(row_total))[:, :, 0])

    attended, log_total = lax.map(block_step, (query_blocks, seg_blocks))
    return (attended.reshape(projected.shape[0], -1), log_total)


def attention_backward(projected, segment, log_total, grad_attended):
    query_blocks, key_heads, value_heads, row_block = split_heads(projected)
    seg_blocks = segment.reshape(-1, row_block)
    grad_blocks = grad_attended.reshape(query_blocks.shape)

    def block_step(totals, items_in):
        grad_keys, grad_values = totals
        query_block, seg_block, log_block, grad_block = items_in
        scores = block_scores(query_block, key_heads, seg_block, segment)
        soft_probs = jnp.exp(scores - log_block[:, :, None])
        grad_values = grad_values + jnp.einsum(
            "hqk,qhd->khd",
            soft_probs.astype(jnp.bfloat16),
            grad_block,
            preferred_element_type=jnp.float32,
        )
        grad_probs = jnp.einsum(
            "qhd,khd->hqk", grad_block, value_heads, preferred_element_type=jnp.float32
        )
        grad_scores = soft_probs * (
            grad_probs - jnp.sum(grad_probs * soft_probs, axis=-1, keepdims=True)
        )
        scaled_grad = (grad_scores * 0.125).astype(jnp.bfloat16)
        grad_query = jnp.einsum(
            "hqk,khd->qhd", scaled_grad, key_heads, preferred_element_type=jnp.float32
        )
        grad_keys = grad_keys + jnp.einsum(
            "hqk,qhd->khd", scaled_grad, query_block, preferred_element_type=jnp.float32
        )
        return ((grad_keys, grad_values), grad_query.astype(jnp.bfloat16))

    zero_heads = jnp.zeros(key_heads.shape, jnp.float32)
    (grad_keys, grad_values), grad_queries = lax.scan(
        block_step, (zero_heads, zero_heads), (query_blocks, seg_blocks, log_total, grad_blocks)
    )
    tok_count = projected.shape[0]
    return jnp.concatenate(
        [
            grad_queries.reshape(tok_count, -1),
            grad_keys.astype(jnp.bfloat16).reshape(tok_count, -1),
            grad_values.astype(jnp.bfloat16).reshape(tok_count, -1),
        ],
        axis=1,
    )


def shards(
    token_ids,
    seq_lengths,
    noise,
    noise_level,
    table,
    w_in,
    b_in,
    gain_first,
    shift_first,
    w_qkv,
    w_out,
    b_out,
    gain_second,
    shift_second,
    w_up,
    b_up,
    w_down,
    b_down,
    cotangent,
):
    tok_count = token_ids.shape[0]
    row_count = table.shape[0]
    group_ids = lax.all_gather(token_ids, "fsdp", axis=0, tiled=True)
    first_row = lax.axis_index("fsdp") * row_count
    owned = (group_ids[:, None] == first_row + jnp.arange(row_count)[None, :]).astype(jnp.bfloat16)
    owned_rows = jnp.dot(owned, table, preferred_element_type=jnp.float32).astype(jnp.bfloat16)
    tok_rows = lax.psum_scatter(owned_rows, "fsdp", scatter_dimension=0, tiled=True)
    tok_rows = tok_rows.astype(jnp.float32)
    vectors = (b_in, gain_first, shift_first, b_out, gain_second, shift_second, b_up, b_down)
    vec_all = lax.all_gather(jnp.concatenate(vectors), "fsdp", axis=0, tiled=False)
    vec_at = [0]
    for vector in vectors:
        vec_at.append(vec_at[-1] + vector.shape[0])
    (
        b_in_all,
        gain_first_all,
        shift_first_all,
        b_out_all,
        gain_second_all,
        shift_second_all,
        b_up_all,
        b_down_all,
    ) = [vec_all[:, lo:hi].reshape(-1) for lo, hi in zip(vec_at[:-1], vec_at[1:])]
    w_in_all = lax.all_gather(w_in, "fsdp", axis=0, tiled=True)
    w_qkv_all = lax.all_gather(w_qkv, "fsdp", axis=0, tiled=True)
    w_out_all = lax.all_gather(w_out, "fsdp", axis=0, tiled=True)
    w_up_all = lax.all_gather(w_up, "fsdp", axis=0, tiled=True)
    w_down_all = lax.all_gather(w_down, "fsdp", axis=0, tiled=True)
    seq_ends = jnp.cumsum(seq_lengths[0], dtype=jnp.int32)
    positions = jnp.arange(tok_count, dtype=jnp.int32)
    segment = jnp.sum((positions[:, None] >= seq_ends[None, :]).astype(jnp.int32), axis=1)
    live_rows = (segment < seq_lengths.shape[1]).astype(jnp.float32)[:, None]
    embedded = row_normalize(tok_rows)
    scale_in = lax.rsqrt(1.0 + noise_level * noise_level)[:, None]
    scaled = ((embedded + noise_level[:, None] * noise.astype(jnp.float32)) * scale_in).astype(
        jnp.bfloat16
    )
    resid_in = jnp.dot(scaled, w_in_all, preferred_element_type=jnp.float32) + b_in_all.astype(
        jnp.float32
    )
    std_first, first_pull = jax.vjp(standardize, resid_in)
    normed_a = (
        std_first * gain_first_all.astype(jnp.float32) + shift_first_all.astype(jnp.float32)
    ).astype(jnp.bfloat16)
    projected = jnp.dot(normed_a, w_qkv_all, preferred_element_type=jnp.float32).astype(
        jnp.bfloat16
    )
    attended, log_total = attention_forward(projected, segment)
    attended = attended.astype(jnp.bfloat16)
    resid_mid = (
        resid_in
        + jnp.dot(attended, w_out_all, preferred_element_type=jnp.float32)
        + b_out_all.astype(jnp.float32)
    )
    std_second, second_pull = jax.vjp(standardize, resid_mid)
    normed_b = (
        std_second * gain_second_all.astype(jnp.float32) + shift_second_all.astype(jnp.float32)
    ).astype(jnp.bfloat16)
    pre_act = jnp.dot(normed_b, w_up_all, preferred_element_type=jnp.float32) + b_up_all.astype(
        jnp.float32
    )
    activated, gelu_pull = jax.vjp(exact_gelu, pre_act)
    hidden = activated.astype(jnp.bfloat16)
    resid_out = (
        resid_mid
        + jnp.dot(hidden, w_down_all, preferred_element_type=jnp.float32)
        + b_down_all.astype(jnp.float32)
    )
    activations = (resid_out * live_rows).astype(jnp.bfloat16)
    grad_out = cotangent.astype(jnp.float32) * live_rows
    grad_down = grad_out.astype(jnp.bfloat16)
    b_down_term = jnp.sum(grad_down.astype(jnp.float32), axis=0)
    w_down_term = jnp.einsum("tf,td->fd", hidden, grad_down, preferred_element_type=jnp.float32)
    grad_hidden = jnp.einsum("td,fd->tf", grad_down, w_down_all, preferred_element_type=jnp.float32)
    grad_act = gelu_pull(grad_hidden)[0].astype(jnp.bfloat16)
    b_up_term = jnp.sum(grad_act.astype(jnp.float32), axis=0)
    w_up_term = jnp.einsum("td,tf->df", normed_b, grad_act, preferred_element_type=jnp.float32)
    grad_nb = jnp.einsum("tf,df->td", grad_act, w_up_all, preferred_element_type=jnp.float32)
    gain_second_term = jnp.sum(grad_nb * std_second, axis=0)
    shift_second_term = jnp.sum(grad_nb, axis=0)
    grad_mid = grad_out + second_pull(grad_nb * gain_second_all.astype(jnp.float32))[0]
    grad_att = grad_mid.astype(jnp.bfloat16)
    b_out_term = jnp.sum(grad_att.astype(jnp.float32), axis=0)
    w_out_term = jnp.einsum("tc,td->cd", attended, grad_att, preferred_element_type=jnp.float32)
    grad_attended = jnp.einsum(
        "td,cd->tc", grad_att, w_out_all, preferred_element_type=jnp.float32
    ).astype(jnp.bfloat16)
    grad_proj = attention_backward(projected, segment, log_total, grad_attended)
    w_qkv_term = jnp.einsum("td,te->de", normed_a, grad_proj, preferred_element_type=jnp.float32)
    grad_na = jnp.einsum("te,de->td", grad_proj, w_qkv_all, preferred_element_type=jnp.float32)
    gain_first_term = jnp.sum(grad_na * std_first, axis=0)
    shift_first_term = jnp.sum(grad_na, axis=0)
    grad_in = grad_mid + first_pull(grad_na * gain_first_all.astype(jnp.float32))[0]
    grad_pin = grad_in.astype(jnp.bfloat16)
    b_in_term = jnp.sum(grad_pin.astype(jnp.float32), axis=0)
    w_in_term = jnp.einsum("te,td->ed", scaled, grad_pin, preferred_element_type=jnp.float32)
    grad_scaled = jnp.einsum("td,ed->te", grad_pin, w_in_all, preferred_element_type=jnp.float32)
    noise_grad = grad_scaled * noise_level[:, None] * scale_in
    grad_embedded = grad_scaled * scale_in
    all_ids = lax.all_gather(token_ids, ("dp", "fsdp"), axis=0, tiled=True)
    all_grads = lax.all_gather(
        grad_embedded.astype(jnp.bfloat16), ("dp", "fsdp"), axis=0, tiled=True
    )
    owners = (first_row + jnp.arange(row_count)[:, None] == all_ids[None, :]).astype(jnp.bfloat16)
    row_grad = jnp.dot(owners, all_grads, preferred_element_type=jnp.float32)
    own_table = table.astype(jnp.float32)
    unused_rows, table_pull = jax.vjp(row_normalize, own_table)
    table_part = table_pull(row_grad)[0]

    def reduce_matrix(term):
        part = lax.psum_scatter(
            term.astype(jnp.bfloat16), "fsdp", scatter_dimension=0, tiled=True
        )
        return lax.psum(part, "dp").astype(jnp.float32)

    vec_terms = (
        b_in_term,
        gain_first_term,
        shift_first_term,
        b_out_term,
        gain_second_term,
        shift_second_term,
        b_up_term,
        b_down_term,
    )
    shard_count = lax.axis_size("fsdp")
    vec_term = jnp.concatenate([v.reshape(shard_count, -1) for v in vec_terms], axis=1)
    vec_part = lax.psum(vec_term, ("dp", "fsdp"))
    own_vec = lax.dynamic_index_in_dim(vec_part, lax.axis_index("fsdp"), 0, keepdims=False)
    vec_grads = [own_vec[lo:hi] for lo, hi in zip(vec_at[:-1], vec_at[1:])]
    return (
        activations,
        noise_grad,
        table_part,
        reduce_matrix(w_in_term),
        vec_grads[0],
        vec_grads[1],
        vec_grads[2],
        reduce_matrix(w_qkv_term),
        reduce_matrix(w_out_term),
        vec_grads[3],
        vec_grads[4],
        vec_grads[5],
        reduce_matrix(w_up_term),
        vec_grads[6],
        reduce_matrix(w_down_term),
        vec_grads[7],
    )


BF = jnp.bfloat16
F32 = jnp.float32
MESH_ID = pl.DeviceIdType.MESH
SEM_COUNT = 400
ROW_UNROLL = 8
HEAD_UNROLL = 4
EACH_UNROLL = 4
VMEM_LIMIT = 63 * 2**20
NT = (((1,), (1,)), ((), ()))
TN = (((0,), (0,)), ((), ()))
DIAG, ACROSS, TWIN = 0, 1, 2
FLIPS = ((1, 1), (1, 0), (0, 1))


def mm(a, b):
    return jnp.dot(a, b, preferred_element_type=F32)


def mm_nt(a, b):
    return lax.dot_general(a, b, NT, preferred_element_type=F32)


def mm_tn(a, b):
    return lax.dot_general(a, b, TN, preferred_element_type=F32)


def part(start, size):
    return pl.ds(pl.multiple_of(start, size), size)


def as_row(pair):
    return jnp.concatenate([pair[0:1, :], pair[1:2, :]], axis=1)


def as_col(pair):
    eye = lax.broadcasted_iota(jnp.int32, (128, 128), 0) == lax.broadcasted_iota(
        jnp.int32, (128, 128), 1
    )
    cols = [
        jnp.sum(jnp.where(eye, pair[k : k + 1, :], 0.0), axis=1, keepdims=True) for k in (0, 1)
    ]
    return jnp.concatenate(cols, axis=0)


def norm_parts(v):
    centred = v - jnp.mean(v, axis=-1, keepdims=True)
    rstd = lax.rsqrt(jnp.mean(centred * centred, axis=-1, keepdims=True) + norm_eps)
    return centred * rstd, rstd


def norm_back(u, n, rstd):
    return rstd * (
        u - jnp.mean(u, axis=-1, keepdims=True) - n * jnp.mean(u * n, axis=-1, keepdims=True)
    )


def layer_kernel(
    small_hbm, noise_hbm, table, w_in_hbm, w_qkv_hbm, w_out_hbm, w_up_hbm, w_down_hbm, cot_hbm,
    act_hbm, ngrad_hbm, tgrad_hbm, vout_hbm, f_in_hbm, f_qkv_hbm, f_out_hbm, f_up_hbm, f_dn_hbm,
    small, noise, w_in, w_qkv, w_out, w_up, w_down, cot,
    act, ngrad, tgrad, vout, f_in, f_qkv, f_out, f_up, f_dn,
    sm, smx, gsm, vec, vg, vq, vgy, vgz, vgf, bup, lives, idr,
    tp, tok, sc, win, wqkv, wout, wup, wdn, s_in, s_qkv, s_out, s_up,
    rin, rmid, gmid, t1, t2, t3, t4, na, proj, pr, att, asend, nb, gd, hid, ga,
    xs, xr, gatt, go, g_in, g_qkv, g_out, g_dn,
    y_in, y_qkv, y_out, y_up, y_dn, z_in, z_qkv, z_out, z_up, z_dn, wis, wir,
    ss, rr, ls,
):
    x = lax.axis_index("dp")
    f = lax.axis_index("fsdp")
    z, y, c = f // 4, lax.rem(f // 2, 2), lax.rem(f, 2)
    q = 2 * z + y
    g = 2 * x + c
    rows_here = table.shape[0]

    def dev(dx, dz, dy, dc):
        xx = lax.rem(x + dx, 2)
        zz = lax.rem(z + dz, 4)
        yy = lax.rem(y + dy, 2)
        cc = lax.rem(c + dc, 2)
        return (xx, zz * 4 + yy * 2 + cc)

    twin = dev(0, 0, 0, 1)
    across = dev(1, 0, 0, 0)
    pair_y = dev(0, 0, 1, 0)
    relay_to = (x, jnp.where(z == 2, 3, 0) * 4 + y * 2 + c)
    rel_dev = [dev(dx, 0, 0, dc) for dx, dc in FLIPS]
    rel_g = [2 * lax.rem(x + dx, 2) + lax.rem(c + dc, 2) for dx, dc in FLIPS]
    other_c = 1 - c

    def far(d):
        return lax.rem(z + 4 - d, 4)

    def to(d):
        return lax.rem(z + d, 4)

    sems = [0]
    pending = []
    inner = jnp.logical_or(z == 1, z == 2)
    outer = jnp.logical_not(inner)

    class Link:
        def __init__(self):
            self.at = sems[0]
            sems[0] += 1
            assert sems[0] <= SEM_COUNT

        def send(self, src, dst, device, arrives=None, only=None):
            self.only = only
            self.copy = pltpu.make_async_remote_copy(
                src_ref=src, dst_ref=dst, send_sem=ss.at[self.at],
                recv_sem=rr.at[self.at if arrives is None else arrives],
                device_id=device, device_id_type=MESH_ID,
            )
            if only is None:
                self.copy.start()
            else:
                pl.when(only)(self.copy.start)
            pending.append(self)
            return self

        def sent(self):
            pending.remove(self)
            if self.only is None:
                self.copy.wait_send()
            else:
                pl.when(self.only)(self.copy.wait_send)

        def got(self, ref):
            arrived(self.at, ref)

    def arrived(at, ref):
        pltpu.make_async_remote_copy(
            src_ref=ref, dst_ref=ref, send_sem=ss.at[0], recv_sem=rr.at[at],
            device_id=twin, device_id_type=MESH_ID,
        ).wait_recv()

    def each_rows(count, size, body):
        def step(i, carry):
            body(part(i * size, size))
            return carry

        lax.fori_loop(0, count // size, step, 0, unroll=ROW_UNROLL)

    def each(count, body, unroll=EACH_UNROLL):
        def step(i, carry):
            body(i)
            return carry

        lax.fori_loop(0, count, step, 0, unroll=unroll)

    local = [0]
    stores = []

    def moved(src, dst):
        copy = pltpu.make_async_copy(src, dst, ls.at[local[0]])
        local[0] += 1
        copy.start()
        return copy

    load_small = moved(small_hbm, small)
    load_in = moved(w_in_hbm, w_in)
    load_qkv = moved(w_qkv_hbm, w_qkv)
    load_cot = moved(cot_hbm, cot)
    own_table = moved(table, tp.at[c, pl.ds(0, rows_here)])
    load_noise = moved(noise_hbm, noise)
    load_out = moved(w_out_hbm, w_out)
    load_up = moved(w_up_hbm, w_up)
    load_down = moved(w_down_hbm, w_down)

    barrier = pltpu.get_barrier_semaphore()
    peers = [dev(0, d, 0, dc) for d in (1, 2, 3) for dc in (0, 1)] + rel_dev + [pair_y]
    for peer in peers:
        pl.semaphore_signal(barrier, inc=1, device_id=peer, device_id_type=MESH_ID)
    pl.semaphore_wait(barrier, len(peers))

    class GroupGather:
        def __init__(self, at):
            self.at = at
            self.across = Link().send(at(g), at(g), across)
            self.twin = Link().send(at(g), at(g), twin)

        def hop(self):
            self.across.got(self.at(rel_g[ACROSS]))
            self.second = Link().send(self.at(rel_g[ACROSS]), self.at(rel_g[ACROSS]), twin)

        def got_twin(self):
            self.twin.got(self.at(rel_g[TWIN]))

        def got_diag(self):
            self.second.got(self.at(rel_g[DIAG]))

    class Gather:
        def __init__(self, whole, mine, theirs, height, twins=None, relay=True):
            self.whole, self.height, self.relay = whole, height, relay
            places = (self.sub(q, c), self.sub(q, c, twins))
            self.links = {}
            for d in (0, 2, 1, 3):
                only = {1: z != 3, 3: z != 0}.get(d) if relay else None
                for dc in (1, 0):
                    if (d, dc) != (0, 0):
                        self.links[d, dc] = Link().send(
                            theirs if dc else mine, places[dc], dev(0, d, 0, dc), only=only
                        )

        def sub(self, block, core, whole=None):
            whole = self.whole if whole is None else whole
            if self.height is None:
                return whole.at[block, core]
            return whole.at[block, part(core * self.height, self.height)]

        def over_y(self, block):
            return Link().send(self.whole.at[block], self.whole.at[block], pair_y)

        def own(self):
            self.links[0, 1].got(self.sub(q, other_c))
            self.y_own = self.over_y(q)

        def second(self):
            block = 2 * far(2) + y
            for dc in (1, 0):
                ref = self.sub(block, other_c if dc else c)
                self.links[2, dc].got(ref)
                if self.relay:
                    Link().send(
                        ref, ref, relay_to, only=inner,
                        arrives=jnp.where(z == 2, self.links[3, dc].at, self.links[1, dc].at),
                    )
            self.y_second = self.over_y(block)

        def near(self):
            self.y_near = self.one(3, 1)

        def last(self):
            self.y_last = self.one(1, 3)

        def one(self, low, high):
            block = 2 * jnp.where(z < 2, far(low), far(high)) + y
            for dc in (1, 0):
                arrived(
                    jnp.where(z < 2, self.links[low, dc].at, self.links[high, dc].at),
                    self.sub(block, other_c if dc else c),
                )
            return self.over_y(block)

        def forward(self):
            self.second()
            self.near()
            self.last()

        def finish(self):
            self.y_own.got(self.whole.at[2 * z + 1 - y])
            self.y_second.got(self.whole.at[2 * far(2) + 1 - y])
            self.y_near.got(self.whole.at[2 * jnp.where(z < 2, far(3), far(1)) + 1 - y])
            self.y_last.got(self.whole.at[2 * jnp.where(z < 2, far(1), far(3)) + 1 - y])

    load_small.wait()
    sm[q, c] = small[...]
    small_links = [Link().send(small, gsm.at[rel], rel_dev[rel]) for rel in (DIAG, ACROSS)]
    gather_small = Gather(sm, small, small, None, relay=False)

    own_rows = tp.at[c, pl.ds(0, rows_here)]
    table_link = Link().send(table, own_rows, twin)
    spare = tp.shape[1] - rows_here
    if spare:
        for core in (0, 1):
            tp[core, pl.ds(rows_here, spare), :] = jnp.zeros((spare, tp.shape[2]), BF)

    def pack(whole, spare_buf, height, pick):
        mine, theirs = pick(g), pick(2 * x + other_c)
        whole[q, part(c * height, height), :] = mine
        spare_buf[...] = theirs

    h = w_qkv.shape[0]
    hin = w_in.shape[0]

    def cols(ref, start, size=256):
        return ref[:, part(start, size)]

    win_at, wout_at = win.at[g], wout.at[g]
    load_in.wait()
    load_qkv.wait()
    win_at[q, c] = cols(w_in, 256 * g)
    s_in[0] = cols(w_in, 256 * (2 * x + other_c))
    gather_in = Gather(win_at, win_at.at[q, c], s_in.at[0], None, win.at[2 * x + other_c], relay=False)
    pack(
        wqkv, s_qkv, h,
        lambda k: jnp.concatenate([cols(w_qkv, 1024 * n + 256 * k) for n in (0, 1, 2)], axis=1),
    )
    gather_qkv = Gather(wqkv, wqkv.at[q, part(c * h, h)], s_qkv, h, relay=False)


    lives[:, 0:1] = jnp.where(as_col(small[18:20, :]) < 7.5, 1.0, 0.0)
    vg[...] = jnp.zeros_like(vg)

    def grad_down_rows(at):
        masked = cot[at, :].astype(F32) * lives[at, 0:1]
        gd[g, at, :] = masked.astype(BF)
        vg[6:7, :] += jnp.sum(masked, axis=0, keepdims=True)

    load_out.wait()
    pack(wout_at, s_out, h, lambda k: cols(w_out, 256 * k))
    gather_out = Gather(
        wout_at, wout_at.at[q, part(c * h, h)], s_out, h, wout.at[2 * x + other_c], relay=False
    )
    load_cot.wait()
    each_rows(256, 32, grad_down_rows)
    group_gd = GroupGather(lambda k: gd.at[k])

    gather_small.own()
    gather_small.forward()

    gather_in.own()
    gather_qkv.own()
    gather_small.finish()
    smx_link = Link().send(sm, smx, across)
    own_table.wait()
    table_link.got(tp.at[other_c, pl.ds(0, rows_here)])
    lane = lax.broadcasted_iota(jnp.int32, (256, tp.shape[1]), 1)

    def look_up(block):
        ids = as_col(sm[block, c, 16:18, :]).astype(jnp.int32)
        total = jnp.zeros((256, 256), F32)
        for core in (0, 1):
            first = (4 * z + 2 * y + core) * rows_here
            hit = jnp.where(lane == ids - first, 1.0, 0.0).astype(BF)
            total += mm(hit, tp[core])
        return total.astype(BF)

    emb_y = [Link() for _ in range(4)]
    for d in range(4):
        tok[d] = look_up(2 * to(d) + 1 - y)
        emb_y[d].send(tok.at[d], tok.at[8 + d], pair_y)

    def own_blocks(d):
        tok[4 + d] = look_up(2 * lax.rem(z + d, 4) + y)

    each(4, own_blocks)
    emb_z = [None]
    for d in (1, 2, 3):
        emb_y[d].got(tok.at[8 + d])
        tok[4 + d] = tok[4 + d] + tok[8 + d]
        emb_z.append(Link().send(tok.at[4 + d], tok.at[11 + d], dev(0, d, 0, 0)))
    emb_y[0].got(tok.at[8])

    for load in (load_noise, load_up, load_down):
        load.wait()
    ct = lax.broadcasted_iota(jnp.int32, (h, 128), 1) < 64
    for j in range(8):
        first = w_up[:, part(128 * (4 * j + x), 128)].astype(F32)
        second = w_up[:, part(128 * (4 * j + 2 + x), 128)].astype(F32)
        low = jnp.where(ct, first, pltpu.roll(second, 64, 1)).astype(BF)
        high = jnp.where(ct, pltpu.roll(first, 64, 1), second).astype(BF)
        wup[q, part(c * h, h), 128 * j : 128 * j + 128] = jnp.where(c == 0, low, high)
        s_up[:, 128 * j : 128 * j + 128] = jnp.where(c == 0, high, low)
    wdn[q, part(c * h, h), :] = w_down[part(g * h, h), :]
    gather_in.forward()
    gather_qkv.forward()
    for j in range(8):
        vec[:, 128 * j : 128 * j + 128] = sm[j, 0, 0:16, :] + sm[j, 1, 0:16, :]

    gather_out.own()
    gather_out.forward()
    gather_in.finish()
    group_in = GroupGather(lambda k: win.at[k])
    group_gd.hop()
    rows_sum = tok[4].astype(F32) + tok[8].astype(F32)
    for d in (1, 2, 3):
        emb_z[d].got(tok.at[11 + d])
        rows_sum += tok[11 + d].astype(F32)
    gather_up = Gather(wup, wup.at[q, part(c * h, h)], s_up, h)
    for d in range(4):
        emb_y[d].sent()
    for d in (1, 2, 3):
        emb_z[d].sent()
    level = as_col(small[20:22, :])
    scale_in = lax.rsqrt(1.0 + level * level)
    embedded = rows_sum * lax.rsqrt(jnp.mean(rows_sum * rows_sum, axis=1, keepdims=True) + norm_eps)
    sc[g] = ((embedded + level * noise[...].astype(F32)) * scale_in).astype(BF)
    group_sc = GroupGather(lambda k: sc.at[k])

    group_in.hop()
    group_in.got_twin()
    group_in.got_diag()

    def win_mat(k):
        return win[k].reshape(256, 256)

    def first_norm(row, keep):
        for k in range(4):
            keep[:, 256 * k : 256 * k + 256] = (
                mm(sc[row], win_mat(k)) + vec[0:1, 256 * k : 256 * k + 256]
            )

        def chunk(at):
            n, _ = norm_parts(keep[at, :])
            na[row, at, :] = (n * vec[1:2, :] + vec[2:3, :]).astype(BF)

        each_rows(256, 32, chunk)

    def project(row):
        def block(k):
            at = part(k * 256, 256)
            proj[row, :, at] = mm(na[row], wqkv[:, :, at].reshape(1024, 256)).astype(BF)

        each(3, block)

    first_norm(g, rin)
    group_sc.hop()
    gather_up.own()
    group_sc.got_twin()
    first_norm(rel_g[TWIN], t1)
    first_norm(rel_g[ACROSS], t1)
    group_sc.got_diag()
    first_norm(rel_g[DIAG], t1)
    gather_qkv.finish()
    for rel in range(3):
        project(rel_g[rel])
    project(g)
    gather_out.finish()
    group_out = GroupGather(lambda k: wout.at[k])

    head_of = lax.broadcasted_iota(jnp.int32, (1, 256), 1) // 64
    small_links[DIAG].got(gsm.at[DIAG])
    small_links[ACROSS].got(gsm.at[ACROSS])

    def attend(row, pair):
        same = as_col(pair) == as_row(pair)
        keys = proj[row, :, 256:512]
        values = proj[row, :, 512:768]
        queries = proj[row, :, 0:256]
        t2[...] = jnp.zeros_like(t2)

        def head(k):
            mine = head_of == k
            q_head = jnp.where(mine, queries, jnp.zeros_like(queries))
            scores = jnp.where(same, mm_nt(q_head, keys) * 0.125, -1e9)
            weights = jnp.exp(scores - jnp.max(scores, axis=-1, keepdims=True))
            low_probs = (weights / jnp.sum(weights, axis=-1, keepdims=True)).astype(BF)
            pr[row * 4 + k] = low_probs
            t2[...] += mm(low_probs, jnp.where(mine, values, jnp.zeros_like(values)))

        each(4, head, HEAD_UNROLL)
        return t2[...].astype(BF)

    att_links = []
    my_cols = part(256 * g, 256)
    for rel in range(3):
        pair = sm[q, other_c, 18:20, :] if rel == TWIN else gsm[rel, 18:20, :]
        asend[rel] = attend(rel_g[rel], pair)
        att_links.append(Link().send(asend.at[rel], att.at[:, my_cols], rel_dev[rel]))
        if rel == DIAG:
            gather_up.second()
            gather_dn = Gather(
                wdn, w_down.at[part(g * h, h)], w_down.at[part((2 * x + other_c) * h, h)], h
            )
    att[:, my_cols] = attend(g, small[18:20, :])
    gather_dn.own()
    group_out.hop()
    gather_up.near()
    gather_up.last()
    group_out.got_twin()
    group_out.got_diag()
    for rel in (TWIN, ACROSS, DIAG):
        att_links[rel].got(att.at[:, part(256 * rel_g[rel], 256)])

    def out_block(k):
        at = part(k * 256, 256)
        rmid[:, at] = rin[:, at] + mm(att[...], wout[k].reshape(1024, 256)) + vec[3:4, at]

    each(4, out_block)

    def second_norm(at):
        n, _ = norm_parts(rmid[at, :])
        nb[g, at, :] = (n * vec[4:5, :] + vec[5:6, :]).astype(BF)

    each_rows(256, 32, second_norm)
    nb_across = Link().send(nb.at[g], nb.at[g], across)
    nb_twin = Link().send(nb.at[g], nb.at[g], twin)
    nb_pass = Link()
    group_gd.got_twin()
    group_gd.got_diag()

    bup[...] = jnp.zeros_like(bup)
    for k in range(4):
        bup[0:1, :] += jnp.where(g == k, vec[7 + k : 8 + k, :], 0.0)

    def ff_hidden(row):
        def block(k):
            at = part(k * 256, 256)
            t2[...] = mm(nb[row], wup[:, :, at].reshape(1024, 256)) + bup[0:1, at]

            def chunk(rows_at):
                pre = t2[rows_at, :]
                cdf = 0.5 + 0.5 * lax.erf(pre * 0.7071067811865476)
                pdf = jnp.exp(-0.5 * pre * pre) * 0.3989422804014327
                t2[rows_at, :] = pre * cdf
                ga[row, rows_at, at] = (cdf + pre * pdf).astype(BF)

            each_rows(256, 32, chunk)
            hid[pl.ds(2 * row, 2), :, at] = t2[...].astype(BF).reshape(2, 128, 256)

        each(4, block)

    def ff_grad(row):
        def block(k):
            at = part(k * 256, 256)
            grad = mm_nt(gd[row], wdn[pl.ds(2 * k, 2)].reshape(256, 1024))
            ga_low = (grad * ga[row, :, at].astype(F32)).astype(BF)
            ga[row, :, at] = ga_low
            bup[1:2, at] += jnp.sum(ga_low.astype(F32), axis=0, keepdims=True)

        each(4, block)

    gather_dn.second()
    gather_up.finish()
    ff_hidden(g)
    gather_dn.near()
    gather_dn.last()
    nb_twin.got(nb.at[rel_g[TWIN]])
    ff_hidden(rel_g[TWIN])
    nb_across.got(nb.at[rel_g[ACROSS]])
    nb_pass.send(nb.at[rel_g[ACROSS]], nb.at[rel_g[ACROSS]], twin)
    ff_hidden(rel_g[ACROSS])
    nb_pass.got(nb.at[rel_g[DIAG]])
    ff_hidden(rel_g[DIAG])

    class GroupSum:
        def __init__(self, sends, gets, partial, puts=None):
            self.sends, self.gets, self.partial = sends, gets, partial
            self.puts = gets if puts is None else puts

        def first(self):
            self.partial(rel_g[DIAG], self.sends[0])
            self.a = Link().send(self.sends[0], self.puts[0], twin)

        def second(self):
            self.partial(rel_g[ACROSS], t1)
            self.a.got(self.gets[0])

            def chunk(at):
                self.sends[1][at, :] = (t1[at, :] + self.gets[0][at, :].astype(F32)).astype(BF)

            each_rows(256, 32, chunk)

        def second_send(self):
            self.b = Link().send(self.sends[1], self.puts[1], across)

        def third(self):
            self.partial(rel_g[TWIN], self.sends[2])
            self.c = Link().send(self.sends[2], self.puts[2], twin)

        def own(self, into):
            self.partial(g, into)
            self.into = into

        def total(self):
            self.c.got(self.gets[2])
            self.b.got(self.gets[1])

        def rows(self, at):
            return (
                self.into[at, :].astype(F32)
                + self.gets[1][at, :].astype(F32)
                + self.gets[2][at, :].astype(F32)
            )

        def release(self):
            for link in (self.a, self.b, self.c):
                link.sent()

    def slots(ref, places):
        return [ref.at[place] for place in places]

    def nb_partial(row, into):
        def block(k):
            into[:, part(k * 256, 256)] = mm_nt(
                ga[row], wup[pl.ds(2 * k, 2)].reshape(256, 1024)
            ).astype(into.dtype)

        each(4, block)

    def out_partial(row, into):
        def block(k):
            at = part(k * 256, 256)
            into[:, at] = mm(
                hid[pl.ds(2 * row, 2)].reshape(256, 1024), wdn[:, :, at].reshape(1024, 256)
            ).astype(into.dtype)

        each(4, block)

    class Scatter:
        def __init__(self, grad, y_buf, z_buf, final, height):
            self.grad, self.y_buf, self.z_buf, self.final, self.height = (
                grad, y_buf, z_buf, final, height,
            )

        def chunks(self, body):
            if self.height is None:
                each(2, body)
            else:
                each_rows(2 * self.height, 32, body)

        def half(self, core):
            if self.height is None:
                return self.grad.at[q, core]
            return self.grad.at[q, part(core * self.height, self.height)]

        def start(self, count=4):
            even = lax.rem(z, 2) == 0
            self.goals = (
                jnp.where(even, 3, 0), jnp.where(even, 1, 2), lax.rem(z + 2, 4), z,
            )
            self.y_links = []
            self.z_links = [Link() for _ in range(4)]
            self.more(count)

        def more(self, count=1):
            for _ in range(count):
                e = len(self.y_links)
                self.y_links.append(
                    Link().send(self.grad.at[2 * self.goals[e] + 1 - y], self.y_buf.at[e], pair_y)
                )

        def add_y(self, e):
            self.y_links[e].got(self.y_buf.at[e])
            block = 2 * self.goals[e] + y

            def chunk(at):
                self.grad[block, at] = (
                    self.grad[block, at].astype(F32) + self.y_buf[e, at].astype(F32)
                ).astype(BF)

            self.chunks(chunk)
            return self.grad.at[block]

        def end_to_end(self):
            ref = self.add_y(0)
            self.z_links[0].send(
                ref, self.z_buf.at[0], (x, (z + 1 - 2 * lax.rem(z, 2)) * 4 + y * 2 + c)
            )

        def near(self):
            ref = self.add_y(1)
            slot = jnp.where(inner, 2, 1)
            self.z_links[1].send(
                ref, self.z_buf.at[slot], (x, self.goals[1] * 4 + y * 2 + c),
                arrives=jnp.where(inner, self.z_links[2].at, self.z_links[1].at),
            )

        def second(self):
            ref = self.add_y(2)
            block = 2 * self.goals[2] + y

            def relayed():
                self.z_links[0].got(self.z_buf.at[0])

                def chunk(at):
                    self.grad[block, at] = (
                        self.grad[block, at].astype(F32) + self.z_buf[0, at].astype(F32)
                    ).astype(BF)

                self.chunks(chunk)

            pl.when(inner)(relayed)
            self.z_links[3].send(ref, self.z_buf.at[3], dev(0, 2, 0, 0))

        def own(self):
            self.add_y(3)

        def middle(self):
            self.end_to_end()
            self.near()
            self.second()
            self.own()

        def last(self):
            def summed(slots):
                def run():
                    for slot in slots:
                        self.z_links[slot].got(self.z_buf.at[slot])

                    def chunk(at):
                        total = self.grad[q, at].astype(F32)
                        for slot in slots:
                            total += self.z_buf[slot, at].astype(F32)
                        self.grad[q, at] = total.astype(BF)

                    self.chunks(chunk)

                return run

            pl.when(inner)(summed((1, 2, 3)))
            pl.when(outer)(summed((0, 3)))
            self.f_links = []
            for rel in range(3):
                core = lax.rem(c + FLIPS[rel][1], 2)
                self.f_links.append(
                    Link().send(
                        self.half(core),
                        self.final.at[g],
                        rel_dev[rel],
                    )
                )
            self.final[g] = self.half(c)[...]

        def finish(self):
            for rel in range(3):
                self.f_links[rel].got(self.final.at[rel_g[rel]])

    scatter_dn = Scatter(g_dn, y_dn, z_dn, f_dn, h)
    scatter_up = Scatter(hid, y_up, z_up, f_up, h)
    sum_out = GroupSum(slots(xs, (3, 4, 5)), slots(xr, (3, 4, 5)), out_partial)

    def dn_block(k):
        at = part(k * 256, 256)
        lhs = hid[:, :, at].reshape(1024, 256)
        g_dn[pl.ds(2 * k, 2)] = mm_tn(lhs, gd[...].reshape(1024, 1024)).astype(BF).reshape(
            2, 128, 1024
        )

    each(4, dn_block)
    scatter_dn.start()
    gather_dn.finish()
    sum_nb = GroupSum(slots(xs, (0, 1, 2)), slots(xr, (0, 1, 2)), nb_partial)
    ff_grad(rel_g[DIAG])
    sum_nb.first()
    ff_grad(rel_g[ACROSS])
    sum_nb.second()
    sum_nb.second_send()
    ff_grad(rel_g[TWIN])
    sum_nb.third()
    ff_grad(g)
    sum_out.first()
    sum_out.second()
    sum_out.third()

    sum_out.own(act)

    def up_block(k):
        at = part(k * 256, 256)
        lhs = nb[:, :, at].reshape(1024, 256)
        hid[pl.ds(2 * k, 2)] = mm_tn(lhs, ga[...].reshape(1024, 1024)).astype(BF).reshape(
            2, 128, 1024
        )

    each(4, up_block)
    scatter_up.start()

    sum_nb.own(t1)
    scatter_dn.end_to_end()
    sum_nb.total()

    def second_back(at):
        grad_nb = sum_nb.rows(at)
        n, rstd = norm_parts(rmid[at, :])
        vg[4:5, :] += jnp.sum(grad_nb * n, axis=0, keepdims=True)
        vg[5:6, :] += jnp.sum(grad_nb, axis=0, keepdims=True)
        mid = gd[g, at, :].astype(F32) + norm_back(grad_nb * vec[4:5, :], n, rstd)
        gmid[at, :] = mid
        low_mid = mid.astype(BF)
        gatt[1, at, :] = low_mid
        vg[3:4, :] += jnp.sum(low_mid.astype(F32), axis=0, keepdims=True)

    each_rows(256, 32, second_back)

    def grad_o_part(to_g):
        total = jnp.zeros((256, 256), F32)
        for k in range(4):
            total += mm_nt(
                gatt[1, :, 256 * k : 256 * k + 256], wout[k, pl.ds(2 * to_g, 2)].reshape(256, 256)
            )
        return total.astype(BF)

    for link in (nb_pass, nb_across, nb_twin, group_gd.second):
        link.sent()
    go_links = []
    for rel in range(3):
        att_links[rel].sent()
        asend[rel] = grad_o_part(rel_g[rel])
        go_links.append(Link().send(asend.at[rel], go.at[g], rel_dev[rel]))
    go[g] = grad_o_part(g)

    def wog_partial(k, into):
        for j in range(4):
            into[:, 256 * j : 256 * j + 256] = mm_tn(
                att[:, 256 * j : 256 * j + 256], gatt[1, :, part(256 * k, 256)]
            ).astype(into.dtype)

    sum_nb.release()
    scatter_dn.near()
    for rel in (TWIN, ACROSS, DIAG):
        go_links[rel].got(go.at[rel_g[rel]])
    sum_wog = GroupSum(
        slots(gd, rel_g), slots(nb, rel_g), wog_partial, slots(nb, (rel_g[ACROSS], g, g))
    )
    sum_wog.first()
    sum_wog.second()
    sum_wog.second_send()
    sum_wog.third()
    sum_wog.own(nb.at[g])

    def attend_back(row):
        keys = proj[row, :, 256:512]
        values = proj[row, :, 512:768]
        queries = proj[row, :, 0:256]
        grad_rows = go[row]
        zero = jnp.zeros_like(keys)
        for buf in (t2, t3, t4):
            buf[...] = jnp.zeros_like(buf)

        def head(k):
            mine = head_of == k
            probs = pr[row * 4 + k]
            g_head = jnp.where(mine, grad_rows, zero)
            t4[...] += mm_tn(probs, g_head)
            grad_p = mm_nt(g_head, values)
            wide = probs.astype(F32)
            grad_s = wide * (grad_p - jnp.sum(grad_p * wide, axis=-1, keepdims=True))
            low_s = (grad_s * 0.125).astype(BF)
            t2[...] += mm(low_s, jnp.where(mine, keys, zero))
            t3[...] += mm_tn(low_s, jnp.where(mine, queries, zero))

        each(4, head, HEAD_UNROLL)
        proj[row, :, 0:256] = t2[...].astype(BF)
        proj[row, :, 256:512] = t3[...].astype(BF)
        proj[row, :, 512:768] = t4[...].astype(BF)

    def na_partial(row, into):
        def block(k):
            into[:, part(k * 256, 256)] = mm_nt(
                proj[row], wqkv[pl.ds(2 * k, 2)].reshape(256, 768)
            ).astype(into.dtype)

        each(4, block)

    sum_na = GroupSum(slots(xs, (0, 1, 2)), slots(xr, (0, 1, 2)), na_partial)
    attend_back(rel_g[DIAG])
    sum_na.first()
    scatter_dn.second()
    attend_back(rel_g[ACROSS])
    sum_na.second()
    sum_na.second_send()
    scatter_dn.own()
    scatter_up.end_to_end()
    attend_back(rel_g[TWIN])
    sum_na.third()
    scatter_up.near()
    sum_out.second_send()
    sum_wog.total()
    scatter_out = Scatter(g_out, y_out, z_out, f_out, h)
    for j in range(4):
        at = slice(256 * j, 256 * j + 256)
        g_out[2 * j : 2 * j + 2] = (
            nb[g, :, at].astype(F32) + nb[rel_g[ACROSS], :, at].astype(F32)
            + nb[rel_g[TWIN], :, at].astype(F32)
        ).astype(BF).reshape(2, 128, 256)
    scatter_out.start()
    attend_back(g)
    sum_na.own(t1)

    scatter_qkv = Scatter(g_qkv, y_qkv, z_qkv, f_qkv, h)
    scatter_in = Scatter(g_in, y_in, z_in, f_in, None)

    def qkv_block(k):
        at = part(k * 256, 256)
        lhs = na[:, :, at].reshape(1024, 256)
        g_qkv[pl.ds(2 * k, 2)] = mm_tn(lhs, proj[...].reshape(1024, 768)).astype(BF).reshape(
            2, 128, 768
        )

    each(4, qkv_block)
    scatter_qkv.start(1)
    scatter_up.second()
    scatter_dn.last()

    sum_na.total()

    def first_back(at):
        grad_na = sum_na.rows(at)
        n, rstd = norm_parts(rin[at, :])
        vg[1:2, :] += jnp.sum(grad_na * n, axis=0, keepdims=True)
        vg[2:3, :] += jnp.sum(grad_na, axis=0, keepdims=True)
        low_in = (gmid[at, :] + norm_back(grad_na * vec[1:2, :], n, rstd)).astype(BF)
        gatt[0, at, :] = low_in
        vg[0:1, :] += jnp.sum(low_in.astype(F32), axis=0, keepdims=True)

    each_rows(256, 32, first_back)
    for k in range(4):
        vg[7 + k : 8 + k, :] = jnp.where(g == k, bup[1:2, :], 0.0)
    for j in range(8):
        vq[j % 2, j // 2] = vg[:, 128 * j : 128 * j + 128]
    vy_link = Link().send(vq.at[1 - y], vgy, pair_y)

    grad_scaled = jnp.zeros((256, 256), F32)
    for k in range(4):
        grad_scaled += mm_nt(gatt[0, :, 256 * k : 256 * k + 256], win_mat(k))
    level = as_col(small[20:22, :])
    scale_in = lax.rsqrt(1.0 + level * level)
    ngrad[...] = grad_scaled * (level * scale_in)
    stores.append(moved(ngrad, ngrad_hbm))

    def set_at(other_x, other_y, other_core):
        return ((lax.rem(x + other_x, 2) * 2 + lax.rem(y + other_y, 2)) * 2 + lax.rem(c + other_core, 2)) * 4

    home = tok.at[set_at(0, 0, 0) + z]
    tok[set_at(0, 0, 0) + z] = (grad_scaled * scale_in).astype(BF)
    tok_z = [None] + [Link().send(home, home, dev(0, d, 0, 0)) for d in (1, 2, 3)]
    tok_x = {}
    tok_y = {}
    tok_t = {}

    def spread(spot, key, across_too):
        ref = tok.at[spot]
        if across_too:
            tok_x[key] = Link().send(ref, ref, across)
        tok_t[across_too, key] = Link().send(ref, ref, twin)

    tok_y[0] = Link().send(home, home, pair_y)
    spread(set_at(0, 0, 0) + z, (0, 0), True)

    scatter_out.end_to_end()

    wi_links = []
    for rel in range(3):
        wis[rel] = mm_tn(sc[g], gatt[0, :, part(256 * rel_g[rel], 256)]).astype(BF)
        wi_links.append(Link().send(wis.at[rel], wir.at[rel], rel_dev[rel]))
    wi_own = mm_tn(sc[g], gatt[0, :, part(256 * g, 256)])

    def tok_from_z(d):
        spot = set_at(0, 0, 0) + far(d)
        tok_z[d].got(tok.at[spot])
        tok_y[d] = Link().send(tok.at[spot], tok.at[spot], pair_y)
        spread(spot, (0, d), True)

    def tok_from_y(d):
        spot = set_at(0, 1, 0) + far(d)
        tok_y[d].got(tok.at[spot])
        spread(spot, (1, d), True)

    def tok_from_x(other_y, d):
        spot = set_at(1, other_y, 0) + far(d)
        tok_x[other_y, d].got(tok.at[spot])
        spread(spot, (other_y, d), False)

    smx_link.got(smx)
    for other_x in (0, 1):
        for yy in (0, 1):
            for core in (0, 1):
                source = sm if other_x == 0 else smx
                for zz in range(4):
                    idr[(other_x * 2 + yy) * 2 + core : (other_x * 2 + yy) * 2 + core + 1, 256 * zz : 256 * zz + 256] = (
                        as_row(source[2 * zz + yy, core, 16:18, :])
                    )

    tile = 400
    base = (f * rows_here).astype(F32)
    tile_row = lax.broadcasted_iota(jnp.int32, (tile, 1024), 0).astype(F32)

    def table_add(other_x, other_y, other_core, begin):
        spot = set_at(other_x, other_y, other_core)
        row = (other_x * 2 + lax.rem(y + other_y, 2)) * 2 + lax.rem(c + other_core, 2)
        ids = idr[pl.ds(row, 1), :] - base

        def block(k):
            at = part(k * tile, tile)
            hit = jnp.where(tile_row == ids - (k * tile).astype(F32), 1.0, 0.0).astype(BF)
            add = mm(hit, tok[pl.ds(spot, 4)].reshape(1024, 256))
            if begin:
                tgrad[at, :] = add
            else:
                tgrad[at, :] += add

        each(rows_here // tile, block)

    def twin_set(from_x, other_y):
        for d in range(4):
            tok_t[from_x == 0, (other_y, d)].got(tok.at[set_at(from_x, other_y, 1) + far(d)])

    tok_from_z(1)
    scatter_qkv.more()
    scatter_up.own()
    scatter_qkv.end_to_end()
    tok_from_z(2)
    scatter_qkv.more()
    scatter_out.near()
    tok_from_z(3)
    scatter_qkv.more()
    table_add(0, 0, 0, True)
    tok_from_y(0)
    scatter_qkv.near()
    for rel in range(3):
        wi_links[rel].got(wir.at[rel])
        wi_own += wir[rel].astype(F32)
    g_in[...] = wi_own.astype(BF).reshape(8, 2, 16, 256)
    scatter_in.start()
    vy_link.got(vgy)
    vq[y] = vq[y] + vgy[...]
    vz_links = [
        Link().send(vq.at[y, to(d)], vgz.at[d - 1], dev(0, d, 0, 0)) for d in (1, 2, 3)
    ]
    tok_from_y(1)
    twin_set(0, 0)
    table_add(0, 0, 1, False)
    tok_from_y(2)
    scatter_qkv.second()
    tok_from_y(3)
    scatter_qkv.own()
    scatter_up.last()
    table_add(0, 1, 0, False)
    scatter_out.second()
    scatter_out.own()
    twin_set(0, 1)
    table_add(0, 1, 1, False)
    scatter_in.middle()
    for d in (1, 2, 3):
        vz_links[d - 1].got(vgz.at[d - 1])
    vtot = vq[y, z] + vgz[0] + vgz[1] + vgz[2]
    vgf[3] = vtot
    vf_links = [Link().send(vgf.at[3], vgf.at[rel], rel_dev[rel]) for rel in range(3)]
    for d in range(4):
        tok_from_x(0, d)
    table_add(1, 0, 0, False)
    sum_out.total()

    def out_rows(at):
        whole = rmid[at, :] + sum_out.rows(at) + vec[6:7, :]
        act[at, :] = (whole * lives[at, 0:1]).astype(BF)

    each_rows(256, 32, out_rows)
    stores.append(moved(act, act_hbm))
    sum_out.release()

    scatter_out.last()
    twin_set(1, 0)
    table_add(1, 0, 1, False)
    scatter_qkv.last()
    for d in range(4):
        tok_from_x(1, d)
    scatter_in.last()
    table_add(1, 1, 0, False)
    twin_set(1, 1)
    table_add(1, 1, 1, False)

    def table_rows(at):
        values = tp[c, at, :].astype(F32)
        r = lax.rsqrt(jnp.mean(values * values, axis=1, keepdims=True) + norm_eps)
        row_grad = tgrad[at, :]
        slope = jnp.mean(row_grad * values, axis=1, keepdims=True)
        tgrad[at, :] = r * row_grad - values * (r * r * r * slope)

    for k in range(rows_here // 200):
        at = pl.ds(k * 200, 200)
        table_rows(at)
        stores.append(moved(tgrad.at[at], tgrad_hbm.at[at]))

    for rel in range(3):
        vf_links[rel].got(vgf.at[rel])
    vout[...] = vgf[0] + vgf[1] + vgf[2] + vgf[3]
    for scatter in (scatter_dn, scatter_up, scatter_qkv, scatter_out, scatter_in):
        scatter.finish()
    for k, (src, dst) in enumerate(((f_in, f_in_hbm), (f_qkv, f_qkv_hbm), (f_out, f_out_hbm), (f_up, f_up_hbm), (f_dn, f_dn_hbm), (vout, vout_hbm))):
        stores.append(moved(src, dst))
    for link in list(pending):
        link.sent()
    for store in stores:
        store.wait()


def finish_kernel(
    act_in, ngrad_in, tgrad_in, vout, f_in, f_qkv, f_out, f_up, f_dn,
    act, ngrad, tgrad, w_in, b_in, gain_a, shift_a, w_qkv, w_out, b_out, gain_b, shift_b,
    w_up, b_up, w_dn, b_dn,
):
    c = lax.rem(lax.axis_index("fsdp"), 2)
    act[...] = act_in[...]
    ngrad[...] = ngrad_in[...]
    tgrad[...] = tgrad_in[...]
    rows = jnp.where(c == 0, vout[...], pltpu.roll(vout[...], 64, 1))
    for k, ref in enumerate((b_in, gain_a, shift_a, b_out, gain_b, shift_b, b_dn)):
        ref[...] = rows[k, 0:64]
    for k in range(4):
        b_up[64 * k : 64 * k + 64] = rows[7 + k, 0:64]
    h = w_out.shape[0]
    low_half = lax.broadcasted_iota(jnp.int32, (h, 128), 1) < 64
    for g in range(4):
        at = slice(256 * g, 256 * g + 256)
        w_in[:, at] = f_in[g].astype(F32)
        w_out[:, at] = f_out[g].astype(F32)
        for n in range(3):
            w_qkv[:, 1024 * n + 256 * g : 1024 * n + 256 * g + 256] = f_qkv[
                g, :, 256 * n : 256 * n + 256
            ].astype(F32)
        w_dn[h * g : h * g + h, :] = f_dn[g].astype(F32)
    for shard in range(16):
        at = slice(128 * (shard // 2), 128 * (shard // 2) + 128)
        for half in (0, 1):
            first, second = f_up[2 * half, :, at].astype(F32), f_up[2 * half + 1, :, at].astype(F32)
            if shard % 2 == 0:
                both = jnp.where(low_half, first, pltpu.roll(second, 64, 1))
            else:
                both = jnp.where(low_half, pltpu.roll(first, 64, 1), second)
            w_up[:, 256 * shard + 128 * half : 256 * shard + 128 * half + 128] = both


def small_pack(seq_lengths, token_ids, noise_level, vectors, b_up):
    tok_count = token_ids.shape[0]
    seq_ends = jnp.cumsum(seq_lengths[0], dtype=jnp.int32)
    positions = jnp.arange(tok_count, dtype=jnp.int32)
    segment = jnp.sum((positions[:, None] >= seq_ends[None, :]).astype(jnp.int32), axis=1)
    vecs = jnp.concatenate([v.reshape(1, -1) for v in vectors] + [b_up.reshape(4, -1)], axis=0)
    vecs = vecs.astype(F32)
    half = (jnp.arange(128) // 64) == lax.axis_index("fsdp") % 2
    vecs = jnp.where(half[None, :], jnp.concatenate([vecs, vecs], axis=1), 0.0)
    blank = jnp.zeros((16 - vecs.shape[0], 128), F32)
    tail = jnp.zeros((2, 128), F32)
    return jnp.concatenate(
        [
            vecs,
            blank,
            token_ids.astype(F32).reshape(2, 128),
            segment.astype(F32).reshape(2, 128),
            noise_level.reshape(2, 128),
            tail,
        ],
        axis=0,
    )


def fused_shards(
    token_ids, seq_lengths, noise, noise_level, table, w_in, b_in, gain_first, shift_first, w_qkv,
    w_out, b_out, gain_second, shift_second, w_up, b_up, w_down, b_down, cotangent,
):
    small = small_pack(
        seq_lengths, token_ids, noise_level,
        (b_in, gain_first, shift_first, b_out, gain_second, shift_second, b_down), b_up,
    )
    vmem = pl.BlockSpec(memory_space=pltpu.VMEM)
    hbm = pl.BlockSpec(memory_space=pl.ANY)

    def shape(*dims, dtype=BF):
        return jax.ShapeDtypeStruct(dims, dtype)

    rows_here = table.shape[0]
    padded = -(-rows_here // 256) * 256
    outs = [
        shape(256, 1024), shape(256, 256, dtype=F32), shape(rows_here, 256, dtype=F32),
        shape(16, 128, dtype=F32), shape(4, 16, 256), shape(4, 64, 768), shape(4, 64, 256),
        shape(4, 64, 1024), shape(4, 64, 1024),
    ]

    held = [pltpu.VMEM(v.shape, v.dtype) for v in (small, noise, w_in, w_qkv, w_out, w_up, w_down, cotangent)]
    held += [pltpu.VMEM(v.shape, v.dtype) for v in outs]

    def bf(*dims):
        return pltpu.VMEM(dims, BF)

    def fl(*dims):
        return pltpu.VMEM(dims, F32)

    scratch = [
        fl(8, 2, 24, 128), fl(8, 2, 24, 128), fl(2, 24, 128),
        fl(16, 1024), fl(16, 1024), fl(2, 4, 16, 128), fl(4, 16, 128), fl(3, 16, 128),
        fl(4, 16, 128), fl(8, 1024), fl(256, 128), fl(8, 1024),
        bf(2, padded, 256), bf(32, 256, 256), bf(4, 256, 256), bf(4, 8, 2, 16, 256),
        bf(8, 128, 768), bf(4, 8, 128, 256), bf(8, 128, 1024), bf(8, 128, 1024),
        bf(2, 16, 256), bf(64, 768), bf(64, 256), bf(64, 1024),
        fl(256, 1024), fl(256, 1024), fl(256, 1024), fl(256, 1024),
        fl(256, 256), fl(256, 256), fl(256, 256),
        bf(4, 256, 1024), bf(4, 256, 768), bf(16, 256, 256), bf(256, 1024), bf(3, 256, 256),
        bf(4, 256, 1024), bf(4, 256, 1024), bf(8, 128, 1024), bf(4, 256, 1024),
        bf(6, 256, 1024), bf(6, 256, 1024), bf(2, 256, 1024), bf(4, 256, 256),
        bf(8, 2, 16, 256), bf(8, 128, 768), bf(8, 128, 256), bf(8, 128, 1024),
        bf(4, 2, 16, 256), bf(4, 128, 768), bf(4, 128, 256), bf(4, 128, 1024), bf(4, 128, 1024),
        bf(4, 2, 16, 256), bf(4, 128, 768), bf(4, 128, 256), bf(4, 128, 1024), bf(4, 128, 1024),
        bf(3, 256, 256), bf(3, 256, 256),
        pltpu.SemaphoreType.DMA((SEM_COUNT,)), pltpu.SemaphoreType.DMA((SEM_COUNT,)),
        pltpu.SemaphoreType.DMA((30,)),
    ]
    parts = pl.pallas_call(
        layer_kernel,
        out_shape=outs,
        in_specs=[hbm] * 9,
        out_specs=[hbm] * len(outs),
        scratch_shapes=held + scratch,
        compiler_params=pltpu.CompilerParams(
            collective_id=0, has_side_effects=True, vmem_limit_bytes=VMEM_LIMIT
        ),
        cost_estimate=pl.CostEstimate(flops=40 * 10**9, bytes_accessed=30 * 10**6, transcendentals=0),
    )(small, noise, table, w_in, w_qkv, w_out, w_up, w_down, cotangent)
    f32 = lambda a: jax.ShapeDtypeStruct(a.shape, F32)
    finals = [
        outs[0], outs[1], outs[2], f32(w_in), f32(b_in), f32(gain_first), f32(shift_first),
        f32(w_qkv), f32(w_out), f32(b_out), f32(gain_second), f32(shift_second), f32(w_up),
        f32(b_up), f32(w_down), f32(b_down),
    ]
    return tuple(
        pl.pallas_call(
            finish_kernel,
            out_shape=finals,
            in_specs=[vmem] * len(outs),
            out_specs=[vmem] * len(finals),
            compiler_params=pltpu.CompilerParams(vmem_limit_bytes=VMEM_LIMIT),
        )(*parts)
    )


def solution(mesh):
    in_specs = (
        P(("dp", "fsdp")),
        P(("dp", "fsdp"), None),
        P(("dp", "fsdp"), None),
        P(("dp", "fsdp")),
        P("fsdp", None),
        P("fsdp", None),
        P("fsdp"),
        P("fsdp"),
        P("fsdp"),
        P("fsdp", None),
        P("fsdp", None),
        P("fsdp"),
        P("fsdp"),
        P("fsdp"),
        P("fsdp", None),
        P("fsdp"),
        P("fsdp", None),
        P("fsdp"),
        P(("dp", "fsdp"), None),
    )
    out_specs = (
        P(("dp", "fsdp"), None),
        P(("dp", "fsdp"), None),
        P("fsdp", None),
        P("fsdp", None),
        P("fsdp"),
        P("fsdp"),
        P("fsdp"),
        P("fsdp", None),
        P("fsdp", None),
        P("fsdp"),
        P("fsdp"),
        P("fsdp"),
        P("fsdp", None),
        P("fsdp"),
        P("fsdp", None),
        P("fsdp"),
    )
    fused = mesh.shape["dp"] == 2 and mesh.shape["fsdp"] == 16
    body = fused_shards if fused else shards
    return jax.shard_map(body, mesh=mesh, in_specs=in_specs, out_specs=out_specs, check_vma=False)
```

```python
import jax
import jax.numpy as jnp
from jax import lax
from jax.experimental import pallas as pl
from jax.experimental.pallas import tpu as pltpu
from jax.sharding import PartitionSpec as P

HEADS = 16
VOCAB = 32000


norm_eps = 1e-05


def standardize(resid):
    centred = resid - jnp.mean(resid, axis=-1, keepdims=True)
    spread = jnp.mean(centred * centred, axis=-1, keepdims=True)
    return centred * lax.rsqrt(spread + norm_eps)


def row_normalize(tok_rows):
    return tok_rows * lax.rsqrt(jnp.mean(tok_rows * tok_rows, axis=1, keepdims=True) + norm_eps)


def exact_gelu(pre_act):
    return jax.nn.gelu(pre_act, approximate=False)


def split_heads(projected):
    tok_count = projected.shape[0]
    width = projected.shape[1] // 3
    head_size = width // HEADS
    key_heads = projected[:, width : 2 * width].reshape(tok_count, HEADS, head_size)
    value_heads = projected[:, 2 * width :].reshape(tok_count, HEADS, head_size)
    row_block = min(512, tok_count)
    query_blocks = projected[:, :width].reshape(tok_count // row_block, row_block, HEADS, head_size)
    return (query_blocks, key_heads, value_heads, row_block)


def block_scores(query_block, key_heads, seg_block, segment):
    raw_scores = (
        jnp.einsum("qhd,khd->hqk", query_block, key_heads, preferred_element_type=jnp.float32)
        * 0.125
    )
    same_seq = seg_block[:, None] == segment[None, :]
    return jnp.where(same_seq[None, :, :], raw_scores, -1000000000.0)


def attention_forward(projected, segment):
    query_blocks, key_heads, value_heads, row_block = split_heads(projected)
    seg_blocks = segment.reshape(-1, row_block)

    def block_step(items_in):
        query_block, seg_block = items_in
        scores = block_scores(query_block, key_heads, seg_block, segment)
        row_max = jnp.max(scores, axis=-1, keepdims=True)
        exp_scores = jnp.exp(scores - row_max)
        row_total = jnp.sum(exp_scores, axis=-1, keepdims=True)
        soft_probs = (exp_scores / row_total).astype(jnp.bfloat16)
        attended = jnp.einsum(
            "hqk,khd->qhd", soft_probs, value_heads, preferred_element_type=jnp.float32
        )
        return (attended, (row_max + jnp.log(row_total))[:, :, 0])

    attended, log_total = lax.map(block_step, (query_blocks, seg_blocks))
    return (attended.reshape(projected.shape[0], -1), log_total)


def attention_backward(projected, segment, log_total, grad_attended):
    query_blocks, key_heads, value_heads, row_block = split_heads(projected)
    seg_blocks = segment.reshape(-1, row_block)
    grad_blocks = grad_attended.reshape(query_blocks.shape)

    def block_step(totals, items_in):
        grad_keys, grad_values = totals
        query_block, seg_block, log_block, grad_block = items_in
        scores = block_scores(query_block, key_heads, seg_block, segment)
        soft_probs = jnp.exp(scores - log_block[:, :, None])
        grad_values = grad_values + jnp.einsum(
            "hqk,qhd->khd",
            soft_probs.astype(jnp.bfloat16),
            grad_block,
            preferred_element_type=jnp.float32,
        )
        grad_probs = jnp.einsum(
            "qhd,khd->hqk", grad_block, value_heads, preferred_element_type=jnp.float32
        )
        grad_scores = soft_probs * (
            grad_probs - jnp.sum(grad_probs * soft_probs, axis=-1, keepdims=True)
        )
        scaled_grad = (grad_scores * 0.125).astype(jnp.bfloat16)
        grad_query = jnp.einsum(
            "hqk,khd->qhd", scaled_grad, key_heads, preferred_element_type=jnp.float32
        )
        grad_keys = grad_keys + jnp.einsum(
            "hqk,qhd->khd", scaled_grad, query_block, preferred_element_type=jnp.float32
        )
        return ((grad_keys, grad_values), grad_query.astype(jnp.bfloat16))

    zero_heads = jnp.zeros(key_heads.shape, jnp.float32)
    (grad_keys, grad_values), grad_queries = lax.scan(
        block_step, (zero_heads, zero_heads), (query_blocks, seg_blocks, log_total, grad_blocks)
    )
    tok_count = projected.shape[0]
    return jnp.concatenate(
        [
            grad_queries.reshape(tok_count, -1),
            grad_keys.astype(jnp.bfloat16).reshape(tok_count, -1),
            grad_values.astype(jnp.bfloat16).reshape(tok_count, -1),
        ],
        axis=1,
    )


def shards(
    token_ids,
    seq_lengths,
    noise,
    noise_level,
    table,
    w_in,
    b_in,
    gain_first,
    shift_first,
    w_qkv,
    w_out,
    b_out,
    gain_second,
    shift_second,
    w_up,
    b_up,
    w_down,
    b_down,
    cotangent,
):
    tok_count = token_ids.shape[0]
    row_count = table.shape[0]
    group_ids = lax.all_gather(token_ids, "fsdp", axis=0, tiled=True)
    first_row = lax.axis_index("fsdp") * row_count
    owned = (group_ids[:, None] == first_row + jnp.arange(row_count)[None, :]).astype(jnp.bfloat16)
    owned_rows = jnp.dot(owned, table, preferred_element_type=jnp.float32).astype(jnp.bfloat16)
    tok_rows = lax.psum_scatter(owned_rows, "fsdp", scatter_dimension=0, tiled=True)
    tok_rows = tok_rows.astype(jnp.float32)
    vectors = (b_in, gain_first, shift_first, b_out, gain_second, shift_second, b_up, b_down)
    vec_all = lax.all_gather(jnp.concatenate(vectors), "fsdp", axis=0, tiled=False)
    vec_at = [0]
    for vector in vectors:
        vec_at.append(vec_at[-1] + vector.shape[0])
    (
        b_in_all,
        gain_first_all,
        shift_first_all,
        b_out_all,
        gain_second_all,
        shift_second_all,
        b_up_all,
        b_down_all,
    ) = [vec_all[:, lo:hi].reshape(-1) for lo, hi in zip(vec_at[:-1], vec_at[1:])]
    w_in_all = lax.all_gather(w_in, "fsdp", axis=0, tiled=True)
    w_qkv_all = lax.all_gather(w_qkv, "fsdp", axis=0, tiled=True)
    w_out_all = lax.all_gather(w_out, "fsdp", axis=0, tiled=True)
    w_up_all = lax.all_gather(w_up, "fsdp", axis=0, tiled=True)
    w_down_all = lax.all_gather(w_down, "fsdp", axis=0, tiled=True)
    seq_ends = jnp.cumsum(seq_lengths[0], dtype=jnp.int32)
    positions = jnp.arange(tok_count, dtype=jnp.int32)
    segment = jnp.sum((positions[:, None] >= seq_ends[None, :]).astype(jnp.int32), axis=1)
    live_rows = (segment < seq_lengths.shape[1]).astype(jnp.float32)[:, None]
    embedded = row_normalize(tok_rows)
    scale_in = lax.rsqrt(1.0 + noise_level * noise_level)[:, None]
    scaled = ((embedded + noise_level[:, None] * noise.astype(jnp.float32)) * scale_in).astype(
        jnp.bfloat16
    )
    resid_in = jnp.dot(scaled, w_in_all, preferred_element_type=jnp.float32) + b_in_all.astype(
        jnp.float32
    )
    std_first, first_pull = jax.vjp(standardize, resid_in)
    normed_a = (
        std_first * gain_first_all.astype(jnp.float32) + shift_first_all.astype(jnp.float32)
    ).astype(jnp.bfloat16)
    projected = jnp.dot(normed_a, w_qkv_all, preferred_element_type=jnp.float32).astype(
        jnp.bfloat16
    )
    attended, log_total = attention_forward(projected, segment)
    attended = attended.astype(jnp.bfloat16)
    resid_mid = (
        resid_in
        + jnp.dot(attended, w_out_all, preferred_element_type=jnp.float32)
        + b_out_all.astype(jnp.float32)
    )
    std_second, second_pull = jax.vjp(standardize, resid_mid)
    normed_b = (
        std_second * gain_second_all.astype(jnp.float32) + shift_second_all.astype(jnp.float32)
    ).astype(jnp.bfloat16)
    pre_act = jnp.dot(normed_b, w_up_all, preferred_element_type=jnp.float32) + b_up_all.astype(
        jnp.float32
    )
    activated, gelu_pull = jax.vjp(exact_gelu, pre_act)
    hidden = activated.astype(jnp.bfloat16)
    resid_out = (
        resid_mid
        + jnp.dot(hidden, w_down_all, preferred_element_type=jnp.float32)
        + b_down_all.astype(jnp.float32)
    )
    activations = (resid_out * live_rows).astype(jnp.bfloat16)
    grad_out = cotangent.astype(jnp.float32) * live_rows
    grad_down = grad_out.astype(jnp.bfloat16)
    b_down_term = jnp.sum(grad_down.astype(jnp.float32), axis=0)
    w_down_term = jnp.einsum("tf,td->fd", hidden, grad_down, preferred_element_type=jnp.float32)
    grad_hidden = jnp.einsum("td,fd->tf", grad_down, w_down_all, preferred_element_type=jnp.float32)
    grad_act = gelu_pull(grad_hidden)[0].astype(jnp.bfloat16)
    b_up_term = jnp.sum(grad_act.astype(jnp.float32), axis=0)
    w_up_term = jnp.einsum("td,tf->df", normed_b, grad_act, preferred_element_type=jnp.float32)
    grad_nb = jnp.einsum("tf,df->td", grad_act, w_up_all, preferred_element_type=jnp.float32)
    gain_second_term = jnp.sum(grad_nb * std_second, axis=0)
    shift_second_term = jnp.sum(grad_nb, axis=0)
    grad_mid = grad_out + second_pull(grad_nb * gain_second_all.astype(jnp.float32))[0]
    grad_att = grad_mid.astype(jnp.bfloat16)
    b_out_term = jnp.sum(grad_att.astype(jnp.float32), axis=0)
    w_out_term = jnp.einsum("tc,td->cd", attended, grad_att, preferred_element_type=jnp.float32)
    grad_attended = jnp.einsum(
        "td,cd->tc", grad_att, w_out_all, preferred_element_type=jnp.float32
    ).astype(jnp.bfloat16)
    grad_proj = attention_backward(projected, segment, log_total, grad_attended)
    w_qkv_term = jnp.einsum("td,te->de", normed_a, grad_proj, preferred_element_type=jnp.float32)
    grad_na = jnp.einsum("te,de->td", grad_proj, w_qkv_all, preferred_element_type=jnp.float32)
    gain_first_term = jnp.sum(grad_na * std_first, axis=0)
    shift_first_term = jnp.sum(grad_na, axis=0)
    grad_in = grad_mid + first_pull(grad_na * gain_first_all.astype(jnp.float32))[0]
    grad_pin = grad_in.astype(jnp.bfloat16)
    b_in_term = jnp.sum(grad_pin.astype(jnp.float32), axis=0)
    w_in_term = jnp.einsum("te,td->ed", scaled, grad_pin, preferred_element_type=jnp.float32)
    grad_scaled = jnp.einsum("td,ed->te", grad_pin, w_in_all, preferred_element_type=jnp.float32)
    noise_grad = grad_scaled * noise_level[:, None] * scale_in
    grad_embedded = grad_scaled * scale_in
    all_ids = lax.all_gather(token_ids, ("dp", "fsdp"), axis=0, tiled=True)
    all_grads = lax.all_gather(
        grad_embedded.astype(jnp.bfloat16), ("dp", "fsdp"), axis=0, tiled=True
    )
    owners = (first_row + jnp.arange(row_count)[:, None] == all_ids[None, :]).astype(jnp.bfloat16)
    row_grad = jnp.dot(owners, all_grads, preferred_element_type=jnp.float32)
    own_table = table.astype(jnp.float32)
    unused_rows, table_pull = jax.vjp(row_normalize, own_table)
    table_part = table_pull(row_grad)[0]

    def reduce_matrix(term):
        part = lax.psum_scatter(
            term.astype(jnp.bfloat16), "fsdp", scatter_dimension=0, tiled=True
        )
        return lax.psum(part, "dp").astype(jnp.float32)

    vec_terms = (
        b_in_term,
        gain_first_term,
        shift_first_term,
        b_out_term,
        gain_second_term,
        shift_second_term,
        b_up_term,
        b_down_term,
    )
    shard_count = lax.axis_size("fsdp")
    vec_term = jnp.concatenate([v.reshape(shard_count, -1) for v in vec_terms], axis=1)
    vec_part = lax.psum(vec_term, ("dp", "fsdp"))
    own_vec = lax.dynamic_index_in_dim(vec_part, lax.axis_index("fsdp"), 0, keepdims=False)
    vec_grads = [own_vec[lo:hi] for lo, hi in zip(vec_at[:-1], vec_at[1:])]
    return (
        activations,
        noise_grad,
        table_part,
        reduce_matrix(w_in_term),
        vec_grads[0],
        vec_grads[1],
        vec_grads[2],
        reduce_matrix(w_qkv_term),
        reduce_matrix(w_out_term),
        vec_grads[3],
        vec_grads[4],
        vec_grads[5],
        reduce_matrix(w_up_term),
        vec_grads[6],
        reduce_matrix(w_down_term),
        vec_grads[7],
    )


BF = jnp.bfloat16
F32 = jnp.float32
MESH_ID = pl.DeviceIdType.MESH
SEM_COUNT = 400
ROW_UNROLL = 8
HEAD_UNROLL = 4
EACH_UNROLL = 4
VMEM_LIMIT = 63 * 2**20
NT = (((1,), (1,)), ((), ()))
TN = (((0,), (0,)), ((), ()))
DIAG, ACROSS, TWIN = 0, 1, 2
FLIPS = ((1, 1), (1, 0), (0, 1))


def mm(a, b):
    return jnp.dot(a, b, preferred_element_type=F32)


def mm_nt(a, b):
    return lax.dot_general(a, b, NT, preferred_element_type=F32)


def mm_tn(a, b):
    return lax.dot_general(a, b, TN, preferred_element_type=F32)


def part(start, size):
    return pl.ds(pl.multiple_of(start, size), size)


def as_row(pair):
    return jnp.concatenate([pair[0:1, :], pair[1:2, :]], axis=1)


def as_col(pair):
    eye = lax.broadcasted_iota(jnp.int32, (128, 128), 0) == lax.broadcasted_iota(
        jnp.int32, (128, 128), 1
    )
    cols = [
        jnp.sum(jnp.where(eye, pair[k : k + 1, :], 0.0), axis=1, keepdims=True) for k in (0, 1)
    ]
    return jnp.concatenate(cols, axis=0)


def norm_parts(v):
    centred = v - jnp.mean(v, axis=-1, keepdims=True)
    rstd = lax.rsqrt(jnp.mean(centred * centred, axis=-1, keepdims=True) + norm_eps)
    return centred * rstd, rstd


def norm_back(u, n, rstd):
    return rstd * (
        u - jnp.mean(u, axis=-1, keepdims=True) - n * jnp.mean(u * n, axis=-1, keepdims=True)
    )


def layer_kernel(
    ids_hbm, lengths_hbm, level_hbm, b_in_hbm, gain_a_hbm, shift_a_hbm, b_out_hbm, gain_b_hbm, shift_b_hbm,
    b_dn_hbm, b_up_hbm, noise_hbm, table, w_in_hbm, w_qkv_hbm, w_out_hbm, w_up_hbm, w_down_hbm, cot_hbm,
    act_hbm, ngrad_hbm, tgrad_hbm, vout_hbm, f_in_hbm, f_qkv_hbm, f_out_hbm, f_up_hbm, f_dn_hbm,
    ids_v, lengths_v, level_v, b_in_v, gain_a_v, shift_a_v, b_out_v, gain_b_v, shift_b_v, b_dn_v, b_up_v,
    small, noise, w_in, w_qkv, w_out, w_up, w_down, cot,
    act, ngrad, tgrad, vout, f_in, f_qkv, f_out, f_up, f_dn,
    sm, smx, gsm, vec, vg, vq, vgy, vgz, vgf, bup, lives, idr,
    tp, tok, sc, win, wqkv, wout, wup, wdn, s_in, s_qkv, s_out, s_up,
    rin, rmid, gmid, t1, t2, t3, t4, na, proj, pr, att, asend, nb, gd, hid, ga,
    xs, xr, gatt, go, g_in, g_qkv, g_out, g_dn,
    y_in, y_qkv, y_out, y_up, y_dn, z_in, z_qkv, z_out, z_up, z_dn,
    ss, rr, ls,
):
    x = lax.axis_index("dp")
    f = lax.axis_index("fsdp")
    z, y, c = f // 4, lax.rem(f // 2, 2), lax.rem(f, 2)
    q = 2 * z + y
    g = 2 * x + c
    rows_here = table.shape[0]

    def dev(dx, dz, dy, dc):
        xx = lax.rem(x + dx, 2)
        zz = lax.rem(z + dz, 4)
        yy = lax.rem(y + dy, 2)
        cc = lax.rem(c + dc, 2)
        return (xx, zz * 4 + yy * 2 + cc)

    twin = dev(0, 0, 0, 1)
    across = dev(1, 0, 0, 0)
    pair_y = dev(0, 0, 1, 0)
    relay_to = (x, jnp.where(z == 2, 3, 0) * 4 + y * 2 + c)
    rel_dev = [dev(dx, 0, 0, dc) for dx, dc in FLIPS]
    rel_g = [2 * lax.rem(x + dx, 2) + lax.rem(c + dc, 2) for dx, dc in FLIPS]
    other_c = 1 - c

    def far(d):
        return lax.rem(z + 4 - d, 4)

    def to(d):
        return lax.rem(z + d, 4)

    sems = [0]
    pending = []
    inner = jnp.logical_or(z == 1, z == 2)
    outer = jnp.logical_not(inner)

    class Link:
        def __init__(self):
            self.at = sems[0]
            sems[0] += 1
            assert sems[0] <= SEM_COUNT

        def send(self, src, dst, device, arrives=None, only=None):
            self.only = only
            self.copy = pltpu.make_async_remote_copy(
                src_ref=src, dst_ref=dst, send_sem=ss.at[self.at],
                recv_sem=rr.at[self.at if arrives is None else arrives],
                device_id=device, device_id_type=MESH_ID,
            )
            if only is None:
                self.copy.start()
            else:
                pl.when(only)(self.copy.start)
            pending.append(self)
            return self

        def sent(self):
            pending.remove(self)
            if self.only is None:
                self.copy.wait_send()
            else:
                pl.when(self.only)(self.copy.wait_send)

        def got(self, ref):
            arrived(self.at, ref)

    def arrived(at, ref):
        pltpu.make_async_remote_copy(
            src_ref=ref, dst_ref=ref, send_sem=ss.at[0], recv_sem=rr.at[at],
            device_id=twin, device_id_type=MESH_ID,
        ).wait_recv()

    def each_rows(count, size, body):
        def step(i, carry):
            body(part(i * size, size))
            return carry

        lax.fori_loop(0, count // size, step, 0, unroll=ROW_UNROLL)

    def each(count, body, unroll=EACH_UNROLL):
        def step(i, carry):
            body(i)
            return carry

        lax.fori_loop(0, count, step, 0, unroll=unroll)

    local = [0]
    stores = []

    def moved(src, dst):
        copy = pltpu.make_async_copy(src, dst, ls.at[local[0]])
        local[0] += 1
        copy.start()
        return copy

    vectors = (b_in_v, gain_a_v, shift_a_v, b_out_v, gain_b_v, shift_b_v, b_dn_v)
    load_small = [
        moved(src, dst)
        for src, dst in (
            (ids_hbm, ids_v), (lengths_hbm, lengths_v), (level_hbm, level_v), (b_in_hbm, b_in_v),
            (gain_a_hbm, gain_a_v), (shift_a_hbm, shift_a_v), (b_out_hbm, b_out_v),
            (gain_b_hbm, gain_b_v), (shift_b_hbm, shift_b_v), (b_dn_hbm, b_dn_v), (b_up_hbm, b_up_v),
        )
    ]
    load_in = moved(w_in_hbm, w_in)
    load_qkv = moved(w_qkv_hbm, w_qkv)
    load_cot = moved(cot_hbm, cot)
    own_table = moved(table, tp.at[c, pl.ds(0, rows_here)])
    load_noise = moved(noise_hbm, noise)
    load_out = moved(w_out_hbm, w_out)
    load_up = moved(w_up_hbm, w_up)
    load_down = moved(w_down_hbm, w_down)

    barrier = pltpu.get_barrier_semaphore()
    peers = [dev(0, d, 0, dc) for d in (1, 2, 3) for dc in (0, 1)] + rel_dev + [pair_y]
    for peer in peers:
        pl.semaphore_signal(barrier, inc=1, device_id=peer, device_id_type=MESH_ID)
    pl.semaphore_wait(barrier, len(peers))

    class GroupGather:
        def __init__(self, at):
            self.at = at
            self.across = Link().send(at(g), at(g), across)
            self.twin = Link().send(at(g), at(g), twin)

        def hop(self):
            self.across.got(self.at(rel_g[ACROSS]))
            self.second = Link().send(self.at(rel_g[ACROSS]), self.at(rel_g[ACROSS]), twin)

        def got_twin(self):
            self.twin.got(self.at(rel_g[TWIN]))

        def got_diag(self):
            self.second.got(self.at(rel_g[DIAG]))

    class Gather:
        def __init__(self, whole, mine, theirs, height, twins=None, relay=True):
            self.whole, self.height, self.relay = whole, height, relay
            places = (self.sub(q, c), self.sub(q, c, twins))
            self.links = {}
            for d in (0, 2, 1, 3):
                only = {1: z != 3, 3: z != 0}.get(d) if relay else None
                for dc in (1, 0):
                    if (d, dc) != (0, 0):
                        self.links[d, dc] = Link().send(
                            theirs if dc else mine, places[dc], dev(0, d, 0, dc), only=only
                        )

        def sub(self, block, core, whole=None):
            whole = self.whole if whole is None else whole
            if self.height is None:
                return whole.at[block, core]
            return whole.at[block, part(core * self.height, self.height)]

        def over_y(self, block):
            return Link().send(self.whole.at[block], self.whole.at[block], pair_y)

        def own(self):
            self.links[0, 1].got(self.sub(q, other_c))
            self.y_own = self.over_y(q)

        def second(self):
            block = 2 * far(2) + y
            for dc in (1, 0):
                ref = self.sub(block, other_c if dc else c)
                self.links[2, dc].got(ref)
                if self.relay:
                    Link().send(
                        ref, ref, relay_to, only=inner,
                        arrives=jnp.where(z == 2, self.links[3, dc].at, self.links[1, dc].at),
                    )
            self.y_second = self.over_y(block)

        def near(self):
            self.y_near = self.one(3, 1)

        def last(self):
            self.y_last = self.one(1, 3)

        def one(self, low, high):
            block = 2 * jnp.where(z < 2, far(low), far(high)) + y
            for dc in (1, 0):
                arrived(
                    jnp.where(z < 2, self.links[low, dc].at, self.links[high, dc].at),
                    self.sub(block, other_c if dc else c),
                )
            return self.over_y(block)

        def forward(self):
            self.second()
            self.near()
            self.last()

        def finish(self):
            self.y_own.got(self.whole.at[2 * z + 1 - y])
            self.y_second.got(self.whole.at[2 * far(2) + 1 - y])
            self.y_near.got(self.whole.at[2 * jnp.where(z < 2, far(3), far(1)) + 1 - y])
            self.y_last.got(self.whole.at[2 * jnp.where(z < 2, far(1), far(3)) + 1 - y])

    class YFirstGather(Gather):
        def __init__(self, whole, mine, theirs, height):
            self.whole, self.height, self.relay = whole, height, True
            self.y_links = [
                Link().send(theirs if dc else mine, self.sub(q, c), dev(0, 0, 1, dc)) for dc in (0, 1)
            ]
            self.mine, self.theirs = mine, theirs

        def along(self):
            Gather.__init__(self, self.whole, self.mine, self.theirs, self.height)

        def cross(self):
            block = 2 * z + 1 - y
            for dc in (0, 1):
                self.y_links[dc].got(self.sub(block, other_c if dc else c))
            ref = self.whole.at[block]
            self.beside = {
                d: Link().send(ref, ref, dev(0, d, 0, 0), only={1: z != 3, 3: z != 0}.get(d))
                for d in (2, 1, 3)
            }

        def over_y(self, block):
            return None

        def second(self):
            Gather.second(self)
            ref = self.whole.at[2 * far(2) + 1 - y]
            self.beside[2].got(ref)
            Link().send(
                ref, ref, relay_to, only=inner,
                arrives=jnp.where(z == 2, self.beside[3].at, self.beside[1].at),
            )

        def finish(self):
            self.links[0, 1].got(self.sub(q, other_c))
            self.near()
            self.last()
            for d in (1, 3):
                self.beside[d].got(self.whole.at[2 * far(d) + 1 - y])

    for load in load_small:
        load.wait()
    lane_at = lax.broadcasted_iota(jnp.int32, (1, 128), 1)
    small[...] = jnp.zeros_like(small)

    def put_half(row, shard):
        small[row : row + 1, :] = jnp.where(
            lane_at // 64 == c, jnp.concatenate([shard, shard], axis=1), 0.0
        )

    def put_pair(row, line):
        small[row : row + 1, :] = line[:, 0:128]
        small[row + 1 : row + 2, :] = line[:, 128:256]

    for k, v in enumerate(vectors):
        put_half(k, v[...].astype(F32).reshape(1, 64))
    up_shard = b_up_v[...].astype(F32).reshape(1, 256)
    for k in range(4):
        put_half(7 + k, up_shard[:, 64 * k : 64 * k + 64])
    put_pair(16, ids_v[...].astype(F32).reshape(1, 256))
    put_pair(20, level_v[...].reshape(1, 256))
    lengths = lengths_v[...].astype(F32)
    slot_at = lax.broadcasted_iota(jnp.int32, lengths.shape, 1)
    spots = (
        lax.broadcasted_iota(jnp.int32, (2, 128), 0) * 128
        + lax.broadcasted_iota(jnp.int32, (2, 128), 1)
    ).astype(F32)
    slot_of = jnp.zeros((2, 128), F32)
    for k in range(8):
        end = jnp.sum(jnp.where(slot_at <= k, lengths, 0.0), axis=1, keepdims=True)
        slot_of += jnp.where(spots >= end, 1.0, 0.0)
    small[18:20, :] = slot_of
    sm[q, c] = small[...]
    small_links = [Link().send(small, gsm.at[rel], rel_dev[rel]) for rel in (DIAG, ACROSS)]
    gather_small = Gather(sm, small, small, None, relay=False)

    own_rows = tp.at[c, pl.ds(0, rows_here)]
    table_link = Link().send(table, own_rows, twin)
    spare = tp.shape[1] - rows_here
    if spare:
        for core in (0, 1):
            tp[core, pl.ds(rows_here, spare), :] = jnp.zeros((spare, tp.shape[2]), BF)

    def pack(whole, spare_buf, height, pick):
        mine, theirs = pick(g), pick(2 * x + other_c)
        whole[q, part(c * height, height), :] = mine
        spare_buf[...] = theirs

    h = w_qkv.shape[0]
    hin = w_in.shape[0]

    def cols(ref, start, size=256):
        return ref[:, part(start, size)]

    win_at, wout_at = win.at[g], wout.at[g]
    load_in.wait()
    load_qkv.wait()
    win_at[q, c] = cols(w_in, 256 * g)
    s_in[0] = cols(w_in, 256 * (2 * x + other_c))
    gather_in = Gather(win_at, win_at.at[q, c], s_in.at[0], None, win.at[2 * x + other_c], relay=False)
    pack(
        wqkv, s_qkv, h,
        lambda k: jnp.concatenate([cols(w_qkv, 1024 * n + 256 * k) for n in (0, 1, 2)], axis=1),
    )
    gather_qkv = Gather(wqkv, wqkv.at[q, part(c * h, h)], s_qkv, h, relay=False)


    lives[:, 0:1] = jnp.where(as_col(small[18:20, :]) < 7.5, 1.0, 0.0)
    vg[...] = jnp.zeros_like(vg)

    def grad_down_rows(at):
        masked = cot[at, :].astype(F32) * lives[at, 0:1]
        gd[g, at, :] = masked.astype(BF)
        vg[6:7, :] += jnp.sum(masked, axis=0, keepdims=True)

    load_out.wait()
    pack(wout_at, s_out, h, lambda k: cols(w_out, 256 * k))
    gather_out = Gather(
        wout_at, wout_at.at[q, part(c * h, h)], s_out, h, wout.at[2 * x + other_c], relay=False
    )
    load_cot.wait()
    each_rows(256, 32, grad_down_rows)
    group_gd = GroupGather(lambda k: gd.at[k])

    gather_small.own()
    gather_small.forward()

    gather_in.own()
    gather_qkv.own()
    gather_small.finish()
    smx_link = Link().send(sm, smx, across)
    own_table.wait()
    table_link.got(tp.at[other_c, pl.ds(0, rows_here)])
    lane = lax.broadcasted_iota(jnp.int32, (256, tp.shape[1]), 1)

    def look_up(block):
        ids = as_col(sm[block, c, 16:18, :]).astype(jnp.int32)
        total = jnp.zeros((256, 256), F32)
        for core in (0, 1):
            first = (4 * z + 2 * y + core) * rows_here
            hit = jnp.where(lane == ids - first, 1.0, 0.0).astype(BF)
            total += mm(hit, tp[core])
        return total.astype(BF)

    emb_y = [Link() for _ in range(4)]
    for d in range(4):
        tok[d] = look_up(2 * to(d) + 1 - y)
        emb_y[d].send(tok.at[d], tok.at[8 + d], pair_y)

    load_down.wait()
    wdn[q, part(c * h, h), :] = w_down[part(g * h, h), :]
    gather_dn_y = YFirstGather(
        wdn.at[:, :, 512:1024], w_down.at[part(g * h, h), 512:1024],
        w_down.at[part((2 * x + other_c) * h, h), 512:1024], h,
    )

    def own_blocks(d):
        tok[4 + d] = look_up(2 * lax.rem(z + d, 4) + y)

    each(4, own_blocks)
    emb_z = [None]
    for d in (1, 2, 3):
        emb_y[d].got(tok.at[8 + d])
        tok[4 + d] = tok[4 + d] + tok[8 + d]
        emb_z.append(Link().send(tok.at[4 + d], tok.at[11 + d], dev(0, d, 0, 0)))
    emb_y[0].got(tok.at[8])

    for load in (load_noise, load_up):
        load.wait()
    ct = lax.broadcasted_iota(jnp.int32, (h, 128), 1) < 64
    for j in range(8):
        first = w_up[:, part(128 * (4 * j + x), 128)].astype(F32)
        second = w_up[:, part(128 * (4 * j + 2 + x), 128)].astype(F32)
        low = jnp.where(ct, first, pltpu.roll(second, 64, 1)).astype(BF)
        high = jnp.where(ct, pltpu.roll(first, 64, 1), second).astype(BF)
        wup[q, part(c * h, h), 128 * j : 128 * j + 128] = jnp.where(c == 0, low, high)
        s_up[:, 128 * j : 128 * j + 128] = jnp.where(c == 0, high, low)
    gather_in.forward()
    gather_qkv.forward()
    for j in range(8):
        vec[:, 128 * j : 128 * j + 128] = sm[j, 0, 0:16, :] + sm[j, 1, 0:16, :]

    gather_out.own()
    gather_out.forward()
    gather_in.finish()
    group_in = GroupGather(lambda k: win.at[k])
    group_gd.hop()
    rows_sum = tok[4].astype(F32) + tok[8].astype(F32)
    for d in (1, 2, 3):
        emb_z[d].got(tok.at[11 + d])
        rows_sum += tok[11 + d].astype(F32)
    gather_up = Gather(wup, wup.at[q, part(c * h, h)], s_up, h)
    level = as_col(small[20:22, :])
    scale_in = lax.rsqrt(1.0 + level * level)
    embedded = rows_sum * lax.rsqrt(jnp.mean(rows_sum * rows_sum, axis=1, keepdims=True) + norm_eps)
    sc[g] = ((embedded + level * noise[...].astype(F32)) * scale_in).astype(BF)
    group_sc = GroupGather(lambda k: sc.at[k])

    group_in.hop()
    group_in.got_twin()
    group_in.got_diag()

    def win_mat(k):
        return win[k].reshape(256, 256)

    def first_norm(row, keep):
        for k in range(4):
            keep[:, 256 * k : 256 * k + 256] = (
                mm(sc[row], win_mat(k)) + vec[0:1, 256 * k : 256 * k + 256]
            )

        def chunk(at):
            n, _ = norm_parts(keep[at, :])
            na[row, at, :] = (n * vec[1:2, :] + vec[2:3, :]).astype(BF)

        each_rows(256, 32, chunk)

    def project(row):
        def block(k):
            at = part(k * 256, 256)
            proj[row, :, at] = mm(na[row], wqkv[:, :, at].reshape(1024, 256)).astype(BF)

        each(3, block)

    first_norm(g, rin)
    group_sc.hop()
    gather_up.own()
    group_sc.got_twin()
    first_norm(rel_g[TWIN], t1)
    first_norm(rel_g[ACROSS], t1)
    group_sc.got_diag()
    first_norm(rel_g[DIAG], t1)
    gather_qkv.finish()
    for rel in range(3):
        project(rel_g[rel])
    project(g)
    gather_out.finish()
    group_out = GroupGather(lambda k: wout.at[k])

    head_of = lax.broadcasted_iota(jnp.int32, (1, 256), 1) // 64
    small_links[DIAG].got(gsm.at[DIAG])
    small_links[ACROSS].got(gsm.at[ACROSS])

    def attend(row, pair):
        same = as_col(pair) == as_row(pair)
        keys = proj[row, :, 256:512]
        values = proj[row, :, 512:768]
        queries = proj[row, :, 0:256]
        t2[...] = jnp.zeros_like(t2)

        def head(k):
            mine = head_of == k
            q_head = jnp.where(mine, queries, jnp.zeros_like(queries))
            scores = jnp.where(same, mm_nt(q_head, keys) * 0.125, -1e9)
            weights = jnp.exp(scores - jnp.max(scores, axis=-1, keepdims=True))
            low_probs = (weights / jnp.sum(weights, axis=-1, keepdims=True)).astype(BF)
            pr[row * 4 + k] = low_probs
            t2[...] += mm(low_probs, jnp.where(mine, values, jnp.zeros_like(values)))

        each(4, head, HEAD_UNROLL)
        return t2[...].astype(BF)

    att_links = []
    my_cols = part(256 * g, 256)
    for rel in range(3):
        pair = sm[q, other_c, 18:20, :] if rel == TWIN else gsm[rel, 18:20, :]
        asend[rel] = attend(rel_g[rel], pair)
        att_links.append(Link().send(asend.at[rel], att.at[:, my_cols], rel_dev[rel]))
        if rel == DIAG:
            gather_up.second()
            for d in range(4):
                emb_y[d].sent()
            for d in (1, 2, 3):
                emb_z[d].sent()
            gather_dn = Gather(
                wdn.at[:, :, 0:512], w_down.at[part(g * h, h), 0:512],
                w_down.at[part((2 * x + other_c) * h, h), 0:512], h,
            )
            gather_dn_y.along()
        if rel == ACROSS:
            gather_dn_y.cross()
    att[:, my_cols] = attend(g, small[18:20, :])
    gather_dn.own()
    group_out.hop()
    gather_up.near()
    gather_up.last()
    group_out.got_twin()
    group_out.got_diag()
    for rel in (TWIN, ACROSS, DIAG):
        att_links[rel].got(att.at[:, part(256 * rel_g[rel], 256)])

    def out_block(k):
        at = part(k * 256, 256)
        rmid[:, at] = rin[:, at] + mm(att[...], wout[k].reshape(1024, 256)) + vec[3:4, at]

    each(4, out_block)

    def second_norm(at):
        n, _ = norm_parts(rmid[at, :])
        nb[g, at, :] = (n * vec[4:5, :] + vec[5:6, :]).astype(BF)

    each_rows(256, 32, second_norm)
    nb_across = Link().send(nb.at[g], nb.at[g], across)
    nb_twin = Link().send(nb.at[g], nb.at[g], twin)
    nb_pass = Link()
    group_gd.got_twin()
    group_gd.got_diag()

    bup[...] = jnp.zeros_like(bup)
    for k in range(4):
        bup[0:1, :] += jnp.where(g == k, vec[7 + k : 8 + k, :], 0.0)

    def ff_hidden(row):
        def block(k):
            at = part(k * 256, 256)
            t2[...] = mm(nb[row], wup[:, :, at].reshape(1024, 256)) + bup[0:1, at]

            def chunk(rows_at):
                pre = t2[rows_at, :]
                cdf = 0.5 + 0.5 * lax.erf(pre * 0.7071067811865476)
                pdf = jnp.exp(-0.5 * pre * pre) * 0.3989422804014327
                t2[rows_at, :] = pre * cdf
                ga[row, rows_at, at] = (cdf + pre * pdf).astype(BF)

            each_rows(256, 32, chunk)
            hid[pl.ds(2 * row, 2), :, at] = t2[...].astype(BF).reshape(2, 128, 256)

        each(4, block)

    def ff_grad(row):
        def block(k):
            at = part(k * 256, 256)
            grad = mm_nt(gd[row], wdn[pl.ds(2 * k, 2)].reshape(256, 1024))
            ga_low = (grad * ga[row, :, at].astype(F32)).astype(BF)
            ga[row, :, at] = ga_low
            bup[1:2, at] += jnp.sum(ga_low.astype(F32), axis=0, keepdims=True)

        each(4, block)

    gather_dn.second()
    gather_up.finish()
    ff_hidden(g)
    gather_dn.near()
    gather_dn.last()
    gather_dn_y.second()
    nb_twin.got(nb.at[rel_g[TWIN]])
    ff_hidden(rel_g[TWIN])
    nb_across.got(nb.at[rel_g[ACROSS]])
    nb_pass.send(nb.at[rel_g[ACROSS]], nb.at[rel_g[ACROSS]], twin)
    ff_hidden(rel_g[ACROSS])
    nb_pass.got(nb.at[rel_g[DIAG]])
    ff_hidden(rel_g[DIAG])

    class GroupSum:
        def __init__(self, sends, gets, partial, puts=None, temp=None):
            self.sends, self.gets, self.partial = sends, gets, partial
            self.temp = t1 if temp is None else temp
            self.puts = gets if puts is None else puts

        def first(self):
            self.partial(rel_g[DIAG], self.sends[0])
            self.a = Link().send(self.sends[0], self.puts[0], twin)

        def second(self):
            self.partial(rel_g[ACROSS], self.temp)
            self.a.got(self.gets[0])

            def chunk(at):
                self.sends[1][at, :] = (
                    self.temp[at, :] + self.gets[0][at, :].astype(F32)
                ).astype(BF)

            each_rows(256, 32, chunk)

        def second_send(self):
            self.b = Link().send(self.sends[1], self.puts[1], across)

        def third(self):
            self.partial(rel_g[TWIN], self.sends[2])
            self.c = Link().send(self.sends[2], self.puts[2], twin)

        def own(self, into):
            self.partial(g, into)
            self.into = into

        def total(self):
            self.c.got(self.gets[2])
            self.b.got(self.gets[1])

        def rows(self, at):
            return (
                self.into[at, :].astype(F32)
                + self.gets[1][at, :].astype(F32)
                + self.gets[2][at, :].astype(F32)
            )

        def release(self):
            for link in (self.a, self.b, self.c):
                link.sent()

    def slots(ref, places):
        return [ref.at[place] for place in places]

    def nb_partial(row, into):
        def block(k):
            into[:, part(k * 256, 256)] = mm_nt(
                ga[row], wup[pl.ds(2 * k, 2)].reshape(256, 1024)
            ).astype(into.dtype)

        each(4, block)

    def out_partial(row, into):
        def block(k):
            at = part(k * 256, 256)
            into[:, at] = mm(
                hid[pl.ds(2 * row, 2)].reshape(256, 1024), wdn[:, :, at].reshape(1024, 256)
            ).astype(into.dtype)

        each(4, block)

    class Scatter:
        def __init__(self, grad, y_buf, z_buf, final, height):
            self.grad, self.y_buf, self.z_buf, self.final, self.height = (
                grad, y_buf, z_buf, final, height,
            )

        def chunks(self, body):
            if self.height is None:
                each(2, body)
            else:
                each_rows(2 * self.height, 32, body)

        def half(self, core):
            if self.height is None:
                return self.grad.at[q, core]
            return self.grad.at[q, part(core * self.height, self.height)]

        def start(self, count=4):
            even = lax.rem(z, 2) == 0
            self.goals = (
                jnp.where(even, 3, 0), jnp.where(even, 1, 2), lax.rem(z + 2, 4), z,
            )
            self.y_links = []
            self.z_links = [Link() for _ in range(4)]
            self.more(count)

        def more(self, count=1):
            for _ in range(count):
                e = len(self.y_links)
                self.y_links.append(
                    Link().send(self.grad.at[2 * self.goals[e] + 1 - y], self.y_buf.at[e], pair_y)
                )

        def add_y(self, e):
            self.y_links[e].got(self.y_buf.at[e])
            block = 2 * self.goals[e] + y

            def chunk(at):
                self.grad[block, at] = (
                    self.grad[block, at].astype(F32) + self.y_buf[e, at].astype(F32)
                ).astype(BF)

            self.chunks(chunk)
            return self.grad.at[block]

        def end_to_end(self):
            ref = self.add_y(0)
            self.z_links[0].send(
                ref, self.z_buf.at[0], (x, (z + 1 - 2 * lax.rem(z, 2)) * 4 + y * 2 + c)
            )

        def near(self):
            ref = self.add_y(1)
            slot = jnp.where(inner, 2, 1)
            self.z_links[1].send(
                ref, self.z_buf.at[slot], (x, self.goals[1] * 4 + y * 2 + c),
                arrives=jnp.where(inner, self.z_links[2].at, self.z_links[1].at),
            )

        def second(self):
            ref = self.add_y(2)
            block = 2 * self.goals[2] + y

            def relayed():
                self.z_links[0].got(self.z_buf.at[0])

                def chunk(at):
                    self.grad[block, at] = (
                        self.grad[block, at].astype(F32) + self.z_buf[0, at].astype(F32)
                    ).astype(BF)

                self.chunks(chunk)

            pl.when(inner)(relayed)
            self.z_links[3].send(ref, self.z_buf.at[3], dev(0, 2, 0, 0))

        def own(self):
            self.add_y(3)

        def middle(self):
            self.end_to_end()
            self.near()
            self.second()
            self.own()

        def last(self):
            def summed(slots):
                def run():
                    for slot in slots:
                        self.z_links[slot].got(self.z_buf.at[slot])

                    def chunk(at):
                        total = self.grad[q, at].astype(F32)
                        for slot in slots:
                            total += self.z_buf[slot, at].astype(F32)
                        self.grad[q, at] = total.astype(BF)

                    self.chunks(chunk)

                return run

            pl.when(inner)(summed((1, 2, 3)))
            pl.when(outer)(summed((0, 3)))
            self.f_links = []
            for rel in range(3):
                core = lax.rem(c + FLIPS[rel][1], 2)
                self.f_links.append(
                    Link().send(
                        self.half(core),
                        self.final.at[g],
                        rel_dev[rel],
                    )
                )
            self.final[g] = self.half(c)[...]

        def finish(self):
            for rel in range(3):
                self.f_links[rel].got(self.final.at[rel_g[rel]])

    scatter_dn = Scatter(g_dn, y_dn, z_dn, f_dn, h)
    scatter_up = Scatter(hid, y_up, z_up, f_up, h)
    sum_out = GroupSum(slots(xs, (3, 4, 5)), slots(xr, (3, 4, 5)), out_partial)

    def dn_block(k):
        at = part(k * 256, 256)
        lhs = hid[:, :, at].reshape(1024, 256)
        g_dn[pl.ds(2 * k, 2)] = mm_tn(lhs, gd[...].reshape(1024, 1024)).astype(BF).reshape(
            2, 128, 1024
        )

    each(4, dn_block)
    scatter_dn.start()
    gather_dn.finish()
    gather_dn_y.finish()
    sum_nb = GroupSum(slots(xs, (0, 1, 2)), slots(xr, (0, 1, 2)), nb_partial)
    ff_grad(rel_g[DIAG])
    sum_nb.first()
    ff_grad(rel_g[ACROSS])
    sum_nb.second()
    sum_nb.second_send()
    ff_grad(rel_g[TWIN])
    sum_nb.third()
    ff_grad(g)
    sum_out.first()
    sum_out.second()
    scatter_dn.end_to_end()
    sum_out.third()

    sum_out.own(act)

    def up_block(k):
        at = part(k * 256, 256)
        lhs = nb[:, :, at].reshape(1024, 256)
        hid[pl.ds(2 * k, 2)] = mm_tn(lhs, ga[...].reshape(1024, 1024)).astype(BF).reshape(
            2, 128, 1024
        )

    each(4, up_block)
    scatter_up.start()

    scatter_dn.near()
    sum_nb.own(t1)
    sum_nb.total()

    def second_back(at):
        grad_nb = sum_nb.rows(at)
        n, rstd = norm_parts(rmid[at, :])
        vg[4:5, :] += jnp.sum(grad_nb * n, axis=0, keepdims=True)
        vg[5:6, :] += jnp.sum(grad_nb, axis=0, keepdims=True)
        mid = gd[g, at, :].astype(F32) + norm_back(grad_nb * vec[4:5, :], n, rstd)
        gmid[at, :] = mid
        low_mid = mid.astype(BF)
        gatt[1, at, :] = low_mid
        vg[3:4, :] += jnp.sum(low_mid.astype(F32), axis=0, keepdims=True)

    each_rows(256, 32, second_back)

    def grad_o_part(to_g):
        total = jnp.zeros((256, 256), F32)
        for k in range(4):
            total += mm_nt(
                gatt[1, :, 256 * k : 256 * k + 256], wout[k, pl.ds(2 * to_g, 2)].reshape(256, 256)
            )
        return total.astype(BF)

    for link in (nb_pass, nb_across, nb_twin, group_gd.second):
        link.sent()
    go_links = []
    for rel in range(3):
        att_links[rel].sent()
        asend[rel] = grad_o_part(rel_g[rel])
        go_links.append(Link().send(asend.at[rel], go.at[g], rel_dev[rel]))
    go[g] = grad_o_part(g)

    def wog_partial(k, into):
        for j in range(4):
            into[:, 256 * j : 256 * j + 256] = mm_tn(
                att[:, 256 * j : 256 * j + 256], gatt[1, :, part(256 * k, 256)]
            ).astype(into.dtype)

    sum_nb.release()
    scatter_dn.second()
    for rel in (TWIN, ACROSS, DIAG):
        go_links[rel].got(go.at[rel_g[rel]])
    sum_wog = GroupSum(
        slots(gd, rel_g), slots(nb, rel_g), wog_partial, slots(nb, (rel_g[ACROSS], g, g))
    )
    sum_wog.first()
    sum_wog.second()
    sum_wog.second_send()
    sum_wog.third()
    sum_wog.own(nb.at[g])

    def attend_back(row):
        keys = proj[row, :, 256:512]
        values = proj[row, :, 512:768]
        queries = proj[row, :, 0:256]
        grad_rows = go[row]
        zero = jnp.zeros_like(keys)
        for buf in (t2, t3, t4):
            buf[...] = jnp.zeros_like(buf)

        def head(k):
            mine = head_of == k
            probs = pr[row * 4 + k]
            g_head = jnp.where(mine, grad_rows, zero)
            t4[...] += mm_tn(probs, g_head)
            grad_p = mm_nt(g_head, values)
            wide = probs.astype(F32)
            grad_s = wide * (grad_p - jnp.sum(grad_p * wide, axis=-1, keepdims=True))
            low_s = (grad_s * 0.125).astype(BF)
            t2[...] += mm(low_s, jnp.where(mine, keys, zero))
            t3[...] += mm_tn(low_s, jnp.where(mine, queries, zero))

        each(4, head, HEAD_UNROLL)
        proj[row, :, 0:256] = t2[...].astype(BF)
        proj[row, :, 256:512] = t3[...].astype(BF)
        proj[row, :, 512:768] = t4[...].astype(BF)

    def na_partial(row, into):
        def block(k):
            into[:, part(k * 256, 256)] = mm_nt(
                proj[row], wqkv[pl.ds(2 * k, 2)].reshape(256, 768)
            ).astype(into.dtype)

        each(4, block)

    sum_na = GroupSum(slots(xs, (0, 1, 2)), slots(xr, (0, 1, 2)), na_partial)
    scatter_dn.own()
    attend_back(rel_g[DIAG])
    sum_na.first()
    scatter_up.end_to_end()
    attend_back(rel_g[ACROSS])
    sum_na.second()
    sum_na.second_send()
    attend_back(rel_g[TWIN])
    sum_na.third()
    scatter_up.near()
    sum_wog.total()
    scatter_out = Scatter(g_out, y_out, z_out, f_out, h)
    for j in range(4):
        at = slice(256 * j, 256 * j + 256)
        g_out[2 * j : 2 * j + 2] = (
            nb[g, :, at].astype(F32) + nb[rel_g[ACROSS], :, at].astype(F32)
            + nb[rel_g[TWIN], :, at].astype(F32)
        ).astype(BF).reshape(2, 128, 256)
    scatter_out.start()
    attend_back(g)
    sum_na.own(t1)

    scatter_qkv = Scatter(g_qkv, y_qkv, z_qkv, f_qkv, h)
    scatter_in = Scatter(g_in, y_in, z_in, f_in, None)

    def qkv_block(k):
        at = part(k * 256, 256)
        lhs = na[:, :, at].reshape(1024, 256)
        g_qkv[pl.ds(2 * k, 2)] = mm_tn(lhs, proj[...].reshape(1024, 768)).astype(BF).reshape(
            2, 128, 768
        )

    each(4, qkv_block)
    scatter_qkv.start()
    scatter_up.second()

    sum_na.total()

    def first_back(at):
        grad_na = sum_na.rows(at)
        n, rstd = norm_parts(rin[at, :])
        vg[1:2, :] += jnp.sum(grad_na * n, axis=0, keepdims=True)
        vg[2:3, :] += jnp.sum(grad_na, axis=0, keepdims=True)
        low_in = (gmid[at, :] + norm_back(grad_na * vec[1:2, :], n, rstd)).astype(BF)
        gatt[0, at, :] = low_in
        vg[0:1, :] += jnp.sum(low_in.astype(F32), axis=0, keepdims=True)

    each_rows(256, 32, first_back)
    for k in range(4):
        vg[7 + k : 8 + k, :] = jnp.where(g == k, bup[1:2, :], 0.0)
    for j in range(8):
        vq[j % 2, j // 2] = vg[:, 128 * j : 128 * j + 128]
    vy_link = Link().send(vq.at[1 - y], vgy, pair_y)

    grad_scaled = jnp.zeros((256, 256), F32)
    for k in range(4):
        grad_scaled += mm_nt(gatt[0, :, 256 * k : 256 * k + 256], win_mat(k))
    level = as_col(small[20:22, :])
    scale_in = lax.rsqrt(1.0 + level * level)
    ngrad[...] = grad_scaled * (level * scale_in)
    stores.append(moved(ngrad, ngrad_hbm))

    def set_at(other_x, other_y, other_core):
        return ((lax.rem(x + other_x, 2) * 2 + lax.rem(y + other_y, 2)) * 2 + lax.rem(c + other_core, 2)) * 4

    home = tok.at[set_at(0, 0, 0) + z]
    tok[set_at(0, 0, 0) + z] = (grad_scaled * scale_in).astype(BF)
    steps = {"own": z, "second": far(2), "near": jnp.where(z < 2, far(3), far(1)), "last": jnp.where(z < 2, far(1), far(3))}

    class Line:
        def __init__(self, ref, first):
            self.first = first
            self.links = {
                d: Link().send(ref, ref, dev(0, d, 0, 0), only={1: z != 3, 3: z != 0}.get(d))
                for d in (2, 1, 3)
            }

        def spot(self, step):
            return self.first + steps[step]

        def got(self, step):
            ref = tok.at[self.spot(step)]
            one, three = self.links[1].at, self.links[3].at
            if step == "second":
                self.links[2].got(ref)
                Link().send(ref, ref, relay_to, only=inner, arrives=jnp.where(z == 2, three, one))
            elif step == "near":
                arrived(jnp.where(z < 2, three, one), ref)
            else:
                arrived(jnp.where(z < 2, one, three), ref)
            return self.spot(step)

    line_own = Line(home, set_at(0, 0, 0))
    tok_x = {}
    tok_y = {}
    tok_t = {}

    def to_twin(spot, own_plane, key):
        tok_t[own_plane, key] = Link().send(tok.at[spot], tok.at[spot], twin)

    tok_x[0, 0] = Link().send(home, home, across)
    tok_y["own"] = Link().send(home, home, pair_y)
    to_twin(set_at(0, 0, 0) + z, True, (0, "own"))
    sum_out.second_send()

    def wig_partial(k, into):
        into[...] = mm_tn(sc[g], gatt[0, :, part(256 * k, 256)]).astype(into.dtype)

    sum_wig = GroupSum(
        slots(pr, (0, 1, 2)), slots(go, rel_g), wig_partial, slots(go, (rel_g[ACROSS], g, g)), t2
    )
    sum_wig.first()
    scatter_out.end_to_end()
    sum_wig.second()
    sum_wig.second_send()
    sum_wig.third()
    sum_wig.own(t3)
    scatter_dn.last()

    beside = set_at(1, 0, 0) + z
    tok_x[0, 0].got(tok.at[beside])
    line_beside = Line(tok.at[beside], set_at(1, 0, 0))
    to_twin(beside, False, (0, "own"))

    def tok_from_z(step):
        spot = line_own.got(step)
        tok_y[step] = Link().send(tok.at[spot], tok.at[spot], pair_y)
        to_twin(spot, True, (0, step))

    def tok_from_y(step):
        spot = set_at(0, 1, 0) + steps[step]
        tok_y[step].got(tok.at[spot])
        tok_x[1, step] = Link().send(tok.at[spot], tok.at[spot], across)
        to_twin(spot, True, (1, step))

    def tok_beside(step):
        to_twin(line_beside.got(step), False, (0, step))

    def tok_from_x(step):
        spot = set_at(1, 1, 0) + steps[step]
        tok_x[1, step].got(tok.at[spot])
        to_twin(spot, False, (1, step))

    smx_link.got(smx)
    for other_x in (0, 1):
        for yy in (0, 1):
            for core in (0, 1):
                source = sm if other_x == 0 else smx
                for zz in range(4):
                    idr[(other_x * 2 + yy) * 2 + core : (other_x * 2 + yy) * 2 + core + 1, 256 * zz : 256 * zz + 256] = (
                        as_row(source[2 * zz + yy, core, 16:18, :])
                    )

    tile = 400
    base = (f * rows_here).astype(F32)
    tile_row = lax.broadcasted_iota(jnp.int32, (tile, 1024), 0).astype(F32)

    def table_add(other_x, other_y, other_core, begin):
        spot = set_at(other_x, other_y, other_core)
        row = (other_x * 2 + lax.rem(y + other_y, 2)) * 2 + lax.rem(c + other_core, 2)
        ids = idr[pl.ds(row, 1), :] - base

        def block(k):
            at = part(k * tile, tile)
            hit = jnp.where(tile_row == ids - (k * tile).astype(F32), 1.0, 0.0).astype(BF)
            add = mm(hit, tok[pl.ds(spot, 4)].reshape(1024, 256))
            if begin:
                tgrad[at, :] = add
            else:
                tgrad[at, :] += add

        each(rows_here // tile, block)

    def twin_set(from_x, other_y):
        for step in steps:
            tok_t[from_x == 0, (other_y, step)].got(tok.at[set_at(from_x, other_y, 1) + steps[step]])

    tok_from_z("second")
    tok_from_z("near")
    scatter_up.own()
    scatter_qkv.end_to_end()
    tok_from_z("last")
    tok_beside("second")
    table_add(0, 0, 0, True)
    scatter_out.near()
    tok_from_y("own")
    scatter_qkv.near()
    twin_set(0, 0)
    table_add(0, 0, 1, False)
    sum_wig.total()
    g_in[...] = (
        t3[...] + go[rel_g[ACROSS]].astype(F32) + go[rel_g[TWIN]].astype(F32)
    ).astype(BF).reshape(8, 2, 16, 256)
    scatter_in.start()
    vy_link.got(vgy)
    vq[y] = vq[y] + vgy[...]
    vz_links = [
        Link().send(vq.at[y, to(d)], vgz.at[d - 1], dev(0, d, 0, 0)) for d in (1, 2, 3)
    ]
    tok_from_y("second")
    scatter_qkv.second()
    tok_from_y("near")
    scatter_qkv.own()
    scatter_out.second()
    scatter_out.own()
    tok_from_y("last")
    table_add(0, 1, 0, False)
    scatter_up.last()
    tok_beside("near")
    tok_beside("last")
    table_add(1, 0, 0, False)
    twin_set(0, 1)
    table_add(0, 1, 1, False)
    scatter_in.middle()
    scatter_qkv.last()
    for d in (1, 2, 3):
        vz_links[d - 1].got(vgz.at[d - 1])
    vtot = vq[y, z] + vgz[0] + vgz[1] + vgz[2]
    vgf[3] = vtot
    vf_links = [Link().send(vgf.at[3], vgf.at[rel], rel_dev[rel]) for rel in range(3)]
    twin_set(1, 0)
    table_add(1, 0, 1, False)
    scatter_out.last()
    scatter_in.last()
    sum_out.total()

    def out_rows(at):
        whole = rmid[at, :] + sum_out.rows(at) + vec[6:7, :]
        act[at, :] = (whole * lives[at, 0:1]).astype(BF)

    each_rows(256, 32, out_rows)
    stores.append(moved(act, act_hbm))
    sum_out.release()

    for step in steps:
        tok_from_x(step)
    table_add(1, 1, 0, False)
    twin_set(1, 1)
    table_add(1, 1, 1, False)

    def table_rows(at):
        values = tp[c, at, :].astype(F32)
        r = lax.rsqrt(jnp.mean(values * values, axis=1, keepdims=True) + norm_eps)
        row_grad = tgrad[at, :]
        slope = jnp.mean(row_grad * values, axis=1, keepdims=True)
        tgrad[at, :] = r * row_grad - values * (r * r * r * slope)

    for k in range(rows_here // 200):
        at = pl.ds(k * 200, 200)
        table_rows(at)
        stores.append(moved(tgrad.at[at], tgrad_hbm.at[at]))

    for rel in range(3):
        vf_links[rel].got(vgf.at[rel])
    vout[...] = vgf[0] + vgf[1] + vgf[2] + vgf[3]
    for scatter in (scatter_dn, scatter_up, scatter_qkv, scatter_out, scatter_in):
        scatter.finish()
    for k, (src, dst) in enumerate(((f_in, f_in_hbm), (f_qkv, f_qkv_hbm), (f_out, f_out_hbm), (f_up, f_up_hbm), (f_dn, f_dn_hbm), (vout, vout_hbm))):
        stores.append(moved(src, dst))
    for link in list(pending):
        link.sent()
    for store in stores:
        store.wait()


def finish_kernel(
    act_in, ngrad_in, tgrad_in, vout, f_in_hbm, f_qkv_hbm, f_out_hbm, f_up_hbm, f_dn_hbm,
    act, ngrad, tgrad, w_in_hbm, b_in, gain_a, shift_a, w_qkv_hbm, w_out_hbm, b_out, gain_b, shift_b,
    w_up_hbm, b_up, w_dn_hbm, b_dn,
    act_v, ngrad_v, tgrad_v, f_in, f_qkv, f_out, f_up, f_dn, w_in, w_qkv, w_out, w_up, w_dn, sems,
):
    count = [0]

    def moved(src, dst):
        copy = pltpu.make_async_copy(src, dst, sems.at[count[0]])
        count[0] += 1
        copy.start()
        return copy

    load_up = moved(f_up_hbm, f_up)
    load_dn = moved(f_dn_hbm, f_dn)
    load_qkv = moved(f_qkv_hbm, f_qkv)
    load_out = moved(f_out_hbm, f_out)
    load_in = moved(f_in_hbm, f_in)
    passed = [(act_in, act_v, act), (ngrad_in, ngrad_v, ngrad)]
    tile = tgrad_v.shape[0] // 5
    for k in range(5):
        at = pl.ds(k * tile, tile)
        passed.append((tgrad_in.at[at], tgrad_v.at[at], tgrad.at[at]))
    passed = [(moved(src, via), via, dst) for src, via, dst in passed]
    stores = []
    c = lax.rem(lax.axis_index("fsdp"), 2)
    rows = jnp.where(c == 0, vout[...], pltpu.roll(vout[...], 64, 1))
    for k, ref in enumerate((b_in, gain_a, shift_a, b_out, gain_b, shift_b, b_dn)):
        ref[...] = rows[k, 0:64]
    for k in range(4):
        b_up[64 * k : 64 * k + 64] = rows[7 + k, 0:64]
    h = w_out.shape[0]
    low_half = lax.broadcasted_iota(jnp.int32, (h, 128), 1) < 64
    load_up.wait()
    for shard in range(16):
        at = slice(128 * (shard // 2), 128 * (shard // 2) + 128)
        for half in (0, 1):
            first, second = f_up[2 * half, :, at].astype(F32), f_up[2 * half + 1, :, at].astype(F32)
            if shard % 2 == 0:
                both = jnp.where(low_half, first, pltpu.roll(second, 64, 1))
            else:
                both = jnp.where(low_half, pltpu.roll(first, 64, 1), second)
            w_up[:, 256 * shard + 128 * half : 256 * shard + 128 * half + 128] = both
    stores.append(moved(w_up, w_up_hbm))
    for load, via, dst in passed:
        load.wait()
        stores.append(moved(via, dst))
    load_dn.wait()
    for g in range(4):
        w_dn[h * g : h * g + h, :] = f_dn[g].astype(F32)
    stores.append(moved(w_dn, w_dn_hbm))
    load_qkv.wait()
    for g in range(4):
        for n in range(3):
            w_qkv[:, 1024 * n + 256 * g : 1024 * n + 256 * g + 256] = f_qkv[
                g, :, 256 * n : 256 * n + 256
            ].astype(F32)
    stores.append(moved(w_qkv, w_qkv_hbm))
    load_out.wait()
    load_in.wait()
    for g in range(4):
        at = slice(256 * g, 256 * g + 256)
        w_in[:, at] = f_in[g].astype(F32)
        w_out[:, at] = f_out[g].astype(F32)
    stores.append(moved(w_out, w_out_hbm))
    stores.append(moved(w_in, w_in_hbm))
    for store in stores:
        store.wait()


def fused_shards(
    token_ids, seq_lengths, noise, noise_level, table, w_in, b_in, gain_first, shift_first, w_qkv,
    w_out, b_out, gain_second, shift_second, w_up, b_up, w_down, b_down, cotangent,
):
    raw = (
        token_ids, seq_lengths, noise_level, b_in, gain_first, shift_first, b_out, gain_second,
        shift_second, b_down, b_up,
    )
    vmem = pl.BlockSpec(memory_space=pltpu.VMEM)
    hbm = pl.BlockSpec(memory_space=pl.ANY)

    def shape(*dims, dtype=BF):
        return jax.ShapeDtypeStruct(dims, dtype)

    rows_here = table.shape[0]
    padded = -(-rows_here // 256) * 256
    outs = [
        shape(256, 1024), shape(256, 256, dtype=F32), shape(rows_here, 256, dtype=F32),
        shape(16, 128, dtype=F32), shape(4, 16, 256), shape(4, 64, 768), shape(4, 64, 256),
        shape(4, 64, 1024), shape(4, 64, 1024),
    ]

    held = [pltpu.VMEM(v.shape, v.dtype) for v in raw] + [pltpu.VMEM((24, 128), F32)]
    held += [pltpu.VMEM(v.shape, v.dtype) for v in (noise, w_in, w_qkv, w_out, w_up, w_down, cotangent)]
    held += [pltpu.VMEM(v.shape, v.dtype) for v in outs]

    def bf(*dims):
        return pltpu.VMEM(dims, BF)

    def fl(*dims):
        return pltpu.VMEM(dims, F32)

    scratch = [
        fl(8, 2, 24, 128), fl(8, 2, 24, 128), fl(2, 24, 128),
        fl(16, 1024), fl(16, 1024), fl(2, 4, 16, 128), fl(4, 16, 128), fl(3, 16, 128),
        fl(4, 16, 128), fl(8, 1024), fl(256, 128), fl(8, 1024),
        bf(2, padded, 256), bf(32, 256, 256), bf(4, 256, 256), bf(4, 8, 2, 16, 256),
        bf(8, 128, 768), bf(4, 8, 128, 256), bf(8, 128, 1024), bf(8, 128, 1024),
        bf(2, 16, 256), bf(64, 768), bf(64, 256), bf(64, 1024),
        fl(256, 1024), fl(256, 1024), fl(256, 1024), fl(256, 1024),
        fl(256, 256), fl(256, 256), fl(256, 256),
        bf(4, 256, 1024), bf(4, 256, 768), bf(16, 256, 256), bf(256, 1024), bf(3, 256, 256),
        bf(4, 256, 1024), bf(4, 256, 1024), bf(8, 128, 1024), bf(4, 256, 1024),
        bf(6, 256, 1024), bf(6, 256, 1024), bf(2, 256, 1024), bf(4, 256, 256),
        bf(8, 2, 16, 256), bf(8, 128, 768), bf(8, 128, 256), bf(8, 128, 1024),
        bf(4, 2, 16, 256), bf(4, 128, 768), bf(4, 128, 256), bf(4, 128, 1024), bf(4, 128, 1024),
        bf(4, 2, 16, 256), bf(4, 128, 768), bf(4, 128, 256), bf(4, 128, 1024), bf(4, 128, 1024),
        pltpu.SemaphoreType.DMA((SEM_COUNT,)), pltpu.SemaphoreType.DMA((SEM_COUNT,)),
        pltpu.SemaphoreType.DMA((45,)),
    ]
    parts = pl.pallas_call(
        layer_kernel,
        out_shape=outs,
        in_specs=[hbm] * 19,
        out_specs=[hbm] * len(outs),
        scratch_shapes=held + scratch,
        compiler_params=pltpu.CompilerParams(
            collective_id=0, has_side_effects=True, vmem_limit_bytes=VMEM_LIMIT
        ),
        cost_estimate=pl.CostEstimate(flops=40 * 10**9, bytes_accessed=30 * 10**6, transcendentals=0),
    )(*raw, noise, table, w_in, w_qkv, w_out, w_up, w_down, cotangent)
    f32 = lambda a: jax.ShapeDtypeStruct(a.shape, F32)
    finals = [
        outs[0], outs[1], outs[2], f32(w_in), f32(b_in), f32(gain_first), f32(shift_first),
        f32(w_qkv), f32(w_out), f32(b_out), f32(gain_second), f32(shift_second), f32(w_up),
        f32(b_up), f32(w_down), f32(b_down),
    ]
    return tuple(
        pl.pallas_call(
            finish_kernel,
            out_shape=finals,
            in_specs=[hbm] * 3 + [vmem] + [hbm] * 5,
            out_specs=[vmem if len(v.shape) == 1 else hbm for v in finals],
            scratch_shapes=[pltpu.VMEM(v.shape, v.dtype) for v in outs[:3] + outs[4:]]
            + [pltpu.VMEM(finals[k].shape, F32) for k in (3, 7, 8, 12, 14)]
            + [pltpu.SemaphoreType.DMA((24,))],
            compiler_params=pltpu.CompilerParams(vmem_limit_bytes=VMEM_LIMIT),
        )(*parts)
    )


def solution(mesh):
    in_specs = (
        P(("dp", "fsdp")),
        P(("dp", "fsdp"), None),
        P(("dp", "fsdp"), None),
        P(("dp", "fsdp")),
        P("fsdp", None),
        P("fsdp", None),
        P("fsdp"),
        P("fsdp"),
        P("fsdp"),
        P("fsdp", None),
        P("fsdp", None),
        P("fsdp"),
        P("fsdp"),
        P("fsdp"),
        P("fsdp", None),
        P("fsdp"),
        P("fsdp", None),
        P("fsdp"),
        P(("dp", "fsdp"), None),
    )
    out_specs = (
        P(("dp", "fsdp"), None),
        P(("dp", "fsdp"), None),
        P("fsdp", None),
        P("fsdp", None),
        P("fsdp"),
        P("fsdp"),
        P("fsdp"),
        P("fsdp", None),
        P("fsdp", None),
        P("fsdp"),
        P("fsdp"),
        P("fsdp"),
        P("fsdp", None),
        P("fsdp"),
        P("fsdp", None),
        P("fsdp"),
    )
    fused = mesh.shape["dp"] == 2 and mesh.shape["fsdp"] == 16
    body = fused_shards if fused else shards
    return jax.shard_map(body, mesh=mesh, in_specs=in_specs, out_specs=out_specs, check_vma=False)
```

```python
import jax
import jax.numpy as jnp
from jax import lax
from jax.experimental import pallas as pl
from jax.experimental.pallas import tpu as pltpu
from jax.sharding import PartitionSpec as P

HEADS = 16
VOCAB = 32000


norm_eps = 1e-05


def standardize(resid):
    centred = resid - jnp.mean(resid, axis=-1, keepdims=True)
    spread = jnp.mean(centred * centred, axis=-1, keepdims=True)
    return centred * lax.rsqrt(spread + norm_eps)


def row_normalize(tok_rows):
    return tok_rows * lax.rsqrt(jnp.mean(tok_rows * tok_rows, axis=1, keepdims=True) + norm_eps)


def exact_gelu(pre_act):
    return jax.nn.gelu(pre_act, approximate=False)


def split_heads(projected):
    tok_count = projected.shape[0]
    width = projected.shape[1] // 3
    head_size = width // HEADS
    key_heads = projected[:, width : 2 * width].reshape(tok_count, HEADS, head_size)
    value_heads = projected[:, 2 * width :].reshape(tok_count, HEADS, head_size)
    row_block = min(512, tok_count)
    query_blocks = projected[:, :width].reshape(tok_count // row_block, row_block, HEADS, head_size)
    return (query_blocks, key_heads, value_heads, row_block)


def block_scores(query_block, key_heads, seg_block, segment):
    raw_scores = (
        jnp.einsum("qhd,khd->hqk", query_block, key_heads, preferred_element_type=jnp.float32)
        * 0.125
    )
    same_seq = seg_block[:, None] == segment[None, :]
    return jnp.where(same_seq[None, :, :], raw_scores, -1000000000.0)


def attention_forward(projected, segment):
    query_blocks, key_heads, value_heads, row_block = split_heads(projected)
    seg_blocks = segment.reshape(-1, row_block)

    def block_step(items_in):
        query_block, seg_block = items_in
        scores = block_scores(query_block, key_heads, seg_block, segment)
        row_max = jnp.max(scores, axis=-1, keepdims=True)
        exp_scores = jnp.exp(scores - row_max)
        row_total = jnp.sum(exp_scores, axis=-1, keepdims=True)
        soft_probs = (exp_scores / row_total).astype(jnp.bfloat16)
        attended = jnp.einsum(
            "hqk,khd->qhd", soft_probs, value_heads, preferred_element_type=jnp.float32
        )
        return (attended, (row_max + jnp.log(row_total))[:, :, 0])

    attended, log_total = lax.map(block_step, (query_blocks, seg_blocks))
    return (attended.reshape(projected.shape[0], -1), log_total)


def attention_backward(projected, segment, log_total, grad_attended):
    query_blocks, key_heads, value_heads, row_block = split_heads(projected)
    seg_blocks = segment.reshape(-1, row_block)
    grad_blocks = grad_attended.reshape(query_blocks.shape)

    def block_step(totals, items_in):
        grad_keys, grad_values = totals
        query_block, seg_block, log_block, grad_block = items_in
        scores = block_scores(query_block, key_heads, seg_block, segment)
        soft_probs = jnp.exp(scores - log_block[:, :, None])
        grad_values = grad_values + jnp.einsum(
            "hqk,qhd->khd",
            soft_probs.astype(jnp.bfloat16),
            grad_block,
            preferred_element_type=jnp.float32,
        )
        grad_probs = jnp.einsum(
            "qhd,khd->hqk", grad_block, value_heads, preferred_element_type=jnp.float32
        )
        grad_scores = soft_probs * (
            grad_probs - jnp.sum(grad_probs * soft_probs, axis=-1, keepdims=True)
        )
        scaled_grad = (grad_scores * 0.125).astype(jnp.bfloat16)
        grad_query = jnp.einsum(
            "hqk,khd->qhd", scaled_grad, key_heads, preferred_element_type=jnp.float32
        )
        grad_keys = grad_keys + jnp.einsum(
            "hqk,qhd->khd", scaled_grad, query_block, preferred_element_type=jnp.float32
        )
        return ((grad_keys, grad_values), grad_query.astype(jnp.bfloat16))

    zero_heads = jnp.zeros(key_heads.shape, jnp.float32)
    (grad_keys, grad_values), grad_queries = lax.scan(
        block_step, (zero_heads, zero_heads), (query_blocks, seg_blocks, log_total, grad_blocks)
    )
    tok_count = projected.shape[0]
    return jnp.concatenate(
        [
            grad_queries.reshape(tok_count, -1),
            grad_keys.astype(jnp.bfloat16).reshape(tok_count, -1),
            grad_values.astype(jnp.bfloat16).reshape(tok_count, -1),
        ],
        axis=1,
    )


def shards(
    token_ids,
    seq_lengths,
    noise,
    noise_level,
    table,
    w_in,
    b_in,
    gain_first,
    shift_first,
    w_qkv,
    w_out,
    b_out,
    gain_second,
    shift_second,
    w_up,
    b_up,
    w_down,
    b_down,
    cotangent,
):
    tok_count = token_ids.shape[0]
    row_count = table.shape[0]
    group_ids = lax.all_gather(token_ids, "fsdp", axis=0, tiled=True)
    first_row = lax.axis_index("fsdp") * row_count
    owned = (group_ids[:, None] == first_row + jnp.arange(row_count)[None, :]).astype(jnp.bfloat16)
    owned_rows = jnp.dot(owned, table, preferred_element_type=jnp.float32).astype(jnp.bfloat16)
    tok_rows = lax.psum_scatter(owned_rows, "fsdp", scatter_dimension=0, tiled=True)
    tok_rows = tok_rows.astype(jnp.float32)
    vectors = (b_in, gain_first, shift_first, b_out, gain_second, shift_second, b_up, b_down)
    vec_all = lax.all_gather(jnp.concatenate(vectors), "fsdp", axis=0, tiled=False)
    vec_at = [0]
    for vector in vectors:
        vec_at.append(vec_at[-1] + vector.shape[0])
    (
        b_in_all,
        gain_first_all,
        shift_first_all,
        b_out_all,
        gain_second_all,
        shift_second_all,
        b_up_all,
        b_down_all,
    ) = [vec_all[:, lo:hi].reshape(-1) for lo, hi in zip(vec_at[:-1], vec_at[1:])]
    w_in_all = lax.all_gather(w_in, "fsdp", axis=0, tiled=True)
    w_qkv_all = lax.all_gather(w_qkv, "fsdp", axis=0, tiled=True)
    w_out_all = lax.all_gather(w_out, "fsdp", axis=0, tiled=True)
    w_up_all = lax.all_gather(w_up, "fsdp", axis=0, tiled=True)
    w_down_all = lax.all_gather(w_down, "fsdp", axis=0, tiled=True)
    seq_ends = jnp.cumsum(seq_lengths[0], dtype=jnp.int32)
    positions = jnp.arange(tok_count, dtype=jnp.int32)
    segment = jnp.sum((positions[:, None] >= seq_ends[None, :]).astype(jnp.int32), axis=1)
    live_rows = (segment < seq_lengths.shape[1]).astype(jnp.float32)[:, None]
    embedded = row_normalize(tok_rows)
    scale_in = lax.rsqrt(1.0 + noise_level * noise_level)[:, None]
    scaled = ((embedded + noise_level[:, None] * noise.astype(jnp.float32)) * scale_in).astype(
        jnp.bfloat16
    )
    resid_in = jnp.dot(scaled, w_in_all, preferred_element_type=jnp.float32) + b_in_all.astype(
        jnp.float32
    )
    std_first, first_pull = jax.vjp(standardize, resid_in)
    normed_a = (
        std_first * gain_first_all.astype(jnp.float32) + shift_first_all.astype(jnp.float32)
    ).astype(jnp.bfloat16)
    projected = jnp.dot(normed_a, w_qkv_all, preferred_element_type=jnp.float32).astype(
        jnp.bfloat16
    )
    attended, log_total = attention_forward(projected, segment)
    attended = attended.astype(jnp.bfloat16)
    resid_mid = (
        resid_in
        + jnp.dot(attended, w_out_all, preferred_element_type=jnp.float32)
        + b_out_all.astype(jnp.float32)
    )
    std_second, second_pull = jax.vjp(standardize, resid_mid)
    normed_b = (
        std_second * gain_second_all.astype(jnp.float32) + shift_second_all.astype(jnp.float32)
    ).astype(jnp.bfloat16)
    pre_act = jnp.dot(normed_b, w_up_all, preferred_element_type=jnp.float32) + b_up_all.astype(
        jnp.float32
    )
    activated, gelu_pull = jax.vjp(exact_gelu, pre_act)
    hidden = activated.astype(jnp.bfloat16)
    resid_out = (
        resid_mid
        + jnp.dot(hidden, w_down_all, preferred_element_type=jnp.float32)
        + b_down_all.astype(jnp.float32)
    )
    activations = (resid_out * live_rows).astype(jnp.bfloat16)
    grad_out = cotangent.astype(jnp.float32) * live_rows
    grad_down = grad_out.astype(jnp.bfloat16)
    b_down_term = jnp.sum(grad_down.astype(jnp.float32), axis=0)
    w_down_term = jnp.einsum("tf,td->fd", hidden, grad_down, preferred_element_type=jnp.float32)
    grad_hidden = jnp.einsum("td,fd->tf", grad_down, w_down_all, preferred_element_type=jnp.float32)
    grad_act = gelu_pull(grad_hidden)[0].astype(jnp.bfloat16)
    b_up_term = jnp.sum(grad_act.astype(jnp.float32), axis=0)
    w_up_term = jnp.einsum("td,tf->df", normed_b, grad_act, preferred_element_type=jnp.float32)
    grad_nb = jnp.einsum("tf,df->td", grad_act, w_up_all, preferred_element_type=jnp.float32)
    gain_second_term = jnp.sum(grad_nb * std_second, axis=0)
    shift_second_term = jnp.sum(grad_nb, axis=0)
    grad_mid = grad_out + second_pull(grad_nb * gain_second_all.astype(jnp.float32))[0]
    grad_att = grad_mid.astype(jnp.bfloat16)
    b_out_term = jnp.sum(grad_att.astype(jnp.float32), axis=0)
    w_out_term = jnp.einsum("tc,td->cd", attended, grad_att, preferred_element_type=jnp.float32)
    grad_attended = jnp.einsum(
        "td,cd->tc", grad_att, w_out_all, preferred_element_type=jnp.float32
    ).astype(jnp.bfloat16)
    grad_proj = attention_backward(projected, segment, log_total, grad_attended)
    w_qkv_term = jnp.einsum("td,te->de", normed_a, grad_proj, preferred_element_type=jnp.float32)
    grad_na = jnp.einsum("te,de->td", grad_proj, w_qkv_all, preferred_element_type=jnp.float32)
    gain_first_term = jnp.sum(grad_na * std_first, axis=0)
    shift_first_term = jnp.sum(grad_na, axis=0)
    grad_in = grad_mid + first_pull(grad_na * gain_first_all.astype(jnp.float32))[0]
    grad_pin = grad_in.astype(jnp.bfloat16)
    b_in_term = jnp.sum(grad_pin.astype(jnp.float32), axis=0)
    w_in_term = jnp.einsum("te,td->ed", scaled, grad_pin, preferred_element_type=jnp.float32)
    grad_scaled = jnp.einsum("td,ed->te", grad_pin, w_in_all, preferred_element_type=jnp.float32)
    noise_grad = grad_scaled * noise_level[:, None] * scale_in
    grad_embedded = grad_scaled * scale_in
    all_ids = lax.all_gather(token_ids, ("dp", "fsdp"), axis=0, tiled=True)
    all_grads = lax.all_gather(
        grad_embedded.astype(jnp.bfloat16), ("dp", "fsdp"), axis=0, tiled=True
    )
    owners = (first_row + jnp.arange(row_count)[:, None] == all_ids[None, :]).astype(jnp.bfloat16)
    row_grad = jnp.dot(owners, all_grads, preferred_element_type=jnp.float32)
    own_table = table.astype(jnp.float32)
    unused_rows, table_pull = jax.vjp(row_normalize, own_table)
    table_part = table_pull(row_grad)[0]

    def reduce_matrix(term):
        part = lax.psum_scatter(
            term.astype(jnp.bfloat16), "fsdp", scatter_dimension=0, tiled=True
        )
        return lax.psum(part, "dp").astype(jnp.float32)

    vec_terms = (
        b_in_term,
        gain_first_term,
        shift_first_term,
        b_out_term,
        gain_second_term,
        shift_second_term,
        b_up_term,
        b_down_term,
    )
    shard_count = lax.axis_size("fsdp")
    vec_term = jnp.concatenate([v.reshape(shard_count, -1) for v in vec_terms], axis=1)
    vec_part = lax.psum(vec_term, ("dp", "fsdp"))
    own_vec = lax.dynamic_index_in_dim(vec_part, lax.axis_index("fsdp"), 0, keepdims=False)
    vec_grads = [own_vec[lo:hi] for lo, hi in zip(vec_at[:-1], vec_at[1:])]
    return (
        activations,
        noise_grad,
        table_part,
        reduce_matrix(w_in_term),
        vec_grads[0],
        vec_grads[1],
        vec_grads[2],
        reduce_matrix(w_qkv_term),
        reduce_matrix(w_out_term),
        vec_grads[3],
        vec_grads[4],
        vec_grads[5],
        reduce_matrix(w_up_term),
        vec_grads[6],
        reduce_matrix(w_down_term),
        vec_grads[7],
    )


BF = jnp.bfloat16
F32 = jnp.float32
MESH_ID = pl.DeviceIdType.MESH
SEM_COUNT = 400
ROW_UNROLL = 8
HEAD_UNROLL = 4
EACH_UNROLL = 4
VMEM_LIMIT = 63 * 2**20
NT = (((1,), (1,)), ((), ()))
TN = (((0,), (0,)), ((), ()))
DIAG, ACROSS, TWIN = 0, 1, 2
FLIPS = ((1, 1), (1, 0), (0, 1))


def mm(a, b):
    return jnp.dot(a, b, preferred_element_type=F32)


def mm_nt(a, b):
    return lax.dot_general(a, b, NT, preferred_element_type=F32)


def mm_tn(a, b):
    return lax.dot_general(a, b, TN, preferred_element_type=F32)


def part(start, size):
    return pl.ds(pl.multiple_of(start, size), size)


def as_row(pair):
    return jnp.concatenate([pair[0:1, :], pair[1:2, :]], axis=1)


def as_col(pair):
    eye = lax.broadcasted_iota(jnp.int32, (128, 128), 0) == lax.broadcasted_iota(
        jnp.int32, (128, 128), 1
    )
    cols = [
        jnp.sum(jnp.where(eye, pair[k : k + 1, :], 0.0), axis=1, keepdims=True) for k in (0, 1)
    ]
    return jnp.concatenate(cols, axis=0)


def norm_parts(v):
    centred = v - jnp.mean(v, axis=-1, keepdims=True)
    rstd = lax.rsqrt(jnp.mean(centred * centred, axis=-1, keepdims=True) + norm_eps)
    return centred * rstd, rstd


def norm_back(u, n, rstd):
    return rstd * (
        u - jnp.mean(u, axis=-1, keepdims=True) - n * jnp.mean(u * n, axis=-1, keepdims=True)
    )


def layer_kernel(
    ids_hbm, lengths_hbm, level_hbm, b_in_hbm, gain_a_hbm, shift_a_hbm, b_out_hbm, gain_b_hbm, shift_b_hbm,
    b_dn_hbm, b_up_hbm, noise_hbm, table, w_in_hbm, w_qkv_hbm, w_out_hbm, w_up_hbm, w_down_hbm, cot_hbm,
    act_hbm, ngrad_hbm, tgrad_hbm, vout_hbm, f_in_hbm, f_qkv_hbm, f_out_hbm, f_up_hbm, f_dn_hbm,
    ids_v, lengths_v, level_v, b_in_v, gain_a_v, shift_a_v, b_out_v, gain_b_v, shift_b_v, b_dn_v, b_up_v,
    small, noise, w_in, w_qkv, w_out, w_up, w_down, cot,
    act, ngrad, tgrad, vout, f_in, f_qkv, f_out, f_up, f_dn,
    sm, smx, gsm, vec, vg, vq, vgy, vgz, vgf, bup, lives, idr,
    tp, tok, sc, win, wqkv, wout, wup, wdn, s_in, s_qkv, s_out, s_up,
    rin, rmid, gmid, t1, t2, t3, t4, na, proj, pr, att, asend, nb, gd, hid, ga,
    xs, xr, gatt, go, g_in, g_qkv, g_out, g_dn,
    y_in, y_qkv, y_out, y_up, y_dn, z_in, z_qkv, z_out, z_up, z_dn,
    ss, rr, ls,
):
    x = lax.axis_index("dp")
    f = lax.axis_index("fsdp")
    z, y, c = f // 4, lax.rem(f // 2, 2), lax.rem(f, 2)
    q = 2 * z + y
    g = 2 * x + c
    rows_here = table.shape[0]

    def dev(dx, dz, dy, dc):
        xx = lax.rem(x + dx, 2)
        zz = lax.rem(z + dz, 4)
        yy = lax.rem(y + dy, 2)
        cc = lax.rem(c + dc, 2)
        return (xx, zz * 4 + yy * 2 + cc)

    twin = dev(0, 0, 0, 1)
    across = dev(1, 0, 0, 0)
    pair_y = dev(0, 0, 1, 0)
    relay_to = (x, jnp.where(z == 2, 3, 0) * 4 + y * 2 + c)
    rel_dev = [dev(dx, 0, 0, dc) for dx, dc in FLIPS]
    rel_g = [2 * lax.rem(x + dx, 2) + lax.rem(c + dc, 2) for dx, dc in FLIPS]
    other_c = 1 - c

    def far(d):
        return lax.rem(z + 4 - d, 4)

    def to(d):
        return lax.rem(z + d, 4)

    sems = [0]
    pending = []
    inner = jnp.logical_or(z == 1, z == 2)
    outer = jnp.logical_not(inner)

    class Link:
        def __init__(self):
            self.at = sems[0]
            sems[0] += 1
            assert sems[0] <= SEM_COUNT

        def send(self, src, dst, device, arrives=None, only=None):
            self.only = only
            self.copy = pltpu.make_async_remote_copy(
                src_ref=src, dst_ref=dst, send_sem=ss.at[self.at],
                recv_sem=rr.at[self.at if arrives is None else arrives],
                device_id=device, device_id_type=MESH_ID,
            )
            if only is None:
                self.copy.start()
            else:
                pl.when(only)(self.copy.start)
            pending.append(self)
            return self

        def sent(self):
            pending.remove(self)
            if self.only is None:
                self.copy.wait_send()
            else:
                pl.when(self.only)(self.copy.wait_send)

        def got(self, ref):
            arrived(self.at, ref)

    def arrived(at, ref):
        pltpu.make_async_remote_copy(
            src_ref=ref, dst_ref=ref, send_sem=ss.at[0], recv_sem=rr.at[at],
            device_id=twin, device_id_type=MESH_ID,
        ).wait_recv()

    def each_rows(count, size, body):
        def step(i, carry):
            body(part(i * size, size))
            return carry

        lax.fori_loop(0, count // size, step, 0, unroll=ROW_UNROLL)

    def each(count, body, unroll=EACH_UNROLL):
        def step(i, carry):
            body(i)
            return carry

        lax.fori_loop(0, count, step, 0, unroll=unroll)

    local = [0]
    stores = []

    def moved(src, dst):
        copy = pltpu.make_async_copy(src, dst, ls.at[local[0]])
        local[0] += 1
        copy.start()
        return copy

    vectors = (b_in_v, gain_a_v, shift_a_v, b_out_v, gain_b_v, shift_b_v, b_dn_v)
    load_small = [
        moved(src, dst)
        for src, dst in (
            (ids_hbm, ids_v), (lengths_hbm, lengths_v), (level_hbm, level_v), (b_in_hbm, b_in_v),
            (gain_a_hbm, gain_a_v), (shift_a_hbm, shift_a_v), (b_out_hbm, b_out_v),
            (gain_b_hbm, gain_b_v), (shift_b_hbm, shift_b_v), (b_dn_hbm, b_dn_v), (b_up_hbm, b_up_v),
        )
    ]
    load_in = moved(w_in_hbm, w_in)
    load_qkv = moved(w_qkv_hbm, w_qkv)
    load_cot = moved(cot_hbm, cot)
    own_table = moved(table, tp.at[c, pl.ds(0, rows_here)])
    load_noise = moved(noise_hbm, noise)
    load_out = moved(w_out_hbm, w_out)
    load_up = moved(w_up_hbm, w_up)
    load_down = moved(w_down_hbm, w_down)

    barrier = pltpu.get_barrier_semaphore()
    peers = [dev(0, d, 0, dc) for d in (1, 2, 3) for dc in (0, 1)] + rel_dev + [pair_y]
    for peer in peers:
        pl.semaphore_signal(barrier, inc=1, device_id=peer, device_id_type=MESH_ID)
    pl.semaphore_wait(barrier, len(peers))

    class GroupGather:
        def __init__(self, at):
            self.at = at
            self.across = Link().send(at(g), at(g), across)
            self.twin = Link().send(at(g), at(g), twin)

        def hop(self):
            self.across.got(self.at(rel_g[ACROSS]))
            self.second = Link().send(self.at(rel_g[ACROSS]), self.at(rel_g[ACROSS]), twin)

        def got_twin(self):
            self.twin.got(self.at(rel_g[TWIN]))

        def got_diag(self):
            self.second.got(self.at(rel_g[DIAG]))

    class Gather:
        def __init__(self, whole, mine, theirs, height, twins=None, relay=True):
            self.whole, self.height, self.relay = whole, height, relay
            places = (self.sub(q, c), self.sub(q, c, twins))
            self.links = {}
            for d in (0, 2, 1, 3):
                only = {1: z != 3, 3: z != 0}.get(d) if relay else None
                for dc in (1, 0):
                    if (d, dc) != (0, 0):
                        self.links[d, dc] = Link().send(
                            theirs if dc else mine, places[dc], dev(0, d, 0, dc), only=only
                        )

        def sub(self, block, core, whole=None):
            whole = self.whole if whole is None else whole
            if self.height is None:
                return whole.at[block, core]
            return whole.at[block, part(core * self.height, self.height)]

        def over_y(self, block):
            return Link().send(self.whole.at[block], self.whole.at[block], pair_y)

        def own(self):
            self.links[0, 1].got(self.sub(q, other_c))
            self.y_own = self.over_y(q)

        def second(self):
            block = 2 * far(2) + y
            for dc in (1, 0):
                ref = self.sub(block, other_c if dc else c)
                self.links[2, dc].got(ref)
                if self.relay:
                    Link().send(
                        ref, ref, relay_to, only=inner,
                        arrives=jnp.where(z == 2, self.links[3, dc].at, self.links[1, dc].at),
                    )
            self.y_second = self.over_y(block)

        def near(self):
            self.y_near = self.one(3, 1)

        def last(self):
            self.y_last = self.one(1, 3)

        def one(self, low, high):
            block = 2 * jnp.where(z < 2, far(low), far(high)) + y
            for dc in (1, 0):
                arrived(
                    jnp.where(z < 2, self.links[low, dc].at, self.links[high, dc].at),
                    self.sub(block, other_c if dc else c),
                )
            return self.over_y(block)

        def forward(self):
            self.second()
            self.near()
            self.last()

        def finish(self):
            self.y_own.got(self.whole.at[2 * z + 1 - y])
            self.y_second.got(self.whole.at[2 * far(2) + 1 - y])
            self.y_near.got(self.whole.at[2 * jnp.where(z < 2, far(3), far(1)) + 1 - y])
            self.y_last.got(self.whole.at[2 * jnp.where(z < 2, far(1), far(3)) + 1 - y])

    class YFirstGather(Gather):
        def __init__(self, whole, mine, theirs, height):
            self.whole, self.height, self.relay = whole, height, True
            self.y_links = [
                Link().send(theirs if dc else mine, self.sub(q, c), dev(0, 0, 1, dc)) for dc in (0, 1)
            ]
            self.mine, self.theirs = mine, theirs

        def along(self):
            Gather.__init__(self, self.whole, self.mine, self.theirs, self.height)

        def cross(self):
            block = 2 * z + 1 - y
            for dc in (0, 1):
                self.y_links[dc].got(self.sub(block, other_c if dc else c))
            ref = self.whole.at[block]
            self.beside = {
                d: Link().send(ref, ref, dev(0, d, 0, 0), only={1: z != 3, 3: z != 0}.get(d))
                for d in (2, 1, 3)
            }

        def over_y(self, block):
            return None

        def second(self):
            Gather.second(self)
            ref = self.whole.at[2 * far(2) + 1 - y]
            self.beside[2].got(ref)
            Link().send(
                ref, ref, relay_to, only=inner,
                arrives=jnp.where(z == 2, self.beside[3].at, self.beside[1].at),
            )

        def finish(self):
            self.links[0, 1].got(self.sub(q, other_c))
            self.near()
            self.last()
            for d in (1, 3):
                self.beside[d].got(self.whole.at[2 * far(d) + 1 - y])

    for load in load_small:
        load.wait()
    lane_at = lax.broadcasted_iota(jnp.int32, (1, 128), 1)
    small[...] = jnp.zeros_like(small)

    def put_half(row, shard):
        small[row : row + 1, :] = jnp.where(
            lane_at // 64 == c, jnp.concatenate([shard, shard], axis=1), 0.0
        )

    def put_pair(row, line):
        small[row : row + 1, :] = line[:, 0:128]
        small[row + 1 : row + 2, :] = line[:, 128:256]

    for k, v in enumerate(vectors):
        put_half(k, v[...].astype(F32).reshape(1, 64))
    up_shard = b_up_v[...].astype(F32).reshape(1, 256)
    for k in range(4):
        put_half(7 + k, up_shard[:, 64 * k : 64 * k + 64])
    put_pair(16, ids_v[...].astype(F32).reshape(1, 256))
    put_pair(20, level_v[...].reshape(1, 256))
    lengths = lengths_v[...].astype(F32)
    slot_at = lax.broadcasted_iota(jnp.int32, lengths.shape, 1)
    spots = (
        lax.broadcasted_iota(jnp.int32, (2, 128), 0) * 128
        + lax.broadcasted_iota(jnp.int32, (2, 128), 1)
    ).astype(F32)
    slot_of = jnp.zeros((2, 128), F32)
    for k in range(8):
        end = jnp.sum(jnp.where(slot_at <= k, lengths, 0.0), axis=1, keepdims=True)
        slot_of += jnp.where(spots >= end, 1.0, 0.0)
    small[18:20, :] = slot_of
    sm[q, c] = small[...]
    small_links = [Link().send(small, gsm.at[rel], rel_dev[rel]) for rel in (DIAG, ACROSS)]
    gather_small = Gather(sm, small, small, None, relay=False)

    own_rows = tp.at[c, pl.ds(0, rows_here)]
    table_link = Link().send(table, own_rows, twin)
    spare = tp.shape[1] - rows_here
    if spare:
        for core in (0, 1):
            tp[core, pl.ds(rows_here, spare), :] = jnp.zeros((spare, tp.shape[2]), BF)

    def pack(whole, spare_buf, height, pick):
        mine, theirs = pick(g), pick(2 * x + other_c)
        whole[q, part(c * height, height), :] = mine
        spare_buf[...] = theirs

    h = w_qkv.shape[0]
    hin = w_in.shape[0]

    def cols(ref, start, size=256):
        return ref[:, part(start, size)]

    win_at, wout_at = win.at[g], wout.at[g]
    load_in.wait()
    load_qkv.wait()
    win_at[q, c] = cols(w_in, 256 * g)
    s_in[0] = cols(w_in, 256 * (2 * x + other_c))
    gather_in = Gather(win_at, win_at.at[q, c], s_in.at[0], None, win.at[2 * x + other_c], relay=False)
    pack(
        wqkv, s_qkv, h,
        lambda k: jnp.concatenate([cols(w_qkv, 1024 * n + 256 * k) for n in (0, 1, 2)], axis=1),
    )
    gather_qkv = Gather(wqkv, wqkv.at[q, part(c * h, h)], s_qkv, h)


    lives[:, 0:1] = jnp.where(as_col(small[18:20, :]) < 7.5, 1.0, 0.0)
    vg[...] = jnp.zeros_like(vg)

    def grad_down_rows(at):
        masked = cot[at, :].astype(F32) * lives[at, 0:1]
        gd[g, at, :] = masked.astype(BF)
        vg[6:7, :] += jnp.sum(masked, axis=0, keepdims=True)

    load_out.wait()
    pack(wout_at, s_out, h, lambda k: cols(w_out, 256 * k))
    gather_out = Gather(
        wout_at, wout_at.at[q, part(c * h, h)], s_out, h, wout.at[2 * x + other_c], relay=False
    )
    load_cot.wait()
    each_rows(256, 32, grad_down_rows)
    group_gd = GroupGather(lambda k: gd.at[k])

    gather_small.own()
    gather_small.forward()

    gather_in.own()
    gather_qkv.own()
    gather_small.finish()
    smx_link = Link().send(sm, smx, across)
    own_table.wait()
    table_link.got(tp.at[other_c, pl.ds(0, rows_here)])
    lane = lax.broadcasted_iota(jnp.int32, (256, tp.shape[1]), 1)

    def look_up(block):
        ids = as_col(sm[block, c, 16:18, :]).astype(jnp.int32)
        total = jnp.zeros((256, 256), F32)
        for core in (0, 1):
            first = (4 * z + 2 * y + core) * rows_here
            hit = jnp.where(lane == ids - first, 1.0, 0.0).astype(BF)
            total += mm(hit, tp[core])
        return total.astype(BF)

    emb_y = [Link() for _ in range(4)]
    for d in range(4):
        tok[d] = look_up(2 * to(d) + 1 - y)
        emb_y[d].send(tok.at[d], tok.at[8 + d], pair_y)

    load_down.wait()
    wdn[q, part(c * h, h), :] = w_down[part(g * h, h), :]
    gather_dn_y = YFirstGather(
        wdn.at[:, :, 512:1024], w_down.at[part(g * h, h), 512:1024],
        w_down.at[part((2 * x + other_c) * h, h), 512:1024], h,
    )

    def own_blocks(d):
        tok[4 + d] = look_up(2 * lax.rem(z + d, 4) + y)

    each(4, own_blocks)
    emb_z = [None]
    for d in (1, 2, 3):
        emb_y[d].got(tok.at[8 + d])
        tok[4 + d] = tok[4 + d] + tok[8 + d]
        emb_z.append(Link().send(tok.at[4 + d], tok.at[11 + d], dev(0, d, 0, 0)))
    emb_y[0].got(tok.at[8])

    for load in (load_noise, load_up):
        load.wait()
    ct = lax.broadcasted_iota(jnp.int32, (h, 128), 1) < 64
    for j in range(8):
        first = w_up[:, part(128 * (4 * j + x), 128)].astype(F32)
        second = w_up[:, part(128 * (4 * j + 2 + x), 128)].astype(F32)
        low = jnp.where(ct, first, pltpu.roll(second, 64, 1)).astype(BF)
        high = jnp.where(ct, pltpu.roll(first, 64, 1), second).astype(BF)
        wup[q, part(c * h, h), 128 * j : 128 * j + 128] = jnp.where(c == 0, low, high)
        s_up[:, 128 * j : 128 * j + 128] = jnp.where(c == 0, high, low)
    gather_in.forward()
    gather_qkv.forward()
    for j in range(8):
        vec[:, 128 * j : 128 * j + 128] = sm[j, 0, 0:16, :] + sm[j, 1, 0:16, :]

    gather_out.own()
    gather_out.forward()
    gather_in.finish()
    group_in = GroupGather(lambda k: win.at[k])
    group_gd.hop()
    rows_sum = tok[4].astype(F32) + tok[8].astype(F32)
    for d in (1, 2, 3):
        emb_z[d].got(tok.at[11 + d])
        rows_sum += tok[11 + d].astype(F32)
    gather_up = Gather(wup, wup.at[q, part(c * h, h)], s_up, h)
    level = as_col(small[20:22, :])
    scale_in = lax.rsqrt(1.0 + level * level)
    embedded = rows_sum * lax.rsqrt(jnp.mean(rows_sum * rows_sum, axis=1, keepdims=True) + norm_eps)
    sc[g] = ((embedded + level * noise[...].astype(F32)) * scale_in).astype(BF)
    group_sc = GroupGather(lambda k: sc.at[k])

    group_in.hop()
    group_in.got_twin()
    group_in.got_diag()

    def win_mat(k):
        return win[k].reshape(256, 256)

    def first_norm(row, keep):
        for k in range(4):
            keep[:, 256 * k : 256 * k + 256] = (
                mm(sc[row], win_mat(k)) + vec[0:1, 256 * k : 256 * k + 256]
            )

        def chunk(at):
            n, _ = norm_parts(keep[at, :])
            na[row, at, :] = (n * vec[1:2, :] + vec[2:3, :]).astype(BF)

        each_rows(256, 32, chunk)

    def project(row):
        def block(k):
            at = part(k * 256, 256)
            proj[row, :, at] = mm(na[row], wqkv[:, :, at].reshape(1024, 256)).astype(BF)

        each(3, block)

    first_norm(g, rin)
    group_sc.hop()
    gather_up.own()
    group_sc.got_twin()
    first_norm(rel_g[TWIN], t1)
    first_norm(rel_g[ACROSS], t1)
    group_sc.got_diag()
    first_norm(rel_g[DIAG], t1)
    gather_qkv.finish()
    for rel in range(3):
        project(rel_g[rel])
    project(g)
    gather_out.finish()
    group_out = GroupGather(lambda k: wout.at[k])

    head_of = lax.broadcasted_iota(jnp.int32, (1, 256), 1) // 64
    small_links[DIAG].got(gsm.at[DIAG])
    small_links[ACROSS].got(gsm.at[ACROSS])

    def attend(row, pair):
        same = as_col(pair) == as_row(pair)
        keys = proj[row, :, 256:512]
        values = proj[row, :, 512:768]
        queries = proj[row, :, 0:256]
        t2[...] = jnp.zeros_like(t2)

        def head(k):
            mine = head_of == k
            q_head = jnp.where(mine, queries, jnp.zeros_like(queries))
            scores = jnp.where(same, mm_nt(q_head, keys) * 0.125, -1e9)
            weights = jnp.exp(scores - jnp.max(scores, axis=-1, keepdims=True))
            low_probs = (weights / jnp.sum(weights, axis=-1, keepdims=True)).astype(BF)
            pr[row * 4 + k] = low_probs
            t2[...] += mm(low_probs, jnp.where(mine, values, jnp.zeros_like(values)))

        each(4, head, HEAD_UNROLL)
        return t2[...].astype(BF)

    att_links = []
    my_cols = part(256 * g, 256)
    for rel in range(3):
        pair = sm[q, other_c, 18:20, :] if rel == TWIN else gsm[rel, 18:20, :]
        asend[rel] = attend(rel_g[rel], pair)
        att_links.append(Link().send(asend.at[rel], att.at[:, my_cols], rel_dev[rel]))
        if rel == DIAG:
            gather_up.second()
            for d in range(4):
                emb_y[d].sent()
            for d in (1, 2, 3):
                emb_z[d].sent()
            gather_dn = Gather(
                wdn.at[:, :, 0:512], w_down.at[part(g * h, h), 0:512],
                w_down.at[part((2 * x + other_c) * h, h), 0:512], h,
            )
            gather_dn_y.along()
        if rel == ACROSS:
            gather_dn_y.cross()
    att[:, my_cols] = attend(g, small[18:20, :])
    gather_dn.own()
    group_out.hop()
    gather_up.near()
    gather_up.last()
    group_out.got_twin()
    group_out.got_diag()
    for rel in (TWIN, ACROSS, DIAG):
        att_links[rel].got(att.at[:, part(256 * rel_g[rel], 256)])

    def out_block(k):
        at = part(k * 256, 256)
        rmid[:, at] = rin[:, at] + mm(att[...], wout[k].reshape(1024, 256)) + vec[3:4, at]

    each(4, out_block)

    def second_norm(at):
        n, _ = norm_parts(rmid[at, :])
        nb[g, at, :] = (n * vec[4:5, :] + vec[5:6, :]).astype(BF)

    each_rows(256, 32, second_norm)
    nb_across = Link().send(nb.at[g], nb.at[g], across)
    nb_twin = Link().send(nb.at[g], nb.at[g], twin)
    nb_pass = Link()
    group_gd.got_twin()
    group_gd.got_diag()

    bup[...] = jnp.zeros_like(bup)
    for k in range(4):
        bup[0:1, :] += jnp.where(g == k, vec[7 + k : 8 + k, :], 0.0)

    def ff_hidden(row):
        def block(k):
            at = part(k * 256, 256)
            t2[...] = mm(nb[row], wup[:, :, at].reshape(1024, 256)) + bup[0:1, at]

            def chunk(rows_at):
                pre = t2[rows_at, :]
                cdf = 0.5 + 0.5 * lax.erf(pre * 0.7071067811865476)
                pdf = jnp.exp(-0.5 * pre * pre) * 0.3989422804014327
                t2[rows_at, :] = pre * cdf
                ga[row, rows_at, at] = (cdf + pre * pdf).astype(BF)

            each_rows(256, 32, chunk)
            hid[pl.ds(2 * row, 2), :, at] = t2[...].astype(BF).reshape(2, 128, 256)

        each(4, block)

    def ff_grad(row):
        def block(k):
            at = part(k * 256, 256)
            grad = mm_nt(gd[row], wdn[pl.ds(2 * k, 2)].reshape(256, 1024))
            ga_low = (grad * ga[row, :, at].astype(F32)).astype(BF)
            ga[row, :, at] = ga_low
            bup[1:2, at] += jnp.sum(ga_low.astype(F32), axis=0, keepdims=True)

        each(4, block)

    gather_dn.second()
    gather_up.finish()
    ff_hidden(g)
    gather_dn.near()
    gather_dn.last()
    gather_dn_y.second()
    nb_twin.got(nb.at[rel_g[TWIN]])
    ff_hidden(rel_g[TWIN])
    nb_across.got(nb.at[rel_g[ACROSS]])
    nb_pass.send(nb.at[rel_g[ACROSS]], nb.at[rel_g[ACROSS]], twin)
    ff_hidden(rel_g[ACROSS])
    nb_pass.got(nb.at[rel_g[DIAG]])
    ff_hidden(rel_g[DIAG])

    class GroupSum:
        def __init__(self, sends, gets, partial, puts=None, temp=None):
            self.sends, self.gets, self.partial = sends, gets, partial
            self.temp = t1 if temp is None else temp
            self.puts = gets if puts is None else puts

        def first(self):
            self.partial(rel_g[DIAG], self.sends[0])
            self.a = Link().send(self.sends[0], self.puts[0], twin)

        def second(self):
            self.partial(rel_g[ACROSS], self.temp)
            self.a.got(self.gets[0])

            def chunk(at):
                self.sends[1][at, :] = (
                    self.temp[at, :] + self.gets[0][at, :].astype(F32)
                ).astype(BF)

            each_rows(256, 32, chunk)

        def second_send(self):
            self.b = Link().send(self.sends[1], self.puts[1], across)

        def third(self):
            self.partial(rel_g[TWIN], self.sends[2])
            self.c = Link().send(self.sends[2], self.puts[2], twin)

        def own(self, into):
            self.partial(g, into)
            self.into = into

        def total(self):
            self.c.got(self.gets[2])
            self.b.got(self.gets[1])

        def rows(self, at):
            return (
                self.into[at, :].astype(F32)
                + self.gets[1][at, :].astype(F32)
                + self.gets[2][at, :].astype(F32)
            )

        def release(self):
            for link in (self.a, self.b, self.c):
                link.sent()

    def slots(ref, places):
        return [ref.at[place] for place in places]

    def nb_partial(row, into):
        def block(k):
            into[:, part(k * 256, 256)] = mm_nt(
                ga[row], wup[pl.ds(2 * k, 2)].reshape(256, 1024)
            ).astype(into.dtype)

        each(4, block)

    def out_partial(row, into):
        def block(k):
            at = part(k * 256, 256)
            into[:, at] = mm(
                hid[pl.ds(2 * row, 2)].reshape(256, 1024), wdn[:, :, at].reshape(1024, 256)
            ).astype(into.dtype)

        each(4, block)

    class Scatter:
        def __init__(self, grad, y_buf, z_buf, final, height):
            self.grad, self.y_buf, self.z_buf, self.final, self.height = (
                grad, y_buf, z_buf, final, height,
            )

        def chunks(self, body):
            if self.height is None:
                each(2, body)
            else:
                each_rows(2 * self.height, 32, body)

        def half(self, core):
            if self.height is None:
                return self.grad.at[q, core]
            return self.grad.at[q, part(core * self.height, self.height)]

        def start(self, count=4):
            even = lax.rem(z, 2) == 0
            self.goals = (
                jnp.where(even, 3, 0), jnp.where(even, 1, 2), lax.rem(z + 2, 4), z,
            )
            self.y_links = []
            self.z_links = [Link() for _ in range(4)]
            self.more(count)

        def more(self, count=1):
            for _ in range(count):
                e = len(self.y_links)
                self.y_links.append(
                    Link().send(self.grad.at[2 * self.goals[e] + 1 - y], self.y_buf.at[e], pair_y)
                )

        def add_y(self, e):
            self.y_links[e].got(self.y_buf.at[e])
            block = 2 * self.goals[e] + y

            def chunk(at):
                self.grad[block, at] = (
                    self.grad[block, at].astype(F32) + self.y_buf[e, at].astype(F32)
                ).astype(BF)

            self.chunks(chunk)
            return self.grad.at[block]

        def end_to_end(self):
            ref = self.add_y(0)
            self.z_links[0].send(
                ref, self.z_buf.at[0], (x, (z + 1 - 2 * lax.rem(z, 2)) * 4 + y * 2 + c)
            )

        def near(self):
            ref = self.add_y(1)
            slot = jnp.where(inner, 2, 1)
            self.z_links[1].send(
                ref, self.z_buf.at[slot], (x, self.goals[1] * 4 + y * 2 + c),
                arrives=jnp.where(inner, self.z_links[2].at, self.z_links[1].at),
            )

        def second(self):
            ref = self.add_y(2)
            block = 2 * self.goals[2] + y

            def relayed():
                self.z_links[0].got(self.z_buf.at[0])

                def chunk(at):
                    self.grad[block, at] = (
                        self.grad[block, at].astype(F32) + self.z_buf[0, at].astype(F32)
                    ).astype(BF)

                self.chunks(chunk)

            pl.when(inner)(relayed)
            self.z_links[3].send(ref, self.z_buf.at[3], dev(0, 2, 0, 0))

        def own(self):
            self.add_y(3)

        def middle(self):
            self.end_to_end()
            self.near()
            self.second()
            self.own()

        def last(self):
            def summed(slots):
                def run():
                    for slot in slots:
                        self.z_links[slot].got(self.z_buf.at[slot])

                    def chunk(at):
                        total = self.grad[q, at].astype(F32)
                        for slot in slots:
                            total += self.z_buf[slot, at].astype(F32)
                        self.grad[q, at] = total.astype(BF)

                    self.chunks(chunk)

                return run

            pl.when(inner)(summed((1, 2, 3)))
            pl.when(outer)(summed((0, 3)))
            self.f_links = []
            for rel in range(3):
                core = lax.rem(c + FLIPS[rel][1], 2)
                self.f_links.append(
                    Link().send(
                        self.half(core),
                        self.final.at[g],
                        rel_dev[rel],
                    )
                )
            self.final[g] = self.half(c)[...]

        def finish(self):
            for rel in range(3):
                self.f_links[rel].got(self.final.at[rel_g[rel]])

    scatter_dn = Scatter(g_dn, y_dn, z_dn, f_dn, h)
    scatter_up = Scatter(hid, y_up, z_up, f_up, h)
    sum_out = GroupSum(slots(xs, (3, 4, 5)), slots(xr, (3, 4, 5)), out_partial)

    def dn_block(k):
        at = part(k * 256, 256)
        lhs = hid[:, :, at].reshape(1024, 256)
        g_dn[pl.ds(2 * k, 2)] = mm_tn(lhs, gd[...].reshape(1024, 1024)).astype(BF).reshape(
            2, 128, 1024
        )

    each(4, dn_block)
    scatter_dn.start()
    gather_dn.finish()
    gather_dn_y.finish()
    sum_nb = GroupSum(slots(xs, (0, 1, 2)), slots(xr, (0, 1, 2)), nb_partial)
    ff_grad(rel_g[DIAG])
    sum_nb.first()
    ff_grad(rel_g[ACROSS])
    sum_nb.second()
    sum_nb.second_send()
    ff_grad(rel_g[TWIN])
    sum_nb.third()
    ff_grad(g)
    sum_out.first()
    sum_out.second()
    scatter_dn.end_to_end()
    sum_out.third()

    sum_out.own(act)

    def up_block(k):
        at = part(k * 256, 256)
        lhs = nb[:, :, at].reshape(1024, 256)
        hid[pl.ds(2 * k, 2)] = mm_tn(lhs, ga[...].reshape(1024, 1024)).astype(BF).reshape(
            2, 128, 1024
        )

    each(4, up_block)
    scatter_up.start()

    scatter_dn.near()
    sum_nb.own(t1)
    sum_nb.total()

    def second_back(at):
        grad_nb = sum_nb.rows(at)
        n, rstd = norm_parts(rmid[at, :])
        vg[4:5, :] += jnp.sum(grad_nb * n, axis=0, keepdims=True)
        vg[5:6, :] += jnp.sum(grad_nb, axis=0, keepdims=True)
        mid = gd[g, at, :].astype(F32) + norm_back(grad_nb * vec[4:5, :], n, rstd)
        gmid[at, :] = mid
        low_mid = mid.astype(BF)
        gatt[1, at, :] = low_mid
        vg[3:4, :] += jnp.sum(low_mid.astype(F32), axis=0, keepdims=True)

    each_rows(256, 32, second_back)

    def grad_o_part(to_g):
        total = jnp.zeros((256, 256), F32)
        for k in range(4):
            total += mm_nt(
                gatt[1, :, 256 * k : 256 * k + 256], wout[k, pl.ds(2 * to_g, 2)].reshape(256, 256)
            )
        return total.astype(BF)

    for link in (nb_pass, nb_across, nb_twin, group_gd.second):
        link.sent()
    go_links = []
    for rel in range(3):
        att_links[rel].sent()
        asend[rel] = grad_o_part(rel_g[rel])
        go_links.append(Link().send(asend.at[rel], go.at[g], rel_dev[rel]))
    go[g] = grad_o_part(g)

    def wog_partial(k, into):
        for j in range(4):
            into[:, 256 * j : 256 * j + 256] = mm_tn(
                att[:, 256 * j : 256 * j + 256], gatt[1, :, part(256 * k, 256)]
            ).astype(into.dtype)

    sum_nb.release()
    scatter_dn.second()
    for rel in (TWIN, ACROSS, DIAG):
        go_links[rel].got(go.at[rel_g[rel]])
    sum_wog = GroupSum(
        slots(gd, rel_g), slots(nb, rel_g), wog_partial, slots(nb, (rel_g[ACROSS], g, g))
    )
    sum_wog.first()
    sum_wog.second()
    sum_wog.second_send()
    sum_wog.third()
    sum_wog.own(nb.at[g])

    def attend_back(row):
        keys = proj[row, :, 256:512]
        values = proj[row, :, 512:768]
        queries = proj[row, :, 0:256]
        grad_rows = go[row]
        zero = jnp.zeros_like(keys)
        for buf in (t2, t3, t4):
            buf[...] = jnp.zeros_like(buf)

        def head(k):
            mine = head_of == k
            probs = pr[row * 4 + k]
            g_head = jnp.where(mine, grad_rows, zero)
            t4[...] += mm_tn(probs, g_head)
            grad_p = mm_nt(g_head, values)
            wide = probs.astype(F32)
            grad_s = wide * (grad_p - jnp.sum(grad_p * wide, axis=-1, keepdims=True))
            low_s = (grad_s * 0.125).astype(BF)
            t2[...] += mm(low_s, jnp.where(mine, keys, zero))
            t3[...] += mm_tn(low_s, jnp.where(mine, queries, zero))

        each(4, head, HEAD_UNROLL)
        proj[row, :, 0:256] = t2[...].astype(BF)
        proj[row, :, 256:512] = t3[...].astype(BF)
        proj[row, :, 512:768] = t4[...].astype(BF)

    def na_partial(row, into):
        def block(k):
            into[:, part(k * 256, 256)] = mm_nt(
                proj[row], wqkv[pl.ds(2 * k, 2)].reshape(256, 768)
            ).astype(into.dtype)

        each(4, block)

    sum_na = GroupSum(slots(xs, (0, 1, 2)), slots(xr, (0, 1, 2)), na_partial)
    scatter_dn.own()
    attend_back(rel_g[DIAG])
    sum_na.first()
    scatter_up.end_to_end()
    attend_back(rel_g[ACROSS])
    sum_na.second()
    sum_na.second_send()
    attend_back(rel_g[TWIN])
    sum_na.third()
    scatter_up.near()
    sum_wog.total()
    scatter_out = Scatter(g_out, y_out, z_out, f_out, h)
    for j in range(4):
        at = slice(256 * j, 256 * j + 256)
        g_out[2 * j : 2 * j + 2] = (
            nb[g, :, at].astype(F32) + nb[rel_g[ACROSS], :, at].astype(F32)
            + nb[rel_g[TWIN], :, at].astype(F32)
        ).astype(BF).reshape(2, 128, 256)
    scatter_out.start()
    attend_back(g)
    sum_na.own(t1)

    scatter_qkv = Scatter(g_qkv, y_qkv, z_qkv, f_qkv, h)
    scatter_in = Scatter(g_in, y_in, z_in, f_in, None)

    def qkv_block(k):
        at = part(k * 256, 256)
        lhs = na[:, :, at].reshape(1024, 256)
        g_qkv[pl.ds(2 * k, 2)] = mm_tn(lhs, proj[...].reshape(1024, 768)).astype(BF).reshape(
            2, 128, 768
        )

    each(4, qkv_block)
    scatter_qkv.start()
    scatter_up.second()

    sum_na.total()

    def first_back(at):
        grad_na = sum_na.rows(at)
        n, rstd = norm_parts(rin[at, :])
        vg[1:2, :] += jnp.sum(grad_na * n, axis=0, keepdims=True)
        vg[2:3, :] += jnp.sum(grad_na, axis=0, keepdims=True)
        low_in = (gmid[at, :] + norm_back(grad_na * vec[1:2, :], n, rstd)).astype(BF)
        gatt[0, at, :] = low_in
        vg[0:1, :] += jnp.sum(low_in.astype(F32), axis=0, keepdims=True)

    each_rows(256, 32, first_back)
    for k in range(4):
        vg[7 + k : 8 + k, :] = jnp.where(g == k, bup[1:2, :], 0.0)
    for j in range(8):
        vq[j % 2, j // 2] = vg[:, 128 * j : 128 * j + 128]
    vy_link = Link().send(vq.at[1 - y], vgy, pair_y)

    grad_scaled = jnp.zeros((256, 256), F32)
    for k in range(4):
        grad_scaled += mm_nt(gatt[0, :, 256 * k : 256 * k + 256], win_mat(k))
    level = as_col(small[20:22, :])
    scale_in = lax.rsqrt(1.0 + level * level)
    ngrad[...] = grad_scaled * (level * scale_in)
    stores.append(moved(ngrad, ngrad_hbm))

    def set_at(other_x, other_y, other_core):
        return ((lax.rem(x + other_x, 2) * 2 + lax.rem(y + other_y, 2)) * 2 + lax.rem(c + other_core, 2)) * 4

    home = tok.at[set_at(0, 0, 0) + z]
    tok[set_at(0, 0, 0) + z] = (grad_scaled * scale_in).astype(BF)
    steps = {"own": z, "second": far(2), "near": jnp.where(z < 2, far(3), far(1)), "last": jnp.where(z < 2, far(1), far(3))}

    class Line:
        def __init__(self, ref, first):
            self.first = first
            self.links = {
                d: Link().send(ref, ref, dev(0, d, 0, 0), only={1: z != 3, 3: z != 0}.get(d))
                for d in (2, 1, 3)
            }

        def spot(self, step):
            return self.first + steps[step]

        def got(self, step):
            ref = tok.at[self.spot(step)]
            one, three = self.links[1].at, self.links[3].at
            if step == "second":
                self.links[2].got(ref)
                Link().send(ref, ref, relay_to, only=inner, arrives=jnp.where(z == 2, three, one))
            elif step == "near":
                arrived(jnp.where(z < 2, three, one), ref)
            else:
                arrived(jnp.where(z < 2, one, three), ref)
            return self.spot(step)

    line_own = Line(home, set_at(0, 0, 0))
    tok_x = {}
    by_y = ("own", "second")
    tok_y = {}
    tok_t = {}

    def to_twin(spot, own_plane, key):
        tok_t[own_plane, key] = Link().send(tok.at[spot], tok.at[spot], twin)

    tok_x[0, 0] = Link().send(home, home, across)
    tok_y["own"] = Link().send(home, home, pair_y)
    to_twin(set_at(0, 0, 0) + z, True, (0, "own"))
    sum_out.second_send()

    def wig_partial(k, into):
        into[...] = mm_tn(sc[g], gatt[0, :, part(256 * k, 256)]).astype(into.dtype)

    sum_wig = GroupSum(
        slots(pr, (0, 1, 2)), slots(go, rel_g), wig_partial, slots(go, (rel_g[ACROSS], g, g)), t2
    )
    sum_wig.first()
    scatter_out.end_to_end()
    sum_wig.second()
    sum_wig.second_send()
    sum_wig.third()
    sum_wig.own(t3)
    scatter_dn.last()

    beside = set_at(1, 0, 0) + z
    tok_x[0, 0].got(tok.at[beside])
    line_beside = Line(tok.at[beside], set_at(1, 0, 0))
    to_twin(beside, False, (0, "own"))
    tok_x[1, "own"] = Link().send(tok.at[beside], tok.at[beside], pair_y)

    def tok_from_z(step):
        spot = line_own.got(step)
        tok_y[step] = Link().send(tok.at[spot], tok.at[spot], pair_y)
        to_twin(spot, True, (0, step))

    def tok_from_y(step):
        spot = set_at(0, 1, 0) + steps[step]
        tok_y[step].got(tok.at[spot])
        if step not in by_y:
            tok_x[1, step] = Link().send(tok.at[spot], tok.at[spot], across)
        to_twin(spot, True, (1, step))

    def tok_beside(step):
        spot = line_beside.got(step)
        to_twin(spot, False, (0, step))
        if step in by_y:
            tok_x[1, step] = Link().send(tok.at[spot], tok.at[spot], pair_y)

    def tok_from_x(step):
        spot = set_at(1, 1, 0) + steps[step]
        tok_x[1, step].got(tok.at[spot])
        to_twin(spot, False, (1, step))

    smx_link.got(smx)
    for other_x in (0, 1):
        for yy in (0, 1):
            for core in (0, 1):
                source = sm if other_x == 0 else smx
                for zz in range(4):
                    idr[(other_x * 2 + yy) * 2 + core : (other_x * 2 + yy) * 2 + core + 1, 256 * zz : 256 * zz + 256] = (
                        as_row(source[2 * zz + yy, core, 16:18, :])
                    )

    tile = 400
    base = (f * rows_here).astype(F32)
    tile_row = lax.broadcasted_iota(jnp.int32, (tile, 1024), 0).astype(F32)

    def table_add(other_x, other_y, other_core, begin):
        spot = set_at(other_x, other_y, other_core)
        row = (other_x * 2 + lax.rem(y + other_y, 2)) * 2 + lax.rem(c + other_core, 2)
        ids = idr[pl.ds(row, 1), :] - base

        def block(k):
            at = part(k * tile, tile)
            hit = jnp.where(tile_row == ids - (k * tile).astype(F32), 1.0, 0.0).astype(BF)
            add = mm(hit, tok[pl.ds(spot, 4)].reshape(1024, 256))
            if begin:
                tgrad[at, :] = add
            else:
                tgrad[at, :] += add

        each(rows_here // tile, block)

    def twin_set(from_x, other_y):
        for step in steps:
            tok_t[from_x == 0, (other_y, step)].got(tok.at[set_at(from_x, other_y, 1) + steps[step]])

    tok_from_z("second")
    tok_from_z("near")
    scatter_up.own()
    scatter_qkv.end_to_end()
    tok_from_z("last")
    tok_beside("second")
    table_add(0, 0, 0, True)
    scatter_up.last()
    scatter_out.near()
    tok_from_y("own")
    scatter_qkv.near()
    twin_set(0, 0)
    table_add(0, 0, 1, False)
    sum_wig.total()
    g_in[...] = (
        t3[...] + go[rel_g[ACROSS]].astype(F32) + go[rel_g[TWIN]].astype(F32)
    ).astype(BF).reshape(8, 2, 16, 256)
    scatter_in.start()
    vy_link.got(vgy)
    vq[y] = vq[y] + vgy[...]
    vz_links = [
        Link().send(vq.at[y, to(d)], vgz.at[d - 1], dev(0, d, 0, 0)) for d in (1, 2, 3)
    ]
    tok_from_y("second")
    scatter_qkv.second()
    tok_from_y("near")
    scatter_qkv.own()
    scatter_out.second()
    scatter_out.own()
    tok_from_y("last")
    table_add(0, 1, 0, False)
    tok_beside("near")
    tok_beside("last")
    table_add(1, 0, 0, False)
    twin_set(0, 1)
    table_add(0, 1, 1, False)
    scatter_in.middle()
    scatter_qkv.last()
    for d in (1, 2, 3):
        vz_links[d - 1].got(vgz.at[d - 1])
    vtot = vq[y, z] + vgz[0] + vgz[1] + vgz[2]
    vgf[3] = vtot
    vf_links = [Link().send(vgf.at[3], vgf.at[rel], rel_dev[rel]) for rel in range(3)]
    twin_set(1, 0)
    table_add(1, 0, 1, False)
    scatter_out.last()
    scatter_in.last()
    sum_out.total()

    def out_rows(at):
        whole = rmid[at, :] + sum_out.rows(at) + vec[6:7, :]
        act[at, :] = (whole * lives[at, 0:1]).astype(BF)

    each_rows(256, 32, out_rows)
    stores.append(moved(act, act_hbm))
    sum_out.release()

    for step in steps:
        tok_from_x(step)
    table_add(1, 1, 0, False)
    twin_set(1, 1)
    table_add(1, 1, 1, False)

    def table_rows(at):
        values = tp[c, at, :].astype(F32)
        r = lax.rsqrt(jnp.mean(values * values, axis=1, keepdims=True) + norm_eps)
        row_grad = tgrad[at, :]
        slope = jnp.mean(row_grad * values, axis=1, keepdims=True)
        tgrad[at, :] = r * row_grad - values * (r * r * r * slope)

    for k in range(rows_here // 200):
        at = pl.ds(k * 200, 200)
        table_rows(at)
        stores.append(moved(tgrad.at[at], tgrad_hbm.at[at]))

    for rel in range(3):
        vf_links[rel].got(vgf.at[rel])
    vout[...] = vgf[0] + vgf[1] + vgf[2] + vgf[3]
    for scatter in (scatter_dn, scatter_up, scatter_qkv, scatter_out, scatter_in):
        scatter.finish()
    for k, (src, dst) in enumerate(((f_in, f_in_hbm), (f_qkv, f_qkv_hbm), (f_out, f_out_hbm), (f_up, f_up_hbm), (f_dn, f_dn_hbm), (vout, vout_hbm))):
        stores.append(moved(src, dst))
    for link in list(pending):
        link.sent()
    for store in stores:
        store.wait()


def finish_kernel(
    act_in, ngrad_in, tgrad_in, vout, f_in_hbm, f_qkv_hbm, f_out_hbm, f_up_hbm, f_dn_hbm,
    act, ngrad, tgrad, w_in_hbm, b_in, gain_a, shift_a, w_qkv_hbm, w_out_hbm, b_out, gain_b, shift_b,
    w_up_hbm, b_up, w_dn_hbm, b_dn,
    act_v, ngrad_v, tgrad_v, f_in, f_qkv, f_out, f_up, f_dn, w_in, w_qkv, w_out, w_up, w_dn, sems,
):
    count = [0]

    def moved(src, dst):
        copy = pltpu.make_async_copy(src, dst, sems.at[count[0]])
        count[0] += 1
        copy.start()
        return copy

    load_up = moved(f_up_hbm, f_up)
    load_dn = moved(f_dn_hbm, f_dn)
    load_qkv = moved(f_qkv_hbm, f_qkv)
    load_out = moved(f_out_hbm, f_out)
    load_in = moved(f_in_hbm, f_in)
    passed = [(act_in, act_v, act), (ngrad_in, ngrad_v, ngrad)]
    tile = tgrad_v.shape[0] // 5
    for k in range(5):
        at = pl.ds(k * tile, tile)
        passed.append((tgrad_in.at[at], tgrad_v.at[at], tgrad.at[at]))
    passed = [(moved(src, via), via, dst) for src, via, dst in passed]
    stores = []
    c = lax.rem(lax.axis_index("fsdp"), 2)
    rows = jnp.where(c == 0, vout[...], pltpu.roll(vout[...], 64, 1))
    for k, ref in enumerate((b_in, gain_a, shift_a, b_out, gain_b, shift_b, b_dn)):
        ref[...] = rows[k, 0:64]
    for k in range(4):
        b_up[64 * k : 64 * k + 64] = rows[7 + k, 0:64]
    h = w_out.shape[0]
    low_half = lax.broadcasted_iota(jnp.int32, (h, 128), 1) < 64
    load_up.wait()
    for shard in range(16):
        at = slice(128 * (shard // 2), 128 * (shard // 2) + 128)
        for half in (0, 1):
            first, second = f_up[2 * half, :, at].astype(F32), f_up[2 * half + 1, :, at].astype(F32)
            if shard % 2 == 0:
                both = jnp.where(low_half, first, pltpu.roll(second, 64, 1))
            else:
                both = jnp.where(low_half, pltpu.roll(first, 64, 1), second)
            w_up[:, 256 * shard + 128 * half : 256 * shard + 128 * half + 128] = both
    stores.append(moved(w_up, w_up_hbm))
    for load, via, dst in passed:
        load.wait()
        stores.append(moved(via, dst))
    load_dn.wait()
    for g in range(4):
        w_dn[h * g : h * g + h, :] = f_dn[g].astype(F32)
    stores.append(moved(w_dn, w_dn_hbm))
    load_qkv.wait()
    for g in range(4):
        for n in range(3):
            w_qkv[:, 1024 * n + 256 * g : 1024 * n + 256 * g + 256] = f_qkv[
                g, :, 256 * n : 256 * n + 256
            ].astype(F32)
    stores.append(moved(w_qkv, w_qkv_hbm))
    load_out.wait()
    load_in.wait()
    for g in range(4):
        at = slice(256 * g, 256 * g + 256)
        w_in[:, at] = f_in[g].astype(F32)
        w_out[:, at] = f_out[g].astype(F32)
    stores.append(moved(w_out, w_out_hbm))
    stores.append(moved(w_in, w_in_hbm))
    for store in stores:
        store.wait()


def fused_shards(
    token_ids, seq_lengths, noise, noise_level, table, w_in, b_in, gain_first, shift_first, w_qkv,
    w_out, b_out, gain_second, shift_second, w_up, b_up, w_down, b_down, cotangent,
):
    raw = (
        token_ids, seq_lengths, noise_level, b_in, gain_first, shift_first, b_out, gain_second,
        shift_second, b_down, b_up,
    )
    vmem = pl.BlockSpec(memory_space=pltpu.VMEM)
    hbm = pl.BlockSpec(memory_space=pl.ANY)

    def shape(*dims, dtype=BF):
        return jax.ShapeDtypeStruct(dims, dtype)

    rows_here = table.shape[0]
    padded = -(-rows_here // 256) * 256
    outs = [
        shape(256, 1024), shape(256, 256, dtype=F32), shape(rows_here, 256, dtype=F32),
        shape(16, 128, dtype=F32), shape(4, 16, 256), shape(4, 64, 768), shape(4, 64, 256),
        shape(4, 64, 1024), shape(4, 64, 1024),
    ]

    held = [pltpu.VMEM(v.shape, v.dtype) for v in raw] + [pltpu.VMEM((24, 128), F32)]
    held += [pltpu.VMEM(v.shape, v.dtype) for v in (noise, w_in, w_qkv, w_out, w_up, w_down, cotangent)]
    held += [pltpu.VMEM(v.shape, v.dtype) for v in outs]

    def bf(*dims):
        return pltpu.VMEM(dims, BF)

    def fl(*dims):
        return pltpu.VMEM(dims, F32)

    scratch = [
        fl(8, 2, 24, 128), fl(8, 2, 24, 128), fl(2, 24, 128),
        fl(16, 1024), fl(16, 1024), fl(2, 4, 16, 128), fl(4, 16, 128), fl(3, 16, 128),
        fl(4, 16, 128), fl(8, 1024), fl(256, 128), fl(8, 1024),
        bf(2, padded, 256), bf(32, 256, 256), bf(4, 256, 256), bf(4, 8, 2, 16, 256),
        bf(8, 128, 768), bf(4, 8, 128, 256), bf(8, 128, 1024), bf(8, 128, 1024),
        bf(2, 16, 256), bf(64, 768), bf(64, 256), bf(64, 1024),
        fl(256, 1024), fl(256, 1024), fl(256, 1024), fl(256, 1024),
        fl(256, 256), fl(256, 256), fl(256, 256),
        bf(4, 256, 1024), bf(4, 256, 768), bf(16, 256, 256), bf(256, 1024), bf(3, 256, 256),
        bf(4, 256, 1024), bf(4, 256, 1024), bf(8, 128, 1024), bf(4, 256, 1024),
        bf(6, 256, 1024), bf(6, 256, 1024), bf(2, 256, 1024), bf(4, 256, 256),
        bf(8, 2, 16, 256), bf(8, 128, 768), bf(8, 128, 256), bf(8, 128, 1024),
        bf(4, 2, 16, 256), bf(4, 128, 768), bf(4, 128, 256), bf(4, 128, 1024), bf(4, 128, 1024),
        bf(4, 2, 16, 256), bf(4, 128, 768), bf(4, 128, 256), bf(4, 128, 1024), bf(4, 128, 1024),
        pltpu.SemaphoreType.DMA((SEM_COUNT,)), pltpu.SemaphoreType.DMA((SEM_COUNT,)),
        pltpu.SemaphoreType.DMA((45,)),
    ]
    parts = pl.pallas_call(
        layer_kernel,
        out_shape=outs,
        in_specs=[hbm] * 19,
        out_specs=[hbm] * len(outs),
        scratch_shapes=held + scratch,
        compiler_params=pltpu.CompilerParams(
            collective_id=0, has_side_effects=True, vmem_limit_bytes=VMEM_LIMIT
        ),
        cost_estimate=pl.CostEstimate(flops=40 * 10**9, bytes_accessed=30 * 10**6, transcendentals=0),
    )(*raw, noise, table, w_in, w_qkv, w_out, w_up, w_down, cotangent)
    f32 = lambda a: jax.ShapeDtypeStruct(a.shape, F32)
    finals = [
        outs[0], outs[1], outs[2], f32(w_in), f32(b_in), f32(gain_first), f32(shift_first),
        f32(w_qkv), f32(w_out), f32(b_out), f32(gain_second), f32(shift_second), f32(w_up),
        f32(b_up), f32(w_down), f32(b_down),
    ]
    return tuple(
        pl.pallas_call(
            finish_kernel,
            out_shape=finals,
            in_specs=[hbm] * 3 + [vmem] + [hbm] * 5,
            out_specs=[vmem if len(v.shape) == 1 else hbm for v in finals],
            scratch_shapes=[pltpu.VMEM(v.shape, v.dtype) for v in outs[:3] + outs[4:]]
            + [pltpu.VMEM(finals[k].shape, F32) for k in (3, 7, 8, 12, 14)]
            + [pltpu.SemaphoreType.DMA((24,))],
            compiler_params=pltpu.CompilerParams(vmem_limit_bytes=VMEM_LIMIT),
        )(*parts)
    )


def solution(mesh):
    in_specs = (
        P(("dp", "fsdp")),
        P(("dp", "fsdp"), None),
        P(("dp", "fsdp"), None),
        P(("dp", "fsdp")),
        P("fsdp", None),
        P("fsdp", None),
        P("fsdp"),
        P("fsdp"),
        P("fsdp"),
        P("fsdp", None),
        P("fsdp", None),
        P("fsdp"),
        P("fsdp"),
        P("fsdp"),
        P("fsdp", None),
        P("fsdp"),
        P("fsdp", None),
        P("fsdp"),
        P(("dp", "fsdp"), None),
    )
    out_specs = (
        P(("dp", "fsdp"), None),
        P(("dp", "fsdp"), None),
        P("fsdp", None),
        P("fsdp", None),
        P("fsdp"),
        P("fsdp"),
        P("fsdp"),
        P("fsdp", None),
        P("fsdp", None),
        P("fsdp"),
        P("fsdp"),
        P("fsdp"),
        P("fsdp", None),
        P("fsdp"),
        P("fsdp", None),
        P("fsdp"),
    )
    fused = mesh.shape["dp"] == 2 and mesh.shape["fsdp"] == 16
    body = fused_shards if fused else shards
    return jax.shard_map(body, mesh=mesh, in_specs=in_specs, out_specs=out_specs, check_vma=False)
```

```python
import jax
import jax.numpy as jnp
from jax import lax
from jax.experimental import pallas as pl
from jax.experimental.pallas import tpu as pltpu
from jax.sharding import PartitionSpec as P

HEADS = 16
VOCAB = 32000


norm_eps = 1e-05


def standardize(resid):
    centred = resid - jnp.mean(resid, axis=-1, keepdims=True)
    spread = jnp.mean(centred * centred, axis=-1, keepdims=True)
    return centred * lax.rsqrt(spread + norm_eps)


def row_normalize(tok_rows):
    return tok_rows * lax.rsqrt(jnp.mean(tok_rows * tok_rows, axis=1, keepdims=True) + norm_eps)


def exact_gelu(pre_act):
    return jax.nn.gelu(pre_act, approximate=False)


def split_heads(projected):
    tok_count = projected.shape[0]
    width = projected.shape[1] // 3
    head_size = width // HEADS
    key_heads = projected[:, width : 2 * width].reshape(tok_count, HEADS, head_size)
    value_heads = projected[:, 2 * width :].reshape(tok_count, HEADS, head_size)
    row_block = min(512, tok_count)
    query_blocks = projected[:, :width].reshape(tok_count // row_block, row_block, HEADS, head_size)
    return (query_blocks, key_heads, value_heads, row_block)


def block_scores(query_block, key_heads, seg_block, segment):
    raw_scores = (
        jnp.einsum("qhd,khd->hqk", query_block, key_heads, preferred_element_type=jnp.float32)
        * 0.125
    )
    same_seq = seg_block[:, None] == segment[None, :]
    return jnp.where(same_seq[None, :, :], raw_scores, -1000000000.0)


def attention_forward(projected, segment):
    query_blocks, key_heads, value_heads, row_block = split_heads(projected)
    seg_blocks = segment.reshape(-1, row_block)

    def block_step(items_in):
        query_block, seg_block = items_in
        scores = block_scores(query_block, key_heads, seg_block, segment)
        row_max = jnp.max(scores, axis=-1, keepdims=True)
        exp_scores = jnp.exp(scores - row_max)
        row_total = jnp.sum(exp_scores, axis=-1, keepdims=True)
        soft_probs = (exp_scores / row_total).astype(jnp.bfloat16)
        attended = jnp.einsum(
            "hqk,khd->qhd", soft_probs, value_heads, preferred_element_type=jnp.float32
        )
        return (attended, (row_max + jnp.log(row_total))[:, :, 0])

    attended, log_total = lax.map(block_step, (query_blocks, seg_blocks))
    return (attended.reshape(projected.shape[0], -1), log_total)


def attention_backward(projected, segment, log_total, grad_attended):
    query_blocks, key_heads, value_heads, row_block = split_heads(projected)
    seg_blocks = segment.reshape(-1, row_block)
    grad_blocks = grad_attended.reshape(query_blocks.shape)

    def block_step(totals, items_in):
        grad_keys, grad_values = totals
        query_block, seg_block, log_block, grad_block = items_in
        scores = block_scores(query_block, key_heads, seg_block, segment)
        soft_probs = jnp.exp(scores - log_block[:, :, None])
        grad_values = grad_values + jnp.einsum(
            "hqk,qhd->khd",
            soft_probs.astype(jnp.bfloat16),
            grad_block,
            preferred_element_type=jnp.float32,
        )
        grad_probs = jnp.einsum(
            "qhd,khd->hqk", grad_block, value_heads, preferred_element_type=jnp.float32
        )
        grad_scores = soft_probs * (
            grad_probs - jnp.sum(grad_probs * soft_probs, axis=-1, keepdims=True)
        )
        scaled_grad = (grad_scores * 0.125).astype(jnp.bfloat16)
        grad_query = jnp.einsum(
            "hqk,khd->qhd", scaled_grad, key_heads, preferred_element_type=jnp.float32
        )
        grad_keys = grad_keys + jnp.einsum(
            "hqk,qhd->khd", scaled_grad, query_block, preferred_element_type=jnp.float32
        )
        return ((grad_keys, grad_values), grad_query.astype(jnp.bfloat16))

    zero_heads = jnp.zeros(key_heads.shape, jnp.float32)
    (grad_keys, grad_values), grad_queries = lax.scan(
        block_step, (zero_heads, zero_heads), (query_blocks, seg_blocks, log_total, grad_blocks)
    )
    tok_count = projected.shape[0]
    return jnp.concatenate(
        [
            grad_queries.reshape(tok_count, -1),
            grad_keys.astype(jnp.bfloat16).reshape(tok_count, -1),
            grad_values.astype(jnp.bfloat16).reshape(tok_count, -1),
        ],
        axis=1,
    )


def shards(
    token_ids,
    seq_lengths,
    noise,
    noise_level,
    table,
    w_in,
    b_in,
    gain_first,
    shift_first,
    w_qkv,
    w_out,
    b_out,
    gain_second,
    shift_second,
    w_up,
    b_up,
    w_down,
    b_down,
    cotangent,
):
    tok_count = token_ids.shape[0]
    row_count = table.shape[0]
    group_ids = lax.all_gather(token_ids, "fsdp", axis=0, tiled=True)
    first_row = lax.axis_index("fsdp") * row_count
    owned = (group_ids[:, None] == first_row + jnp.arange(row_count)[None, :]).astype(jnp.bfloat16)
    owned_rows = jnp.dot(owned, table, preferred_element_type=jnp.float32).astype(jnp.bfloat16)
    tok_rows = lax.psum_scatter(owned_rows, "fsdp", scatter_dimension=0, tiled=True)
    tok_rows = tok_rows.astype(jnp.float32)
    vectors = (b_in, gain_first, shift_first, b_out, gain_second, shift_second, b_up, b_down)
    vec_all = lax.all_gather(jnp.concatenate(vectors), "fsdp", axis=0, tiled=False)
    vec_at = [0]
    for vector in vectors:
        vec_at.append(vec_at[-1] + vector.shape[0])
    (
        b_in_all,
        gain_first_all,
        shift_first_all,
        b_out_all,
        gain_second_all,
        shift_second_all,
        b_up_all,
        b_down_all,
    ) = [vec_all[:, lo:hi].reshape(-1) for lo, hi in zip(vec_at[:-1], vec_at[1:])]
    w_in_all = lax.all_gather(w_in, "fsdp", axis=0, tiled=True)
    w_qkv_all = lax.all_gather(w_qkv, "fsdp", axis=0, tiled=True)
    w_out_all = lax.all_gather(w_out, "fsdp", axis=0, tiled=True)
    w_up_all = lax.all_gather(w_up, "fsdp", axis=0, tiled=True)
    w_down_all = lax.all_gather(w_down, "fsdp", axis=0, tiled=True)
    seq_ends = jnp.cumsum(seq_lengths[0], dtype=jnp.int32)
    positions = jnp.arange(tok_count, dtype=jnp.int32)
    segment = jnp.sum((positions[:, None] >= seq_ends[None, :]).astype(jnp.int32), axis=1)
    live_rows = (segment < seq_lengths.shape[1]).astype(jnp.float32)[:, None]
    embedded = row_normalize(tok_rows)
    scale_in = lax.rsqrt(1.0 + noise_level * noise_level)[:, None]
    scaled = ((embedded + noise_level[:, None] * noise.astype(jnp.float32)) * scale_in).astype(
        jnp.bfloat16
    )
    resid_in = jnp.dot(scaled, w_in_all, preferred_element_type=jnp.float32) + b_in_all.astype(
        jnp.float32
    )
    std_first, first_pull = jax.vjp(standardize, resid_in)
    normed_a = (
        std_first * gain_first_all.astype(jnp.float32) + shift_first_all.astype(jnp.float32)
    ).astype(jnp.bfloat16)
    projected = jnp.dot(normed_a, w_qkv_all, preferred_element_type=jnp.float32).astype(
        jnp.bfloat16
    )
    attended, log_total = attention_forward(projected, segment)
    attended = attended.astype(jnp.bfloat16)
    resid_mid = (
        resid_in
        + jnp.dot(attended, w_out_all, preferred_element_type=jnp.float32)
        + b_out_all.astype(jnp.float32)
    )
    std_second, second_pull = jax.vjp(standardize, resid_mid)
    normed_b = (
        std_second * gain_second_all.astype(jnp.float32) + shift_second_all.astype(jnp.float32)
    ).astype(jnp.bfloat16)
    pre_act = jnp.dot(normed_b, w_up_all, preferred_element_type=jnp.float32) + b_up_all.astype(
        jnp.float32
    )
    activated, gelu_pull = jax.vjp(exact_gelu, pre_act)
    hidden = activated.astype(jnp.bfloat16)
    resid_out = (
        resid_mid
        + jnp.dot(hidden, w_down_all, preferred_element_type=jnp.float32)
        + b_down_all.astype(jnp.float32)
    )
    activations = (resid_out * live_rows).astype(jnp.bfloat16)
    grad_out = cotangent.astype(jnp.float32) * live_rows
    grad_down = grad_out.astype(jnp.bfloat16)
    b_down_term = jnp.sum(grad_down.astype(jnp.float32), axis=0)
    w_down_term = jnp.einsum("tf,td->fd", hidden, grad_down, preferred_element_type=jnp.float32)
    grad_hidden = jnp.einsum("td,fd->tf", grad_down, w_down_all, preferred_element_type=jnp.float32)
    grad_act = gelu_pull(grad_hidden)[0].astype(jnp.bfloat16)
    b_up_term = jnp.sum(grad_act.astype(jnp.float32), axis=0)
    w_up_term = jnp.einsum("td,tf->df", normed_b, grad_act, preferred_element_type=jnp.float32)
    grad_nb = jnp.einsum("tf,df->td", grad_act, w_up_all, preferred_element_type=jnp.float32)
    gain_second_term = jnp.sum(grad_nb * std_second, axis=0)
    shift_second_term = jnp.sum(grad_nb, axis=0)
    grad_mid = grad_out + second_pull(grad_nb * gain_second_all.astype(jnp.float32))[0]
    grad_att = grad_mid.astype(jnp.bfloat16)
    b_out_term = jnp.sum(grad_att.astype(jnp.float32), axis=0)
    w_out_term = jnp.einsum("tc,td->cd", attended, grad_att, preferred_element_type=jnp.float32)
    grad_attended = jnp.einsum(
        "td,cd->tc", grad_att, w_out_all, preferred_element_type=jnp.float32
    ).astype(jnp.bfloat16)
    grad_proj = attention_backward(projected, segment, log_total, grad_attended)
    w_qkv_term = jnp.einsum("td,te->de", normed_a, grad_proj, preferred_element_type=jnp.float32)
    grad_na = jnp.einsum("te,de->td", grad_proj, w_qkv_all, preferred_element_type=jnp.float32)
    gain_first_term = jnp.sum(grad_na * std_first, axis=0)
    shift_first_term = jnp.sum(grad_na, axis=0)
    grad_in = grad_mid + first_pull(grad_na * gain_first_all.astype(jnp.float32))[0]
    grad_pin = grad_in.astype(jnp.bfloat16)
    b_in_term = jnp.sum(grad_pin.astype(jnp.float32), axis=0)
    w_in_term = jnp.einsum("te,td->ed", scaled, grad_pin, preferred_element_type=jnp.float32)
    grad_scaled = jnp.einsum("td,ed->te", grad_pin, w_in_all, preferred_element_type=jnp.float32)
    noise_grad = grad_scaled * noise_level[:, None] * scale_in
    grad_embedded = grad_scaled * scale_in
    all_ids = lax.all_gather(token_ids, ("dp", "fsdp"), axis=0, tiled=True)
    all_grads = lax.all_gather(
        grad_embedded.astype(jnp.bfloat16), ("dp", "fsdp"), axis=0, tiled=True
    )
    owners = (first_row + jnp.arange(row_count)[:, None] == all_ids[None, :]).astype(jnp.bfloat16)
    row_grad = jnp.dot(owners, all_grads, preferred_element_type=jnp.float32)
    own_table = table.astype(jnp.float32)
    unused_rows, table_pull = jax.vjp(row_normalize, own_table)
    table_part = table_pull(row_grad)[0]

    def reduce_matrix(term):
        part = lax.psum_scatter(
            term.astype(jnp.bfloat16), "fsdp", scatter_dimension=0, tiled=True
        )
        return lax.psum(part, "dp").astype(jnp.float32)

    vec_terms = (
        b_in_term,
        gain_first_term,
        shift_first_term,
        b_out_term,
        gain_second_term,
        shift_second_term,
        b_up_term,
        b_down_term,
    )
    shard_count = lax.axis_size("fsdp")
    vec_term = jnp.concatenate([v.reshape(shard_count, -1) for v in vec_terms], axis=1)
    vec_part = lax.psum(vec_term, ("dp", "fsdp"))
    own_vec = lax.dynamic_index_in_dim(vec_part, lax.axis_index("fsdp"), 0, keepdims=False)
    vec_grads = [own_vec[lo:hi] for lo, hi in zip(vec_at[:-1], vec_at[1:])]
    return (
        activations,
        noise_grad,
        table_part,
        reduce_matrix(w_in_term),
        vec_grads[0],
        vec_grads[1],
        vec_grads[2],
        reduce_matrix(w_qkv_term),
        reduce_matrix(w_out_term),
        vec_grads[3],
        vec_grads[4],
        vec_grads[5],
        reduce_matrix(w_up_term),
        vec_grads[6],
        reduce_matrix(w_down_term),
        vec_grads[7],
    )


BF = jnp.bfloat16
F32 = jnp.float32
MESH_ID = pl.DeviceIdType.MESH
SEM_COUNT = 400
ROW_UNROLL = 8
HEAD_UNROLL = 4
EACH_UNROLL = 4
VMEM_LIMIT = 63 * 2**20
NT = (((1,), (1,)), ((), ()))
TN = (((0,), (0,)), ((), ()))
DIAG, ACROSS, TWIN = 0, 1, 2
FLIPS = ((1, 1), (1, 0), (0, 1))


def mm(a, b):
    return jnp.dot(a, b, preferred_element_type=F32)


def mm_nt(a, b):
    return lax.dot_general(a, b, NT, preferred_element_type=F32)


def mm_tn(a, b):
    return lax.dot_general(a, b, TN, preferred_element_type=F32)


def part(start, size):
    return pl.ds(pl.multiple_of(start, size), size)


def as_row(pair):
    return jnp.concatenate([pair[0:1, :], pair[1:2, :]], axis=1)


def as_col(pair):
    eye = lax.broadcasted_iota(jnp.int32, (128, 128), 0) == lax.broadcasted_iota(
        jnp.int32, (128, 128), 1
    )
    cols = [
        jnp.sum(jnp.where(eye, pair[k : k + 1, :], 0.0), axis=1, keepdims=True) for k in (0, 1)
    ]
    return jnp.concatenate(cols, axis=0)


def norm_parts(v):
    centred = v - jnp.mean(v, axis=-1, keepdims=True)
    rstd = lax.rsqrt(jnp.mean(centred * centred, axis=-1, keepdims=True) + norm_eps)
    return centred * rstd, rstd


def norm_back(u, n, rstd):
    return rstd * (
        u - jnp.mean(u, axis=-1, keepdims=True) - n * jnp.mean(u * n, axis=-1, keepdims=True)
    )


def layer_kernel(
    ids_hbm, lengths_hbm, level_hbm, b_in_hbm, gain_a_hbm, shift_a_hbm, b_out_hbm, gain_b_hbm, shift_b_hbm,
    b_dn_hbm, b_up_hbm, noise_hbm, table, w_in_hbm, w_qkv_hbm, w_out_hbm, w_up_hbm, w_down_hbm, cot_hbm,
    act_hbm, ngrad_hbm, tgrad_hbm, vout_hbm, f_in_hbm, f_qkv_hbm, f_out_hbm, f_up_hbm, f_dn_hbm,
    ids_v, lengths_v, level_v, b_in_v, gain_a_v, shift_a_v, b_out_v, gain_b_v, shift_b_v, b_dn_v, b_up_v,
    small, noise, w_in, w_qkv, w_out, w_up, w_down, cot,
    act, ngrad, tgrad, vout, f_in, f_qkv, f_out, f_up, f_dn,
    sm, smx, gsm, vec, vg, vq, vgy, vgz, vgf, bup, lives, idr,
    tp, tok, sc, win, wqkv, wout, wup, wdn, s_in, s_qkv, s_out, s_up,
    rin, rmid, gmid, t1, t2, t3, t4, na, proj, pr, att, asend, nb, gd, hid, ga,
    xs, xr, gatt, go, g_in, g_qkv, g_out, g_dn,
    y_in, y_qkv, y_out, y_up, y_dn, z_in, z_qkv, z_out, z_up, z_dn,
    ss, rr, ls,
):
    x = lax.axis_index("dp")
    f = lax.axis_index("fsdp")
    z, y, c = f // 4, lax.rem(f // 2, 2), lax.rem(f, 2)
    q = 2 * z + y
    g = 2 * x + c
    rows_here = table.shape[0]

    def dev(dx, dz, dy, dc):
        xx = lax.rem(x + dx, 2)
        zz = lax.rem(z + dz, 4)
        yy = lax.rem(y + dy, 2)
        cc = lax.rem(c + dc, 2)
        return (xx, zz * 4 + yy * 2 + cc)

    twin = dev(0, 0, 0, 1)
    across = dev(1, 0, 0, 0)
    pair_y = dev(0, 0, 1, 0)
    relay_to = (x, jnp.where(z == 2, 3, 0) * 4 + y * 2 + c)
    rel_dev = [dev(dx, 0, 0, dc) for dx, dc in FLIPS]
    rel_g = [2 * lax.rem(x + dx, 2) + lax.rem(c + dc, 2) for dx, dc in FLIPS]
    other_c = 1 - c

    def far(d):
        return lax.rem(z + 4 - d, 4)

    def to(d):
        return lax.rem(z + d, 4)

    sems = [0]
    pending = []
    inner = jnp.logical_or(z == 1, z == 2)
    outer = jnp.logical_not(inner)

    class Link:
        def __init__(self):
            self.at = sems[0]
            sems[0] += 1
            assert sems[0] <= SEM_COUNT

        def send(self, src, dst, device, arrives=None, only=None):
            self.only = only
            self.copy = pltpu.make_async_remote_copy(
                src_ref=src, dst_ref=dst, send_sem=ss.at[self.at],
                recv_sem=rr.at[self.at if arrives is None else arrives],
                device_id=device, device_id_type=MESH_ID,
            )
            if only is None:
                self.copy.start()
            else:
                pl.when(only)(self.copy.start)
            pending.append(self)
            return self

        def sent(self):
            pending.remove(self)
            if self.only is None:
                self.copy.wait_send()
            else:
                pl.when(self.only)(self.copy.wait_send)

        def got(self, ref):
            arrived(self.at, ref)

    def arrived(at, ref):
        pltpu.make_async_remote_copy(
            src_ref=ref, dst_ref=ref, send_sem=ss.at[0], recv_sem=rr.at[at],
            device_id=twin, device_id_type=MESH_ID,
        ).wait_recv()

    def each_rows(count, size, body, unroll=ROW_UNROLL):
        def step(i, carry):
            body(part(i * size, size))
            return carry

        lax.fori_loop(0, count // size, step, 0, unroll=unroll)

    def each(count, body, unroll=EACH_UNROLL):
        def step(i, carry):
            body(i)
            return carry

        lax.fori_loop(0, count, step, 0, unroll=unroll)

    local = [0]
    stores = []

    def moved(src, dst):
        copy = pltpu.make_async_copy(src, dst, ls.at[local[0]])
        local[0] += 1
        copy.start()
        return copy

    vectors = (b_in_v, gain_a_v, shift_a_v, b_out_v, gain_b_v, shift_b_v, b_dn_v)
    load_small = [
        moved(src, dst)
        for src, dst in (
            (ids_hbm, ids_v), (lengths_hbm, lengths_v), (level_hbm, level_v), (b_in_hbm, b_in_v),
            (gain_a_hbm, gain_a_v), (shift_a_hbm, shift_a_v), (b_out_hbm, b_out_v),
            (gain_b_hbm, gain_b_v), (shift_b_hbm, shift_b_v), (b_dn_hbm, b_dn_v), (b_up_hbm, b_up_v),
        )
    ]
    load_in = moved(w_in_hbm, w_in)
    load_qkv = moved(w_qkv_hbm, w_qkv)
    load_cot = moved(cot_hbm, cot)
    own_table = moved(table, tp.at[c, pl.ds(0, rows_here)])
    load_noise = moved(noise_hbm, noise)
    load_out = moved(w_out_hbm, w_out)
    load_up = moved(w_up_hbm, w_up)
    load_down = moved(w_down_hbm, w_down)

    barrier = pltpu.get_barrier_semaphore()
    peers = [dev(0, d, 0, dc) for d in (1, 2, 3) for dc in (0, 1)] + rel_dev + [pair_y]
    for peer in peers:
        pl.semaphore_signal(barrier, inc=1, device_id=peer, device_id_type=MESH_ID)
    pl.semaphore_wait(barrier, len(peers))

    class GroupGather:
        def __init__(self, at):
            self.at = at
            self.across = Link().send(at(g), at(g), across)
            self.twin = Link().send(at(g), at(g), twin)

        def hop(self):
            self.across.got(self.at(rel_g[ACROSS]))
            self.second = Link().send(self.at(rel_g[ACROSS]), self.at(rel_g[ACROSS]), twin)

        def got_twin(self):
            self.twin.got(self.at(rel_g[TWIN]))

        def got_diag(self):
            self.second.got(self.at(rel_g[DIAG]))

    class Gather:
        def __init__(self, whole, mine, theirs, height, twins=None, relay=True):
            self.whole, self.height, self.relay = whole, height, relay
            places = (self.sub(q, c), self.sub(q, c, twins))
            self.links = {}
            for d in (0, 2, 1, 3):
                only = {1: z != 3, 3: z != 0}.get(d) if relay else None
                for dc in (1, 0):
                    if (d, dc) != (0, 0):
                        self.links[d, dc] = Link().send(
                            theirs if dc else mine, places[dc], dev(0, d, 0, dc), only=only
                        )

        def sub(self, block, core, whole=None):
            whole = self.whole if whole is None else whole
            if self.height is None:
                return whole.at[block, core]
            return whole.at[block, part(core * self.height, self.height)]

        def over_y(self, block):
            return Link().send(self.whole.at[block], self.whole.at[block], pair_y)

        def own(self):
            self.links[0, 1].got(self.sub(q, other_c))
            self.y_own = self.over_y(q)

        def second(self):
            block = 2 * far(2) + y
            for dc in (1, 0):
                ref = self.sub(block, other_c if dc else c)
                self.links[2, dc].got(ref)
                if self.relay:
                    Link().send(
                        ref, ref, relay_to, only=inner,
                        arrives=jnp.where(z == 2, self.links[3, dc].at, self.links[1, dc].at),
                    )
            self.y_second = self.over_y(block)

        def near(self):
            self.y_near = self.one(3, 1)

        def last(self):
            self.y_last = self.one(1, 3)

        def one(self, low, high):
            block = 2 * jnp.where(z < 2, far(low), far(high)) + y
            for dc in (1, 0):
                arrived(
                    jnp.where(z < 2, self.links[low, dc].at, self.links[high, dc].at),
                    self.sub(block, other_c if dc else c),
                )
            return self.over_y(block)

        def forward(self):
            self.second()
            self.near()
            self.last()

        def finish(self):
            self.y_own.got(self.whole.at[2 * z + 1 - y])
            self.y_second.got(self.whole.at[2 * far(2) + 1 - y])
            self.y_near.got(self.whole.at[2 * jnp.where(z < 2, far(3), far(1)) + 1 - y])
            self.y_last.got(self.whole.at[2 * jnp.where(z < 2, far(1), far(3)) + 1 - y])

    class YFirstGather(Gather):
        def __init__(self, whole, mine, theirs, height):
            self.whole, self.height, self.relay = whole, height, True
            self.y_links = [
                Link().send(theirs if dc else mine, self.sub(q, c), dev(0, 0, 1, dc)) for dc in (0, 1)
            ]
            self.mine, self.theirs = mine, theirs

        def along(self):
            Gather.__init__(self, self.whole, self.mine, self.theirs, self.height)

        def cross(self):
            block = 2 * z + 1 - y
            for dc in (0, 1):
                self.y_links[dc].got(self.sub(block, other_c if dc else c))
            ref = self.whole.at[block]
            self.beside = {
                d: Link().send(ref, ref, dev(0, d, 0, 0), only={1: z != 3, 3: z != 0}.get(d))
                for d in (2, 1, 3)
            }

        def over_y(self, block):
            return None

        def second(self):
            Gather.second(self)
            ref = self.whole.at[2 * far(2) + 1 - y]
            self.beside[2].got(ref)
            Link().send(
                ref, ref, relay_to, only=inner,
                arrives=jnp.where(z == 2, self.beside[3].at, self.beside[1].at),
            )

        def finish(self):
            self.links[0, 1].got(self.sub(q, other_c))
            self.near()
            self.last()
            for d in (1, 3):
                self.beside[d].got(self.whole.at[2 * far(d) + 1 - y])

    for load in load_small:
        load.wait()
    lane_at = lax.broadcasted_iota(jnp.int32, (1, 128), 1)
    small[...] = jnp.zeros_like(small)

    def put_half(row, shard):
        small[row : row + 1, :] = jnp.where(
            lane_at // 64 == c, jnp.concatenate([shard, shard], axis=1), 0.0
        )

    def put_pair(row, line):
        small[row : row + 1, :] = line[:, 0:128]
        small[row + 1 : row + 2, :] = line[:, 128:256]

    for k, v in enumerate(vectors):
        put_half(k, v[...].astype(F32).reshape(1, 64))
    up_shard = b_up_v[...].astype(F32).reshape(1, 256)
    for k in range(4):
        put_half(7 + k, up_shard[:, 64 * k : 64 * k + 64])
    put_pair(16, ids_v[...].astype(F32).reshape(1, 256))
    put_pair(20, level_v[...].reshape(1, 256))
    lengths = lengths_v[...].astype(F32)
    slot_at = lax.broadcasted_iota(jnp.int32, lengths.shape, 1)
    spots = (
        lax.broadcasted_iota(jnp.int32, (2, 128), 0) * 128
        + lax.broadcasted_iota(jnp.int32, (2, 128), 1)
    ).astype(F32)
    slot_of = jnp.zeros((2, 128), F32)
    for k in range(8):
        end = jnp.sum(jnp.where(slot_at <= k, lengths, 0.0), axis=1, keepdims=True)
        slot_of += jnp.where(spots >= end, 1.0, 0.0)
    small[18:20, :] = slot_of
    sm[q, c] = small[...]
    small_links = [Link().send(small, gsm.at[rel], rel_dev[rel]) for rel in (DIAG, ACROSS)]
    gather_small = Gather(sm, small, small, None, relay=False)

    own_rows = tp.at[c, pl.ds(0, rows_here)]
    table_link = Link().send(table, own_rows, twin)
    spare = tp.shape[1] - rows_here
    if spare:
        for core in (0, 1):
            tp[core, pl.ds(rows_here, spare), :] = jnp.zeros((spare, tp.shape[2]), BF)

    def pack(whole, spare_buf, height, pick):
        mine, theirs = pick(g), pick(2 * x + other_c)
        whole[q, part(c * height, height), :] = mine
        spare_buf[...] = theirs

    h = w_qkv.shape[0]
    hin = w_in.shape[0]

    def cols(ref, start, size=256):
        return ref[:, part(start, size)]

    win_at, wout_at = win.at[g], wout.at[g]
    load_in.wait()
    load_qkv.wait()
    win_at[q, c] = cols(w_in, 256 * g)
    s_in[0] = cols(w_in, 256 * (2 * x + other_c))
    gather_in = Gather(win_at, win_at.at[q, c], s_in.at[0], None, win.at[2 * x + other_c], relay=False)
    pack(
        wqkv, s_qkv, h,
        lambda k: jnp.concatenate([cols(w_qkv, 1024 * n + 256 * k) for n in (0, 1, 2)], axis=1),
    )
    gather_qkv = Gather(wqkv, wqkv.at[q, part(c * h, h)], s_qkv, h)


    lives[:, 0:1] = jnp.where(as_col(small[18:20, :]) < 7.5, 1.0, 0.0)
    vg[...] = jnp.zeros_like(vg)

    def grad_down_rows(at):
        masked = cot[at, :].astype(F32) * lives[at, 0:1]
        gd[g, at, :] = masked.astype(BF)
        vg[6:7, :] += jnp.sum(masked, axis=0, keepdims=True)

    load_out.wait()
    pack(wout_at, s_out, h, lambda k: cols(w_out, 256 * k))
    gather_out = Gather(
        wout_at, wout_at.at[q, part(c * h, h)], s_out, h, wout.at[2 * x + other_c], relay=False
    )
    load_cot.wait()
    each_rows(256, 32, grad_down_rows)
    group_gd = GroupGather(lambda k: gd.at[k])

    gather_small.own()
    gather_small.forward()

    gather_in.own()
    gather_qkv.own()
    gather_small.finish()
    smx_link = Link().send(sm, smx, across)
    own_table.wait()
    table_link.got(tp.at[other_c, pl.ds(0, rows_here)])
    lane = lax.broadcasted_iota(jnp.int32, (256, tp.shape[1]), 1)

    def look_up(block):
        ids = as_col(sm[block, c, 16:18, :]).astype(jnp.int32)
        total = jnp.zeros((256, 256), F32)
        for core in (0, 1):
            first = (4 * z + 2 * y + core) * rows_here
            hit = jnp.where(lane == ids - first, 1.0, 0.0).astype(BF)
            total += mm(hit, tp[core])
        return total.astype(BF)

    emb_y = [Link() for _ in range(4)]
    for d in range(4):
        tok[d] = look_up(2 * to(d) + 1 - y)
        emb_y[d].send(tok.at[d], tok.at[8 + d], pair_y)

    load_down.wait()
    wdn[q, part(c * h, h), :] = w_down[part(g * h, h), :]
    gather_dn_y = YFirstGather(
        wdn.at[:, :, 512:1024], w_down.at[part(g * h, h), 512:1024],
        w_down.at[part((2 * x + other_c) * h, h), 512:1024], h,
    )

    def own_blocks(d):
        tok[4 + d] = look_up(2 * lax.rem(z + d, 4) + y)

    each(4, own_blocks, 1)
    emb_z = [None]
    for d in (1, 2, 3):
        emb_y[d].got(tok.at[8 + d])
        tok[4 + d] = tok[4 + d] + tok[8 + d]
        emb_z.append(Link().send(tok.at[4 + d], tok.at[11 + d], dev(0, d, 0, 0)))
    emb_y[0].got(tok.at[8])

    for load in (load_noise, load_up):
        load.wait()
    ct = lax.broadcasted_iota(jnp.int32, (h, 128), 1) < 64
    for j in range(8):
        first = w_up[:, part(128 * (4 * j + x), 128)].astype(F32)
        second = w_up[:, part(128 * (4 * j + 2 + x), 128)].astype(F32)
        low = jnp.where(ct, first, pltpu.roll(second, 64, 1)).astype(BF)
        high = jnp.where(ct, pltpu.roll(first, 64, 1), second).astype(BF)
        wup[q, part(c * h, h), 128 * j : 128 * j + 128] = jnp.where(c == 0, low, high)
        s_up[:, 128 * j : 128 * j + 128] = jnp.where(c == 0, high, low)
    gather_in.forward()
    gather_qkv.forward()
    for j in range(8):
        vec[:, 128 * j : 128 * j + 128] = sm[j, 0, 0:16, :] + sm[j, 1, 0:16, :]

    gather_out.own()
    gather_out.forward()
    gather_in.finish()
    group_in = GroupGather(lambda k: win.at[k])
    group_gd.hop()
    rows_sum = tok[4].astype(F32) + tok[8].astype(F32)
    for d in (1, 2, 3):
        emb_z[d].got(tok.at[11 + d])
        rows_sum += tok[11 + d].astype(F32)
    gather_up = Gather(wup, wup.at[q, part(c * h, h)], s_up, h)
    level = as_col(small[20:22, :])
    scale_in = lax.rsqrt(1.0 + level * level)
    embedded = rows_sum * lax.rsqrt(jnp.mean(rows_sum * rows_sum, axis=1, keepdims=True) + norm_eps)
    sc[g] = ((embedded + level * noise[...].astype(F32)) * scale_in).astype(BF)
    group_sc = GroupGather(lambda k: sc.at[k])

    group_in.hop()
    group_in.got_twin()
    group_in.got_diag()

    def win_mat(k):
        return win[k].reshape(256, 256)

    def first_norm(row, keep):
        for k in range(4):
            keep[:, 256 * k : 256 * k + 256] = (
                mm(sc[row], win_mat(k)) + vec[0:1, 256 * k : 256 * k + 256]
            )

        def chunk(at):
            n, _ = norm_parts(keep[at, :])
            na[row, at, :] = (n * vec[1:2, :] + vec[2:3, :]).astype(BF)

        each_rows(256, 32, chunk)

    def project(row):
        def block(k):
            at = part(k * 256, 256)
            proj[row, :, at] = mm(na[row], wqkv[:, :, at].reshape(1024, 256)).astype(BF)

        each(3, block)

    first_norm(g, rin)
    group_sc.hop()
    gather_up.own()
    group_sc.got_twin()
    first_norm(rel_g[TWIN], t1)
    first_norm(rel_g[ACROSS], t1)
    group_sc.got_diag()
    first_norm(rel_g[DIAG], t1)
    gather_qkv.finish()
    each(4, project, 1)
    gather_out.finish()
    group_out = GroupGather(lambda k: wout.at[k])

    head_of = lax.broadcasted_iota(jnp.int32, (1, 256), 1) // 64
    small_links[DIAG].got(gsm.at[DIAG])
    small_links[ACROSS].got(gsm.at[ACROSS])

    def attend(row, pair):
        same = as_col(pair) == as_row(pair)
        keys = proj[row, :, 256:512]
        values = proj[row, :, 512:768]
        queries = proj[row, :, 0:256]
        t2[...] = jnp.zeros_like(t2)

        def head(k):
            mine = head_of == k
            q_head = jnp.where(mine, queries, jnp.zeros_like(queries))
            scores = jnp.where(same, mm_nt(q_head, keys) * 0.125, -1e9)
            weights = jnp.exp(scores - jnp.max(scores, axis=-1, keepdims=True))
            low_probs = (weights / jnp.sum(weights, axis=-1, keepdims=True)).astype(BF)
            pr[row * 4 + k] = low_probs
            t2[...] += mm(low_probs, jnp.where(mine, values, jnp.zeros_like(values)))

        each(4, head, HEAD_UNROLL)
        return t2[...].astype(BF)

    att_links = []
    my_cols = part(256 * g, 256)
    for rel in range(3):
        pair = sm[q, other_c, 18:20, :] if rel == TWIN else gsm[rel, 18:20, :]
        asend[rel] = attend(rel_g[rel], pair)
        att_links.append(Link().send(asend.at[rel], att.at[:, my_cols], rel_dev[rel]))
        if rel == DIAG:
            gather_up.second()
            for d in range(4):
                emb_y[d].sent()
            for d in (1, 2, 3):
                emb_z[d].sent()
            gather_dn = Gather(
                wdn.at[:, :, 0:512], w_down.at[part(g * h, h), 0:512],
                w_down.at[part((2 * x + other_c) * h, h), 0:512], h,
            )
            gather_dn_y.along()
        if rel == ACROSS:
            gather_dn_y.cross()
    att[:, my_cols] = attend(g, small[18:20, :])
    gather_dn.own()
    group_out.hop()
    gather_up.near()
    gather_up.last()
    group_out.got_twin()
    group_out.got_diag()
    for rel in (TWIN, ACROSS, DIAG):
        att_links[rel].got(att.at[:, part(256 * rel_g[rel], 256)])

    def out_block(k):
        at = part(k * 256, 256)
        rmid[:, at] = rin[:, at] + mm(att[...], wout[k].reshape(1024, 256)) + vec[3:4, at]

    each(4, out_block)

    def second_norm(at):
        n, _ = norm_parts(rmid[at, :])
        nb[g, at, :] = (n * vec[4:5, :] + vec[5:6, :]).astype(BF)

    each_rows(256, 32, second_norm)
    nb_across = Link().send(nb.at[g], nb.at[g], across)
    nb_twin = Link().send(nb.at[g], nb.at[g], twin)
    nb_pass = Link()
    group_gd.got_twin()
    group_gd.got_diag()

    bup[...] = jnp.zeros_like(bup)
    for k in range(4):
        bup[0:1, :] += jnp.where(g == k, vec[7 + k : 8 + k, :], 0.0)

    def ff_hidden(row):
        def block(k):
            at = part(k * 256, 256)
            t2[...] = mm(nb[row], wup[:, :, at].reshape(1024, 256)) + bup[0:1, at]

            def chunk(rows_at):
                pre = t2[rows_at, :]
                cdf = 0.5 + 0.5 * lax.erf(pre * 0.7071067811865476)
                pdf = jnp.exp(-0.5 * pre * pre) * 0.3989422804014327
                t2[rows_at, :] = pre * cdf
                ga[row, rows_at, at] = (cdf + pre * pdf).astype(BF)

            each_rows(256, 32, chunk)
            hid[pl.ds(2 * row, 2), :, at] = t2[...].astype(BF).reshape(2, 128, 256)

        each(4, block)

    def ff_grad(row):
        def block(k):
            at = part(k * 256, 256)
            grad = mm_nt(gd[row], wdn[pl.ds(2 * k, 2)].reshape(256, 1024))
            ga_low = (grad * ga[row, :, at].astype(F32)).astype(BF)
            ga[row, :, at] = ga_low
            bup[1:2, at] += jnp.sum(ga_low.astype(F32), axis=0, keepdims=True)

        each(4, block)

    gather_dn.second()
    gather_up.finish()
    ff_hidden(g)
    gather_dn.near()
    gather_dn.last()
    gather_dn_y.second()
    nb_twin.got(nb.at[rel_g[TWIN]])
    ff_hidden(rel_g[TWIN])
    nb_across.got(nb.at[rel_g[ACROSS]])
    nb_pass.send(nb.at[rel_g[ACROSS]], nb.at[rel_g[ACROSS]], twin)
    ff_hidden(rel_g[ACROSS])
    nb_pass.got(nb.at[rel_g[DIAG]])
    ff_hidden(rel_g[DIAG])

    class GroupSum:
        def __init__(self, sends, gets, partial, puts=None, temp=None):
            self.sends, self.gets, self.partial = sends, gets, partial
            self.temp = t1 if temp is None else temp
            self.puts = gets if puts is None else puts

        def first(self):
            self.partial(rel_g[DIAG], self.sends[0])
            self.a = Link().send(self.sends[0], self.puts[0], twin)

        def second(self):
            self.partial(rel_g[ACROSS], self.temp)
            self.a.got(self.gets[0])

            def chunk(at):
                self.sends[1][at, :] = (
                    self.temp[at, :] + self.gets[0][at, :].astype(F32)
                ).astype(BF)

            each_rows(256, 32, chunk, 2)

        def second_send(self):
            self.b = Link().send(self.sends[1], self.puts[1], across)

        def third(self):
            self.partial(rel_g[TWIN], self.sends[2])
            self.c = Link().send(self.sends[2], self.puts[2], twin)

        def own(self, into):
            self.partial(g, into)
            self.into = into

        def total(self):
            self.c.got(self.gets[2])
            self.b.got(self.gets[1])

        def rows(self, at):
            return (
                self.into[at, :].astype(F32)
                + self.gets[1][at, :].astype(F32)
                + self.gets[2][at, :].astype(F32)
            )

        def release(self):
            for link in (self.a, self.b, self.c):
                link.sent()

    def slots(ref, places):
        return [ref.at[place] for place in places]

    def nb_partial(row, into):
        def block(k):
            into[:, part(k * 256, 256)] = mm_nt(
                ga[row], wup[pl.ds(2 * k, 2)].reshape(256, 1024)
            ).astype(into.dtype)

        each(4, block, 2)

    def out_partial(row, into):
        def block(k):
            at = part(k * 256, 256)
            into[:, at] = mm(
                hid[pl.ds(2 * row, 2)].reshape(256, 1024), wdn[:, :, at].reshape(1024, 256)
            ).astype(into.dtype)

        each(4, block, 2)

    class Scatter:
        def __init__(self, grad, y_buf, z_buf, final, height):
            self.grad, self.y_buf, self.z_buf, self.final, self.height = (
                grad, y_buf, z_buf, final, height,
            )

        def chunks(self, body):
            if self.height is None:
                each(2, body, 1)
            else:
                each_rows(2 * self.height, 32, body, 1)

        def half(self, core):
            if self.height is None:
                return self.grad.at[q, core]
            return self.grad.at[q, part(core * self.height, self.height)]

        def start(self, count=4):
            even = lax.rem(z, 2) == 0
            self.goals = (
                jnp.where(even, 3, 0), jnp.where(even, 1, 2), lax.rem(z + 2, 4), z,
            )
            self.y_links = []
            self.z_links = [Link() for _ in range(4)]
            self.more(count)

        def more(self, count=1):
            for _ in range(count):
                e = len(self.y_links)
                self.y_links.append(
                    Link().send(self.grad.at[2 * self.goals[e] + 1 - y], self.y_buf.at[e], pair_y)
                )

        def add_y(self, e):
            self.y_links[e].got(self.y_buf.at[e])
            block = 2 * self.goals[e] + y

            def chunk(at):
                self.grad[block, at] = (
                    self.grad[block, at].astype(F32) + self.y_buf[e, at].astype(F32)
                ).astype(BF)

            self.chunks(chunk)
            return self.grad.at[block]

        def end_to_end(self):
            ref = self.add_y(0)
            self.z_links[0].send(
                ref, self.z_buf.at[0], (x, (z + 1 - 2 * lax.rem(z, 2)) * 4 + y * 2 + c)
            )

        def near(self):
            ref = self.add_y(1)
            slot = jnp.where(inner, 2, 1)
            self.z_links[1].send(
                ref, self.z_buf.at[slot], (x, self.goals[1] * 4 + y * 2 + c),
                arrives=jnp.where(inner, self.z_links[2].at, self.z_links[1].at),
            )

        def second(self):
            ref = self.add_y(2)
            block = 2 * self.goals[2] + y

            def relayed():
                self.z_links[0].got(self.z_buf.at[0])

                def chunk(at):
                    self.grad[block, at] = (
                        self.grad[block, at].astype(F32) + self.z_buf[0, at].astype(F32)
                    ).astype(BF)

                self.chunks(chunk)

            pl.when(inner)(relayed)
            self.z_links[3].send(ref, self.z_buf.at[3], dev(0, 2, 0, 0))

        def own(self):
            self.add_y(3)

        def middle(self):
            self.end_to_end()
            self.near()
            self.second()
            self.own()

        def last(self):
            def summed(slots):
                def run():
                    for slot in slots:
                        self.z_links[slot].got(self.z_buf.at[slot])

                    def chunk(at):
                        total = self.grad[q, at].astype(F32)
                        for slot in slots:
                            total += self.z_buf[slot, at].astype(F32)
                        self.grad[q, at] = total.astype(BF)

                    self.chunks(chunk)

                return run

            pl.when(inner)(summed((1, 2, 3)))
            pl.when(outer)(summed((0, 3)))
            self.f_links = []
            for rel in range(3):
                core = lax.rem(c + FLIPS[rel][1], 2)
                self.f_links.append(
                    Link().send(
                        self.half(core),
                        self.final.at[g],
                        rel_dev[rel],
                    )
                )
            self.final[g] = self.half(c)[...]

        def finish(self):
            for rel in range(3):
                self.f_links[rel].got(self.final.at[rel_g[rel]])

    scatter_dn = Scatter(g_dn, y_dn, z_dn, f_dn, h)
    scatter_up = Scatter(hid, y_up, z_up, f_up, h)
    sum_out = GroupSum(slots(xs, (3, 4, 5)), slots(xr, (3, 4, 5)), out_partial)

    def dn_block(k):
        at = part(k * 256, 256)
        lhs = hid[:, :, at].reshape(1024, 256)
        g_dn[pl.ds(2 * k, 2)] = mm_tn(lhs, gd[...].reshape(1024, 1024)).astype(BF).reshape(
            2, 128, 1024
        )

    each(4, dn_block, 1)
    scatter_dn.start()
    gather_dn.finish()
    gather_dn_y.finish()
    sum_nb = GroupSum(slots(xs, (0, 1, 2)), slots(xr, (0, 1, 2)), nb_partial)
    ff_grad(rel_g[DIAG])
    sum_nb.first()
    ff_grad(rel_g[ACROSS])
    sum_nb.second()
    sum_nb.second_send()
    ff_grad(rel_g[TWIN])
    sum_nb.third()
    ff_grad(g)
    sum_out.first()
    sum_out.second()
    scatter_dn.end_to_end()
    sum_out.third()

    sum_out.own(act)

    def up_block(k):
        at = part(k * 256, 256)
        lhs = nb[:, :, at].reshape(1024, 256)
        hid[pl.ds(2 * k, 2)] = mm_tn(lhs, ga[...].reshape(1024, 1024)).astype(BF).reshape(
            2, 128, 1024
        )

    each(4, up_block, 1)
    scatter_up.start()

    scatter_dn.near()
    sum_nb.own(t1)
    sum_nb.total()

    def second_back(at):
        grad_nb = sum_nb.rows(at)
        n, rstd = norm_parts(rmid[at, :])
        vg[4:5, :] += jnp.sum(grad_nb * n, axis=0, keepdims=True)
        vg[5:6, :] += jnp.sum(grad_nb, axis=0, keepdims=True)
        mid = gd[g, at, :].astype(F32) + norm_back(grad_nb * vec[4:5, :], n, rstd)
        gmid[at, :] = mid
        low_mid = mid.astype(BF)
        gatt[1, at, :] = low_mid
        vg[3:4, :] += jnp.sum(low_mid.astype(F32), axis=0, keepdims=True)

    each_rows(256, 32, second_back)

    def grad_o_part(to_g):
        total = jnp.zeros((256, 256), F32)
        for k in range(4):
            total += mm_nt(
                gatt[1, :, 256 * k : 256 * k + 256], wout[k, pl.ds(2 * to_g, 2)].reshape(256, 256)
            )
        return total.astype(BF)

    for link in (nb_pass, nb_across, nb_twin, group_gd.second):
        link.sent()
    go_links = []
    for rel in range(3):
        att_links[rel].sent()
        asend[rel] = grad_o_part(rel_g[rel])
        go_links.append(Link().send(asend.at[rel], go.at[g], rel_dev[rel]))
    go[g] = grad_o_part(g)

    def wog_partial(k, into):
        for j in range(4):
            into[:, 256 * j : 256 * j + 256] = mm_tn(
                att[:, 256 * j : 256 * j + 256], gatt[1, :, part(256 * k, 256)]
            ).astype(into.dtype)

    sum_nb.release()
    scatter_dn.second()
    for rel in (TWIN, ACROSS, DIAG):
        go_links[rel].got(go.at[rel_g[rel]])
    sum_wog = GroupSum(
        slots(gd, rel_g), slots(nb, rel_g), wog_partial, slots(nb, (rel_g[ACROSS], g, g))
    )
    sum_wog.first()
    sum_wog.second()
    sum_wog.second_send()
    sum_wog.third()
    sum_wog.own(nb.at[g])

    def attend_back(row):
        keys = proj[row, :, 256:512]
        values = proj[row, :, 512:768]
        queries = proj[row, :, 0:256]
        grad_rows = go[row]
        zero = jnp.zeros_like(keys)
        for buf in (t2, t3, t4):
            buf[...] = jnp.zeros_like(buf)

        def head(k):
            mine = head_of == k
            probs = pr[row * 4 + k]
            g_head = jnp.where(mine, grad_rows, zero)
            t4[...] += mm_tn(probs, g_head)
            grad_p = mm_nt(g_head, values)
            wide = probs.astype(F32)
            grad_s = wide * (grad_p - jnp.sum(grad_p * wide, axis=-1, keepdims=True))
            low_s = (grad_s * 0.125).astype(BF)
            t2[...] += mm(low_s, jnp.where(mine, keys, zero))
            t3[...] += mm_tn(low_s, jnp.where(mine, queries, zero))

        each(4, head, HEAD_UNROLL)
        proj[row, :, 0:256] = t2[...].astype(BF)
        proj[row, :, 256:512] = t3[...].astype(BF)
        proj[row, :, 512:768] = t4[...].astype(BF)

    def na_partial(row, into):
        def block(k):
            into[:, part(k * 256, 256)] = mm_nt(
                proj[row], wqkv[pl.ds(2 * k, 2)].reshape(256, 768)
            ).astype(into.dtype)

        each(4, block)

    sum_na = GroupSum(slots(xs, (0, 1, 2)), slots(xr, (0, 1, 2)), na_partial)
    scatter_dn.own()
    attend_back(rel_g[DIAG])
    sum_na.first()
    scatter_up.end_to_end()
    attend_back(rel_g[ACROSS])
    sum_na.second()
    sum_na.second_send()
    attend_back(rel_g[TWIN])
    sum_na.third()
    scatter_up.near()
    sum_wog.total()
    scatter_out = Scatter(g_out, y_out, z_out, f_out, h)
    for j in range(4):
        at = slice(256 * j, 256 * j + 256)
        g_out[2 * j : 2 * j + 2] = (
            nb[g, :, at].astype(F32) + nb[rel_g[ACROSS], :, at].astype(F32)
            + nb[rel_g[TWIN], :, at].astype(F32)
        ).astype(BF).reshape(2, 128, 256)
    scatter_out.start()
    attend_back(g)
    sum_na.own(t1)

    scatter_qkv = Scatter(g_qkv, y_qkv, z_qkv, f_qkv, h)
    scatter_in = Scatter(g_in, y_in, z_in, f_in, None)

    def qkv_block(k):
        at = part(k * 256, 256)
        lhs = na[:, :, at].reshape(1024, 256)
        g_qkv[pl.ds(2 * k, 2)] = mm_tn(lhs, proj[...].reshape(1024, 768)).astype(BF).reshape(
            2, 128, 768
        )

    each(4, qkv_block)
    scatter_qkv.start()
    scatter_up.second()

    sum_na.total()

    def first_back(at):
        grad_na = sum_na.rows(at)
        n, rstd = norm_parts(rin[at, :])
        vg[1:2, :] += jnp.sum(grad_na * n, axis=0, keepdims=True)
        vg[2:3, :] += jnp.sum(grad_na, axis=0, keepdims=True)
        low_in = (gmid[at, :] + norm_back(grad_na * vec[1:2, :], n, rstd)).astype(BF)
        gatt[0, at, :] = low_in
        vg[0:1, :] += jnp.sum(low_in.astype(F32), axis=0, keepdims=True)

    each_rows(256, 32, first_back)
    for k in range(4):
        vg[7 + k : 8 + k, :] = jnp.where(g == k, bup[1:2, :], 0.0)
    for j in range(8):
        vq[j % 2, j // 2] = vg[:, 128 * j : 128 * j + 128]
    vy_link = Link().send(vq.at[1 - y], vgy, pair_y)

    grad_scaled = jnp.zeros((256, 256), F32)
    for k in range(4):
        grad_scaled += mm_nt(gatt[0, :, 256 * k : 256 * k + 256], win_mat(k))
    level = as_col(small[20:22, :])
    scale_in = lax.rsqrt(1.0 + level * level)
    ngrad[...] = grad_scaled * (level * scale_in)
    stores.append(moved(ngrad, ngrad_hbm))

    def set_at(other_x, other_y, other_core):
        return ((lax.rem(x + other_x, 2) * 2 + lax.rem(y + other_y, 2)) * 2 + lax.rem(c + other_core, 2)) * 4

    home = tok.at[set_at(0, 0, 0) + z]
    tok[set_at(0, 0, 0) + z] = (grad_scaled * scale_in).astype(BF)
    steps = {"own": z, "second": far(2), "near": jnp.where(z < 2, far(3), far(1)), "last": jnp.where(z < 2, far(1), far(3))}

    class Line:
        def __init__(self, ref, first):
            self.first = first
            self.links = {
                d: Link().send(ref, ref, dev(0, d, 0, 0), only={1: z != 3, 3: z != 0}.get(d))
                for d in (2, 1, 3)
            }

        def spot(self, step):
            return self.first + steps[step]

        def got(self, step):
            ref = tok.at[self.spot(step)]
            one, three = self.links[1].at, self.links[3].at
            if step == "second":
                self.links[2].got(ref)
                Link().send(ref, ref, relay_to, only=inner, arrives=jnp.where(z == 2, three, one))
            elif step == "near":
                arrived(jnp.where(z < 2, three, one), ref)
            else:
                arrived(jnp.where(z < 2, one, three), ref)
            return self.spot(step)

    line_own = Line(home, set_at(0, 0, 0))
    tok_x = {}
    by_y = ("own", "second")
    tok_y = {}
    tok_t = {}

    def to_twin(spot, own_plane, key):
        tok_t[own_plane, key] = Link().send(tok.at[spot], tok.at[spot], twin)

    tok_x[0, 0] = Link().send(home, home, across)
    tok_y["own"] = Link().send(home, home, pair_y)
    to_twin(set_at(0, 0, 0) + z, True, (0, "own"))
    sum_out.second_send()

    def wig_partial(k, into):
        into[...] = mm_tn(sc[g], gatt[0, :, part(256 * k, 256)]).astype(into.dtype)

    sum_wig = GroupSum(
        slots(pr, (0, 1, 2)), slots(go, rel_g), wig_partial, slots(go, (rel_g[ACROSS], g, g)), t2
    )
    sum_wig.first()
    scatter_out.end_to_end()
    sum_wig.second()
    sum_wig.second_send()
    sum_wig.third()
    sum_wig.own(t3)
    scatter_dn.last()

    beside = set_at(1, 0, 0) + z
    tok_x[0, 0].got(tok.at[beside])
    line_beside = Line(tok.at[beside], set_at(1, 0, 0))
    to_twin(beside, False, (0, "own"))
    tok_x[1, "own"] = Link().send(tok.at[beside], tok.at[beside], pair_y)

    def tok_from_z(step):
        spot = line_own.got(step)
        tok_y[step] = Link().send(tok.at[spot], tok.at[spot], pair_y)
        to_twin(spot, True, (0, step))

    def tok_from_y(step):
        spot = set_at(0, 1, 0) + steps[step]
        tok_y[step].got(tok.at[spot])
        if step not in by_y:
            tok_x[1, step] = Link().send(tok.at[spot], tok.at[spot], across)
        to_twin(spot, True, (1, step))

    def tok_beside(step):
        spot = line_beside.got(step)
        to_twin(spot, False, (0, step))
        if step in by_y:
            tok_x[1, step] = Link().send(tok.at[spot], tok.at[spot], pair_y)

    def tok_from_x(step):
        spot = set_at(1, 1, 0) + steps[step]
        tok_x[1, step].got(tok.at[spot])
        to_twin(spot, False, (1, step))

    smx_link.got(smx)
    for other_x in (0, 1):
        for yy in (0, 1):
            for core in (0, 1):
                source = sm if other_x == 0 else smx
                for zz in range(4):
                    idr[(other_x * 2 + yy) * 2 + core : (other_x * 2 + yy) * 2 + core + 1, 256 * zz : 256 * zz + 256] = (
                        as_row(source[2 * zz + yy, core, 16:18, :])
                    )

    tile = 400
    base = (f * rows_here).astype(F32)
    tile_row = lax.broadcasted_iota(jnp.int32, (tile, 1024), 0).astype(F32)

    def table_add(other_x, other_y, other_core, begin):
        spot = set_at(other_x, other_y, other_core)
        row = (other_x * 2 + lax.rem(y + other_y, 2)) * 2 + lax.rem(c + other_core, 2)
        ids = idr[pl.ds(row, 1), :] - base

        def block(k):
            at = part(k * tile, tile)
            hit = jnp.where(tile_row == ids - (k * tile).astype(F32), 1.0, 0.0).astype(BF)
            add = mm(hit, tok[pl.ds(spot, 4)].reshape(1024, 256))
            if begin:
                tgrad[at, :] = add
            else:
                tgrad[at, :] += add

        each(rows_here // tile, block, 1)

    def twin_set(from_x, other_y):
        for step in steps:
            tok_t[from_x == 0, (other_y, step)].got(tok.at[set_at(from_x, other_y, 1) + steps[step]])

    tok_from_z("second")
    tok_from_z("near")
    scatter_up.own()
    scatter_qkv.end_to_end()
    tok_from_z("last")
    tok_beside("second")
    table_add(0, 0, 0, True)
    scatter_up.last()
    scatter_out.near()
    tok_from_y("own")
    scatter_qkv.near()
    twin_set(0, 0)
    table_add(0, 0, 1, False)
    sum_wig.total()
    g_in[...] = (
        t3[...] + go[rel_g[ACROSS]].astype(F32) + go[rel_g[TWIN]].astype(F32)
    ).astype(BF).reshape(8, 2, 16, 256)
    scatter_in.start()
    vy_link.got(vgy)
    vq[y] = vq[y] + vgy[...]
    vz_links = [
        Link().send(vq.at[y, to(d)], vgz.at[d - 1], dev(0, d, 0, 0)) for d in (1, 2, 3)
    ]
    tok_from_y("second")
    scatter_qkv.second()
    tok_from_y("near")
    scatter_qkv.own()
    scatter_out.second()
    scatter_out.own()
    tok_from_y("last")
    table_add(0, 1, 0, False)
    tok_beside("near")
    tok_beside("last")
    table_add(1, 0, 0, False)
    twin_set(0, 1)
    table_add(0, 1, 1, False)
    scatter_in.middle()
    scatter_qkv.last()
    for d in (1, 2, 3):
        vz_links[d - 1].got(vgz.at[d - 1])
    vtot = vq[y, z] + vgz[0] + vgz[1] + vgz[2]
    vgf[3] = vtot
    vf_links = [Link().send(vgf.at[3], vgf.at[rel], rel_dev[rel]) for rel in range(3)]
    twin_set(1, 0)
    table_add(1, 0, 1, False)
    scatter_out.last()
    scatter_in.last()
    sum_out.total()

    def out_rows(at):
        whole = rmid[at, :] + sum_out.rows(at) + vec[6:7, :]
        act[at, :] = (whole * lives[at, 0:1]).astype(BF)

    each_rows(256, 32, out_rows)
    stores.append(moved(act, act_hbm))
    sum_out.release()

    for step in steps:
        tok_from_x(step)
    table_add(1, 1, 0, False)
    twin_set(1, 1)
    table_add(1, 1, 1, False)

    def table_rows(at):
        values = tp[c, at, :].astype(F32)
        r = lax.rsqrt(jnp.mean(values * values, axis=1, keepdims=True) + norm_eps)
        row_grad = tgrad[at, :]
        slope = jnp.mean(row_grad * values, axis=1, keepdims=True)
        tgrad[at, :] = r * row_grad - values * (r * r * r * slope)

    for k in range(rows_here // 200):
        at = pl.ds(k * 200, 200)
        table_rows(at)
        stores.append(moved(tgrad.at[at], tgrad_hbm.at[at]))

    for rel in range(3):
        vf_links[rel].got(vgf.at[rel])
    vout[...] = vgf[0] + vgf[1] + vgf[2] + vgf[3]
    for scatter in (scatter_dn, scatter_up, scatter_qkv, scatter_out, scatter_in):
        scatter.finish()
    for k, (src, dst) in enumerate(((f_in, f_in_hbm), (f_qkv, f_qkv_hbm), (f_out, f_out_hbm), (f_up, f_up_hbm), (f_dn, f_dn_hbm), (vout, vout_hbm))):
        stores.append(moved(src, dst))
    for link in list(pending):
        link.sent()
    for store in stores:
        store.wait()


def finish_kernel(
    act_in, ngrad_in, tgrad_in, vout, f_in_hbm, f_qkv_hbm, f_out_hbm, f_up_hbm, f_dn_hbm,
    act, ngrad, tgrad, w_in_hbm, b_in, gain_a, shift_a, w_qkv_hbm, w_out_hbm, b_out, gain_b, shift_b,
    w_up_hbm, b_up, w_dn_hbm, b_dn,
    act_v, ngrad_v, tgrad_v, f_in, f_qkv, f_out, f_up, f_dn, w_in, w_qkv, w_out, w_up, w_dn, sems,
):
    count = [0]

    def moved(src, dst):
        copy = pltpu.make_async_copy(src, dst, sems.at[count[0]])
        count[0] += 1
        copy.start()
        return copy

    load_up = moved(f_up_hbm, f_up)
    load_dn = moved(f_dn_hbm, f_dn)
    load_qkv = moved(f_qkv_hbm, f_qkv)
    load_out = moved(f_out_hbm, f_out)
    load_in = moved(f_in_hbm, f_in)
    passed = [(act_in, act_v, act), (ngrad_in, ngrad_v, ngrad)]
    tile = tgrad_v.shape[0] // 5
    for k in range(5):
        at = pl.ds(k * tile, tile)
        passed.append((tgrad_in.at[at], tgrad_v.at[at], tgrad.at[at]))
    passed = [(moved(src, via), via, dst) for src, via, dst in passed]
    stores = []
    c = lax.rem(lax.axis_index("fsdp"), 2)
    rows = jnp.where(c == 0, vout[...], pltpu.roll(vout[...], 64, 1))
    for k, ref in enumerate((b_in, gain_a, shift_a, b_out, gain_b, shift_b, b_dn)):
        ref[...] = rows[k, 0:64]
    for k in range(4):
        b_up[64 * k : 64 * k + 64] = rows[7 + k, 0:64]
    h = w_out.shape[0]
    low_half = lax.broadcasted_iota(jnp.int32, (h, 128), 1) < 64
    load_up.wait()
    for shard in range(16):
        at = slice(128 * (shard // 2), 128 * (shard // 2) + 128)
        for half in (0, 1):
            first, second = f_up[2 * half, :, at].astype(F32), f_up[2 * half + 1, :, at].astype(F32)
            if shard % 2 == 0:
                both = jnp.where(low_half, first, pltpu.roll(second, 64, 1))
            else:
                both = jnp.where(low_half, pltpu.roll(first, 64, 1), second)
            w_up[:, 256 * shard + 128 * half : 256 * shard + 128 * half + 128] = both
    stores.append(moved(w_up, w_up_hbm))
    for load, via, dst in passed:
        load.wait()
        stores.append(moved(via, dst))
    load_dn.wait()
    for g in range(4):
        w_dn[h * g : h * g + h, :] = f_dn[g].astype(F32)
    stores.append(moved(w_dn, w_dn_hbm))
    load_qkv.wait()
    for g in range(4):
        for n in range(3):
            w_qkv[:, 1024 * n + 256 * g : 1024 * n + 256 * g + 256] = f_qkv[
                g, :, 256 * n : 256 * n + 256
            ].astype(F32)
    stores.append(moved(w_qkv, w_qkv_hbm))
    load_out.wait()
    load_in.wait()
    for g in range(4):
        at = slice(256 * g, 256 * g + 256)
        w_in[:, at] = f_in[g].astype(F32)
        w_out[:, at] = f_out[g].astype(F32)
    stores.append(moved(w_out, w_out_hbm))
    stores.append(moved(w_in, w_in_hbm))
    for store in stores:
        store.wait()


def fused_shards(
    token_ids, seq_lengths, noise, noise_level, table, w_in, b_in, gain_first, shift_first, w_qkv,
    w_out, b_out, gain_second, shift_second, w_up, b_up, w_down, b_down, cotangent,
):
    raw = (
        token_ids, seq_lengths, noise_level, b_in, gain_first, shift_first, b_out, gain_second,
        shift_second, b_down, b_up,
    )
    vmem = pl.BlockSpec(memory_space=pltpu.VMEM)
    hbm = pl.BlockSpec(memory_space=pl.ANY)

    def shape(*dims, dtype=BF):
        return jax.ShapeDtypeStruct(dims, dtype)

    rows_here = table.shape[0]
    padded = -(-rows_here // 256) * 256
    outs = [
        shape(256, 1024), shape(256, 256, dtype=F32), shape(rows_here, 256, dtype=F32),
        shape(16, 128, dtype=F32), shape(4, 16, 256), shape(4, 64, 768), shape(4, 64, 256),
        shape(4, 64, 1024), shape(4, 64, 1024),
    ]

    held = [pltpu.VMEM(v.shape, v.dtype) for v in raw] + [pltpu.VMEM((24, 128), F32)]
    held += [pltpu.VMEM(v.shape, v.dtype) for v in (noise, w_in, w_qkv, w_out, w_up, w_down, cotangent)]
    held += [pltpu.VMEM(v.shape, v.dtype) for v in outs]

    def bf(*dims):
        return pltpu.VMEM(dims, BF)

    def fl(*dims):
        return pltpu.VMEM(dims, F32)

    scratch = [
        fl(8, 2, 24, 128), fl(8, 2, 24, 128), fl(2, 24, 128),
        fl(16, 1024), fl(16, 1024), fl(2, 4, 16, 128), fl(4, 16, 128), fl(3, 16, 128),
        fl(4, 16, 128), fl(8, 1024), fl(256, 128), fl(8, 1024),
        bf(2, padded, 256), bf(32, 256, 256), bf(4, 256, 256), bf(4, 8, 2, 16, 256),
        bf(8, 128, 768), bf(4, 8, 128, 256), bf(8, 128, 1024), bf(8, 128, 1024),
        bf(2, 16, 256), bf(64, 768), bf(64, 256), bf(64, 1024),
        fl(256, 1024), fl(256, 1024), fl(256, 1024), fl(256, 1024),
        fl(256, 256), fl(256, 256), fl(256, 256),
        bf(4, 256, 1024), bf(4, 256, 768), bf(16, 256, 256), bf(256, 1024), bf(3, 256, 256),
        bf(4, 256, 1024), bf(4, 256, 1024), bf(8, 128, 1024), bf(4, 256, 1024),
        bf(6, 256, 1024), bf(6, 256, 1024), bf(2, 256, 1024), bf(4, 256, 256),
        bf(8, 2, 16, 256), bf(8, 128, 768), bf(8, 128, 256), bf(8, 128, 1024),
        bf(4, 2, 16, 256), bf(4, 128, 768), bf(4, 128, 256), bf(4, 128, 1024), bf(4, 128, 1024),
        bf(4, 2, 16, 256), bf(4, 128, 768), bf(4, 128, 256), bf(4, 128, 1024), bf(4, 128, 1024),
        pltpu.SemaphoreType.DMA((SEM_COUNT,)), pltpu.SemaphoreType.DMA((SEM_COUNT,)),
        pltpu.SemaphoreType.DMA((45,)),
    ]
    parts = pl.pallas_call(
        layer_kernel,
        out_shape=outs,
        in_specs=[hbm] * 19,
        out_specs=[hbm] * len(outs),
        scratch_shapes=held + scratch,
        compiler_params=pltpu.CompilerParams(
            collective_id=0, has_side_effects=True, vmem_limit_bytes=VMEM_LIMIT
        ),
        cost_estimate=pl.CostEstimate(flops=40 * 10**9, bytes_accessed=30 * 10**6, transcendentals=0),
    )(*raw, noise, table, w_in, w_qkv, w_out, w_up, w_down, cotangent)
    f32 = lambda a: jax.ShapeDtypeStruct(a.shape, F32)
    finals = [
        outs[0], outs[1], outs[2], f32(w_in), f32(b_in), f32(gain_first), f32(shift_first),
        f32(w_qkv), f32(w_out), f32(b_out), f32(gain_second), f32(shift_second), f32(w_up),
        f32(b_up), f32(w_down), f32(b_down),
    ]
    return tuple(
        pl.pallas_call(
            finish_kernel,
            out_shape=finals,
            in_specs=[hbm] * 3 + [vmem] + [hbm] * 5,
            out_specs=[vmem if len(v.shape) == 1 else hbm for v in finals],
            scratch_shapes=[pltpu.VMEM(v.shape, v.dtype) for v in outs[:3] + outs[4:]]
            + [pltpu.VMEM(finals[k].shape, F32) for k in (3, 7, 8, 12, 14)]
            + [pltpu.SemaphoreType.DMA((24,))],
            compiler_params=pltpu.CompilerParams(vmem_limit_bytes=VMEM_LIMIT),
        )(*parts)
    )


def solution(mesh):
    in_specs = (
        P(("dp", "fsdp")),
        P(("dp", "fsdp"), None),
        P(("dp", "fsdp"), None),
        P(("dp", "fsdp")),
        P("fsdp", None),
        P("fsdp", None),
        P("fsdp"),
        P("fsdp"),
        P("fsdp"),
        P("fsdp", None),
        P("fsdp", None),
        P("fsdp"),
        P("fsdp"),
        P("fsdp"),
        P("fsdp", None),
        P("fsdp"),
        P("fsdp", None),
        P("fsdp"),
        P(("dp", "fsdp"), None),
    )
    out_specs = (
        P(("dp", "fsdp"), None),
        P(("dp", "fsdp"), None),
        P("fsdp", None),
        P("fsdp", None),
        P("fsdp"),
        P("fsdp"),
        P("fsdp"),
        P("fsdp", None),
        P("fsdp", None),
        P("fsdp"),
        P("fsdp"),
        P("fsdp"),
        P("fsdp", None),
        P("fsdp"),
        P("fsdp", None),
        P("fsdp"),
    )
    fused = mesh.shape["dp"] == 2 and mesh.shape["fsdp"] == 16
    body = fused_shards if fused else shards
    return jax.shard_map(body, mesh=mesh, in_specs=in_specs, out_specs=out_specs, check_vma=False)
```

```python
import jax
import jax.numpy as jnp
from jax import lax
from jax.experimental import pallas as pl
from jax.experimental.pallas import tpu as pltpu
from jax.sharding import PartitionSpec as P

HEADS = 16
VOCAB = 32000


norm_eps = 1e-05


def standardize(resid):
    centred = resid - jnp.mean(resid, axis=-1, keepdims=True)
    spread = jnp.mean(centred * centred, axis=-1, keepdims=True)
    return centred * lax.rsqrt(spread + norm_eps)


def row_normalize(tok_rows):
    return tok_rows * lax.rsqrt(jnp.mean(tok_rows * tok_rows, axis=1, keepdims=True) + norm_eps)


def exact_gelu(pre_act):
    return jax.nn.gelu(pre_act, approximate=False)


def split_heads(projected):
    tok_count = projected.shape[0]
    width = projected.shape[1] // 3
    head_size = width // HEADS
    key_heads = projected[:, width : 2 * width].reshape(tok_count, HEADS, head_size)
    value_heads = projected[:, 2 * width :].reshape(tok_count, HEADS, head_size)
    row_block = min(512, tok_count)
    query_blocks = projected[:, :width].reshape(tok_count // row_block, row_block, HEADS, head_size)
    return (query_blocks, key_heads, value_heads, row_block)


def block_scores(query_block, key_heads, seg_block, segment):
    raw_scores = (
        jnp.einsum("qhd,khd->hqk", query_block, key_heads, preferred_element_type=jnp.float32)
        * 0.125
    )
    same_seq = seg_block[:, None] == segment[None, :]
    return jnp.where(same_seq[None, :, :], raw_scores, -1000000000.0)


def attention_forward(projected, segment):
    query_blocks, key_heads, value_heads, row_block = split_heads(projected)
    seg_blocks = segment.reshape(-1, row_block)

    def block_step(items_in):
        query_block, seg_block = items_in
        scores = block_scores(query_block, key_heads, seg_block, segment)
        row_max = jnp.max(scores, axis=-1, keepdims=True)
        exp_scores = jnp.exp(scores - row_max)
        row_total = jnp.sum(exp_scores, axis=-1, keepdims=True)
        soft_probs = (exp_scores / row_total).astype(jnp.bfloat16)
        attended = jnp.einsum(
            "hqk,khd->qhd", soft_probs, value_heads, preferred_element_type=jnp.float32
        )
        return (attended, (row_max + jnp.log(row_total))[:, :, 0])

    attended, log_total = lax.map(block_step, (query_blocks, seg_blocks))
    return (attended.reshape(projected.shape[0], -1), log_total)


def attention_backward(projected, segment, log_total, grad_attended):
    query_blocks, key_heads, value_heads, row_block = split_heads(projected)
    seg_blocks = segment.reshape(-1, row_block)
    grad_blocks = grad_attended.reshape(query_blocks.shape)

    def block_step(totals, items_in):
        grad_keys, grad_values = totals
        query_block, seg_block, log_block, grad_block = items_in
        scores = block_scores(query_block, key_heads, seg_block, segment)
        soft_probs = jnp.exp(scores - log_block[:, :, None])
        grad_values = grad_values + jnp.einsum(
            "hqk,qhd->khd",
            soft_probs.astype(jnp.bfloat16),
            grad_block,
            preferred_element_type=jnp.float32,
        )
        grad_probs = jnp.einsum(
            "qhd,khd->hqk", grad_block, value_heads, preferred_element_type=jnp.float32
        )
        grad_scores = soft_probs * (
            grad_probs - jnp.sum(grad_probs * soft_probs, axis=-1, keepdims=True)
        )
        scaled_grad = (grad_scores * 0.125).astype(jnp.bfloat16)
        grad_query = jnp.einsum(
            "hqk,khd->qhd", scaled_grad, key_heads, preferred_element_type=jnp.float32
        )
        grad_keys = grad_keys + jnp.einsum(
            "hqk,qhd->khd", scaled_grad, query_block, preferred_element_type=jnp.float32
        )
        return ((grad_keys, grad_values), grad_query.astype(jnp.bfloat16))

    zero_heads = jnp.zeros(key_heads.shape, jnp.float32)
    (grad_keys, grad_values), grad_queries = lax.scan(
        block_step, (zero_heads, zero_heads), (query_blocks, seg_blocks, log_total, grad_blocks)
    )
    tok_count = projected.shape[0]
    return jnp.concatenate(
        [
            grad_queries.reshape(tok_count, -1),
            grad_keys.astype(jnp.bfloat16).reshape(tok_count, -1),
            grad_values.astype(jnp.bfloat16).reshape(tok_count, -1),
        ],
        axis=1,
    )


def shards(
    token_ids,
    seq_lengths,
    noise,
    noise_level,
    table,
    w_in,
    b_in,
    gain_first,
    shift_first,
    w_qkv,
    w_out,
    b_out,
    gain_second,
    shift_second,
    w_up,
    b_up,
    w_down,
    b_down,
    cotangent,
):
    tok_count = token_ids.shape[0]
    row_count = table.shape[0]
    group_ids = lax.all_gather(token_ids, "fsdp", axis=0, tiled=True)
    first_row = lax.axis_index("fsdp") * row_count
    owned = (group_ids[:, None] == first_row + jnp.arange(row_count)[None, :]).astype(jnp.bfloat16)
    owned_rows = jnp.dot(owned, table, preferred_element_type=jnp.float32).astype(jnp.bfloat16)
    tok_rows = lax.psum_scatter(owned_rows, "fsdp", scatter_dimension=0, tiled=True)
    tok_rows = tok_rows.astype(jnp.float32)
    vectors = (b_in, gain_first, shift_first, b_out, gain_second, shift_second, b_up, b_down)
    vec_all = lax.all_gather(jnp.concatenate(vectors), "fsdp", axis=0, tiled=False)
    vec_at = [0]
    for vector in vectors:
        vec_at.append(vec_at[-1] + vector.shape[0])
    (
        b_in_all,
        gain_first_all,
        shift_first_all,
        b_out_all,
        gain_second_all,
        shift_second_all,
        b_up_all,
        b_down_all,
    ) = [vec_all[:, lo:hi].reshape(-1) for lo, hi in zip(vec_at[:-1], vec_at[1:])]
    w_in_all = lax.all_gather(w_in, "fsdp", axis=0, tiled=True)
    w_qkv_all = lax.all_gather(w_qkv, "fsdp", axis=0, tiled=True)
    w_out_all = lax.all_gather(w_out, "fsdp", axis=0, tiled=True)
    w_up_all = lax.all_gather(w_up, "fsdp", axis=0, tiled=True)
    w_down_all = lax.all_gather(w_down, "fsdp", axis=0, tiled=True)
    seq_ends = jnp.cumsum(seq_lengths[0], dtype=jnp.int32)
    positions = jnp.arange(tok_count, dtype=jnp.int32)
    segment = jnp.sum((positions[:, None] >= seq_ends[None, :]).astype(jnp.int32), axis=1)
    live_rows = (segment < seq_lengths.shape[1]).astype(jnp.float32)[:, None]
    embedded = row_normalize(tok_rows)
    scale_in = lax.rsqrt(1.0 + noise_level * noise_level)[:, None]
    scaled = ((embedded + noise_level[:, None] * noise.astype(jnp.float32)) * scale_in).astype(
        jnp.bfloat16
    )
    resid_in = jnp.dot(scaled, w_in_all, preferred_element_type=jnp.float32) + b_in_all.astype(
        jnp.float32
    )
    std_first, first_pull = jax.vjp(standardize, resid_in)
    normed_a = (
        std_first * gain_first_all.astype(jnp.float32) + shift_first_all.astype(jnp.float32)
    ).astype(jnp.bfloat16)
    projected = jnp.dot(normed_a, w_qkv_all, preferred_element_type=jnp.float32).astype(
        jnp.bfloat16
    )
    attended, log_total = attention_forward(projected, segment)
    attended = attended.astype(jnp.bfloat16)
    resid_mid = (
        resid_in
        + jnp.dot(attended, w_out_all, preferred_element_type=jnp.float32)
        + b_out_all.astype(jnp.float32)
    )
    std_second, second_pull = jax.vjp(standardize, resid_mid)
    normed_b = (
        std_second * gain_second_all.astype(jnp.float32) + shift_second_all.astype(jnp.float32)
    ).astype(jnp.bfloat16)
    pre_act = jnp.dot(normed_b, w_up_all, preferred_element_type=jnp.float32) + b_up_all.astype(
        jnp.float32
    )
    activated, gelu_pull = jax.vjp(exact_gelu, pre_act)
    hidden = activated.astype(jnp.bfloat16)
    resid_out = (
        resid_mid
        + jnp.dot(hidden, w_down_all, preferred_element_type=jnp.float32)
        + b_down_all.astype(jnp.float32)
    )
    activations = (resid_out * live_rows).astype(jnp.bfloat16)
    grad_out = cotangent.astype(jnp.float32) * live_rows
    grad_down = grad_out.astype(jnp.bfloat16)
    b_down_term = jnp.sum(grad_down.astype(jnp.float32), axis=0)
    w_down_term = jnp.einsum("tf,td->fd", hidden, grad_down, preferred_element_type=jnp.float32)
    grad_hidden = jnp.einsum("td,fd->tf", grad_down, w_down_all, preferred_element_type=jnp.float32)
    grad_act = gelu_pull(grad_hidden)[0].astype(jnp.bfloat16)
    b_up_term = jnp.sum(grad_act.astype(jnp.float32), axis=0)
    w_up_term = jnp.einsum("td,tf->df", normed_b, grad_act, preferred_element_type=jnp.float32)
    grad_nb = jnp.einsum("tf,df->td", grad_act, w_up_all, preferred_element_type=jnp.float32)
    gain_second_term = jnp.sum(grad_nb * std_second, axis=0)
    shift_second_term = jnp.sum(grad_nb, axis=0)
    grad_mid = grad_out + second_pull(grad_nb * gain_second_all.astype(jnp.float32))[0]
    grad_att = grad_mid.astype(jnp.bfloat16)
    b_out_term = jnp.sum(grad_att.astype(jnp.float32), axis=0)
    w_out_term = jnp.einsum("tc,td->cd", attended, grad_att, preferred_element_type=jnp.float32)
    grad_attended = jnp.einsum(
        "td,cd->tc", grad_att, w_out_all, preferred_element_type=jnp.float32
    ).astype(jnp.bfloat16)
    grad_proj = attention_backward(projected, segment, log_total, grad_attended)
    w_qkv_term = jnp.einsum("td,te->de", normed_a, grad_proj, preferred_element_type=jnp.float32)
    grad_na = jnp.einsum("te,de->td", grad_proj, w_qkv_all, preferred_element_type=jnp.float32)
    gain_first_term = jnp.sum(grad_na * std_first, axis=0)
    shift_first_term = jnp.sum(grad_na, axis=0)
    grad_in = grad_mid + first_pull(grad_na * gain_first_all.astype(jnp.float32))[0]
    grad_pin = grad_in.astype(jnp.bfloat16)
    b_in_term = jnp.sum(grad_pin.astype(jnp.float32), axis=0)
    w_in_term = jnp.einsum("te,td->ed", scaled, grad_pin, preferred_element_type=jnp.float32)
    grad_scaled = jnp.einsum("td,ed->te", grad_pin, w_in_all, preferred_element_type=jnp.float32)
    noise_grad = grad_scaled * noise_level[:, None] * scale_in
    grad_embedded = grad_scaled * scale_in
    all_ids = lax.all_gather(token_ids, ("dp", "fsdp"), axis=0, tiled=True)
    all_grads = lax.all_gather(
        grad_embedded.astype(jnp.bfloat16), ("dp", "fsdp"), axis=0, tiled=True
    )
    owners = (first_row + jnp.arange(row_count)[:, None] == all_ids[None, :]).astype(jnp.bfloat16)
    row_grad = jnp.dot(owners, all_grads, preferred_element_type=jnp.float32)
    own_table = table.astype(jnp.float32)
    unused_rows, table_pull = jax.vjp(row_normalize, own_table)
    table_part = table_pull(row_grad)[0]

    def reduce_matrix(term):
        part = lax.psum_scatter(
            term.astype(jnp.bfloat16), "fsdp", scatter_dimension=0, tiled=True
        )
        return lax.psum(part, "dp").astype(jnp.float32)

    vec_terms = (
        b_in_term,
        gain_first_term,
        shift_first_term,
        b_out_term,
        gain_second_term,
        shift_second_term,
        b_up_term,
        b_down_term,
    )
    shard_count = lax.axis_size("fsdp")
    vec_term = jnp.concatenate([v.reshape(shard_count, -1) for v in vec_terms], axis=1)
    vec_part = lax.psum(vec_term, ("dp", "fsdp"))
    own_vec = lax.dynamic_index_in_dim(vec_part, lax.axis_index("fsdp"), 0, keepdims=False)
    vec_grads = [own_vec[lo:hi] for lo, hi in zip(vec_at[:-1], vec_at[1:])]
    return (
        activations,
        noise_grad,
        table_part,
        reduce_matrix(w_in_term),
        vec_grads[0],
        vec_grads[1],
        vec_grads[2],
        reduce_matrix(w_qkv_term),
        reduce_matrix(w_out_term),
        vec_grads[3],
        vec_grads[4],
        vec_grads[5],
        reduce_matrix(w_up_term),
        vec_grads[6],
        reduce_matrix(w_down_term),
        vec_grads[7],
    )


BF = jnp.bfloat16
F32 = jnp.float32
MESH_ID = pl.DeviceIdType.MESH
SEM_COUNT = 400
ROW_UNROLL = 8
HEAD_UNROLL = 4
EACH_UNROLL = 4
VMEM_LIMIT = 63 * 2**20
NT = (((1,), (1,)), ((), ()))
TN = (((0,), (0,)), ((), ()))
DIAG, ACROSS, TWIN = 0, 1, 2
FLIPS = ((1, 1), (1, 0), (0, 1))


def mm(a, b):
    return jnp.dot(a, b, preferred_element_type=F32)


def mm_nt(a, b):
    return lax.dot_general(a, b, NT, preferred_element_type=F32)


def mm_tn(a, b):
    return lax.dot_general(a, b, TN, preferred_element_type=F32)


def part(start, size):
    return pl.ds(pl.multiple_of(start, size), size)


def as_row(pair):
    return jnp.concatenate([pair[0:1, :], pair[1:2, :]], axis=1)


def as_col(pair):
    eye = lax.broadcasted_iota(jnp.int32, (128, 128), 0) == lax.broadcasted_iota(
        jnp.int32, (128, 128), 1
    )
    cols = [
        jnp.sum(jnp.where(eye, pair[k : k + 1, :], 0.0), axis=1, keepdims=True) for k in (0, 1)
    ]
    return jnp.concatenate(cols, axis=0)


def norm_parts(v):
    centred = v - jnp.mean(v, axis=-1, keepdims=True)
    rstd = lax.rsqrt(jnp.mean(centred * centred, axis=-1, keepdims=True) + norm_eps)
    return centred * rstd, rstd


def norm_back(u, n, rstd):
    return rstd * (
        u - jnp.mean(u, axis=-1, keepdims=True) - n * jnp.mean(u * n, axis=-1, keepdims=True)
    )


def layer_kernel(
    ids_hbm, lengths_hbm, level_hbm, b_in_hbm, gain_a_hbm, shift_a_hbm, b_out_hbm, gain_b_hbm, shift_b_hbm,
    b_dn_hbm, b_up_hbm, noise_hbm, table, w_in_hbm, w_qkv_hbm, w_out_hbm, w_up_hbm, w_down_hbm, cot_hbm,
    act_hbm, ngrad_hbm, tgrad_hbm, vout_hbm, f_in_hbm, f_qkv_hbm, f_out_hbm, f_up_hbm, f_dn_hbm,
    ids_v, lengths_v, level_v, b_in_v, gain_a_v, shift_a_v, b_out_v, gain_b_v, shift_b_v, b_dn_v, b_up_v,
    small, noise, w_in, w_qkv, w_out, w_up, w_down, cot,
    act, ngrad, tgrad, vout, f_in, f_qkv, f_out, f_up, f_dn,
    sm, smx, gsm, vec, vg, vq, vgy, vgz, vgf, bup, lives, idr,
    tp, tok, sc, win, wqkv, wout, wup, wdn, s_in, s_qkv, s_out, s_up,
    rin, rmid, gmid, t1, t2, t3, t4, na, proj, pr, att, asend, nb, gd, hid, ga,
    xs, xr, gatt, go, g_in, g_qkv, g_out, g_dn,
    y_in, y_qkv, y_out, y_up, y_dn, z_in, z_qkv, z_out, z_up, z_dn,
    ss, rr, ls,
):
    x = lax.axis_index("dp")
    f = lax.axis_index("fsdp")
    z, y, c = f // 4, lax.rem(f // 2, 2), lax.rem(f, 2)
    q = 2 * z + y
    g = 2 * x + c
    rows_here = table.shape[0]

    def dev(dx, dz, dy, dc):
        xx = lax.rem(x + dx, 2)
        zz = lax.rem(z + dz, 4)
        yy = lax.rem(y + dy, 2)
        cc = lax.rem(c + dc, 2)
        return (xx, zz * 4 + yy * 2 + cc)

    twin = dev(0, 0, 0, 1)
    across = dev(1, 0, 0, 0)
    pair_y = dev(0, 0, 1, 0)
    relay_to = (x, jnp.where(z == 2, 3, 0) * 4 + y * 2 + c)
    rel_dev = [dev(dx, 0, 0, dc) for dx, dc in FLIPS]
    rel_g = [2 * lax.rem(x + dx, 2) + lax.rem(c + dc, 2) for dx, dc in FLIPS]
    other_c = 1 - c

    def far(d):
        return lax.rem(z + 4 - d, 4)

    def to(d):
        return lax.rem(z + d, 4)

    sems = [0]
    pending = []
    inner = jnp.logical_or(z == 1, z == 2)
    outer = jnp.logical_not(inner)

    class Link:
        def __init__(self):
            self.at = sems[0]
            sems[0] += 1
            assert sems[0] <= SEM_COUNT

        def send(self, src, dst, device, arrives=None, only=None):
            self.only = only
            self.copy = pltpu.make_async_remote_copy(
                src_ref=src, dst_ref=dst, send_sem=ss.at[self.at],
                recv_sem=rr.at[self.at if arrives is None else arrives],
                device_id=device, device_id_type=MESH_ID,
            )
            if only is None:
                self.copy.start()
            else:
                pl.when(only)(self.copy.start)
            pending.append(self)
            return self

        def sent(self):
            pending.remove(self)
            if self.only is None:
                self.copy.wait_send()
            else:
                pl.when(self.only)(self.copy.wait_send)

        def got(self, ref):
            arrived(self.at, ref)

    def arrived(at, ref):
        pltpu.make_async_remote_copy(
            src_ref=ref, dst_ref=ref, send_sem=ss.at[0], recv_sem=rr.at[at],
            device_id=twin, device_id_type=MESH_ID,
        ).wait_recv()

    def each_rows(count, size, body, unroll=ROW_UNROLL):
        def step(i, carry):
            body(part(i * size, size))
            return carry

        lax.fori_loop(0, count // size, step, 0, unroll=unroll)

    def each(count, body, unroll=EACH_UNROLL):
        def step(i, carry):
            body(i)
            return carry

        lax.fori_loop(0, count, step, 0, unroll=unroll)

    local = [0]
    stores = []

    def moved(src, dst):
        copy = pltpu.make_async_copy(src, dst, ls.at[local[0]])
        local[0] += 1
        copy.start()
        return copy

    vectors = (b_in_v, gain_a_v, shift_a_v, b_out_v, gain_b_v, shift_b_v, b_dn_v)
    load_small = [
        moved(src, dst)
        for src, dst in (
            (ids_hbm, ids_v), (lengths_hbm, lengths_v), (level_hbm, level_v), (b_in_hbm, b_in_v),
            (gain_a_hbm, gain_a_v), (shift_a_hbm, shift_a_v), (b_out_hbm, b_out_v),
            (gain_b_hbm, gain_b_v), (shift_b_hbm, shift_b_v), (b_dn_hbm, b_dn_v), (b_up_hbm, b_up_v),
        )
    ]
    load_in = moved(w_in_hbm, w_in)
    load_qkv = moved(w_qkv_hbm, w_qkv)
    load_cot = moved(cot_hbm, cot)
    own_table = moved(table, tp.at[c, pl.ds(0, rows_here)])
    load_noise = moved(noise_hbm, noise)
    load_out = moved(w_out_hbm, w_out)
    load_up = moved(w_up_hbm, w_up)
    load_down = moved(w_down_hbm, w_down)

    barrier = pltpu.get_barrier_semaphore()
    peers = [dev(0, d, 0, dc) for d in (1, 2, 3) for dc in (0, 1)] + rel_dev + [pair_y]
    for peer in peers:
        pl.semaphore_signal(barrier, inc=1, device_id=peer, device_id_type=MESH_ID)
    pl.semaphore_wait(barrier, len(peers))

    class GroupGather:
        def __init__(self, at):
            self.at = at
            self.across = Link().send(at(g), at(g), across)
            self.twin = Link().send(at(g), at(g), twin)

        def hop(self):
            self.across.got(self.at(rel_g[ACROSS]))
            self.second = Link().send(self.at(rel_g[ACROSS]), self.at(rel_g[ACROSS]), twin)

        def got_twin(self):
            self.twin.got(self.at(rel_g[TWIN]))

        def got_diag(self):
            self.second.got(self.at(rel_g[DIAG]))

    class Gather:
        def __init__(self, whole, mine, theirs, height, twins=None, relay=True):
            self.whole, self.height, self.relay = whole, height, relay
            places = (self.sub(q, c), self.sub(q, c, twins))
            self.links = {}
            for d in (0, 2, 1, 3):
                only = {1: z != 3, 3: z != 0}.get(d) if relay else None
                for dc in (1, 0):
                    if (d, dc) != (0, 0):
                        self.links[d, dc] = Link().send(
                            theirs if dc else mine, places[dc], dev(0, d, 0, dc), only=only
                        )

        def sub(self, block, core, whole=None):
            whole = self.whole if whole is None else whole
            if self.height is None:
                return whole.at[block, core]
            return whole.at[block, part(core * self.height, self.height)]

        def over_y(self, block):
            return Link().send(self.whole.at[block], self.whole.at[block], pair_y)

        def own(self):
            self.links[0, 1].got(self.sub(q, other_c))
            self.y_own = self.over_y(q)

        def second(self):
            block = 2 * far(2) + y
            for dc in (1, 0):
                ref = self.sub(block, other_c if dc else c)
                self.links[2, dc].got(ref)
                if self.relay:
                    Link().send(
                        ref, ref, relay_to, only=inner,
                        arrives=jnp.where(z == 2, self.links[3, dc].at, self.links[1, dc].at),
                    )
            self.y_second = self.over_y(block)

        def near(self):
            self.y_near = self.one(3, 1)

        def last(self):
            self.y_last = self.one(1, 3)

        def one(self, low, high):
            block = 2 * jnp.where(z < 2, far(low), far(high)) + y
            for dc in (1, 0):
                arrived(
                    jnp.where(z < 2, self.links[low, dc].at, self.links[high, dc].at),
                    self.sub(block, other_c if dc else c),
                )
            return self.over_y(block)

        def forward(self):
            self.second()
            self.near()
            self.last()

        def finish(self):
            self.y_own.got(self.whole.at[2 * z + 1 - y])
            self.y_second.got(self.whole.at[2 * far(2) + 1 - y])
            self.y_near.got(self.whole.at[2 * jnp.where(z < 2, far(3), far(1)) + 1 - y])
            self.y_last.got(self.whole.at[2 * jnp.where(z < 2, far(1), far(3)) + 1 - y])

    class YFirstGather(Gather):
        def __init__(self, whole, mine, theirs, height):
            self.whole, self.height, self.relay = whole, height, True
            self.y_links = [
                Link().send(theirs if dc else mine, self.sub(q, c), dev(0, 0, 1, dc)) for dc in (0, 1)
            ]
            self.mine, self.theirs = mine, theirs

        def along(self):
            Gather.__init__(self, self.whole, self.mine, self.theirs, self.height)

        def cross(self):
            block = 2 * z + 1 - y
            for dc in (0, 1):
                self.y_links[dc].got(self.sub(block, other_c if dc else c))
            ref = self.whole.at[block]
            self.beside = {
                d: Link().send(ref, ref, dev(0, d, 0, 0), only={1: z != 3, 3: z != 0}.get(d))
                for d in (2, 1, 3)
            }

        def over_y(self, block):
            return None

        def second(self):
            Gather.second(self)
            ref = self.whole.at[2 * far(2) + 1 - y]
            self.beside[2].got(ref)
            Link().send(
                ref, ref, relay_to, only=inner,
                arrives=jnp.where(z == 2, self.beside[3].at, self.beside[1].at),
            )

        def finish(self):
            self.links[0, 1].got(self.sub(q, other_c))
            self.near()
            self.last()
            for d in (1, 3):
                self.beside[d].got(self.whole.at[2 * far(d) + 1 - y])

    for load in load_small:
        load.wait()
    lane_at = lax.broadcasted_iota(jnp.int32, (1, 128), 1)
    small[...] = jnp.zeros_like(small)

    def put_half(row, shard):
        small[row : row + 1, :] = jnp.where(
            lane_at // 64 == c, jnp.concatenate([shard, shard], axis=1), 0.0
        )

    def put_pair(row, line):
        small[row : row + 1, :] = line[:, 0:128]
        small[row + 1 : row + 2, :] = line[:, 128:256]

    for k, v in enumerate(vectors):
        put_half(k, v[...].astype(F32).reshape(1, 64))
    up_shard = b_up_v[...].astype(F32).reshape(1, 256)
    for k in range(4):
        put_half(7 + k, up_shard[:, 64 * k : 64 * k + 64])
    put_pair(16, ids_v[...].astype(F32).reshape(1, 256))
    put_pair(20, level_v[...].reshape(1, 256))
    lengths = lengths_v[...].astype(F32)
    slot_at = lax.broadcasted_iota(jnp.int32, lengths.shape, 1)
    spots = (
        lax.broadcasted_iota(jnp.int32, (2, 128), 0) * 128
        + lax.broadcasted_iota(jnp.int32, (2, 128), 1)
    ).astype(F32)
    slot_of = jnp.zeros((2, 128), F32)
    for k in range(8):
        end = jnp.sum(jnp.where(slot_at <= k, lengths, 0.0), axis=1, keepdims=True)
        slot_of += jnp.where(spots >= end, 1.0, 0.0)
    small[18:20, :] = slot_of
    sm[q, c] = small[...]
    small_links = [Link().send(small, gsm.at[rel], rel_dev[rel]) for rel in (DIAG, ACROSS)]
    gather_small = Gather(sm, small, small, None, relay=False)

    own_rows = tp.at[c, pl.ds(0, rows_here)]
    table_link = Link().send(table, own_rows, twin)
    spare = tp.shape[1] - rows_here
    if spare:
        for core in (0, 1):
            tp[core, pl.ds(rows_here, spare), :] = jnp.zeros((spare, tp.shape[2]), BF)

    def pack(whole, spare_buf, height, pick):
        mine, theirs = pick(g), pick(2 * x + other_c)
        whole[q, part(c * height, height), :] = mine
        spare_buf[...] = theirs

    h = w_qkv.shape[0]
    hin = w_in.shape[0]

    def cols(ref, start, size=256):
        return ref[:, part(start, size)]

    win_at, wout_at = win.at[g], wout.at[g]
    load_in.wait()
    load_qkv.wait()
    win_at[q, c] = cols(w_in, 256 * g)
    s_in[0] = cols(w_in, 256 * (2 * x + other_c))
    gather_in = Gather(win_at, win_at.at[q, c], s_in.at[0], None, win.at[2 * x + other_c], relay=False)
    pack(
        wqkv, s_qkv, h,
        lambda k: jnp.concatenate([cols(w_qkv, 1024 * n + 256 * k) for n in (0, 1, 2)], axis=1),
    )
    gather_qkv = Gather(wqkv, wqkv.at[q, part(c * h, h)], s_qkv, h)


    lives[:, 0:1] = jnp.where(as_col(small[18:20, :]) < 7.5, 1.0, 0.0)
    vg[...] = jnp.zeros_like(vg)

    def grad_down_rows(at):
        masked = cot[at, :].astype(F32) * lives[at, 0:1]
        gd[g, at, :] = masked.astype(BF)
        vg[6:7, :] += jnp.sum(masked, axis=0, keepdims=True)

    load_out.wait()
    pack(wout_at, s_out, h, lambda k: cols(w_out, 256 * k))
    gather_out = Gather(
        wout_at, wout_at.at[q, part(c * h, h)], s_out, h, wout.at[2 * x + other_c], relay=False
    )
    load_cot.wait()
    each_rows(256, 32, grad_down_rows)
    group_gd = GroupGather(lambda k: gd.at[k])

    gather_small.own()
    gather_small.forward()

    gather_in.own()
    gather_qkv.own()
    gather_small.finish()
    smx_link = Link().send(sm, smx, across)
    own_table.wait()
    table_link.got(tp.at[other_c, pl.ds(0, rows_here)])
    lane = lax.broadcasted_iota(jnp.int32, (256, tp.shape[1]), 1)

    def look_up(block):
        ids = as_col(sm[block, c, 16:18, :]).astype(jnp.int32)
        total = jnp.zeros((256, 256), F32)
        for core in (0, 1):
            first = (4 * z + 2 * y + core) * rows_here
            hit = jnp.where(lane == ids - first, 1.0, 0.0).astype(BF)
            total += mm(hit, tp[core])
        return total.astype(BF)

    emb_y = [Link() for _ in range(4)]
    for d in range(4):
        tok[d] = look_up(2 * to(d) + 1 - y)
        emb_y[d].send(tok.at[d], tok.at[8 + d], pair_y)

    load_down.wait()
    wdn[q, part(c * h, h), :] = w_down[part(g * h, h), :]
    gather_dn_y = YFirstGather(
        wdn.at[:, :, 512:1024], w_down.at[part(g * h, h), 512:1024],
        w_down.at[part((2 * x + other_c) * h, h), 512:1024], h,
    )

    def own_blocks(d):
        tok[4 + d] = look_up(2 * lax.rem(z + d, 4) + y)

    each(4, own_blocks, 1)
    emb_z = [None]
    for d in (1, 2, 3):
        emb_y[d].got(tok.at[8 + d])
        tok[4 + d] = tok[4 + d] + tok[8 + d]
        emb_z.append(Link().send(tok.at[4 + d], tok.at[11 + d], dev(0, d, 0, 0)))
    emb_y[0].got(tok.at[8])

    for load in (load_noise, load_up):
        load.wait()
    ct = lax.broadcasted_iota(jnp.int32, (h, 128), 1) < 64
    for j in range(8):
        first = w_up[:, part(128 * (4 * j + x), 128)].astype(F32)
        second = w_up[:, part(128 * (4 * j + 2 + x), 128)].astype(F32)
        low = jnp.where(ct, first, pltpu.roll(second, 64, 1)).astype(BF)
        high = jnp.where(ct, pltpu.roll(first, 64, 1), second).astype(BF)
        wup[q, part(c * h, h), 128 * j : 128 * j + 128] = jnp.where(c == 0, low, high)
        s_up[:, 128 * j : 128 * j + 128] = jnp.where(c == 0, high, low)
    gather_in.forward()
    gather_qkv.forward()
    for j in range(8):
        vec[:, 128 * j : 128 * j + 128] = sm[j, 0, 0:16, :] + sm[j, 1, 0:16, :]

    gather_out.own()
    gather_out.forward()
    gather_in.finish()
    group_in = GroupGather(lambda k: win.at[k])
    group_gd.hop()
    rows_sum = tok[4].astype(F32) + tok[8].astype(F32)
    for d in (1, 2, 3):
        emb_z[d].got(tok.at[11 + d])
        rows_sum += tok[11 + d].astype(F32)
    gather_up = Gather(wup, wup.at[q, part(c * h, h)], s_up, h)
    level = as_col(small[20:22, :])
    scale_in = lax.rsqrt(1.0 + level * level)
    embedded = rows_sum * lax.rsqrt(jnp.mean(rows_sum * rows_sum, axis=1, keepdims=True) + norm_eps)
    sc[g] = ((embedded + level * noise[...].astype(F32)) * scale_in).astype(BF)
    group_sc = GroupGather(lambda k: sc.at[k])

    group_in.hop()
    group_in.got_twin()
    group_in.got_diag()

    def win_mat(k):
        return win[k].reshape(256, 256)

    def first_norm(row, keep):
        for k in range(4):
            keep[:, 256 * k : 256 * k + 256] = (
                mm(sc[row], win_mat(k)) + vec[0:1, 256 * k : 256 * k + 256]
            )

        def chunk(at):
            n, _ = norm_parts(keep[at, :])
            na[row, at, :] = (n * vec[1:2, :] + vec[2:3, :]).astype(BF)

        each_rows(256, 32, chunk)

    def project(row):
        def block(k):
            at = part(k * 256, 256)
            proj[row, :, at] = mm(na[row], wqkv[:, :, at].reshape(1024, 256)).astype(BF)

        each(3, block)

    first_norm(g, rin)
    group_sc.hop()
    gather_up.own()
    group_sc.got_twin()
    first_norm(rel_g[TWIN], t1)
    first_norm(rel_g[ACROSS], t1)
    group_sc.got_diag()
    first_norm(rel_g[DIAG], t1)
    gather_qkv.finish()
    each(4, project, 1)
    gather_out.finish()
    group_out = GroupGather(lambda k: wout.at[k])

    head_of = lax.broadcasted_iota(jnp.int32, (1, 256), 1) // 64
    small_links[DIAG].got(gsm.at[DIAG])
    small_links[ACROSS].got(gsm.at[ACROSS])

    def attend(row, pair):
        same = as_col(pair) == as_row(pair)
        keys = proj[row, :, 256:512]
        values = proj[row, :, 512:768]
        queries = proj[row, :, 0:256]
        t2[...] = jnp.zeros_like(t2)

        def head(k):
            mine = head_of == k
            q_head = jnp.where(mine, queries, jnp.zeros_like(queries))
            scores = jnp.where(same, mm_nt(q_head, keys) * 0.125, -1e9)
            weights = jnp.exp(scores - jnp.max(scores, axis=-1, keepdims=True))
            low_probs = (weights / jnp.sum(weights, axis=-1, keepdims=True)).astype(BF)
            pr[row * 4 + k] = low_probs
            t2[...] += mm(low_probs, jnp.where(mine, values, jnp.zeros_like(values)))

        each(4, head, HEAD_UNROLL)
        return t2[...].astype(BF)

    att_links = []
    my_cols = part(256 * g, 256)
    for rel in range(3):
        pair = sm[q, other_c, 18:20, :] if rel == TWIN else gsm[rel, 18:20, :]
        asend[rel] = attend(rel_g[rel], pair)
        att_links.append(Link().send(asend.at[rel], att.at[:, my_cols], rel_dev[rel]))
        if rel == DIAG:
            gather_up.second()
            for d in range(4):
                emb_y[d].sent()
            for d in (1, 2, 3):
                emb_z[d].sent()
            gather_dn = Gather(
                wdn.at[:, :, 0:512], w_down.at[part(g * h, h), 0:512],
                w_down.at[part((2 * x + other_c) * h, h), 0:512], h,
            )
            gather_dn_y.along()
        if rel == ACROSS:
            gather_dn_y.cross()
    att[:, my_cols] = attend(g, small[18:20, :])
    gather_dn.own()
    group_out.hop()
    gather_up.near()
    gather_up.last()
    group_out.got_twin()
    group_out.got_diag()
    for rel in (TWIN, ACROSS, DIAG):
        att_links[rel].got(att.at[:, part(256 * rel_g[rel], 256)])

    def out_block(k):
        at = part(k * 256, 256)
        rmid[:, at] = rin[:, at] + mm(att[...], wout[k].reshape(1024, 256)) + vec[3:4, at]

    each(4, out_block)

    def second_norm(at):
        n, _ = norm_parts(rmid[at, :])
        nb[g, at, :] = (n * vec[4:5, :] + vec[5:6, :]).astype(BF)

    each_rows(256, 32, second_norm)
    nb_across = Link().send(nb.at[g], nb.at[g], across)
    nb_twin = Link().send(nb.at[g], nb.at[g], twin)
    nb_pass = Link()
    group_gd.got_twin()
    group_gd.got_diag()

    bup[...] = jnp.zeros_like(bup)
    for k in range(4):
        bup[0:1, :] += jnp.where(g == k, vec[7 + k : 8 + k, :], 0.0)

    def ff_hidden(row):
        def block(k):
            at = part(k * 256, 256)
            t2[...] = mm(nb[row], wup[:, :, at].reshape(1024, 256)) + bup[0:1, at]

            def chunk(rows_at):
                pre = t2[rows_at, :]
                cdf = 0.5 + 0.5 * lax.erf(pre * 0.7071067811865476)
                pdf = jnp.exp(-0.5 * pre * pre) * 0.3989422804014327
                t2[rows_at, :] = pre * cdf
                ga[row, rows_at, at] = (cdf + pre * pdf).astype(BF)

            each_rows(256, 32, chunk)
            hid[pl.ds(2 * row, 2), :, at] = t2[...].astype(BF).reshape(2, 128, 256)

        each(4, block)

    def ff_grad(row):
        def block(k):
            at = part(k * 256, 256)
            grad = mm_nt(gd[row], wdn[pl.ds(2 * k, 2)].reshape(256, 1024))
            ga_low = (grad * ga[row, :, at].astype(F32)).astype(BF)
            ga[row, :, at] = ga_low
            bup[1:2, at] += jnp.sum(ga_low.astype(F32), axis=0, keepdims=True)

        each(4, block)

    gather_dn.second()
    gather_up.finish()
    ff_hidden(g)
    gather_dn.near()
    gather_dn.last()
    gather_dn_y.second()
    nb_twin.got(nb.at[rel_g[TWIN]])
    ff_hidden(rel_g[TWIN])
    nb_across.got(nb.at[rel_g[ACROSS]])
    nb_pass.send(nb.at[rel_g[ACROSS]], nb.at[rel_g[ACROSS]], twin)
    ff_hidden(rel_g[ACROSS])
    nb_pass.got(nb.at[rel_g[DIAG]])
    ff_hidden(rel_g[DIAG])

    class GroupSum:
        def __init__(self, sends, gets, partial, puts=None, temp=None):
            self.sends, self.gets, self.partial = sends, gets, partial
            self.temp = t1 if temp is None else temp
            self.puts = gets if puts is None else puts

        def first(self):
            self.partial(rel_g[DIAG], self.sends[0])
            self.a = Link().send(self.sends[0], self.puts[0], twin)

        def second(self):
            self.partial(rel_g[ACROSS], self.temp)
            self.a.got(self.gets[0])

            def chunk(at):
                self.sends[1][at, :] = (
                    self.temp[at, :] + self.gets[0][at, :].astype(F32)
                ).astype(BF)

            each_rows(256, 32, chunk, 2)

        def second_send(self):
            self.b = Link().send(self.sends[1], self.puts[1], across)

        def third(self):
            self.partial(rel_g[TWIN], self.sends[2])
            self.c = Link().send(self.sends[2], self.puts[2], twin)

        def own(self, into):
            self.partial(g, into)
            self.into = into

        def total(self):
            self.c.got(self.gets[2])
            self.b.got(self.gets[1])

        def rows(self, at):
            return (
                self.into[at, :].astype(F32)
                + self.gets[1][at, :].astype(F32)
                + self.gets[2][at, :].astype(F32)
            )

        def release(self):
            for link in (self.a, self.b, self.c):
                link.sent()

    def slots(ref, places):
        return [ref.at[place] for place in places]

    def nb_partial(row, into):
        def block(k):
            into[:, part(k * 256, 256)] = mm_nt(
                ga[row], wup[pl.ds(2 * k, 2)].reshape(256, 1024)
            ).astype(into.dtype)

        each(4, block, 2)

    def out_partial(row, into):
        def block(k):
            at = part(k * 256, 256)
            into[:, at] = mm(
                hid[pl.ds(2 * row, 2)].reshape(256, 1024), wdn[:, :, at].reshape(1024, 256)
            ).astype(into.dtype)

        each(4, block, 2)

    class Scatter:
        def __init__(self, grad, y_buf, z_buf, final, height):
            self.grad, self.y_buf, self.z_buf, self.final, self.height = (
                grad, y_buf, z_buf, final, height,
            )

        def chunks(self, body):
            if self.height is None:
                each(2, body, 1)
            else:
                each_rows(2 * self.height, 32, body, 1)

        def half(self, core):
            if self.height is None:
                return self.grad.at[q, core]
            return self.grad.at[q, part(core * self.height, self.height)]

        def start(self, count=4):
            even = lax.rem(z, 2) == 0
            self.goals = (
                jnp.where(even, 3, 0), jnp.where(even, 1, 2), lax.rem(z + 2, 4), z,
            )
            self.y_links = []
            self.z_links = [Link() for _ in range(4)]
            self.more(count)

        def more(self, count=1):
            for _ in range(count):
                e = len(self.y_links)
                self.y_links.append(
                    Link().send(self.grad.at[2 * self.goals[e] + 1 - y], self.y_buf.at[e], pair_y)
                )

        def add_y(self, e):
            self.y_links[e].got(self.y_buf.at[e])
            block = 2 * self.goals[e] + y

            def chunk(at):
                self.grad[block, at] = (
                    self.grad[block, at].astype(F32) + self.y_buf[e, at].astype(F32)
                ).astype(BF)

            self.chunks(chunk)
            return self.grad.at[block]

        def end_to_end(self):
            ref = self.add_y(0)
            self.z_links[0].send(
                ref, self.z_buf.at[0], (x, (z + 1 - 2 * lax.rem(z, 2)) * 4 + y * 2 + c)
            )

        def near(self):
            ref = self.add_y(1)
            slot = jnp.where(inner, 2, 1)
            self.z_links[1].send(
                ref, self.z_buf.at[slot], (x, self.goals[1] * 4 + y * 2 + c),
                arrives=jnp.where(inner, self.z_links[2].at, self.z_links[1].at),
            )

        def second(self):
            ref = self.add_y(2)
            block = 2 * self.goals[2] + y

            def relayed():
                self.z_links[0].got(self.z_buf.at[0])

                def chunk(at):
                    self.grad[block, at] = (
                        self.grad[block, at].astype(F32) + self.z_buf[0, at].astype(F32)
                    ).astype(BF)

                self.chunks(chunk)

            pl.when(inner)(relayed)
            self.z_links[3].send(ref, self.z_buf.at[3], dev(0, 2, 0, 0))

        def own(self):
            self.add_y(3)

        def middle(self):
            self.end_to_end()
            self.near()
            self.second()
            self.own()

        def last(self):
            def summed(slots):
                def run():
                    for slot in slots:
                        self.z_links[slot].got(self.z_buf.at[slot])

                    def chunk(at):
                        total = self.grad[q, at].astype(F32)
                        for slot in slots:
                            total += self.z_buf[slot, at].astype(F32)
                        self.grad[q, at] = total.astype(BF)

                    self.chunks(chunk)

                return run

            pl.when(inner)(summed((1, 2, 3)))
            pl.when(outer)(summed((0, 3)))
            self.f_links = []
            for rel in range(3):
                core = lax.rem(c + FLIPS[rel][1], 2)
                self.f_links.append(
                    Link().send(
                        self.half(core),
                        self.final.at[g],
                        rel_dev[rel],
                    )
                )
            self.final[g] = self.half(c)[...]

        def finish(self):
            for rel in range(3):
                self.f_links[rel].got(self.final.at[rel_g[rel]])

    scatter_dn = Scatter(g_dn, y_dn, z_dn, f_dn, h)
    scatter_up = Scatter(hid, y_up, z_up, f_up, h)
    sum_out = GroupSum(slots(xs, (3, 4, 5)), slots(xr, (3, 4, 5)), out_partial)

    def dn_block(k):
        at = part(k * 256, 256)
        lhs = hid[:, :, at].reshape(1024, 256)
        g_dn[pl.ds(2 * k, 2)] = mm_tn(lhs, gd[...].reshape(1024, 1024)).astype(BF).reshape(
            2, 128, 1024
        )

    each(4, dn_block, 1)
    scatter_dn.start()
    gather_dn.finish()
    gather_dn_y.finish()
    sum_nb = GroupSum(slots(xs, (0, 1, 2)), slots(xr, (0, 1, 2)), nb_partial)
    ff_grad(rel_g[DIAG])
    sum_nb.first()
    ff_grad(rel_g[ACROSS])
    sum_nb.second()
    sum_nb.second_send()
    ff_grad(rel_g[TWIN])
    sum_nb.third()
    ff_grad(g)
    sum_out.first()
    sum_out.second()
    scatter_dn.end_to_end()
    sum_out.third()

    sum_out.own(act)

    def up_block(k):
        at = part(k * 256, 256)
        lhs = nb[:, :, at].reshape(1024, 256)
        hid[pl.ds(2 * k, 2)] = mm_tn(lhs, ga[...].reshape(1024, 1024)).astype(BF).reshape(
            2, 128, 1024
        )

    each(4, up_block, 1)
    scatter_up.start()

    scatter_dn.near()
    sum_nb.own(t1)
    sum_nb.total()

    def second_back(at):
        grad_nb = sum_nb.rows(at)
        n, rstd = norm_parts(rmid[at, :])
        vg[4:5, :] += jnp.sum(grad_nb * n, axis=0, keepdims=True)
        vg[5:6, :] += jnp.sum(grad_nb, axis=0, keepdims=True)
        mid = gd[g, at, :].astype(F32) + norm_back(grad_nb * vec[4:5, :], n, rstd)
        gmid[at, :] = mid
        low_mid = mid.astype(BF)
        gatt[1, at, :] = low_mid
        vg[3:4, :] += jnp.sum(low_mid.astype(F32), axis=0, keepdims=True)

    each_rows(256, 32, second_back)

    def grad_o_part(to_g):
        total = jnp.zeros((256, 256), F32)
        for k in range(4):
            total += mm_nt(
                gatt[1, :, 256 * k : 256 * k + 256], wout[k, pl.ds(2 * to_g, 2)].reshape(256, 256)
            )
        return total.astype(BF)

    for link in (nb_pass, nb_across, nb_twin, group_gd.second):
        link.sent()
    go_links = []
    for rel in range(3):
        att_links[rel].sent()
        asend[rel] = grad_o_part(rel_g[rel])
        go_links.append(Link().send(asend.at[rel], go.at[g], rel_dev[rel]))
    go[g] = grad_o_part(g)

    def wog_partial(k, into):
        def block(j):
            at = part(256 * j, 256)
            into[:, at] = mm_tn(att[:, at], gatt[1, :, part(256 * k, 256)]).astype(into.dtype)

        each(4, block, 1)

    sum_nb.release()
    scatter_dn.second()
    for rel in (TWIN, ACROSS, DIAG):
        go_links[rel].got(go.at[rel_g[rel]])
    sum_wog = GroupSum(
        slots(gd, rel_g), slots(nb, rel_g), wog_partial, slots(nb, (rel_g[ACROSS], g, g))
    )
    sum_wog.first()
    sum_wog.second()
    sum_wog.second_send()
    sum_wog.third()
    sum_wog.own(nb.at[g])

    def attend_back(row):
        keys = proj[row, :, 256:512]
        values = proj[row, :, 512:768]
        queries = proj[row, :, 0:256]
        grad_rows = go[row]
        zero = jnp.zeros_like(keys)
        for buf in (t2, t3, t4):
            buf[...] = jnp.zeros_like(buf)

        def head(k):
            mine = head_of == k
            probs = pr[row * 4 + k]
            g_head = jnp.where(mine, grad_rows, zero)
            t4[...] += mm_tn(probs, g_head)
            grad_p = mm_nt(g_head, values)
            wide = probs.astype(F32)
            grad_s = wide * (grad_p - jnp.sum(grad_p * wide, axis=-1, keepdims=True))
            low_s = (grad_s * 0.125).astype(BF)
            t2[...] += mm(low_s, jnp.where(mine, keys, zero))
            t3[...] += mm_tn(low_s, jnp.where(mine, queries, zero))

        each(4, head, HEAD_UNROLL)
        proj[row, :, 0:256] = t2[...].astype(BF)
        proj[row, :, 256:512] = t3[...].astype(BF)
        proj[row, :, 512:768] = t4[...].astype(BF)

    def na_partial(row, into):
        def block(k):
            into[:, part(k * 256, 256)] = mm_nt(
                proj[row], wqkv[pl.ds(2 * k, 2)].reshape(256, 768)
            ).astype(into.dtype)

        each(4, block)

    sum_na = GroupSum(slots(xs, (0, 1, 2)), slots(xr, (0, 1, 2)), na_partial)
    scatter_dn.own()
    attend_back(rel_g[DIAG])
    sum_na.first()
    scatter_up.end_to_end()
    attend_back(rel_g[ACROSS])
    sum_na.second()
    sum_na.second_send()
    attend_back(rel_g[TWIN])
    sum_na.third()
    scatter_up.near()
    sum_wog.total()
    scatter_out = Scatter(g_out, y_out, z_out, f_out, h)
    for j in range(4):
        at = slice(256 * j, 256 * j + 256)
        g_out[2 * j : 2 * j + 2] = (
            nb[g, :, at].astype(F32) + nb[rel_g[ACROSS], :, at].astype(F32)
            + nb[rel_g[TWIN], :, at].astype(F32)
        ).astype(BF).reshape(2, 128, 256)
    scatter_out.start()
    attend_back(g)
    sum_na.own(t1)

    scatter_qkv = Scatter(g_qkv, y_qkv, z_qkv, f_qkv, h)
    scatter_in = Scatter(g_in, y_in, z_in, f_in, None)

    def qkv_block(k):
        at = part(k * 256, 256)
        lhs = na[:, :, at].reshape(1024, 256)
        g_qkv[pl.ds(2 * k, 2)] = mm_tn(lhs, proj[...].reshape(1024, 768)).astype(BF).reshape(
            2, 128, 768
        )

    each(4, qkv_block)
    scatter_qkv.start()
    scatter_up.second()

    sum_na.total()

    def first_back(at):
        grad_na = sum_na.rows(at)
        n, rstd = norm_parts(rin[at, :])
        vg[1:2, :] += jnp.sum(grad_na * n, axis=0, keepdims=True)
        vg[2:3, :] += jnp.sum(grad_na, axis=0, keepdims=True)
        low_in = (gmid[at, :] + norm_back(grad_na * vec[1:2, :], n, rstd)).astype(BF)
        gatt[0, at, :] = low_in
        vg[0:1, :] += jnp.sum(low_in.astype(F32), axis=0, keepdims=True)

    each_rows(256, 32, first_back)
    for k in range(4):
        vg[7 + k : 8 + k, :] = jnp.where(g == k, bup[1:2, :], 0.0)
    for j in range(8):
        vq[j % 2, j // 2] = vg[:, 128 * j : 128 * j + 128]
    vy_link = Link().send(vq.at[1 - y], vgy, pair_y)

    grad_scaled = jnp.zeros((256, 256), F32)
    for k in range(4):
        grad_scaled += mm_nt(gatt[0, :, 256 * k : 256 * k + 256], win_mat(k))
    level = as_col(small[20:22, :])
    scale_in = lax.rsqrt(1.0 + level * level)
    ngrad[...] = grad_scaled * (level * scale_in)
    stores.append(moved(ngrad, ngrad_hbm))

    def set_at(other_x, other_y, other_core):
        return ((lax.rem(x + other_x, 2) * 2 + lax.rem(y + other_y, 2)) * 2 + lax.rem(c + other_core, 2)) * 4

    home = tok.at[set_at(0, 0, 0) + z]
    tok[set_at(0, 0, 0) + z] = (grad_scaled * scale_in).astype(BF)
    steps = {"own": z, "second": far(2), "near": jnp.where(z < 2, far(3), far(1)), "last": jnp.where(z < 2, far(1), far(3))}

    class Line:
        def __init__(self, ref, first):
            self.first = first
            self.links = {
                d: Link().send(ref, ref, dev(0, d, 0, 0), only={1: z != 3, 3: z != 0}.get(d))
                for d in (2, 1, 3)
            }

        def spot(self, step):
            return self.first + steps[step]

        def got(self, step):
            ref = tok.at[self.spot(step)]
            one, three = self.links[1].at, self.links[3].at
            if step == "second":
                self.links[2].got(ref)
                Link().send(ref, ref, relay_to, only=inner, arrives=jnp.where(z == 2, three, one))
            elif step == "near":
                arrived(jnp.where(z < 2, three, one), ref)
            else:
                arrived(jnp.where(z < 2, one, three), ref)
            return self.spot(step)

    line_own = Line(home, set_at(0, 0, 0))
    tok_x = {}
    by_y = ("own", "second")
    tok_y = {}
    tok_t = {}

    def to_twin(spot, own_plane, key):
        tok_t[own_plane, key] = Link().send(tok.at[spot], tok.at[spot], twin)

    tok_x[0, 0] = Link().send(home, home, across)
    tok_y["own"] = Link().send(home, home, pair_y)
    to_twin(set_at(0, 0, 0) + z, True, (0, "own"))
    sum_out.second_send()

    def wig_partial(k, into):
        into[...] = mm_tn(sc[g], gatt[0, :, part(256 * k, 256)]).astype(into.dtype)

    sum_wig = GroupSum(
        slots(pr, (0, 1, 2)), slots(go, rel_g), wig_partial, slots(go, (rel_g[ACROSS], g, g)), t2
    )
    sum_wig.first()
    scatter_out.end_to_end()
    sum_wig.second()
    sum_wig.second_send()
    sum_wig.third()
    sum_wig.own(t3)
    scatter_dn.last()

    beside = set_at(1, 0, 0) + z
    tok_x[0, 0].got(tok.at[beside])
    line_beside = Line(tok.at[beside], set_at(1, 0, 0))
    to_twin(beside, False, (0, "own"))
    tok_x[1, "own"] = Link().send(tok.at[beside], tok.at[beside], pair_y)

    def tok_from_z(step):
        spot = line_own.got(step)
        tok_y[step] = Link().send(tok.at[spot], tok.at[spot], pair_y)
        to_twin(spot, True, (0, step))

    def tok_from_y(step):
        spot = set_at(0, 1, 0) + steps[step]
        tok_y[step].got(tok.at[spot])
        if step not in by_y:
            tok_x[1, step] = Link().send(tok.at[spot], tok.at[spot], across)
        to_twin(spot, True, (1, step))

    def tok_beside(step):
        spot = line_beside.got(step)
        to_twin(spot, False, (0, step))
        if step in by_y:
            tok_x[1, step] = Link().send(tok.at[spot], tok.at[spot], pair_y)

    def tok_from_x(step):
        spot = set_at(1, 1, 0) + steps[step]
        tok_x[1, step].got(tok.at[spot])
        to_twin(spot, False, (1, step))

    smx_link.got(smx)
    for other_x in (0, 1):
        for yy in (0, 1):
            for core in (0, 1):
                source = sm if other_x == 0 else smx
                for zz in range(4):
                    idr[(other_x * 2 + yy) * 2 + core : (other_x * 2 + yy) * 2 + core + 1, 256 * zz : 256 * zz + 256] = (
                        as_row(source[2 * zz + yy, core, 16:18, :])
                    )

    tile = 400
    base = (f * rows_here).astype(F32)
    tile_row = lax.broadcasted_iota(jnp.int32, (tile, 1024), 0).astype(F32)

    def table_add(other_x, other_y, other_core, begin):
        spot = set_at(other_x, other_y, other_core)
        row = (other_x * 2 + lax.rem(y + other_y, 2)) * 2 + lax.rem(c + other_core, 2)
        ids = idr[pl.ds(row, 1), :] - base

        def block(k):
            at = part(k * tile, tile)
            hit = jnp.where(tile_row == ids - (k * tile).astype(F32), 1.0, 0.0).astype(BF)
            add = mm(hit, tok[pl.ds(spot, 4)].reshape(1024, 256))
            if begin:
                tgrad[at, :] = add
            else:
                tgrad[at, :] += add

        each(rows_here // tile, block, 1)

    def twin_set(from_x, other_y):
        for step in steps:
            tok_t[from_x == 0, (other_y, step)].got(tok.at[set_at(from_x, other_y, 1) + steps[step]])

    tok_from_z("second")
    tok_from_z("near")
    scatter_up.own()
    scatter_qkv.end_to_end()
    tok_from_z("last")
    tok_beside("second")
    table_add(0, 0, 0, True)
    scatter_up.last()
    scatter_out.near()
    tok_from_y("own")
    scatter_qkv.near()
    twin_set(0, 0)
    table_add(0, 0, 1, False)
    sum_wig.total()
    g_in[...] = (
        t3[...] + go[rel_g[ACROSS]].astype(F32) + go[rel_g[TWIN]].astype(F32)
    ).astype(BF).reshape(8, 2, 16, 256)
    scatter_in.start()
    vy_link.got(vgy)
    vq[y] = vq[y] + vgy[...]
    vz_links = [
        Link().send(vq.at[y, to(d)], vgz.at[d - 1], dev(0, d, 0, 0)) for d in (1, 2, 3)
    ]
    tok_from_y("second")
    scatter_qkv.second()
    tok_from_y("near")
    scatter_qkv.own()
    scatter_out.second()
    scatter_out.own()
    tok_from_y("last")
    table_add(0, 1, 0, False)
    tok_beside("near")
    tok_beside("last")
    table_add(1, 0, 0, False)
    twin_set(0, 1)
    table_add(0, 1, 1, False)
    scatter_in.middle()
    scatter_qkv.last()
    for d in (1, 2, 3):
        vz_links[d - 1].got(vgz.at[d - 1])
    vtot = vq[y, z] + vgz[0] + vgz[1] + vgz[2]
    vgf[3] = vtot
    vf_links = [Link().send(vgf.at[3], vgf.at[rel], rel_dev[rel]) for rel in range(3)]
    twin_set(1, 0)
    table_add(1, 0, 1, False)
    scatter_out.last()
    scatter_in.last()
    sum_out.total()

    def out_rows(at):
        whole = rmid[at, :] + sum_out.rows(at) + vec[6:7, :]
        act[at, :] = (whole * lives[at, 0:1]).astype(BF)

    each_rows(256, 32, out_rows)
    stores.append(moved(act, act_hbm))
    sum_out.release()

    for step in steps:
        tok_from_x(step)
    table_add(1, 1, 0, False)
    twin_set(1, 1)
    table_add(1, 1, 1, False)

    def table_rows(at):
        values = tp[c, at, :].astype(F32)
        r = lax.rsqrt(jnp.mean(values * values, axis=1, keepdims=True) + norm_eps)
        row_grad = tgrad[at, :]
        slope = jnp.mean(row_grad * values, axis=1, keepdims=True)
        tgrad[at, :] = r * row_grad - values * (r * r * r * slope)

    for k in range(rows_here // 200):
        at = pl.ds(k * 200, 200)
        table_rows(at)
        stores.append(moved(tgrad.at[at], tgrad_hbm.at[at]))

    for rel in range(3):
        vf_links[rel].got(vgf.at[rel])
    vout[...] = vgf[0] + vgf[1] + vgf[2] + vgf[3]
    for scatter in (scatter_dn, scatter_up, scatter_qkv, scatter_out, scatter_in):
        scatter.finish()
    for k, (src, dst) in enumerate(((f_in, f_in_hbm), (f_qkv, f_qkv_hbm), (f_out, f_out_hbm), (f_up, f_up_hbm), (f_dn, f_dn_hbm), (vout, vout_hbm))):
        stores.append(moved(src, dst))
    for link in list(pending):
        link.sent()
    for store in stores:
        store.wait()


def finish_kernel(
    act_in, ngrad_in, tgrad_in, vout, f_in_hbm, f_qkv_hbm, f_out_hbm, f_up_hbm, f_dn_hbm,
    act, ngrad, tgrad, w_in_hbm, b_in, gain_a, shift_a, w_qkv_hbm, w_out_hbm, b_out, gain_b, shift_b,
    w_up_hbm, b_up, w_dn_hbm, b_dn,
    act_v, ngrad_v, tgrad_v, f_in, f_qkv, f_out, f_up, f_dn, w_in, w_qkv, w_out, w_up, w_dn, sems,
):
    count = [0]

    def moved(src, dst):
        copy = pltpu.make_async_copy(src, dst, sems.at[count[0]])
        count[0] += 1
        copy.start()
        return copy

    load_up = moved(f_up_hbm, f_up)
    load_dn = moved(f_dn_hbm, f_dn)
    load_qkv = moved(f_qkv_hbm, f_qkv)
    load_out = moved(f_out_hbm, f_out)
    load_in = moved(f_in_hbm, f_in)
    passed = [(act_in, act_v, act), (ngrad_in, ngrad_v, ngrad)]
    tile = tgrad_v.shape[0] // 5
    for k in range(5):
        at = pl.ds(k * tile, tile)
        passed.append((tgrad_in.at[at], tgrad_v.at[at], tgrad.at[at]))
    passed = [(moved(src, via), via, dst) for src, via, dst in passed]
    stores = []
    c = lax.rem(lax.axis_index("fsdp"), 2)
    rows = jnp.where(c == 0, vout[...], pltpu.roll(vout[...], 64, 1))
    for k, ref in enumerate((b_in, gain_a, shift_a, b_out, gain_b, shift_b, b_dn)):
        ref[...] = rows[k, 0:64]
    for k in range(4):
        b_up[64 * k : 64 * k + 64] = rows[7 + k, 0:64]
    h = w_out.shape[0]
    low_half = lax.broadcasted_iota(jnp.int32, (h, 128), 1) < 64
    load_up.wait()
    for shard in range(16):
        at = slice(128 * (shard // 2), 128 * (shard // 2) + 128)
        for half in (0, 1):
            first, second = f_up[2 * half, :, at].astype(F32), f_up[2 * half + 1, :, at].astype(F32)
            if shard % 2 == 0:
                both = jnp.where(low_half, first, pltpu.roll(second, 64, 1))
            else:
                both = jnp.where(low_half, pltpu.roll(first, 64, 1), second)
            w_up[:, 256 * shard + 128 * half : 256 * shard + 128 * half + 128] = both
    stores.append(moved(w_up, w_up_hbm))
    for load, via, dst in passed:
        load.wait()
        stores.append(moved(via, dst))
    load_dn.wait()
    for g in range(4):
        w_dn[h * g : h * g + h, :] = f_dn[g].astype(F32)
    stores.append(moved(w_dn, w_dn_hbm))
    load_qkv.wait()
    for g in range(4):
        for n in range(3):
            w_qkv[:, 1024 * n + 256 * g : 1024 * n + 256 * g + 256] = f_qkv[
                g, :, 256 * n : 256 * n + 256
            ].astype(F32)
    stores.append(moved(w_qkv, w_qkv_hbm))
    load_out.wait()
    load_in.wait()
    for g in range(4):
        at = slice(256 * g, 256 * g + 256)
        w_in[:, at] = f_in[g].astype(F32)
        w_out[:, at] = f_out[g].astype(F32)
    stores.append(moved(w_out, w_out_hbm))
    stores.append(moved(w_in, w_in_hbm))
    for store in stores:
        store.wait()


def fused_shards(
    token_ids, seq_lengths, noise, noise_level, table, w_in, b_in, gain_first, shift_first, w_qkv,
    w_out, b_out, gain_second, shift_second, w_up, b_up, w_down, b_down, cotangent,
):
    raw = (
        token_ids, seq_lengths, noise_level, b_in, gain_first, shift_first, b_out, gain_second,
        shift_second, b_down, b_up,
    )
    vmem = pl.BlockSpec(memory_space=pltpu.VMEM)
    hbm = pl.BlockSpec(memory_space=pl.ANY)

    def shape(*dims, dtype=BF):
        return jax.ShapeDtypeStruct(dims, dtype)

    rows_here = table.shape[0]
    padded = -(-rows_here // 256) * 256
    outs = [
        shape(256, 1024), shape(256, 256, dtype=F32), shape(rows_here, 256, dtype=F32),
        shape(16, 128, dtype=F32), shape(4, 16, 256), shape(4, 64, 768), shape(4, 64, 256),
        shape(4, 64, 1024), shape(4, 64, 1024),
    ]

    held = [pltpu.VMEM(v.shape, v.dtype) for v in raw] + [pltpu.VMEM((24, 128), F32)]
    held += [pltpu.VMEM(v.shape, v.dtype) for v in (noise, w_in, w_qkv, w_out, w_up, w_down, cotangent)]
    held += [pltpu.VMEM(v.shape, v.dtype) for v in outs]

    def bf(*dims):
        return pltpu.VMEM(dims, BF)

    def fl(*dims):
        return pltpu.VMEM(dims, F32)

    scratch = [
        fl(8, 2, 24, 128), fl(8, 2, 24, 128), fl(2, 24, 128),
        fl(16, 1024), fl(16, 1024), fl(2, 4, 16, 128), fl(4, 16, 128), fl(3, 16, 128),
        fl(4, 16, 128), fl(8, 1024), fl(256, 128), fl(8, 1024),
        bf(2, padded, 256), bf(32, 256, 256), bf(4, 256, 256), bf(4, 8, 2, 16, 256),
        bf(8, 128, 768), bf(4, 8, 128, 256), bf(8, 128, 1024), bf(8, 128, 1024),
        bf(2, 16, 256), bf(64, 768), bf(64, 256), bf(64, 1024),
        fl(256, 1024), fl(256, 1024), fl(256, 1024), fl(256, 1024),
        fl(256, 256), fl(256, 256), fl(256, 256),
        bf(4, 256, 1024), bf(4, 256, 768), bf(16, 256, 256), bf(256, 1024), bf(3, 256, 256),
        bf(4, 256, 1024), bf(4, 256, 1024), bf(8, 128, 1024), bf(4, 256, 1024),
        bf(6, 256, 1024), bf(6, 256, 1024), bf(2, 256, 1024), bf(4, 256, 256),
        bf(8, 2, 16, 256), bf(8, 128, 768), bf(8, 128, 256), bf(8, 128, 1024),
        bf(4, 2, 16, 256), bf(4, 128, 768), bf(4, 128, 256), bf(4, 128, 1024), bf(4, 128, 1024),
        bf(4, 2, 16, 256), bf(4, 128, 768), bf(4, 128, 256), bf(4, 128, 1024), bf(4, 128, 1024),
        pltpu.SemaphoreType.DMA((SEM_COUNT,)), pltpu.SemaphoreType.DMA((SEM_COUNT,)),
        pltpu.SemaphoreType.DMA((45,)),
    ]
    parts = pl.pallas_call(
        layer_kernel,
        out_shape=outs,
        in_specs=[hbm] * 19,
        out_specs=[hbm] * len(outs),
        scratch_shapes=held + scratch,
        compiler_params=pltpu.CompilerParams(
            collective_id=0, has_side_effects=True, vmem_limit_bytes=VMEM_LIMIT
        ),
        cost_estimate=pl.CostEstimate(flops=40 * 10**9, bytes_accessed=30 * 10**6, transcendentals=0),
    )(*raw, noise, table, w_in, w_qkv, w_out, w_up, w_down, cotangent)
    f32 = lambda a: jax.ShapeDtypeStruct(a.shape, F32)
    finals = [
        outs[0], outs[1], outs[2], f32(w_in), f32(b_in), f32(gain_first), f32(shift_first),
        f32(w_qkv), f32(w_out), f32(b_out), f32(gain_second), f32(shift_second), f32(w_up),
        f32(b_up), f32(w_down), f32(b_down),
    ]
    return tuple(
        pl.pallas_call(
            finish_kernel,
            out_shape=finals,
            in_specs=[hbm] * 3 + [vmem] + [hbm] * 5,
            out_specs=[vmem if len(v.shape) == 1 else hbm for v in finals],
            scratch_shapes=[pltpu.VMEM(v.shape, v.dtype) for v in outs[:3] + outs[4:]]
            + [pltpu.VMEM(finals[k].shape, F32) for k in (3, 7, 8, 12, 14)]
            + [pltpu.SemaphoreType.DMA((24,))],
            compiler_params=pltpu.CompilerParams(vmem_limit_bytes=VMEM_LIMIT),
        )(*parts)
    )


def solution(mesh):
    in_specs = (
        P(("dp", "fsdp")),
        P(("dp", "fsdp"), None),
        P(("dp", "fsdp"), None),
        P(("dp", "fsdp")),
        P("fsdp", None),
        P("fsdp", None),
        P("fsdp"),
        P("fsdp"),
        P("fsdp"),
        P("fsdp", None),
        P("fsdp", None),
        P("fsdp"),
        P("fsdp"),
        P("fsdp"),
        P("fsdp", None),
        P("fsdp"),
        P("fsdp", None),
        P("fsdp"),
        P(("dp", "fsdp"), None),
    )
    out_specs = (
        P(("dp", "fsdp"), None),
        P(("dp", "fsdp"), None),
        P("fsdp", None),
        P("fsdp", None),
        P("fsdp"),
        P("fsdp"),
        P("fsdp"),
        P("fsdp", None),
        P("fsdp", None),
        P("fsdp"),
        P("fsdp"),
        P("fsdp"),
        P("fsdp", None),
        P("fsdp"),
        P("fsdp", None),
        P("fsdp"),
    )
    fused = mesh.shape["dp"] == 2 and mesh.shape["fsdp"] == 16
    body = fused_shards if fused else shards
    return jax.shard_map(body, mesh=mesh, in_specs=in_specs, out_specs=out_specs, check_vma=False)
```
